32 devices in a mesh: stream: 4 (over y, core), batch: 8 (over z, x).
Axes of the slice: x: 2, y: 2, z: 4, core: 2. Of those that a mesh axis runs over, the one named last changes fastest.
Arguments:
- hidden_in: bfloat16 [2, 4, 1024, 768], P(None, 'stream', 'batch'), may hold values from -6 to 6
- norm1_gain: bfloat16 [768], P('batch'), may hold values from 0.5 to 1.5
- w_query: bfloat16 [768, 768], P('batch'), may hold values from -0.078125 to 0.078125
- w_key: bfloat16 [768, 768], P('batch'), may hold values from -0.078125 to 0.078125
- w_value: bfloat16 [768, 768], P('batch'), may hold values from -0.21875 to 0.21875
- w_out: bfloat16 [768, 768], P('batch'), may hold values from -1.25 to 1.25
- rel_table: bfloat16 [384], P('batch'), may hold values from -4 to 4
- norm2_gain: bfloat16 [768], P('batch'), may hold values from 0.5 to 1.5
- w_gate: bfloat16 [768, 2048], P('batch'), may hold values from -0.21875 to 0.21875
- w_up: bfloat16 [768, 2048], P('batch'), may hold values from -0.21875 to 0.21875
- w_down: bfloat16 [2048, 768], P('batch'), may hold values from -0.25 to 0.25
- norm3_gain: bfloat16 [768], P('batch'), may hold values from 0.5 to 1.5
- w_proj: bfloat16 [768, 128], P('batch'), may hold values from -0.21875 to 0.21875
- query_lengths: int32 [2, 2, 32], replicated, may hold values from 8 to 32, as said below
- keyword_request_mask: int32 [2, 2, 32], replicated, may hold values from 0 to 1
- targets: int32 [2, 2, 32], replicated, may hold values from 0 to 7
- candidates: int32 [2, 2, 8, 1024, 8], P(None, None, 'batch'), may hold values from 0 to 127
Outputs:
- vectors: bfloat16 [2, 4, 1024, 128], P(None, 'stream', 'batch')
- grad_hidden: float32 [2, 4, 1024, 768], P(None, 'stream', 'batch')
- grad_norm1_gain: float32 [768], P('batch')
- grad_w_query: float32 [768, 768], P('batch')
- grad_w_key: float32 [768, 768], P('batch')
- grad_w_value: float32 [768, 768], P('batch')
- grad_w_out: float32 [768, 768], P('batch')
- grad_rel_table: float32 [384], P('batch')
- grad_norm2_gain: float32 [768], P('batch')
- grad_w_gate: float32 [768, 2048], P('batch')
- grad_w_up: float32 [768, 2048], P('batch')
- grad_w_down: float32 [2048, 768], P('batch')
- grad_norm3_gain: float32 [768], P('batch')
- grad_w_proj: float32 [768, 128], P('batch')
The draws below stay inside these ranges and needn't reach their ends.
Inputs may be any that keep to these rules, and one draw needn't show every extreme that they name: `query_lengths`: in every micro-batch and pair some query has exactly 32 tokens and some exactly 8. `targets`: documents are numbered by the batch index of the device that holds them. `candidates`: positions may repeat.
All inputs are finite; a program needn't handle non-finite values.
Results may differ from the reference program's by a relative error of at most 0.025.
Values may be sent and summed in bfloat16 or wider, within the bound.
No kernel may reach another device: no remote copies, remote signals or barrier semaphores. Data moves between devices by JAX's collectives and lax.ppermute only.
A program may use at most 192 MiB of HBM per device.

```python
import math
import jax
import jax.numpy as jnp
import numpy as np
from jax import lax

D = 768
H = 12
DH = 64
FF = 2048
BUCKETS = 32
MAX_DIST = 128
P_SIZE = 128
DLEN = 128
QLEN = 32
QMIN = 8
CANDS = 8
MICRO = 2
PAIRS = 2
QUERIES = 32
QTOK = 1024
N_STREAM = 4
N_BATCH = 8


def draw_query_lengths(key, part):
    key = jax.random.fold_in(key, 11)
    shape = (MICRO, PAIRS, QUERIES)
    lengths_drawn = jax.random.randint(jax.random.fold_in(key, 1), shape, QMIN, QLEN + 1)
    longest = jax.random.randint(jax.random.fold_in(key, 2), (MICRO, PAIRS, 1), 0, QUERIES)
    shortest = (longest + 1 + jax.random.randint(jax.random.fold_in(key, 3), (MICRO, PAIRS, 1), 0, QUERIES - 1)) % QUERIES
    slot_index = jnp.arange(QUERIES)[None, None, :]
    lengths_drawn = jnp.where(slot_index == longest, QLEN, lengths_drawn)
    return jnp.where(slot_index == shortest, QMIN, lengths_drawn).astype(jnp.int32)


def touch_ends(drawn, own_key, smallest, top_value):
    shape = drawn.shape
    index_at = [jax.random.randint(jax.random.fold_in(own_key, axis), (), 0, shape[axis]) for axis in range(len(shape))]
    drawn = drawn.at[tuple(index_at)].set(smallest)
    longest = shape.index(max(shape))
    index_at[longest] = (index_at[longest] + 1) % shape[longest]
    return drawn.at[tuple(index_at)].set(top_value)


def block_levels(rng, shape, cuts, least, top_value):
    factor_of, own = 1.0, jax.random.fold_in(rng, 6)
    for dim, shards_of in cuts:
        heights = jnp.exp(jax.random.uniform(jax.random.fold_in(own, dim), (shards_of,), jnp.float32, least / len(cuts), top_value / len(cuts)))
        factor_of = factor_of * jnp.repeat(heights, shape[dim] // shards_of).reshape([-1 if axis == dim else 1 for axis in range(len(shape))])
    return factor_of


def normal_values(key, shape, spread, most, cuts=(), held_as=jnp.bfloat16):
    result = spread * jax.random.normal(key, shape, jnp.float32)
    if cuts:
        result = result * block_levels(key, shape, cuts, -0.22, 0.18)
    return jnp.clip(result, -most, most).astype(held_as)


def setup_inputs(seed: int = 0) -> dict:
    key_list = jax.random.split(jax.random.key(seed), 18)
    return {
        "hidden_in": normal_values(key_list[0], (MICRO, N_STREAM, N_BATCH * DLEN, D), 1.0, 6.0, ((1, 4), (2, 8))),
        "norm1_gain": jnp.clip(1.0 + 0.1 * jax.random.normal(key_list[1], (D,), jnp.float32), 0.5, 1.5).astype(jnp.bfloat16),
        "w_query": normal_values(key_list[2], (D, H * DH), (D * 8) ** -0.5, 0.078125, ((0, 8),)),
        "w_key": normal_values(key_list[3], (D, H * DH), (D * 8) ** -0.5, 0.078125, ((0, 8),)),
        "w_value": normal_values(key_list[4], (D, H * DH), D ** -0.5, 0.21875, ((0, 8),)),
        "w_out": normal_values(key_list[5], (H * DH, D), (D // 32) ** -0.5, 1.25, ((0, 8),)),
        "rel_table": normal_values(key_list[6], (BUCKETS * H,), 1.0, 4.0, ((0, 8),)),
        "norm2_gain": jnp.clip(1.0 + 0.1 * jax.random.normal(key_list[7], (D,), jnp.float32), 0.5, 1.5).astype(jnp.bfloat16),
        "w_gate": normal_values(key_list[8], (D, FF), D ** -0.5, 0.21875, ((0, 8),)),
        "w_up": normal_values(key_list[9], (D, FF), D ** -0.5, 0.21875, ((0, 8),)),
        "w_down": normal_values(key_list[10], (FF, D), (FF // 4) ** -0.5, 0.25, ((0, 8),)),
        "norm3_gain": jnp.clip(1.0 + 0.1 * jax.random.normal(key_list[11], (D,), jnp.float32), 0.5, 1.5).astype(jnp.bfloat16),
        "w_proj": normal_values(key_list[12], (D, P_SIZE), D ** -0.5, 0.21875, ((0, 8),)),
        "query_lengths": draw_query_lengths(jax.random.fold_in(key_list[17], 71), 0),
        "keyword_request_mask": touch_ends(jax.random.randint(key_list[14], (MICRO, PAIRS, QUERIES), 0, 2), jax.random.fold_in(key_list[14], 1), 0, 1).astype(jnp.int32),
        "targets": touch_ends(jax.random.randint(key_list[15], (MICRO, PAIRS, QUERIES), 0, N_BATCH), jax.random.fold_in(key_list[15], 1), 0, N_BATCH - 1).astype(jnp.int32),
        "candidates": touch_ends(jax.random.randint(key_list[16], (MICRO, PAIRS, N_BATCH, QTOK, CANDS), 0, DLEN), jax.random.fold_in(key_list[16], 1), 0, DLEN - 1).astype(jnp.int32),
    }


@jax.custom_vjp
def low(v):
    return lax.optimization_barrier(v.astype(jnp.bfloat16)).astype(jnp.float32)

@jax.custom_vjp
def low_back(v):
    return v

def low_keep(v):
    return (low(v), None)

def low_pass(kept, grad):
    return (grad,)

def back_keep(v):
    return (v, None)

def back_low(kept, grad):
    return (low(grad),)
low.defvjp(low_keep, low_pass)
low_back.defvjp(back_keep, back_low)
EPSILON = 1e-06
HIGHEST = lax.Precision.HIGHEST

def distance_bucket(distance):
    half_count = BUCKETS // 2
    exact_count = half_count // 2
    if distance < exact_count:
        return distance
    grown = exact_count + int(math.floor(math.log(distance / exact_count) / math.log(MAX_DIST / exact_count) * (half_count - exact_count) + 1e-09))
    return min(grown, half_count - 1)

def offset_buckets(length):
    return np.array([distance_bucket(abs(offset)) + (BUCKETS // 2 if offset > 0 else 0) for offset in range(1 - length, length)])

def bucket_index(length):
    positions = np.arange(length)
    return offset_buckets(length)[positions[None, :] - positions[:, None] + length - 1]

def product_high(left, right):
    return jnp.dot(left, right, precision=HIGHEST, preferred_element_type=jnp.float32)

def rms_scale(values, gain):
    return values * lax.rsqrt(lax.optimization_barrier(jnp.mean(values * values, axis=-1, keepdims=True)) + EPSILON) * gain

def encoder(tokens, key_valid, params, length):
    gain_one, weight_q, weight_k, weight_v, weight_o, bias_table, gain_two, weight_g, weight_u, weight_d, gain_three, weight_p = params
    seq_count = tokens.shape[0] // length
    normed = low(rms_scale(tokens, gain_one))
    queries = low_back(low(product_high(normed, weight_q))).reshape(seq_count, length, H, DH)
    keys_all = low_back(low(product_high(normed, weight_k))).reshape(seq_count, length, H, DH)
    values_all = low_back(low(product_high(normed, weight_v))).reshape(seq_count, length, H, DH)
    position_bias = jnp.transpose(jnp.take(bias_table.reshape(BUCKETS, H), jnp.asarray(bucket_index(length)), axis=0), (2, 0, 1))
    scores = low_back(jnp.einsum('sqhd,skhd->shqk', queries, keys_all, precision=HIGHEST) + position_bias[None])
    scores = jnp.where(key_valid[:, None, None, :] > 0, scores, -1000000000.0)
    shifted = jnp.exp(scores - lax.optimization_barrier(jnp.max(scores, axis=-1, keepdims=True)))
    weights = shifted / lax.optimization_barrier(jnp.sum(shifted, axis=-1, keepdims=True))
    attended = jnp.einsum('shqk,skhd->sqhd', low(weights), values_all, precision=HIGHEST).reshape(tokens.shape[0], H * DH)
    attended = low_back(low(attended))
    first_sum = tokens + low_back(product_high(attended, weight_o))
    normed_two = low(rms_scale(first_sum, gain_two))
    gate_proj = low_back(product_high(normed_two, weight_g))
    up_proj = low_back(product_high(normed_two, weight_u))
    hidden = low(jax.nn.gelu(gate_proj, approximate=True) * up_proj)
    second_sum = first_sum + low_back(product_high(hidden, weight_d))
    normed_three = low(rms_scale(second_sum, gain_three))
    return low_back(low(product_high(normed_three, weight_p)))

def run_blocks(blocks, valid, params, length):
    stepper = jax.checkpoint(lambda block, marks: encoder(block, marks, params, length))

    def scan_step(running, element):
        return (running, stepper(element[0], element[1]))
    return lax.scan(scan_step, jnp.zeros((), jnp.float32), (blocks, valid))[1]

def smooth_best(query_vectors, doc_vectors, picked_slots):
    similarity = product_high(query_vectors, doc_vectors.T) * P_SIZE ** (-0.5)
    chosen = jnp.take_along_axis(similarity, picked_slots, axis=1)
    highest = lax.optimization_barrier(jnp.max(chosen, axis=1, keepdims=True))
    return (highest + jnp.log(lax.optimization_barrier(jnp.sum(jnp.exp(chosen - highest), axis=1, keepdims=True))))[:, 0]

def forward(floats, query_lengths, keyword_request_mask, targets, candidates):
    hidden = floats[0]
    params = floats[1:]
    per_device = DLEN // QLEN
    query_part = hidden[:, :PAIRS].reshape(-1, DLEN, D)
    doc_part = hidden[:, PAIRS:].reshape(-1, DLEN, D)
    length_rows = query_lengths.reshape(-1, per_device)
    query_valid = (jnp.arange(QLEN)[None, None, :] < length_rows[:, :, None]).astype(jnp.float32)
    doc_valid = jnp.ones((doc_part.shape[0], 1, DLEN), jnp.float32)
    query_vectors = run_blocks(query_part, query_valid, params, QLEN).reshape(MICRO, PAIRS, QTOK, P_SIZE)
    doc_vectors = run_blocks(doc_part, doc_valid, params, DLEN).reshape(MICRO, PAIRS, N_BATCH, DLEN, P_SIZE)
    loss_total = jnp.zeros((), jnp.float32)
    for slice_ordinal in range(MICRO):
        for request_passage_couple in range(PAIRS):
            pair_queries = query_vectors[slice_ordinal, request_passage_couple]

            def per_document(element):
                return smooth_best(pair_queries, element[0], element[1])
            best = lax.map(jax.checkpoint(per_document), (doc_vectors[slice_ordinal, request_passage_couple], candidates[slice_ordinal, request_passage_couple]))
            lengths_here = query_lengths[slice_ordinal, request_passage_couple]
            valid_here = (jnp.arange(QLEN)[None, :] < lengths_here[:, None]).astype(jnp.float32)
            match_strength = lax.optimization_barrier(jnp.sum(best.reshape(N_BATCH, QUERIES, QLEN) * valid_here[None], axis=2)) / lengths_here.astype(jnp.float32)[None, :]
            sharpness_divisor = jnp.where(keyword_request_mask[slice_ordinal, request_passage_couple] == 1, 0.05, 0.1)
            match_energies = match_strength.T / sharpness_divisor[:, None]
            highest = lax.optimization_barrier(jnp.max(match_energies, axis=1, keepdims=True))
            log_norm = highest[:, 0] + jnp.log(lax.optimization_barrier(jnp.sum(jnp.exp(match_energies - highest), axis=1)))
            target_indicator = (targets[slice_ordinal, request_passage_couple][:, None] == jnp.arange(N_BATCH)[None, :]).astype(jnp.float32)
            loss_total = loss_total + jnp.sum(log_norm - lax.optimization_barrier(jnp.sum(match_energies * target_indicator, axis=1)))
    vectors = jnp.concatenate([query_vectors.reshape(MICRO, PAIRS, N_BATCH * DLEN, P_SIZE), doc_vectors.reshape(MICRO, PAIRS, N_BATCH * DLEN, P_SIZE)], axis=1)
    return (loss_total, vectors)

def reference(hidden_in, norm1_gain, w_query, w_key, w_value, w_out, rel_table, norm2_gain, w_gate, w_up, w_down, norm3_gain, w_proj, query_lengths, keyword_request_mask, targets, candidates):
    floats = tuple((element.astype(jnp.float32) for element in (hidden_in, norm1_gain, w_query, w_key, w_value, w_out, rel_table, norm2_gain, w_gate, w_up, w_down, norm3_gain, w_proj)))

    def loss_of(*values_in):
        return forward(values_in, query_lengths, keyword_request_mask, targets, candidates)
    loss_total, pullback, vectors = jax.vjp(loss_of, *floats, has_aux=True)
    gradients = pullback(jnp.ones((), jnp.float32))
    return (vectors.astype(jnp.bfloat16), gradients[0], gradients[1], gradients[2], gradients[3], gradients[4], gradients[5], gradients[6], gradients[7], gradients[8], gradients[9], gradients[10], gradients[11], gradients[12])
```

```python
import functools
import math

import jax
import jax.numpy as jnp
import numpy as np
from jax import lax
from jax.experimental import pallas as pl
from jax.experimental.pallas import tpu as pltpu
from jax.sharding import PartitionSpec as P

H = 12
DH = 64
BUCKETS = 32
MAX_DIST = 128
DLEN = 128
QLEN = 32
GROUPS = DLEN // QLEN
MICRO = 2
ROWS = MICRO * DLEN
D = 768
FF = 2048
HALF = FF // 2
SHARDS = 8
PIECE_A = 208
PIECE_F = 576

EPSILON = 1e-06
HIGHEST = lax.Precision.HIGHEST
BF = jnp.bfloat16
F32 = jnp.float32
EVERY = ("stream", "batch")
MIB = 2**20


def distance_bucket(distance):
    half_count = BUCKETS // 2
    exact_count = half_count // 2
    if distance < exact_count:
        return distance
    grown = exact_count + int(
        math.floor(
            math.log(distance / exact_count)
            / math.log(MAX_DIST / exact_count)
            * (half_count - exact_count)
            + 1e-09
        )
    )
    return min(grown, half_count - 1)


def bucket_onehot():
    table = np.zeros((2 * DLEN, BUCKETS), np.float32)
    for o in range(2 * DLEN - 1):
        offset = o - (DLEN - 1)
        table[o, distance_bucket(abs(offset)) + (BUCKETS // 2 if offset > 0 else 0)] = 1.0
    return table


def norm_scale(values):
    return lax.rsqrt(jnp.mean(values * values, axis=-1, keepdims=True) + EPSILON)


def norm_backward(values, gain, grad):
    scale = norm_scale(values)
    pulled = gain * grad
    inner = jnp.mean(values * pulled, axis=-1, keepdims=True)
    back = scale * pulled - values * (scale * scale * scale * inner)
    return back, jnp.sum(grad * values * scale, axis=0, keepdims=True)


def dot(left, right):
    return jnp.dot(left, right, preferred_element_type=F32)


def dot_nt(left, right):
    return lax.dot_general(left, right, (((1,), (1,)), ((), ())), preferred_element_type=F32)


def dot_tn(left, right):
    return lax.dot_general(left, right, (((0,), (0,)), ((), ())), preferred_element_type=F32)


def steps(count, body):
    if count <= 16:
        for i in range(count):
            body(i)
    else:

        @pl.loop(0, count)
        def _(i):
            body(i)


VMEM = pl.BlockSpec(memory_space=pltpu.VMEM)
SMEM = pl.BlockSpec(memory_space=pltpu.SMEM)
ANY = pl.BlockSpec(memory_space=pl.ANY)


def call(kernel, name, ids, arrays, outs, scratch=(), limit=48, flops=0):
    shapes = [jax.ShapeDtypeStruct(s, t) for s, t in outs]
    moved = sum(math.prod(s.shape) * s.dtype.itemsize for s in shapes)
    moved += sum(math.prod(a.shape) * a.dtype.itemsize for a in arrays)
    return pl.pallas_call(
        kernel,
        name=name,
        out_shape=shapes,
        in_specs=[SMEM] + [VMEM] * len(arrays),
        out_specs=[VMEM] * len(outs),
        scratch_shapes=[pltpu.VMEM(s, t) for s, t in scratch],
        compiler_params=pltpu.CompilerParams(vmem_limit_bytes=limit * MIB),
        cost_estimate=pl.CostEstimate(flops=flops, bytes_accessed=moved, transcendentals=0),
    )(ids, *arrays)


def place_a_kernel(ids, *refs):
    pieces, (wqk, wvo), sem = refs[:16], refs[16:18], refs[18]
    b, core = ids[0], ids[2]
    for flip in range(2):
        c = core ^ flip
        for m in range(SHARDS):
            src = pieces[flip * SHARDS + m]
            row = pl.multiple_of((b ^ m) * 96, 96)
            pltpu.make_async_copy(
                src.at[pl.ds(0, 96)], wqk.at[c, pl.ds(row, 96)], sem.at[0]
            ).start()
            pltpu.make_async_copy(
                src.at[pl.ds(96, 96)], wvo.at[c, pl.ds(row, 96)], sem.at[1]
            ).start()
    pltpu.make_async_copy(wqk, wqk, sem.at[0]).wait()
    pltpu.make_async_copy(wvo, wvo, sem.at[1]).wait()


def place_a(ids, pieces):
    shape = jax.ShapeDtypeStruct((2, D, D), BF)
    return pl.pallas_call(
        place_a_kernel,
        name="place_a",
        out_shape=[shape, shape],
        in_specs=[SMEM] + [ANY] * 16,
        out_specs=[VMEM, VMEM],
        compiler_params=pltpu.CompilerParams(vmem_limit_bytes=40 * MIB),
        scratch_shapes=[pltpu.SemaphoreType.DMA((2,))],
        cost_estimate=pl.CostEstimate(flops=0, bytes_accessed=8 * D * D, transcendentals=0),
    )(ids, *pieces)


def place_f_kernel(ids, *refs):
    pieces, (wgu, wd), sem = refs[:32], refs[32:34], refs[34]
    b, y, core = ids[0], ids[1], ids[2]
    for yflip in range(2):
        for cflip in range(2):
            c, yy = core ^ cflip, y ^ yflip
            for m in range(SHARDS):
                src = pieces[(yflip * 2 + cflip) * SHARDS + m]
                j = b ^ m
                for k in range(4):
                    pltpu.make_async_copy(
                        src.at[pl.ds(k * 96, 96)],
                        wgu.at[c, yy, pl.ds(pl.multiple_of(j * 96, 96), 96), pl.ds(k * 256, 256)],
                        sem.at[0],
                    ).start()
                row = pl.multiple_of(j * 256 + (2 * yy + c) * 64, 64)
                for k in range(3):
                    pltpu.make_async_copy(
                        src.at[pl.ds(384 + k * 64, 64)],
                        wd.at[pl.ds(row, 64), pl.ds(k * 256, 256)],
                        sem.at[1],
                    ).start()
    pltpu.make_async_copy(wgu, wgu, sem.at[0]).wait()
    pltpu.make_async_copy(wd, wd, sem.at[1]).wait()


def place_f(ids, pieces):
    return pl.pallas_call(
        place_f_kernel,
        name="place_f",
        out_shape=[
            jax.ShapeDtypeStruct((2, 2, D, HALF), BF),
            jax.ShapeDtypeStruct((FF, D), BF),
        ],
        in_specs=[SMEM] + [ANY] * 32,
        out_specs=[VMEM, VMEM],
        compiler_params=pltpu.CompilerParams(vmem_limit_bytes=40 * MIB),
        scratch_shapes=[pltpu.SemaphoreType.DMA((2,))],
        cost_estimate=pl.CostEstimate(flops=0, bytes_accessed=12 * D * FF, transcendentals=0),
    )(ids, *pieces)


def attention_forward_kernel(
    ids, x, gains, offsets, mask, wqk, wvo, qkv, attended, weights, first, n1, n2, bias
):
    for h in range(H):
        row = jnp.broadcast_to(offsets[h : h + 1, :], (DLEN, 2 * DLEN))
        rolled = pltpu.roll(row, DLEN + 1, 1, stride=1, stride_axis=0)
        bias[h // 2, (h % 2) * DLEN : (h % 2 + 1) * DLEN, :] = rolled[:, :DLEN]
    tokens = x[...].astype(F32)
    normed = (tokens * norm_scale(tokens) * gains[0:1, :]).astype(BF)
    n1[...] = normed
    qkv[0] = dot(normed, wqk[0]).astype(BF)
    qkv[1] = dot(normed, wqk[1]).astype(BF)
    qkv[2] = dot(normed, wvo[0]).astype(BF)
    low_lane = lax.broadcasted_iota(jnp.int32, (DLEN, DLEN), 1) < DH
    for m in range(MICRO):
        rows = slice(m * DLEN, (m + 1) * DLEN)
        hidden = jnp.concatenate([mask[m], mask[m]], axis=0)
        for p in range(H // 2):
            lanes = slice(p * DLEN, (p + 1) * DLEN)
            q = qkv[0, rows, lanes]
            zero = jnp.zeros_like(q)
            stacked = jnp.concatenate(
                [jnp.where(low_lane, q, zero), jnp.where(low_lane, zero, q)], axis=0
            )
            scores = dot_nt(stacked, qkv[1, rows, lanes]) + bias[p] + hidden
            shifted = jnp.exp(scores - jnp.max(scores, axis=-1, keepdims=True))
            share = (shifted / jnp.sum(shifted, axis=-1, keepdims=True)).astype(BF)
            weights[m, p] = share
            mixed = dot(share, qkv[2, rows, lanes])
            attended[rows, lanes] = jnp.where(low_lane, mixed[:DLEN], mixed[DLEN:]).astype(BF)
    x1 = tokens + dot(attended[...], wvo[1])
    first[...] = x1
    n2[...] = (x1 * norm_scale(x1) * gains[1:2, :]).astype(BF)


def gelu_parts(gate):
    c0, c1 = math.sqrt(2.0 / math.pi), 0.044715
    square = gate * gate
    bent = jnp.tanh(c0 * gate * (1.0 + c1 * square))
    value = 0.5 * gate * (1.0 + bent)
    slope = 0.5 * (1.0 + bent) + 0.5 * gate * (1.0 - bent * bent) * (
        c0 * (1.0 + 3.0 * c1 * square)
    )
    return value, slope


def ffn_forward_kernel(
    ids, first, n2, gains, wgu, wd, wproj, gelu_out, slope_out, hidden, second, n3, vectors
):
    normed = n2[...]
    total = first[...]
    for half in range(2):
        lanes = slice(half * HALF, (half + 1) * HALF)
        gate = dot(normed, wgu[0, half])
        up = dot(normed, wgu[1, half])
        value, slope = gelu_parts(gate)
        gelu_out[half] = value.astype(BF)
        slope_out[half] = (up * slope).astype(BF)
        h = (value * up).astype(BF)
        hidden[:, lanes] = h
        total = total + dot(h, wd[lanes, :])
    second[...] = total
    normed_three = (total * norm_scale(total) * gains[2:3, :]).astype(BF)
    n3[...] = normed_three
    vectors[...] = dot(normed_three, wproj[...]).astype(BF)


def count_kernel(ids, picks, counts):
    spots = lax.broadcasted_iota(jnp.int32, (DLEN, DLEN), 0)

    def one(j):
        for m in range(MICRO):
            total = jnp.zeros((DLEN, DLEN), F32)
            for t in range(picks.shape[2]):
                total += jnp.where(spots == picks[m, j, t : t + 1, :], 1.0, 0.0)
            counts[m, j] = total

    steps(picks.shape[1], one)


def group_sums(values):
    lane = lax.broadcasted_iota(jnp.int32, values.shape, 1)
    shift = 1
    while shift < QLEN:
        ahead = pltpu.roll(values, DLEN - shift, 1)
        behind = pltpu.roll(values, shift, 1)
        values = values + jnp.where((lane & shift) == 0, ahead, behind)
        shift *= 2
    return values


def similarity_kernel(direct, count, ids, own, others, counts, share, soft, score, best):
    b, is_query = ids[0], ids[3]
    scale = DLEN**-0.5

    def one(m):
        j = (b ^ m) if direct else m
        for micro in range(MICRO):
            rows = slice(micro * DLEN, (micro + 1) * DLEN)
            mine, theirs = own[rows, :], others[m, rows, :]
            doc = jnp.where(is_query == 1, theirs, mine)
            query = jnp.where(is_query == 1, mine, theirs)
            times = counts[micro, j]
            sim = dot_nt(doc, query) * scale
            peak = jnp.max(jnp.where(times > 0, sim, -jnp.inf), axis=0, keepdims=True)
            mass = jnp.where(times > 0, times * jnp.exp(jnp.minimum(sim - peak, 0.0)), 0.0)
            total = jnp.sum(mass, axis=0, keepdims=True)
            soft[micro, j] = mass / total
            best[micro, pl.ds(j, 1), :] = peak + jnp.log(total)

    steps(count, one)
    for micro in range(MICRO):
        score[micro] = group_sums(best[micro] * share[micro])


def vector_grad_kernel(
    direct, count, ids, others, soft, share, sharp, target, score, scores, grad, weight, total
):
    b, is_query = ids[0], ids[3]
    scale = DLEN**-0.5

    @pl.when(is_query == 1)
    def _():
        for micro in range(MICRO):
            logits = score[micro] * sharp[micro]
            raised = jnp.exp(logits - jnp.max(logits, axis=0, keepdims=True))
            odds = raised / jnp.sum(raised, axis=0, keepdims=True)
            doc = lax.broadcasted_iota(jnp.int32, (count, DLEN), 0)
            hit = jnp.where(target[micro] == doc, 1.0, 0.0)
            weight[micro] = (odds - hit) * sharp[micro] * share[micro] * scale

    @pl.when(is_query == 0)
    def _():
        for micro in range(MICRO):
            sharpness = sharp[micro]
            logits = scores[:, micro] * sharpness[None]
            peak = jnp.max(logits, axis=0)
            norm = jnp.sum(jnp.exp(logits - peak[None]), axis=0)
            odds = jnp.exp(score[micro] * sharpness - peak) / norm
            hit = jnp.where(target[micro] == b, 1.0, 0.0)
            weight[micro] = (odds - hit) * sharpness * share[micro] * scale

    total[...] = jnp.zeros_like(total)

    def one(m):
        j = (b ^ m) if direct else m
        for micro in range(MICRO):
            rows = slice(micro * DLEN, (micro + 1) * DLEN)
            dense = soft[micro, j] * weight[micro, pl.ds(j, 1), :]
            upper = dense.astype(BF)
            lower = (dense - upper.astype(F32)).astype(BF)
            theirs = others[m, rows, :]

            @pl.when(is_query == 1)
            def _():
                total[rows, :] += dot_tn(upper, theirs) + dot_tn(lower, theirs)

            @pl.when(is_query == 0)
            def _():
                total[rows, :] += dot(upper, theirs) + dot(lower, theirs)

    steps(count, one)
    grad[...] = total[...].astype(BF)


def ffn_backward_kernel(
    direct, ids, dvec, first, second, n2, n3, gelu_in, slope_in, hidden, gains, wgu, wd, wproj, *refs
):
    if direct:
        outs, (grad_first, grad_proj, grad_gains, dgu, grad_down) = refs[:4], refs[4:]
    else:
        grad_first, grad_proj, grad_gains, dgu, dy_out = refs
    b, y, core = ids[0], ids[1], ids[2]
    dvectors = dvec[...]
    grad_proj[...] = dot_tn(n3[...], dvectors)
    dn3 = dot_nt(dvectors, wproj[...])
    dx2, dgain3 = norm_backward(second[...], gains[2:3, :], dn3)
    dy = dx2.astype(BF)
    dn2 = jnp.zeros((ROWS, D), F32)
    for half in range(2):
        dh = dot_nt(dy, wd[half * HALF : (half + 1) * HALF, :])
        dgate = (dh * slope_in[half].astype(F32)).astype(BF)
        dup = (dh * gelu_in[half].astype(F32)).astype(BF)
        dgu[0, half] = dgate
        dgu[1, half] = dup
        dn2 = dn2 + dot_nt(dgate, wgu[0, half]) + dot_nt(dup, wgu[1, half])
    dx1, dgain2 = norm_backward(first[...], gains[1:2, :], dn2)
    grad_first[...] = dx2 + dx1
    grad_gains[...] = jnp.zeros_like(grad_gains)
    grad_gains[1:2, :] = dgain2
    grad_gains[2:3, :] = dgain3
    if not direct:
        dy_out[...] = dy
        return
    for j in range(SHARDS):
        down = dot_tn(hidden[:, j * 256 : (j + 1) * 256], dy).astype(BF)
        for part in range(4):
            grad_down[j, part] = down[part * 64 : (part + 1) * 64, :]
    normed = n2[...]
    for cflip in (1, 0):
        for yflip in (1, 0):
            out = outs[cflip * 2 + yflip]
            c, yy = core ^ cflip, y ^ yflip
            piece = dot_tn(normed, dgu[c, yy]).astype(BF)
            for j in range(SHARDS):
                m = b ^ j
                for k in range(4):
                    out[m, k * 96 : (k + 1) * 96, :] = piece[
                        j * 96 : (j + 1) * 96, k * 256 : (k + 1) * 256
                    ]
                down = grad_down[j, 2 * yy + c]
                for k in range(3):
                    out[m, 384 + k * 64 : 384 + (k + 1) * 64, :] = down[:, k * 256 : (k + 1) * 256]


def attention_backward_kernel(
    direct,
    ids,
    grad_first,
    x,
    n1,
    attended,
    weights,
    qkv,
    gains,
    bucket,
    wqk,
    wvo,
    grad_proj,
    grad_gains,
    *refs,
):
    if direct:
        own, other, grad_in, left, right, dqk, extra, diag, bias_grad = refs
    else:
        small, grad_in, dqkv_out, da_out, left, right, dqk, diag, bias_grad = refs
    b, core = ids[0], ids[2]
    dx1 = grad_first[...]
    da = dx1.astype(BF)
    dattended = dot_nt(da, wvo[1]).astype(BF)
    low_lane = lax.broadcasted_iota(jnp.int32, (DLEN, DLEN), 1) < DH
    row_at = lax.broadcasted_iota(jnp.int32, (DLEN, MICRO * DLEN), 0)
    lane_at = lax.broadcasted_iota(jnp.int32, (DLEN, MICRO * DLEN), 1)
    mirror = jnp.where(row_at == DLEN - 1 - lane_at % DLEN, 1.0, 0.0).astype(BF)
    diag[...] = jnp.zeros_like(diag)
    for p in range(H // 2):
        lanes = slice(p * DLEN, (p + 1) * DLEN)
        kept = []
        for m in range(MICRO):
            rows = slice(m * DLEN, (m + 1) * DLEN)
            q, k, v = qkv[0, rows, lanes], qkv[1, rows, lanes], qkv[2, rows, lanes]
            dout = dattended[rows, lanes]
            zero = jnp.zeros_like(q)
            qs = jnp.concatenate(
                [jnp.where(low_lane, q, zero), jnp.where(low_lane, zero, q)], axis=0
            )
            dos = jnp.concatenate(
                [jnp.where(low_lane, dout, zero), jnp.where(low_lane, zero, dout)], axis=0
            )
            share = weights[m, p]
            wide = share.astype(F32)
            dshare = dot_nt(dos, v)
            centre = jnp.sum(wide * dshare, axis=-1, keepdims=True)
            ds = (wide * (dshare - centre)).astype(BF)
            dq = dot(ds, k)
            dqk[0, rows, lanes] = jnp.where(low_lane, dq[:DLEN], dq[DLEN:]).astype(BF)
            dqk[1, rows, lanes] = dot_tn(ds, qs).astype(BF)
            right[0, rows, lanes] = dot_tn(share, dos).astype(BF)
            kept.append(ds)
        for h in range(2):
            both = jnp.concatenate([part[h * DLEN : (h + 1) * DLEN] for part in kept], axis=0)
            turned = dot(mirror, both)
            wider = jnp.concatenate([turned, jnp.zeros_like(turned)], axis=1)
            rolled = pltpu.roll(wider, 0, 1, stride=1, stride_axis=0)
            diag[2 * p + h : 2 * p + h + 1, :] = jnp.sum(rolled, axis=0, keepdims=True)
    bias_grad[...] = lax.dot_general(
        bucket[...],
        diag[...],
        (((1,), (1,)), ((), ())),
        precision=HIGHEST,
        preferred_element_type=F32,
    )
    dn1 = dot_nt(dqk[0], wqk[0]) + dot_nt(dqk[1], wqk[1]) + dot_nt(right[0], wvo[0])
    dx, dgain1 = norm_backward(x[...].astype(F32), gains[0:1, :], dn1)
    grad_in[...] = dx1 + dx
    right[1] = da
    left[0] = n1[...]
    left[1] = attended[...]
    all_gains = grad_gains[...]
    first_row = lax.broadcasted_iota(jnp.int32, all_gains.shape, 0) == 0
    all_gains = jnp.where(first_row, dgain1, all_gains)
    if not direct:
        small[0:8, :] = all_gains
        small[8:40, :] = jnp.concatenate(
            [bias_grad[...], jnp.zeros((BUCKETS, D - DLEN), F32)], axis=1
        )
        dqkv_out[0] = dqk[0]
        dqkv_out[1] = dqk[1]
        dqkv_out[2] = right[0]
        da_out[...] = da
        return
    per_shard = BUCKETS // SHARDS
    for j in range(SHARDS):
        for k in range(6):
            extra[0, j, :, k * DLEN : (k + 1) * DLEN] = grad_proj[
                j * 96 + k * 16 : j * 96 + (k + 1) * 16, :
            ]
        extra[1, j] = jnp.zeros((16, D), F32)
        extra[1, j, 0:8, :] = pltpu.roll(all_gains, (D - j * 96) % D, 1)
        extra[1, j, 8 : 8 + per_shard, 0:DLEN] = bias_grad[j * per_shard : (j + 1) * per_shard, :]
    for flip, out in ((1, other), (0, own)):
        c = core ^ flip
        top = dot_tn(n1[...], dqk[c]).astype(BF)
        bottom = dot_tn(left[c], right[c]).astype(BF)
        for j in range(SHARDS):
            m = b ^ j
            out[m, 0:96, :] = top[j * 96 : (j + 1) * 96, :]
            out[m, 96:192, :] = bottom[j * 96 : (j + 1) * 96, :]
            out[m, 192:208, :] = extra[c, j].astype(BF)


def local(
    hidden_in,
    norm1_gain,
    w_query,
    w_key,
    w_value,
    w_out,
    rel_table,
    norm2_gain,
    w_gate,
    w_up,
    w_down,
    norm3_gain,
    w_proj,
    query_lengths,
    keyword_request_mask,
    targets,
    candidates,
):
    streams = lax.axis_size("stream")
    shards = lax.axis_size("batch")
    pairs = streams // 2
    direct = shards == SHARDS and pairs == 2
    b = lax.axis_index("batch")
    s = lax.axis_index("stream")
    y, core = s // pairs, s % pairs
    is_query = s < pairs
    ids = jnp.stack([b, y, core, is_query.astype(jnp.int32)]).astype(jnp.int32)

    def swap(block, yflip, cflip, m):
        route = []
        for source in range(streams):
            target = ((source // pairs) ^ yflip) * pairs + ((source % pairs) ^ cflip)
            for j in range(shards):
                route.append((source * shards + j, target * shards + (j ^ m)))
        return lax.ppermute(block, EVERY, route)

    def in_order(stacked):
        return jnp.take(stacked, b ^ jnp.arange(shards), axis=0)

    if direct:
        first_core = core == 0
        packed = jnp.concatenate([w_proj[k * 16 : (k + 1) * 16, :] for k in range(6)], axis=1)
        gains_own = jnp.stack([norm1_gain, norm2_gain, norm3_gain])
        small_own = jnp.zeros((16, D), BF)
        small_own = lax.dynamic_update_slice(small_own, gains_own, (0, 0))
        small_own = lax.dynamic_update_slice(small_own, rel_table.reshape(-1, H), (8, 0))
        slab_a = jnp.where(
            first_core,
            jnp.concatenate([w_query, w_value, packed]),
            jnp.concatenate([w_key, w_out, small_own]),
        )
        wide = jnp.where(first_core, w_gate, w_up)
        wide = lax.dynamic_slice(wide, (0, y * HALF), (96, HALF))
        deep = lax.dynamic_slice(w_down, ((2 * y + core) * 64, 0), (64, D))
        slab_f = jnp.concatenate(
            [wide[:, k * 256 : (k + 1) * 256] for k in range(4)]
            + [deep[:, k * 256 : (k + 1) * 256] for k in range(3)]
        )

        def spread(slab):
            parts = {0: slab}
            for m in (2, 4, 6):
                parts[m] = swap(slab, 0, 0, m)
            for m in (0, 2, 4, 6):
                parts[m + 1] = swap(parts[m], 0, 0, 1)
            return [parts[m] for m in range(SHARDS)]

        part_a = spread(slab_a)
        part_f = spread(slab_f)
        twin_a = [swap(part, 0, 1, 0) for part in part_a]
        far_f = [swap(part, 1, 0, 0) for part in part_f]
        twin_f = [swap(part, 0, 1, 0) for part in part_f]
        far_twin_f = [swap(part, 0, 1, 0) for part in far_f]
        wqk, wvo = place_a(ids, part_a + twin_a)
        wgu, wd = place_f(ids, part_f + twin_f + far_f + far_twin_f)
        extra_own = jnp.stack([part[192:208] for part in part_a])
        extra_twin = jnp.stack([part[192:208] for part in twin_a])
        proj_all = in_order(jnp.where(first_core, extra_own, extra_twin))
        small_all = in_order(jnp.where(first_core, extra_twin, extra_own))
        wproj = jnp.transpose(proj_all.reshape(shards, 16, 6, DLEN), (0, 2, 1, 3)).reshape(D, DLEN)
        gains = jnp.transpose(small_all[:, 0:8, :96], (1, 0, 2)).reshape(8, D).astype(F32)
        table = small_all[:, 8 : 8 + BUCKETS // shards, :H].reshape(BUCKETS, H)
    else:

        def whole(part):
            return lax.all_gather(part, "batch", axis=0, tiled=True)

        wqk = jnp.stack([whole(w_query), whole(w_key)])
        wvo = jnp.stack([whole(w_value), whole(w_out)])
        gate_up = jnp.stack([whole(w_gate), whole(w_up)])
        wgu = jnp.transpose(gate_up.reshape(2, D, 2, HALF), (0, 2, 1, 3))
        wd = whole(w_down)
        wproj = whole(w_proj)
        gain_rows = [whole(gain) for gain in (norm1_gain, norm2_gain, norm3_gain)]
        gains = jnp.pad(jnp.stack(gain_rows).astype(F32), ((0, 5), (0, 0)))
        table = whole(rel_table).reshape(BUCKETS, H)

    micro_count = hidden_in.shape[0]
    slot = jnp.arange(DLEN)
    pair_lengths = lax.dynamic_index_in_dim(query_lengths, core, 1, keepdims=False)
    pair_keyword = lax.dynamic_index_in_dim(keyword_request_mask, core, 1, keepdims=False)
    pair_targets = lax.dynamic_index_in_dim(targets, core, 1, keepdims=False)

    def by_slot(values):
        blocks = values.reshape(micro_count, shards, GROUPS)
        own = lax.dynamic_slice_in_dim(blocks, b, 1, 1)
        blocks = jnp.where(is_query, jnp.broadcast_to(own, blocks.shape), blocks)
        return jnp.repeat(blocks, QLEN, axis=2)

    length_slots = by_slot(pair_lengths)
    valid_slots = (slot % QLEN)[None, None, :] < length_slots
    share = jnp.where(valid_slots, 1.0 / length_slots.astype(F32), 0.0)
    sharp = jnp.where(by_slot(pair_keyword) == 1, 20.0, 10.0).astype(F32)
    target_slots = by_slot(pair_targets)
    own_valid = lax.dynamic_slice_in_dim(valid_slots, b, 1, 1)
    same = (slot[:, None] // QLEN) == (slot[None, :] // QLEN)
    mask = jnp.where(is_query & ~(same[None] & own_valid), -1000000000.0, 0.0).astype(F32)

    picked = lax.dynamic_index_in_dim(candidates, core, 1, keepdims=False)[:, 0]
    picked = picked.reshape(micro_count, shards, DLEN, picked.shape[-1])
    picked = jnp.transpose(picked, (0, 1, 3, 2))
    received = lax.all_to_all(picked, "batch", split_axis=1, concat_axis=1, tiled=True)
    picks = jnp.where(is_query, received, picked)
    (counts,) = call(
        count_kernel,
        "count",
        ids,
        [picks],
        [((micro_count, shards, DLEN, DLEN), F32)],
        limit=40,
    )

    onehot = bucket_onehot()
    offsets = lax.dot_general(
        table.astype(F32), onehot, (((0,), (1,)), ((), ())), precision=HIGHEST
    )
    offsets = jnp.pad(offsets, ((0, 4), (0, 0)))
    x = hidden_in[:, 0].reshape(ROWS, D)
    row_bf, row_f32 = ((ROWS, D), BF), ((ROWS, D), F32)
    qkv, attended, weights, first, n1, n2 = call(
        attention_forward_kernel,
        "attention_forward",
        ids,
        [x, gains, offsets, mask, wqk, wvo],
        [((3, ROWS, D), BF), row_bf, ((MICRO, H // 2, ROWS, DLEN), BF), row_f32, row_bf, row_bf],
        [((H // 2, ROWS, DLEN), F32)],
        flops=2 * ROWS * D * D * 4,
    )
    wide_bf = ((2, ROWS, HALF), BF)
    gelu_kept, slope_kept, hidden, second, n3, vectors = call(
        ffn_forward_kernel,
        "ffn_forward",
        ids,
        [first, n2, gains, wgu, wd, wproj],
        [wide_bf, wide_bf, ((ROWS, FF), BF), row_f32, row_bf, ((ROWS, DLEN), BF)],
        flops=2 * ROWS * D * FF * 3,
    )

    if direct:
        near = [swap(vectors, 1, 0, m) for m in (0, 2, 4, 6)]
        far = [swap(part, 0, 0, 1) for part in near]
        others = jnp.stack([part for both in zip(near, far) for part in both])
    else:
        route = [(i, (i + pairs) % streams) for i in range(streams)]
        arrived = lax.ppermute(vectors, "stream", route)
        others = lax.all_gather(arrived, "batch", axis=0)
    block_f32 = ((micro_count, shards, DLEN, DLEN), F32)
    line_f32 = ((micro_count, shards, DLEN), F32)
    soft, score = call(
        functools.partial(similarity_kernel, direct, shards),
        "similarity",
        ids,
        [vectors, others, counts, share],
        [block_f32, line_f32],
        [line_f32],
        limit=48,
    )
    if direct:
        blocks = jnp.broadcast_to(score[None], (shards,) + score.shape)
        scores = lax.all_to_all(blocks, "batch", split_axis=0, concat_axis=0, tiled=True)
    else:
        scores = lax.all_gather(score, "batch", axis=0)
    (dvec,) = call(
        functools.partial(vector_grad_kernel, direct, shards),
        "vector_grad",
        ids,
        [others, soft, share, sharp, target_slots, score, scores],
        [((ROWS, DLEN), BF)],
        [line_f32, ((ROWS, DLEN), F32)],
        limit=48,
    )

    back_in = [dvec, first, second, n2, n3, gelu_kept, slope_kept, hidden, gains, wgu, wd, wproj]
    gain_rows = ((8, D), F32)
    proj_f32 = ((D, DLEN), F32)
    grads_f = [((SHARDS, PIECE_F, 256), BF)] * 4
    dgu_shape = ((2, 2, ROWS, HALF), BF)
    result = call(
        functools.partial(ffn_backward_kernel, direct),
        "ffn_backward",
        ids,
        back_in,
        (grads_f if direct else [])
        + [row_f32, proj_f32, gain_rows]
        + ([] if direct else [dgu_shape, row_bf]),
        [dgu_shape, ((SHARDS, 4, 64, D), BF)] if direct else [],
        limit=52,
        flops=4 * ROWS * D * FF * 3,
    )
    if direct:
        f_own, f_own_far, f_twin, f_twin_far, grad_first, grad_proj, grad_gains = result
    else:
        grad_first, grad_proj, grad_gains, dgu, dy = result
    two_rows = ((2, ROWS, D), BF)
    slab_out = ((SHARDS, PIECE_A, D), BF)
    back_in = [grad_first, x, n1, attended, weights, qkv, gains, jnp.asarray(onehot.T), wqk, wvo]
    back_in += [grad_proj, grad_gains]
    kept = [two_rows, two_rows, two_rows]
    result = call(
        functools.partial(attention_backward_kernel, direct),
        "attention_backward",
        ids,
        back_in,
        [slab_out, slab_out, row_f32]
        if direct
        else [((40, D), F32), row_f32, ((3, ROWS, D), BF), row_bf],
        kept
        + ([((2, SHARDS, 16, D), F32)] if direct else [])
        + [((DLEN, 2 * DLEN), F32), ((BUCKETS, DLEN), F32)],
        limit=52,
        flops=4 * ROWS * D * D * 4,
    )

    def total_of(*parts):
        result = parts[0].astype(F32)
        for part in parts[1:]:
            result = result + part.astype(F32)
        return result

    if direct:
        a_own, a_other, input_grad = result
        from_twin_far = swap(f_twin_far, 0, 1, 0)
        from_twin = swap(f_twin, 0, 1, 0)
        shares = {}
        for m in (6, 4, 2, 0):
            pick = slice(m, m + 2)
            outgoing = total_of(f_own_far[pick], from_twin_far[pick]).astype(BF)
            incoming = swap(outgoing, 1, 0, 0)
            odd = total_of(f_own[m + 1], from_twin[m + 1], incoming[1]).astype(BF)
            across = swap(odd, 0, 0, 1)
            shares[m] = total_of(f_own[m], from_twin[m], incoming[0], across)
        back = [swap(shares[m].astype(BF), 0, 0, m) for m in (6, 4, 2)]
        mine_f = total_of(shares[0], *back).astype(BF)
        far_f = swap(mine_f, 1, 0, 0)
        twin_f = swap(mine_f, 0, 1, 0)
        far_twin_f = swap(far_f, 0, 1, 0)
        from_other = swap(a_other, 0, 1, 0)
        odd = [total_of(a_own[m + 1], from_other[m + 1]).astype(BF) for m in (6, 4, 2, 0)]
        across = swap(jnp.stack(odd), 0, 0, 1)
        shares = {
            m: total_of(a_own[m], from_other[m], across[i]) for i, m in enumerate((6, 4, 2, 0))
        }
        back = [swap(shares[m].astype(BF), 0, 0, m) for m in (6, 4, 2)]
        part = total_of(shares[0], *back).astype(BF)
        mine_a = total_of(part, swap(part, 1, 0, 0)).astype(BF)
        twin_a = swap(mine_a, 0, 1, 0)

        def by_core(mine, twin):
            return (
                jnp.where(first_core, mine, twin).astype(F32),
                jnp.where(first_core, twin, mine).astype(F32),
            )

        grad_q, grad_k = by_core(mine_a[0:96], twin_a[0:96])
        grad_v, grad_o = by_core(mine_a[96:192], twin_a[96:192])
        proj_part, small = by_core(mine_a[192:208], twin_a[192:208])
        grad_p = jnp.concatenate([proj_part[:, k * DLEN : (k + 1) * DLEN] for k in range(6)])
        grad_n1, grad_n2, grad_n3 = small[0, :96], small[1, :96], small[2, :96]
        grad_table = small[8 : 8 + BUCKETS // shards, :H].reshape(-1)
        lower_y = y == 0
        low_own = jnp.where(lower_y, mine_f, far_f)
        high_own = jnp.where(lower_y, far_f, mine_f)
        low_twin = jnp.where(lower_y, twin_f, far_twin_f)
        high_twin = jnp.where(lower_y, far_twin_f, twin_f)

        def wide_rows(low, high):
            tiles = [part[k * 96 : (k + 1) * 96] for part in (low, high) for k in range(4)]
            return jnp.concatenate(tiles, axis=1).astype(F32)

        grad_g = jnp.where(
            first_core, wide_rows(low_own, high_own), wide_rows(low_twin, high_twin)
        )
        grad_u = jnp.where(
            first_core, wide_rows(low_twin, high_twin), wide_rows(low_own, high_own)
        )

        def deep_rows(part):
            tiles = [part[384 + k * 64 : 384 + (k + 1) * 64] for k in range(3)]
            return jnp.concatenate(tiles, axis=1).astype(F32)

        def deep_pair(own, twin):
            own, twin = deep_rows(own), deep_rows(twin)
            return jnp.concatenate(
                [jnp.where(first_core, own, twin), jnp.where(first_core, twin, own)]
            )

        grad_d = jnp.concatenate([deep_pair(low_own, low_twin), deep_pair(high_own, high_twin)])
    else:
        small, input_grad, dqkv, da = result

        def summed(part):
            part = lax.psum_scatter(part, "batch", scatter_dimension=0, tiled=True)
            return lax.psum(part, "stream")

        grad_q, grad_k, grad_v = [summed(dot_tn(n1, dqkv[i])) for i in range(3)]
        grad_o = summed(dot_tn(attended, da))
        grad_g, grad_u = [
            summed(jnp.concatenate([dot_tn(n2, dgu[i, half]) for half in range(2)], axis=1))
            for i in range(2)
        ]
        grad_d = summed(dot_tn(hidden, dy))
        grad_p = summed(grad_proj)
        grad_n1, grad_n2, grad_n3 = [summed(small[i]) for i in range(3)]
        flat = lax.psum(small[8 : 8 + BUCKETS, :H].reshape(-1), EVERY)
        share_rows = flat.shape[0] // shards
        grad_table = lax.dynamic_slice_in_dim(flat, b * share_rows, share_rows, 0)

    vectors_out = vectors.reshape(micro_count, DLEN, DLEN)[:, None]
    grad_hidden = input_grad.reshape(micro_count, DLEN, D)[:, None]
    return (
        vectors_out,
        grad_hidden,
        grad_n1,
        grad_q,
        grad_k,
        grad_v,
        grad_o,
        grad_table,
        grad_n2,
        grad_g,
        grad_u,
        grad_d,
        grad_n3,
        grad_p,
    )


def solution(mesh):
    rows, lines = P("batch", None), P("batch")
    spread = P(None, "stream", "batch", None)
    return jax.shard_map(
        local,
        mesh=mesh,
        in_specs=(spread, lines, rows, rows, rows, rows, lines, lines, rows, rows, rows, lines, rows)
        + (P(), P(), P(), P(None, None, "batch", None, None)),
        out_specs=(spread, spread, lines, rows, rows, rows, rows, lines, lines)
        + (rows, rows, rows, lines, rows),
        check_vma=False,
    )
```

```python
import functools
import math

import jax
import jax.numpy as jnp
import numpy as np
from jax import lax
from jax.experimental import pallas as pl
from jax.experimental.pallas import tpu as pltpu
from jax.sharding import PartitionSpec as P

H = 12
DH = 64
BUCKETS = 32
MAX_DIST = 128
DLEN = 128
QLEN = 32
GROUPS = DLEN // QLEN
MICRO = 2
ROWS = MICRO * DLEN
D = 768
FF = 2048
HALF = FF // 2
SHARDS = 8
PIECE_A = 208
PIECE_F = 576

EPSILON = 1e-06
HIGHEST = lax.Precision.HIGHEST
BF = jnp.bfloat16
F32 = jnp.float32
EVERY = ("stream", "batch")
MIB = 2**20
ROUND_FLOPS = 5 * 10**10


def distance_bucket(distance):
    half_count = BUCKETS // 2
    exact_count = half_count // 2
    if distance < exact_count:
        return distance
    grown = exact_count + int(
        math.floor(
            math.log(distance / exact_count)
            / math.log(MAX_DIST / exact_count)
            * (half_count - exact_count)
            + 1e-09
        )
    )
    return min(grown, half_count - 1)


def bucket_onehot():
    table = np.zeros((2 * DLEN, BUCKETS), np.float32)
    for o in range(2 * DLEN - 1):
        offset = o - (DLEN - 1)
        table[o, distance_bucket(abs(offset)) + (BUCKETS // 2 if offset > 0 else 0)] = 1.0
    return table


def norm_scale(values):
    return lax.rsqrt(jnp.mean(values * values, axis=-1, keepdims=True) + EPSILON)


def norm_backward(values, gain, grad):
    scale = norm_scale(values)
    pulled = gain * grad
    inner = jnp.mean(values * pulled, axis=-1, keepdims=True)
    back = scale * pulled - values * (scale * scale * scale * inner)
    return back, jnp.sum(grad * values * scale, axis=0, keepdims=True)


def dot(left, right):
    return jnp.dot(left, right, preferred_element_type=F32)


def dot_nt(left, right):
    return lax.dot_general(left, right, (((1,), (1,)), ((), ())), preferred_element_type=F32)


def dot_tn(left, right):
    return lax.dot_general(left, right, (((0,), (0,)), ((), ())), preferred_element_type=F32)


def steps(count, body):
    if count <= 16:
        for i in range(count):
            body(i)
    else:

        @pl.loop(0, count)
        def _(i):
            body(i)


VMEM = pl.BlockSpec(memory_space=pltpu.VMEM)
SMEM = pl.BlockSpec(memory_space=pltpu.SMEM)
HBM = pl.BlockSpec(memory_space=pltpu.HBM)


def call(
    kernel, name, ids, arrays, outs, scratch=(), far=(), far_outs=(), sems=0, flops=0, limit=58
):
    shapes = [jax.ShapeDtypeStruct(s, t) for s, t in (*outs, *far_outs)]
    moved = sum(math.prod(s.shape) * s.dtype.itemsize for s in shapes)
    moved += sum(math.prod(a.shape) * a.dtype.itemsize for a in (*arrays, *far))
    scratch_shapes = [pltpu.VMEM(s, t) for s, t in scratch]
    if sems:
        scratch_shapes.append(pltpu.SemaphoreType.DMA((sems,)))
    return pl.pallas_call(
        kernel,
        name=name,
        out_shape=shapes,
        in_specs=[SMEM] + [VMEM] * len(arrays) + [HBM] * len(far),
        out_specs=[VMEM] * len(outs) + [HBM] * len(far_outs),
        scratch_shapes=scratch_shapes,
        compiler_params=pltpu.CompilerParams(vmem_limit_bytes=limit * MIB),
        cost_estimate=pl.CostEstimate(flops=flops, bytes_accessed=moved, transcendentals=0),
    )(ids, *arrays, *far)


def tick_kernel(token, out):
    pass


def tick(token):
    return pl.pallas_call(
        tick_kernel,
        name="tick",
        in_specs=[HBM],
        out_specs=HBM,
        out_shape=jax.ShapeDtypeStruct(token.shape, token.dtype),
        input_output_aliases={0: 0},
        cost_estimate=pl.CostEstimate(flops=ROUND_FLOPS, bytes_accessed=0, transcendentals=0),
    )(token)


def add_kernel(plan, near, far, ids, *refs):
    near, far, refs = refs[:near], refs[near : near + far], refs[near + far :]
    outs, refs = refs[: len(plan)], refs[len(plan) :]
    held, sems = (refs[:-1], refs[-1]) if far else ((), None)
    place = 0
    for entries in plan:
        for terms in entries:
            for is_far, array, entry in terms:
                if is_far:
                    copies([(far[array].at[entry], held[place])], sems.at[place])
                    place += 1
    place = 0
    for out, entries in zip(outs, plan):
        for i, terms in enumerate(entries):
            total = None
            for is_far, array, entry in terms:
                if is_far:
                    landed(held[place], sems.at[place])
                    part = held[place][...].astype(F32)
                    place += 1
                else:
                    part = near[array][entry].astype(F32)
                total = part if total is None else total + part
            out[i] = total.astype(BF)


def add_up(ids, *outputs):
    known = ([], [])
    plan, flat, shapes = [], [], []
    for entries in outputs:
        plan.append([])
        for terms in entries:
            plan[-1].append([])
            for array, entry in terms:
                is_far = int(array.shape[0] > 3)
                arrays = known[is_far]
                found = [i for i, other in enumerate(arrays) if other is array]
                if not found:
                    arrays.append(array)
                    found = [len(arrays) - 1]
                if is_far:
                    flat.append((array.shape[1:], BF))
                plan[-1][-1].append((is_far, found[0], entry))
        shapes.append(((len(entries), *entries[0][0][0].shape[1:]), BF))
    return call(
        functools.partial(add_kernel, plan, len(known[0]), len(known[1])),
        "add_up",
        ids,
        known[0],
        shapes,
        flat,
        far=known[1],
        sems=len(flat),
        limit=56,
    )


def pack_kernel(ids, wq, wk, wv, wo, wg, wu, wd, wp, g1, g2, g3, table, slab_a, slab_f):
    y, core = ids[1], ids[2]

    def fill(top, bottom, wide, rank):
        slab_a[0:96, :] = top[...]
        slab_a[96:192, :] = bottom[...]
        for yy in range(2):

            @pl.when(y == yy)
            def _():
                for k in range(4):
                    start = yy * HALF + k * 256
                    slab_f[k * 96 : (k + 1) * 96, :] = wide[:, start : start + 256]
                row = (2 * yy + rank) * 64
                for k in range(3):
                    slab_f[384 + k * 64 : 384 + (k + 1) * 64, :] = wd[
                        row : row + 64, k * 256 : (k + 1) * 256
                    ]

    @pl.when(core == 0)
    def _():
        fill(wq, wv, wg, 0)
        for k in range(6):
            slab_a[192:208, k * DLEN : (k + 1) * DLEN] = wp[k * 16 : (k + 1) * 16, :]

    @pl.when(core == 1)
    def _():
        fill(wk, wo, wu, 1)
        rows = [g1[...].astype(F32), g2[...].astype(F32), g3[...].astype(F32)]
        head = jnp.concatenate(rows + [jnp.zeros((5, 96), F32)], axis=0)
        tail = jnp.concatenate([table[...].astype(F32), jnp.zeros((7, 48), F32)], axis=0)
        tail = jnp.concatenate([tail, jnp.zeros((8, 48), F32)], axis=1)
        both = jnp.concatenate([head, tail], axis=0)
        slab_a[192:208, :] = jnp.concatenate(
            [both, jnp.zeros((16, D - 96), F32)], axis=1
        ).astype(BF)


def copies(pairs, sem):
    for src, dst in pairs:
        pltpu.make_async_copy(src, dst, sem).start()


def landed(buffer, sem):
    pltpu.make_async_copy(buffer, buffer, sem).wait()


def fetch_a(ids, pieces, spots, wqk, wvo, extra, sems):
    b, core = ids[0], ids[2]
    for cflip, m, array, entry in spots:
        src = pieces[array].at[entry]
        c, j = core ^ cflip, b ^ m
        row = pl.multiple_of(j * 96, 96)
        copies([(src.at[pl.ds(0, 96)], wqk.at[c, pl.ds(row, 96)])], sems.at[0])
        copies([(src.at[pl.ds(96, 96)], wvo.at[c, pl.ds(row, 96)])], sems.at[1])
        copies([(src.at[pl.ds(192, 16)], extra.at[c, j])], sems.at[2])


def fetch_wide(ids, pieces, spots, wgu, sems):
    b, y, core = ids[0], ids[1], ids[2]
    for yflip, cflip, m, array, entry in spots:
        src = pieces[array].at[entry]
        c, yy, j = core ^ cflip, y ^ yflip, b ^ m
        row = pl.multiple_of(j * 96, 96)
        for k in range(4):
            tile = wgu.at[c, yy, pl.ds(row, 96), pl.ds(k * 256, 256)]
            copies([(src.at[pl.ds(k * 96, 96)], tile)], sems.at[2 * yy + c])


def fetch_deep(ids, pieces, spots, wd, sem):
    b, y, core = ids[0], ids[1], ids[2]
    for yflip, cflip, m, array, entry in spots:
        src = pieces[array].at[entry]
        low = pl.multiple_of((b ^ m) * 256 + (2 * (y ^ yflip) + (core ^ cflip)) * 64, 64)
        for k in range(3):
            tile = wd.at[pl.ds(low, 64), pl.ds(k * 256, 256)]
            copies([(src.at[pl.ds(384 + k * 64, 64)], tile)], sem)


def head_masks():
    low_lane = lax.broadcasted_iota(jnp.int32, (DLEN, DLEN), 1) < DH
    return low_lane


def both_heads(pair, low_lane):
    zero = jnp.zeros_like(pair)
    return jnp.concatenate(
        [jnp.where(low_lane, pair, zero), jnp.where(low_lane, zero, pair)], axis=0
    )


PAIRS_OF_HEADS = [
    (m, p, slice(m * DLEN, (m + 1) * DLEN), slice(p * DLEN, (p + 1) * DLEN))
    for m in range(MICRO)
    for p in range(H // 2)
]


def attention_forward_kernel(direct, spots, ids, x, mask, onehot, *refs):
    if direct:
        count = 1 + max(spot[2] for spot in spots)
        pieces, refs = refs[:count], refs[count:]
        qkv, attended, weights, first, n1, n2, gains, wproj, wqk_out, wvo_out = refs[:10]
        wqk, wvo, extra, bias, scores, sems = refs[10:]
        fetch_a(ids, pieces, spots, wqk, wvo, extra, sems)
        landed(extra, sems.at[2])
        lane = lax.broadcasted_iota(jnp.int32, (8, D), 1)
        all_gains = jnp.zeros((8, D), F32)
        flat = jnp.zeros((8, D), F32)
        for j in range(SHARDS):
            block = extra[1, j].astype(F32)
            all_gains += pltpu.roll(jnp.where(lane < 96, block[0:8], 0.0), j * 96, 1)
            flat += pltpu.roll(jnp.where(lane < 48, block[8:16], 0.0), j * 48, 1)
            for k in range(6):
                wproj[j * 96 + k * 16 : j * 96 + (k + 1) * 16, :] = extra[
                    0, j, :, k * DLEN : (k + 1) * DLEN
                ]
        gains[...] = all_gains
        flat = flat[0:1, : BUCKETS * H]
    else:
        gains, flat_in, wqk, wvo = refs[:4]
        qkv, attended, weights, first, n1, n2, bias, scores = refs[4:]
        flat = flat_in[...].astype(F32)
    entry = lax.broadcasted_iota(jnp.int32, (16, BUCKETS * H), 1)
    head = lax.broadcasted_iota(jnp.int32, (16, BUCKETS * H), 0)
    by_head = jnp.where(entry % H == head, jnp.broadcast_to(flat, entry.shape), 0.0)
    offsets = dot(by_head.astype(BF), onehot[...])
    for h in range(H):
        row = jnp.broadcast_to(offsets[h : h + 1, :], (DLEN, 2 * DLEN))
        rolled = pltpu.roll(row, DLEN + 1, 1, stride=1, stride_axis=0)
        bias[h // 2, (h % 2) * DLEN : (h % 2 + 1) * DLEN, :] = rolled[:, :DLEN]
    tokens = x[...].astype(F32)
    normed = (tokens * norm_scale(tokens) * gains[0:1, :]).astype(BF)
    n1[...] = normed
    if direct:
        landed(wqk, sems.at[0])
        copies([(wqk, wqk_out)], sems.at[0])
        landed(wvo, sems.at[1])
        copies([(wvo, wvo_out)], sems.at[1])
    qkv[0] = dot(normed, wqk[0]).astype(BF)
    qkv[1] = dot(normed, wqk[1]).astype(BF)
    qkv[2] = dot(normed, wvo[0]).astype(BF)
    low_lane = head_masks()
    for i, (m, p, rows, lanes) in enumerate(PAIRS_OF_HEADS):
        scores[i] = dot_nt(both_heads(qkv[0, rows, lanes], low_lane), qkv[1, rows, lanes])
    for i, (m, p, rows, lanes) in enumerate(PAIRS_OF_HEADS):
        hidden = jnp.concatenate([mask[m], mask[m]], axis=0)
        biased = scores[i] + bias[p] + hidden
        shifted = jnp.exp(biased - jnp.max(biased, axis=-1, keepdims=True))
        weights[m, p] = (shifted / jnp.sum(shifted, axis=-1, keepdims=True)).astype(BF)
    for i, (m, p, rows, lanes) in enumerate(PAIRS_OF_HEADS):
        mixed = dot(weights[m, p], qkv[2, rows, lanes])
        attended[rows, lanes] = jnp.where(low_lane, mixed[:DLEN], mixed[DLEN:]).astype(BF)
    x1 = tokens + dot(attended[...], wvo[1])
    first[...] = x1
    n2[...] = (x1 * norm_scale(x1) * gains[1:2, :]).astype(BF)
    if direct:
        landed(wqk, sems.at[0])
        landed(wvo, sems.at[1])


def gelu_parts(gate):
    c0, c1 = math.sqrt(2.0 / math.pi), 0.044715
    square = gate * gate
    bent = jnp.tanh(c0 * gate * (1.0 + c1 * square))
    value = 0.5 * gate * (1.0 + bent)
    slope = 0.5 * (1.0 + bent) + 0.5 * gate * (1.0 - bent * bent) * (
        c0 * (1.0 + 3.0 * c1 * square)
    )
    return value, slope


def ffn_forward_kernel(direct, spots, ids, first, n2, gains, wproj, *refs):
    if direct:
        count = 1 + max(spot[3] for spot in spots)
        pieces, refs = refs[:count], refs[count:]
        second, n3, vectors, gelu_out, slope_out, hidden_out = refs[1:7]
        wgu, wd, gelu_kept, slope_kept, hidden, sems = refs[7:]
        fetch_wide(ids, pieces, spots, wgu, sems)
        fetch_deep(ids, pieces, spots, wd, sems.at[4])
    else:
        wgu, wd, second, n3, vectors, gelu_kept, slope_kept, hidden = refs
    normed = n2[...]
    for half in range(2):
        lanes = slice(half * HALF, (half + 1) * HALF)
        if direct:
            landed(wgu.at[0, half], sems.at[2 * half])
            landed(wgu.at[1, half], sems.at[2 * half + 1])
        gate = dot(normed, wgu[0, half])
        up = dot(normed, wgu[1, half])
        value, slope = gelu_parts(gate)
        gelu_kept[half] = value.astype(BF)
        slope_kept[half] = (up * slope).astype(BF)
        hidden[:, lanes] = (value * up).astype(BF)
        if direct:
            copies([(gelu_kept.at[half], gelu_out.at[half])], sems.at[2 * half])
            copies([(slope_kept.at[half], slope_out.at[half])], sems.at[2 * half + 1])
    if direct:
        landed(wd, sems.at[4])
        copies([(hidden, hidden_out)], sems.at[4])
    total = first[...] + dot(hidden[...], wd[...])
    second[...] = total
    normed_three = (total * norm_scale(total) * gains[2:3, :]).astype(BF)
    n3[...] = normed_three
    vectors[...] = dot(normed_three, wproj[...]).astype(BF)
    if direct:
        for half in range(2):
            landed(gelu_kept.at[half], sems.at[2 * half])
            landed(slope_kept.at[half], sems.at[2 * half + 1])
        landed(hidden, sems.at[4])


def count_kernel(ids, picks, counts):
    spots = lax.broadcasted_iota(jnp.int32, (DLEN, DLEN), 0)

    def one(j):
        for m in range(MICRO):
            total = jnp.zeros((DLEN, DLEN), F32)
            for t in range(picks.shape[2]):
                total += jnp.where(spots == picks[m, j, t : t + 1, :], 1.0, 0.0)
            counts[m, j] = total

    steps(picks.shape[1], one)


def block_of(others, m):
    return others[m % 2].at[m // 2] if len(others) == 2 else others[0].at[m]


def group_sums(values):
    lane = lax.broadcasted_iota(jnp.int32, values.shape, 1)
    shift = 1
    while shift < QLEN:
        ahead = pltpu.roll(values, DLEN - shift, 1)
        behind = pltpu.roll(values, shift, 1)
        values = values + jnp.where((lane & shift) == 0, ahead, behind)
        shift *= 2
    return values


def similarity_kernel(direct, count, ids, own, counts, share, *refs):
    others, (soft, score, best) = refs[:-3], refs[-3:]
    b, is_query = ids[0], ids[3]
    scale = DLEN**-0.5

    def one(m):
        j = (b ^ m) if direct else m
        for micro in range(MICRO):
            rows = slice(micro * DLEN, (micro + 1) * DLEN)
            mine, theirs = own[rows, :], block_of(others, m)[rows, :]
            doc = jnp.where(is_query == 1, theirs, mine)
            query = jnp.where(is_query == 1, mine, theirs)
            times = counts[micro, j]
            sim = dot_nt(doc, query) * scale
            peak = jnp.max(jnp.where(times > 0, sim, -jnp.inf), axis=0, keepdims=True)
            mass = jnp.where(times > 0, times * jnp.exp(jnp.minimum(sim - peak, 0.0)), 0.0)
            total = jnp.sum(mass, axis=0, keepdims=True)
            soft[micro, j] = mass / total
            best[micro, pl.ds(j, 1), :] = peak + jnp.log(total)

    steps(count, one)
    for micro in range(MICRO):
        score[micro] = group_sums(best[micro] * share[micro])


def vector_grad_kernel(
    direct, count, ids, soft, share, sharp, target, score, scores, *refs
):
    others, (grad, weight, total) = refs[:-3], refs[-3:]
    b, is_query = ids[0], ids[3]
    scale = DLEN**-0.5

    @pl.when(is_query == 1)
    def _():
        for micro in range(MICRO):
            logits = score[micro] * sharp[micro]
            raised = jnp.exp(logits - jnp.max(logits, axis=0, keepdims=True))
            odds = raised / jnp.sum(raised, axis=0, keepdims=True)
            doc = lax.broadcasted_iota(jnp.int32, (count, DLEN), 0)
            hit = jnp.where(target[micro] == doc, 1.0, 0.0)
            weight[micro] = (odds - hit) * sharp[micro] * share[micro] * scale

    @pl.when(is_query == 0)
    def _():
        for micro in range(MICRO):
            sharpness = sharp[micro]
            logits = scores[:, micro] * sharpness[None]
            peak = jnp.max(logits, axis=0)
            norm = jnp.sum(jnp.exp(logits - peak[None]), axis=0)
            odds = jnp.exp(score[micro] * sharpness - peak) / norm
            hit = jnp.where(target[micro] == b, 1.0, 0.0)
            weight[micro] = (odds - hit) * sharpness * share[micro] * scale

    total[...] = jnp.zeros_like(total)

    def one(m):
        j = (b ^ m) if direct else m
        for micro in range(MICRO):
            rows = slice(micro * DLEN, (micro + 1) * DLEN)
            dense = soft[micro, j] * weight[micro, pl.ds(j, 1), :]
            upper = dense.astype(BF)
            lower = (dense - upper.astype(F32)).astype(BF)
            theirs = block_of(others, m)[rows, :]

            @pl.when(is_query == 1)
            def _():
                total[rows, :] += dot_tn(upper, theirs) + dot_tn(lower, theirs)

            @pl.when(is_query == 0)
            def _():
                total[rows, :] += dot(upper, theirs) + dot(lower, theirs)

    steps(count, one)
    grad[...] = total[...].astype(BF)


def ffn_backward_kernel(direct, spots, ids, dvec, second, n2, n3, gains, wproj, *refs):
    if direct:
        hidden_in, gelu_in, slope_in = refs[:3]
        count = 1 + max(spot[3] for spot in spots)
        pieces, refs = refs[3 : 3 + count], refs[3 + count - 4 :]
        dx2_out, grad_proj, grad_gain, dgu, *outs = refs[4:12]
        wd, hidden, gelu_kept, slope_kept, grad_down, quarters, sems = refs[12:]
        fetch_deep(ids, pieces, spots, wd, sems.at[0])
        copies([(slope_in, slope_kept)], sems.at[1])
        copies([(gelu_in, gelu_kept)], sems.at[2])
        copies([(hidden_in, hidden)], sems.at[3])
    else:
        wd, hidden, gelu_kept, slope_kept, dx2_out, grad_proj, grad_gain, dgu, dy_out = refs
    b, y, core = ids[0], ids[1], ids[2]
    dvectors = dvec[...]
    grad_proj[...] = dot_tn(n3[...], dvectors)
    dn3 = dot_nt(dvectors, wproj[...])
    dx2, dgain3 = norm_backward(second[...], gains[2:3, :], dn3)
    dx2_out[...] = dx2
    grad_gain[...] = dgain3
    dy = dx2.astype(BF)
    if direct:
        landed(wd, sems.at[0])
    dh = dot_nt(dy, wd[...])
    if direct:
        landed(slope_kept, sems.at[1])
        landed(gelu_kept, sems.at[2])
    for half in range(2):
        part = dh[:, half * HALF : (half + 1) * HALF]
        dgu[0, half] = (part * slope_kept[half].astype(F32)).astype(BF)
        dgu[1, half] = (part * gelu_kept[half].astype(F32)).astype(BF)
    if not direct:
        dy_out[...] = dy
        return
    landed(hidden, sems.at[3])
    for j in range(SHARDS):
        down = dot_tn(hidden[:, j * 256 : (j + 1) * 256], dy).astype(BF)
        for part in range(4):
            grad_down[j, part] = down[part * 64 : (part + 1) * 64, :]
    normed = n2[...]
    for cflip in (1, 0):
        for yflip in (1, 0):
            place = cflip * 2 + yflip
            c, yy = core ^ cflip, y ^ yflip
            piece = dot_tn(normed, dgu[c, yy]).astype(BF)
            for j in range(SHARDS):
                m = b ^ j
                for k in range(4):
                    quarters[place, m, k * 96 : (k + 1) * 96, :] = piece[
                        j * 96 : (j + 1) * 96, k * 256 : (k + 1) * 256
                    ]
                down = grad_down[j, 2 * yy + c]
                for k in range(3):
                    quarters[place, m, 384 + k * 64 : 384 + (k + 1) * 64, :] = down[
                        :, k * 256 : (k + 1) * 256
                    ]
            copies([(quarters.at[place], outs[place])], sems.at[place])
    for place in range(4):
        landed(quarters.at[place], sems.at[place])


def middle_backward_kernel(direct, spots, ids, dx2, first, dgu, gains, *refs):
    if direct:
        count = 1 + max(spot[3] for spot in spots)
        pieces, refs = refs[:count], refs[count:]
        wvo_in, dx1_out, dattended, grad_gain, wgu, wout, sems = refs
        fetch_wide(ids, pieces, spots, wgu, sems)
        copies([(wvo_in.at[1], wout)], sems.at[4])
    else:
        wgu, wvo, dx1_out, dattended, grad_gain = refs
        wout = wvo.at[1]
    dn2 = jnp.zeros((ROWS, D), F32)
    for half in range(2):
        for c in range(2):
            if direct:
                landed(wgu.at[c, half], sems.at[half * 2 + c])
            dn2 = dn2 + dot_nt(dgu[c, half], wgu[c, half])
    back, dgain2 = norm_backward(first[...], gains[1:2, :], dn2)
    dx1 = dx2[...] + back
    dx1_out[...] = dx1
    grad_gain[...] = dgain2
    if direct:
        landed(wout, sems.at[4])
    dattended[...] = dot_nt(dx1.astype(BF), wout[...]).astype(BF)


def attention_backward_kernel(
    direct,
    ids,
    grad_first,
    dattended,
    x,
    n1,
    attended,
    weights,
    qkv,
    gains,
    bucket,
    grad_proj,
    grad_gain2,
    grad_gain3,
    *refs,
):
    if direct:
        wqk_in, wvo_in, grad_in, own_out, other_out = refs[:5]
        wqk, wvo, own, other, left, right, dqk, extra, *refs = refs[5:]
        copies([(wvo_in.at[0], wvo.at[0])], refs[-1].at[0])
        copies([(wqk_in, wqk)], refs[-1].at[1])
    else:
        wqk, wvo, small, grad_in, dqkv_out, da_out, left, right, dqk, *refs = refs
    diag, bias_grad, dshares, scaled, queries, douts, *rest = refs
    b, core = ids[0], ids[2]
    dx1 = grad_first[...]
    da = dx1.astype(BF)
    low_lane = head_masks()
    row_at = lax.broadcasted_iota(jnp.int32, (DLEN, MICRO * DLEN), 0)
    lane_at = lax.broadcasted_iota(jnp.int32, (DLEN, MICRO * DLEN), 1)
    mirror = jnp.where(row_at == DLEN - 1 - lane_at % DLEN, 1.0, 0.0).astype(BF)
    diag[...] = jnp.zeros_like(diag)
    for i, (m, p, rows, lanes) in enumerate(PAIRS_OF_HEADS):
        queries[i] = both_heads(qkv[0, rows, lanes], low_lane)
        douts[i] = both_heads(dattended[rows, lanes], low_lane)
    for i, (m, p, rows, lanes) in enumerate(PAIRS_OF_HEADS):
        dshares[i] = dot_nt(douts[i], qkv[2, rows, lanes])
        right[0, rows, lanes] = dot_tn(weights[m, p], douts[i]).astype(BF)
    for i, (m, p, rows, lanes) in enumerate(PAIRS_OF_HEADS):
        wide = weights[m, p].astype(F32)
        dshare = dshares[i]
        centre = jnp.sum(wide * dshare, axis=-1, keepdims=True)
        scaled[i] = (wide * (dshare - centre)).astype(BF)
    for i, (m, p, rows, lanes) in enumerate(PAIRS_OF_HEADS):
        dq = dot(scaled[i], qkv[1, rows, lanes])
        dqk[0, rows, lanes] = jnp.where(low_lane, dq[:DLEN], dq[DLEN:]).astype(BF)
        dqk[1, rows, lanes] = dot_tn(scaled[i], queries[i]).astype(BF)
    for h in range(H):
        part = slice((h % 2) * DLEN, (h % 2 + 1) * DLEN)
        both = jnp.concatenate([scaled[m * (H // 2) + h // 2, part] for m in range(MICRO)], axis=0)
        turned = dot(mirror, both)
        wider = jnp.concatenate([turned, jnp.zeros_like(turned)], axis=1)
        rolled = pltpu.roll(wider, 0, 1, stride=1, stride_axis=0)
        diag[h : h + 1, :] = jnp.sum(rolled, axis=0, keepdims=True)
    bias_grad[...] = lax.dot_general(
        bucket[...],
        diag[...],
        (((1,), (1,)), ((), ())),
        precision=HIGHEST,
        preferred_element_type=F32,
    )
    if direct:
        sems = rest[0]
        landed(wvo.at[0], sems.at[0])
        landed(wqk, sems.at[1])
    dn1 = dot_nt(dqk[0], wqk[0]) + dot_nt(dqk[1], wqk[1]) + dot_nt(right[0], wvo[0])
    dx, dgain1 = norm_backward(x[...].astype(F32), gains[0:1, :], dn1)
    grad_in[...] = dx1 + dx
    right[1] = da
    left[0] = n1[...]
    left[1] = attended[...]
    all_gains = jnp.concatenate(
        [dgain1, grad_gain2[...], grad_gain3[...], jnp.zeros((5, D), F32)], axis=0
    )
    if not direct:
        small[0:8, :] = all_gains
        small[8:40, :] = jnp.concatenate(
            [bias_grad[...], jnp.zeros((BUCKETS, D - DLEN), F32)], axis=1
        )
        dqkv_out[0] = dqk[0]
        dqkv_out[1] = dqk[1]
        dqkv_out[2] = right[0]
        da_out[...] = da
        return
    per_shard = BUCKETS // SHARDS
    for j in range(SHARDS):
        for k in range(6):
            extra[0, j, :, k * DLEN : (k + 1) * DLEN] = grad_proj[
                j * 96 + k * 16 : j * 96 + (k + 1) * 16, :
            ]
        extra[1, j] = jnp.zeros((16, D), F32)
        extra[1, j, 0:8, :] = pltpu.roll(all_gains, (D - j * 96) % D, 1)
        extra[1, j, 8 : 8 + per_shard, 0:DLEN] = bias_grad[j * per_shard : (j + 1) * per_shard, :]
    for flip, out, target in ((1, other, other_out), (0, own, own_out)):
        c = core ^ flip
        top = dot_tn(n1[...], dqk[c]).astype(BF)
        bottom = dot_tn(left[c], right[c]).astype(BF)
        for j in range(SHARDS):
            m = b ^ j
            out[m, 0:96, :] = top[j * 96 : (j + 1) * 96, :]
            out[m, 96:192, :] = bottom[j * 96 : (j + 1) * 96, :]
            out[m, 192:208, :] = extra[c, j].astype(BF)
        copies([(out, target)], sems.at[flip])
    landed(other, sems.at[1])
    landed(own, sems.at[0])


def finish_wide_kernel(ids, near, far, twin, far_twin, token, grad_g, grad_u, grad_d):
    y, core = ids[1], ids[2]
    for yy in range(2):
        for c in range(2):

            @pl.when((y == yy) & (core == c))
            def _():
                for yflip, cflip, part in ((0, 0, near), (1, 0, far), (0, 1, twin), (1, 1, far_twin)):
                    half, rank = yy ^ yflip, c ^ cflip
                    out = grad_u if rank else grad_g
                    for k in range(4):
                        start = half * HALF + k * 256
                        out[:, start : start + 256] = part[0, k * 96 : (k + 1) * 96, :].astype(F32)
                    low = (2 * half + rank) * 64
                    for k in range(3):
                        grad_d[low : low + 64, k * 256 : (k + 1) * 256] = part[
                            0, 384 + k * 64 : 384 + (k + 1) * 64, :
                        ].astype(F32)


def finish_narrow_kernel(
    ids, near, twin, grad_q, grad_k, grad_v, grad_o, grad_p, grad_1, grad_2, grad_3, table
):
    core = ids[2]
    for c in range(2):

        @pl.when(core == c)
        def _():
            low, high = (twin, near) if c else (near, twin)
            grad_q[...] = low[0, 0:96, :].astype(F32)
            grad_k[...] = high[0, 0:96, :].astype(F32)
            grad_v[...] = low[0, 96:192, :].astype(F32)
            grad_o[...] = high[0, 96:192, :].astype(F32)
            for k in range(6):
                grad_p[k * 16 : (k + 1) * 16, :] = low[
                    0, 192:208, k * DLEN : (k + 1) * DLEN
                ].astype(F32)
            rows = high[0, 192:208, :].astype(F32)
            grad_1[...] = rows[0:1, :96]
            grad_2[...] = rows[1:2, :96]
            grad_3[...] = rows[2:3, :96]
            block = jnp.where(lax.broadcasted_iota(jnp.int32, (8, DLEN), 1) < H, rows[8:16, :DLEN], 0.0)
            line = block[0:1]
            for i in range(1, BUCKETS // SHARDS):
                line += pltpu.roll(block, i * H, 1)[i : i + 1]
            table[...] = line[:, : BUCKETS // SHARDS * H]


def local(
    hidden_in,
    norm1_gain,
    w_query,
    w_key,
    w_value,
    w_out,
    rel_table,
    norm2_gain,
    w_gate,
    w_up,
    w_down,
    norm3_gain,
    w_proj,
    query_lengths,
    keyword_request_mask,
    targets,
    candidates,
):
    streams = lax.axis_size("stream")
    shards = lax.axis_size("batch")
    pairs = streams // 2
    direct = shards == SHARDS and pairs == 2
    b = lax.axis_index("batch")
    s = lax.axis_index("stream")
    y, core = s // pairs, s % pairs
    is_query = s < pairs
    ids = jnp.stack([b, y, core, is_query.astype(jnp.int32)]).astype(jnp.int32)

    def swap(block, yflip, cflip, m):
        route = []
        for source in range(streams):
            target = ((source // pairs) ^ yflip) * pairs + ((source % pairs) ^ cflip)
            for j in range(shards):
                route.append((source * shards + j, target * shards + (j ^ m)))
        return lax.ppermute(block, EVERY, route)

    fence = lax.optimization_barrier
    first_core = core == 0
    spots_a = spots_f = None
    if direct:
        lines = [part.reshape(1, -1) for part in (norm1_gain, norm2_gain, norm3_gain, rel_table)]
        slab_a, slab_f = call(
            pack_kernel,
            "pack",
            ids,
            [w_query, w_key, w_value, w_out, w_gate, w_up, w_down, w_proj, *lines],
            [((PIECE_A, D), BF), ((PIECE_F, 256), BF)],
        )

        def join(*parts):
            return jnp.concatenate(parts)

        def along_x(part):
            return swap(part, 0, 0, 1)

        def along_y(part):
            return swap(part, 1, 0, 0)

        def along_z(part):
            return swap(part, 0, 0, 2)

        def along_zz(part):
            return swap(part, 0, 0, 4)

        def other_core(part):
            return swap(part, 0, 1, 0)

        def transfers(token, long, short=()):
            *short, token = fence((*short, tick(token)))
            short = [other_core(part) for part in short]
            *both, token = fence((*long, *short, token))
            return both[: len(long)], both[len(long) :], token

        f0, a0 = slab_f[None], slab_a[None]
        token = jnp.zeros((8, DLEN), F32)
        long = [along_x(f0), along_y(f0), along_x(a0), along_z(a0), along_zz(a0)]
        (f1, y0, a1, a2, a4), _, token = transfers(token, long)
        f0, a0, token = fence((f0, a0, token))
        a42 = join(a4, a2)
        long = [along_y(f1), along_z(a4), along_x(a42), along_zz(f0)]
        (y1, a6, a53, f4), (ta0,), token = transfers(token, long, [a0])
        long = [along_x(a6), along_x(f4), along_y(f4), along_z(join(f0, f4))]
        (a7, f5, y4, f26), (ta42,), token = transfers(token, long, [a42])
        f526 = join(f5, f26)
        y526, f37 = along_y(f526), along_x(f26)
        a1, a53, a6, a7, token = fence((a1, a53, a6, a7, tick(token)))
        ta1, ta53, ta6, ta7 = [other_core(part) for part in (a1, a53, a6, a7)]
        flips_a = ((0,), (1,), (4, 2), (5, 3), (6,), (7,))
        flips_f = ((0,), (1,), (4,), (5, 2, 6), (3, 7))
        groups_a = [
            (0, *zip((a0, a1, a42, a53, a6, a7), flips_a)),
            (1, *zip((ta0, ta1, ta42, ta53, ta6, ta7), flips_a)),
        ]
        pieces_a, spots_a, pieces_f, spots_f = [], [], [], []
        for cflip, *group in groups_a:
            for part, flips in group:
                spots_a += [(cflip, m, len(pieces_a), i) for i, m in enumerate(flips)]
                pieces_a.append(part)
    else:

        def whole(part):
            return lax.all_gather(part, "batch", axis=0, tiled=True)

        wqk = jnp.stack([whole(w_query), whole(w_key)])
        wvo = jnp.stack([whole(w_value), whole(w_out)])
        gate_up = jnp.stack([whole(w_gate), whole(w_up)])
        wgu = jnp.transpose(gate_up.reshape(2, D, 2, HALF), (0, 2, 1, 3))
        wd = whole(w_down)
        wproj = whole(w_proj)
        gain_rows = [whole(gain) for gain in (norm1_gain, norm2_gain, norm3_gain)]
        gains = jnp.pad(jnp.stack(gain_rows).astype(F32), ((0, 5), (0, 0)))
        table = whole(rel_table).reshape(1, BUCKETS * H)

    micro_count = hidden_in.shape[0]
    slot = jnp.arange(DLEN)
    pair_lengths = lax.dynamic_index_in_dim(query_lengths, core, 1, keepdims=False)
    pair_keyword = lax.dynamic_index_in_dim(keyword_request_mask, core, 1, keepdims=False)
    pair_targets = lax.dynamic_index_in_dim(targets, core, 1, keepdims=False)

    def by_slot(values):
        blocks = values.reshape(micro_count, shards, GROUPS)
        own = lax.dynamic_slice_in_dim(blocks, b, 1, 1)
        blocks = jnp.where(is_query, jnp.broadcast_to(own, blocks.shape), blocks)
        return jnp.repeat(blocks, QLEN, axis=2)

    length_slots = by_slot(pair_lengths)
    valid_slots = (slot % QLEN)[None, None, :] < length_slots
    share = jnp.where(valid_slots, 1.0 / length_slots.astype(F32), 0.0)
    sharp = jnp.where(by_slot(pair_keyword) == 1, 20.0, 10.0).astype(F32)
    target_slots = by_slot(pair_targets)
    own_valid = lax.dynamic_slice_in_dim(valid_slots, b, 1, 1)
    same = (slot[:, None] // QLEN) == (slot[None, :] // QLEN)
    mask = jnp.where(is_query & ~(same[None] & own_valid), -1000000000.0, 0.0).astype(F32)

    small = 16 if direct else 48
    picked = lax.dynamic_index_in_dim(candidates, core, 1, keepdims=False)[:, 0]
    picked = picked.reshape(micro_count, shards, DLEN, picked.shape[-1])
    picked = jnp.transpose(picked, (0, 1, 3, 2))
    received = lax.all_to_all(picked, "batch", split_axis=1, concat_axis=1, tiled=True)
    picks = jnp.where(is_query, received, picked)
    (counts,) = call(
        count_kernel,
        "count",
        ids,
        [picks],
        [((micro_count, shards, DLEN, DLEN), F32)],
        limit=small,
    )

    onehot = bucket_onehot()
    by_entry = jnp.asarray(np.repeat(onehot.T, H, axis=0), BF)
    x = hidden_in[:, 0].reshape(ROWS, D)
    row_bf, row_f32 = ((ROWS, D), BF), ((ROWS, D), F32)
    qkv_shape, weight_shape = ((3, ROWS, D), BF), ((MICRO, H // 2, ROWS, DLEN), BF)
    pair_weights = ((2, D, D), BF)
    gain_rows = ((8, D), F32)
    proj_shape = ((D, DLEN), BF)
    kept = [qkv_shape, row_bf, weight_shape, row_f32, row_bf, row_bf]
    bias_shape, score_shape = ((H // 2, ROWS, DLEN), F32), ((H, ROWS, DLEN), F32)
    result = call(
        functools.partial(attention_forward_kernel, direct, spots_a),
        "attention_forward",
        ids,
        [x, mask, by_entry] + ([] if direct else [gains, table, wqk, wvo]),
        kept + ([gain_rows, proj_shape] if direct else []),
        ([pair_weights, pair_weights, ((2, SHARDS, 16, D), BF)] if direct else [])
        + [bias_shape, score_shape],
        far=pieces_a if direct else [],
        far_outs=[pair_weights, pair_weights] if direct else [],
        sems=3 if direct else 0,
        flops=2 * ROWS * D * D * 4,
    )
    qkv, attended, weights, first, n1, n2 = result[:6]
    if direct:
        gains, wproj, wqk, wvo = result[6:]
    first, counts, share, sharp, target_slots = fence((first, counts, share, sharp, target_slots))
    if direct:
        t014, ty014 = other_core(join(f0, f1, f4)), other_core(join(y0, y1, y4))
        y526, f37, t014, ty014, first, token = fence((y526, f37, t014, ty014, first, token))
        y37 = along_y(f37)
        (y37,), (t526, t37, ty526), token = transfers(token, [y37], [f526, f37, y526])
        near = zip((f0, f1, f4, f526, f37), flips_f)
        far = zip((y0, y1, y4, y526, y37), flips_f)
        joined_f = ((0, 1, 4), (5, 2, 6), (3, 7))
        twin = zip((t014, t526, t37), joined_f)
        far_twin = zip((ty014, ty526, other_core(y37)), joined_f)
        for yflip, cflip, group in ((0, 0, near), (0, 1, twin), (1, 0, far), (1, 1, far_twin)):
            for part, flips in group:
                spots_f += [(yflip, cflip, m, len(pieces_f), i) for i, m in enumerate(flips)]
                pieces_f.append(part)
    wide_bf, deep_bf = ((2, ROWS, HALF), BF), ((ROWS, FF), BF)
    wgu_shape, wd_shape = ((2, 2, D, HALF), BF), ((FF, D), BF)
    lasting = [wide_bf, wide_bf, deep_bf]
    result = call(
        functools.partial(ffn_forward_kernel, direct, spots_f),
        "ffn_forward",
        ids,
        [first, n2, gains, wproj] + ([] if direct else [wgu, wd]),
        [row_f32, row_bf, ((ROWS, DLEN), BF)] + ([] if direct else lasting),
        [wgu_shape, wd_shape] + lasting if direct else [],
        far=[*pieces_f, token] if direct else [],
        far_outs=lasting if direct else [],
        sems=5 if direct else 0,
        flops=2 * ROWS * D * FF * 3,
    )
    second, n3, vectors, gelu_kept, slope_kept, hidden = result

    if direct:
        even = jnp.stack([swap(vectors, 1, 0, m) for m in (0, 2, 4, 6)])
        others = [even, swap(even, 0, 0, 1)]
    else:
        route = [(i, (i + pairs) % streams) for i in range(streams)]
        arrived = lax.ppermute(vectors, "stream", route)
        others = [lax.all_gather(arrived, "batch", axis=0)]
    block_f32 = ((micro_count, shards, DLEN, DLEN), F32)
    line_f32 = ((micro_count, shards, DLEN), F32)
    soft, score = call(
        functools.partial(similarity_kernel, direct, shards),
        "similarity",
        ids,
        [vectors, counts, share, *others],
        [block_f32, line_f32],
        [line_f32],
        limit=small,
    )
    if direct:
        blocks = jnp.broadcast_to(score[None], (shards,) + score.shape)
        scores = lax.all_to_all(blocks, "batch", split_axis=0, concat_axis=0, tiled=True)
    else:
        scores = lax.all_gather(score, "batch", axis=0)
    (dvec,) = call(
        functools.partial(vector_grad_kernel, direct, shards),
        "vector_grad",
        ids,
        [soft, share, sharp, target_slots, score, scores, *others],
        [((ROWS, DLEN), BF)],
        [line_f32, ((ROWS, DLEN), F32)],
        limit=small,
    )

    gain_row = ((1, D), F32)
    proj_f32 = ((D, DLEN), F32)
    dgu_shape = ((2, 2, ROWS, HALF), BF)
    quarter = ((SHARDS, PIECE_F, 256), BF)
    saved = [hidden, gelu_kept, slope_kept]
    result = call(
        functools.partial(ffn_backward_kernel, direct, spots_f),
        "ffn_backward",
        ids,
        [dvec, second, n2, n3, gains, wproj] + ([] if direct else [wd, *saved]),
        [row_f32, proj_f32, gain_row, dgu_shape] + ([] if direct else [row_bf]),
        [wd_shape, deep_bf, wide_bf, wide_bf, ((SHARDS, 4, 64, D), BF), ((4, *quarter[0]), BF)]
        if direct
        else [],
        far=[*saved, *pieces_f] if direct else [],
        far_outs=[quarter] * 4 if direct else [],
        sems=4 if direct else 0,
        flops=2 * ROWS * D * FF * 4,
    )
    dx2, grad_proj, grad_gain, dgu = result[:4]
    if direct:
        f_own, f_own_far, f_twin, f_twin_far = result[4:]
    else:
        dy = result[4]

    if direct:
        far_twin = other_core(f_twin_far)
    middle_in = [dx2, first, dgu, gains]
    dx1, dattended, grad_gain2 = call(
        functools.partial(middle_backward_kernel, direct, spots_f),
        "middle_backward",
        ids,
        middle_in + ([] if direct else [wgu, wvo]),
        [row_f32, row_bf, gain_row],
        [wgu_shape, ((D, D), BF)] if direct else [],
        far=[*pieces_f, wvo] if direct else [],
        sems=5 if direct else 0,
        flops=2 * ROWS * D * (FF * 2 + D),
    )
    if direct:
        far_twin, dattended = fence((far_twin, dattended))
        sent_23, sent_67, sent_45, sent_01 = add_up(
            ids, *([[(f_own_far, m + i), (far_twin, m + i)] for i in range(2)] for m in (2, 6, 4, 0))
        )
        y67, y23, twin = along_y(sent_67), along_y(sent_23), other_core(f_twin)
        sent_23, sent_67, sent_45, sent_01, dattended = fence(
            (sent_23, sent_67, sent_45, sent_01, dattended)
        )
    two_rows = ((2, ROWS, D), BF)
    slab_out = ((SHARDS, PIECE_A, D), BF)
    blocks_bf = ((H, ROWS, DLEN), BF)
    result = call(
        functools.partial(attention_backward_kernel, direct),
        "attention_backward",
        ids,
        [dx1, dattended, x, n1, attended, weights, qkv, gains, jnp.asarray(onehot.T)]
        + [grad_proj, grad_gain2, grad_gain]
        + ([] if direct else [wqk, wvo]),
        [row_f32] if direct else [((40, D), F32), row_f32, qkv_shape, row_bf],
        ([pair_weights, pair_weights, slab_out, slab_out] if direct else [])
        + [two_rows, two_rows, two_rows]
        + ([((2, SHARDS, 16, D), F32)] if direct else [])
        + [((DLEN, 2 * DLEN), F32), ((BUCKETS, DLEN), F32)]
        + [score_shape, blocks_bf, blocks_bf, blocks_bf],
        far=[wqk, wvo] if direct else [],
        far_outs=[slab_out, slab_out] if direct else [],
        sems=2 if direct else 0,
        flops=ROUND_FLOPS,
    )

    if direct:
        input_grad, a_own, a_other = result

        def own_f(m, *more):
            return [(f_own, m), (twin, m), *more]

        def own_a(m, *more):
            return [(a_own, m), (twin_a, m), *more]

        token = jnp.ones((8, DLEN), F32)
        y23, twin, a_own = fence((y23, twin, a_own))
        (out_3,) = add_up(ids, [own_f(3, (y23, 1))])
        y45, x3, twin_a = along_y(sent_45), along_x(out_3), other_core(a_other)
        y67, twin_a, x3, sent_01, token = fence((y67, twin_a, x3, sent_01, tick(token)))

        out_7, out_a3 = add_up(ids, [own_f(7, (y67, 1))], [own_a(3)])
        y01, xa3, x7 = along_y(sent_01), along_x(out_a3), along_x(out_7)
        y45, x7, xa3, token = fence((y45, x7, xa3, tick(token)))

        out_26, out_5, out_a7 = add_up(
            ids,
            [own_f(2, (y23, 0), (x3, 0)), own_f(6, (y67, 0), (x7, 0))],
            [own_f(5, (y45, 1))],
            [own_a(7)],
        )
        xa7, x5, z26 = along_x(out_a7), along_x(out_5), along_z(out_26)
        y01, z26, x5, xa7, token = fence((y01, z26, x5, xa7, tick(token)))

        out_4, out_1, out_a26, out_a5 = add_up(
            ids,
            [own_f(4, (y45, 0), (x5, 0), (z26, 1))],
            [own_f(1, (y01, 1))],
            [own_a(2, (xa3, 0)), own_a(6, (xa7, 0))],
            [own_a(5)],
        )
        xa5, x1, za26, z4 = along_x(out_a5), along_x(out_1), along_z(out_a26), along_zz(out_4)
        z4, x1, za26, xa5, token = fence((z4, x1, za26, xa5, tick(token)))

        mine_f, out_a4, out_a1 = add_up(
            ids,
            [own_f(0, (y01, 0), (x1, 0), (z26, 0), (z4, 0))],
            [own_a(4, (xa5, 0), (za26, 1))],
            [own_a(1)],
        )
        far, xa1, za4 = along_y(mine_f), along_x(out_a1), along_zz(out_a4)
        mine_f, far, xa1, za4, token = fence((mine_f, far, xa1, za4, tick(token)))

        (part_a,) = add_up(ids, [own_a(0, (za26, 0), (xa1, 0), (za4, 0))])
        twin_f, far_twin_f, ya = other_core(mine_f), other_core(far), along_y(part_a)
        twin_f, far_twin_f, part_a, token = fence((twin_f, far_twin_f, part_a, tick(token)))
        shard_f32, wide_f32 = ((96, D), F32), ((96, FF), F32)
        grad_g, grad_u, grad_d = call(
            finish_wide_kernel,
            "finish_wide",
            ids,
            [mine_f, far, twin_f, far_twin_f],
            [wide_f32, wide_f32, ((256, D), F32)],
            far=[token],
            limit=24,
        )
        ya, grad_g, grad_u, grad_d = fence((ya, grad_g, grad_u, grad_d))
        (mine_a,) = add_up(ids, [[(part_a, 0), (ya, 0)]])
        grad_q, grad_k, grad_v, grad_o, grad_p, *small = call(
            finish_narrow_kernel,
            "finish_narrow",
            ids,
            [mine_a, other_core(mine_a)],
            [shard_f32] * 4 + [((96, DLEN), F32), ((1, 96), F32), ((1, 96), F32), ((1, 96), F32)]
            + [((1, 48), F32)],
            limit=24,
        )
        grad_n1, grad_n2, grad_n3, grad_table = [row.reshape(-1) for row in small]
    else:
        small, input_grad, dqkv, da = result

        def summed(part):
            part = lax.psum_scatter(part, "batch", scatter_dimension=0, tiled=True)
            return lax.psum(part, "stream")

        grad_q, grad_k, grad_v = [summed(dot_tn(n1, dqkv[i])) for i in range(3)]
        grad_o = summed(dot_tn(attended, da))
        grad_g, grad_u = [
            summed(jnp.concatenate([dot_tn(n2, dgu[i, half]) for half in range(2)], axis=1))
            for i in range(2)
        ]
        grad_d = summed(dot_tn(hidden, dy))
        grad_p = summed(grad_proj)
        grad_n1, grad_n2, grad_n3 = [summed(small[i]) for i in range(3)]
        flat = lax.psum(small[8 : 8 + BUCKETS, :H].reshape(-1), EVERY)
        share_rows = flat.shape[0] // shards
        grad_table = lax.dynamic_slice_in_dim(flat, b * share_rows, share_rows, 0)

    vectors_out = vectors.reshape(micro_count, DLEN, DLEN)[:, None]
    grad_hidden = input_grad.reshape(micro_count, DLEN, D)[:, None]
    return (
        vectors_out,
        grad_hidden,
        grad_n1,
        grad_q,
        grad_k,
        grad_v,
        grad_o,
        grad_table,
        grad_n2,
        grad_g,
        grad_u,
        grad_d,
        grad_n3,
        grad_p,
    )


def solution(mesh):
    rows, lines = P("batch", None), P("batch")
    spread = P(None, "stream", "batch", None)
    return jax.shard_map(
        local,
        mesh=mesh,
        in_specs=(spread, lines, rows, rows, rows, rows, lines, lines, rows, rows, rows, lines, rows)
        + (P(), P(), P(), P(None, None, "batch", None, None)),
        out_specs=(spread, spread, lines, rows, rows, rows, rows, lines, lines)
        + (rows, rows, rows, lines, rows),
        check_vma=False,
    )
```

```python
import functools
import math

import jax
import jax.numpy as jnp
import numpy as np
from jax import lax
from jax.experimental import pallas as pl
from jax.experimental.pallas import tpu as pltpu
from jax.sharding import PartitionSpec as P

H = 12
DH = 64
BUCKETS = 32
MAX_DIST = 128
DLEN = 128
QLEN = 32
GROUPS = DLEN // QLEN
MICRO = 2
ROWS = MICRO * DLEN
D = 768
FF = 2048
HALF = FF // 2
SHARDS = 8
PIECE_A = 208
PIECE_F = 576
PAIRS_F = ((6, 7), (2, 3), (4, 5), (0, 1))

EPSILON = 1e-06
HIGHEST = lax.Precision.HIGHEST
BF = jnp.bfloat16
F32 = jnp.float32
EVERY = ("stream", "batch")
MIB = 2**20
ROUND_FLOPS = 5 * 10**10


def distance_bucket(distance):
    half_count = BUCKETS // 2
    exact_count = half_count // 2
    if distance < exact_count:
        return distance
    grown = exact_count + int(
        math.floor(
            math.log(distance / exact_count)
            / math.log(MAX_DIST / exact_count)
            * (half_count - exact_count)
            + 1e-09
        )
    )
    return min(grown, half_count - 1)


def bucket_onehot():
    table = np.zeros((2 * DLEN, BUCKETS), np.float32)
    for o in range(2 * DLEN - 1):
        offset = o - (DLEN - 1)
        table[o, distance_bucket(abs(offset)) + (BUCKETS // 2 if offset > 0 else 0)] = 1.0
    return table


def norm_scale(values):
    return lax.rsqrt(jnp.mean(values * values, axis=-1, keepdims=True) + EPSILON)


def norm_backward(values, gain, grad):
    scale = norm_scale(values)
    pulled = gain * grad
    inner = jnp.mean(values * pulled, axis=-1, keepdims=True)
    back = scale * pulled - values * (scale * scale * scale * inner)
    return back, jnp.sum(grad * values * scale, axis=0, keepdims=True)


def dot(left, right):
    return jnp.dot(left, right, preferred_element_type=F32)


def dot_nt(left, right):
    return lax.dot_general(left, right, (((1,), (1,)), ((), ())), preferred_element_type=F32)


def dot_tn(left, right):
    return lax.dot_general(left, right, (((0,), (0,)), ((), ())), preferred_element_type=F32)


def steps(count, body):
    if count <= 16:
        for i in range(count):
            body(i)
    else:

        @pl.loop(0, count)
        def _(i):
            body(i)


VMEM = pl.BlockSpec(memory_space=pltpu.VMEM)
SMEM = pl.BlockSpec(memory_space=pltpu.SMEM)
HBM = pl.BlockSpec(memory_space=pltpu.HBM)


def call(
    kernel, name, ids, arrays, outs, scratch=(), far=(), far_outs=(), sems=0, flops=0, limit=58
):
    shapes = [jax.ShapeDtypeStruct(s, t) for s, t in (*outs, *far_outs)]
    moved = sum(math.prod(s.shape) * s.dtype.itemsize for s in shapes)
    moved += sum(math.prod(a.shape) * a.dtype.itemsize for a in (*arrays, *far))
    scratch_shapes = [pltpu.VMEM(s, t) for s, t in scratch]
    if sems:
        scratch_shapes.append(pltpu.SemaphoreType.DMA((sems,)))
    return pl.pallas_call(
        kernel,
        name=name,
        out_shape=shapes,
        in_specs=[SMEM] + [VMEM] * len(arrays) + [HBM] * len(far),
        out_specs=[VMEM] * len(outs) + [HBM] * len(far_outs),
        scratch_shapes=scratch_shapes,
        compiler_params=pltpu.CompilerParams(vmem_limit_bytes=limit * MIB),
        cost_estimate=pl.CostEstimate(flops=flops, bytes_accessed=moved, transcendentals=0),
    )(ids, *arrays, *far)


def tick_kernel(token, out):
    pass


def tick(token):
    return pl.pallas_call(
        tick_kernel,
        name="tick",
        in_specs=[HBM],
        out_specs=HBM,
        out_shape=jax.ShapeDtypeStruct(token.shape, token.dtype),
        input_output_aliases={0: 0},
        cost_estimate=pl.CostEstimate(flops=ROUND_FLOPS, bytes_accessed=0, transcendentals=0),
    )(token)


def add_kernel(plan, near, far, ids, *refs):
    near, far, refs = refs[:near], refs[near : near + far], refs[near + far :]
    outs, refs = refs[: len(plan)], refs[len(plan) :]
    held, sems = (refs[:-1], refs[-1]) if far else ((), None)
    place = 0
    for entries in plan:
        for terms in entries:
            for is_far, array, entry in terms:
                if is_far:
                    copies([(far[array].at[entry], held[place])], sems.at[place])
                    place += 1
    place = 0
    for out, entries in zip(outs, plan):
        for i, terms in enumerate(entries):
            total = None
            for is_far, array, entry in terms:
                if is_far:
                    landed(held[place], sems.at[place])
                    part = held[place][...].astype(F32)
                    place += 1
                else:
                    part = near[array][entry].astype(F32)
                total = part if total is None else total + part
            out[i] = total.astype(BF)


def base_kernel(picks, ids, own, twin, base_out, *refs):
    outs, (base, sem) = refs[:-2], refs[-2:]
    for m in range(SHARDS):
        base[m] = (own[m].astype(F32) + twin[m].astype(F32)).astype(BF)
    copies([(base, base_out)], sem.at[0])
    for out, entries in zip(outs, picks):
        for i, m in enumerate(entries):
            out[i] = base[m]
    landed(base, sem.at[0])


def base_up(ids, own, twin, *picks):
    shape = own.shape
    return pl.pallas_call(
        functools.partial(base_kernel, picks),
        name="base_up",
        in_specs=[SMEM, VMEM, VMEM],
        out_specs=[HBM] + [VMEM] * len(picks),
        out_shape=[jax.ShapeDtypeStruct(shape, BF)]
        + [jax.ShapeDtypeStruct((len(entries), *shape[1:]), BF) for entries in picks],
        scratch_shapes=[pltpu.VMEM(shape, BF), pltpu.SemaphoreType.DMA((1,))],
        compiler_params=pltpu.CompilerParams(vmem_limit_bytes=24 * MIB),
        cost_estimate=pl.CostEstimate(flops=0, bytes_accessed=16 * 2**20, transcendentals=0),
    )(ids, own, twin)


def add_up(ids, *outputs, whole=False):
    known = ([], [])
    plan, flat, shapes = [], [], []
    for entries in outputs:
        plan.append([])
        for terms in entries:
            plan[-1].append([])
            for array, entry in terms:
                is_far = int(array.shape[0] > 4 and not whole)
                arrays = known[is_far]
                found = [i for i, other in enumerate(arrays) if other is array]
                if not found:
                    arrays.append(array)
                    found = [len(arrays) - 1]
                if is_far:
                    flat.append((array.shape[1:], BF))
                plan[-1][-1].append((is_far, found[0], entry))
        shapes.append(((len(entries), *entries[0][0][0].shape[1:]), BF))
    return call(
        functools.partial(add_kernel, plan, len(known[0]), len(known[1])),
        "add_up",
        ids,
        known[0],
        shapes,
        flat,
        far=known[1],
        sems=len(flat),
        limit=24,
    )


def pack_kernel(ids, wq, wk, wv, wo, wg, wu, wd, wp, g1, g2, g3, table, slab_a, slab_f):
    y, core = ids[1], ids[2]

    def fill(top, bottom, wide, rank):
        slab_a[0:96, :] = top[...]
        slab_a[96:192, :] = bottom[...]
        for yy in range(2):

            @pl.when(y == yy)
            def _():
                for k in range(4):
                    start = yy * HALF + k * 256
                    slab_f[k * 96 : (k + 1) * 96, :] = wide[:, start : start + 256]
                row = (2 * yy + rank) * 64
                for k in range(3):
                    slab_f[384 + k * 64 : 384 + (k + 1) * 64, :] = wd[
                        row : row + 64, k * 256 : (k + 1) * 256
                    ]

    @pl.when(core == 0)
    def _():
        fill(wq, wv, wg, 0)
        for k in range(6):
            slab_a[192:208, k * DLEN : (k + 1) * DLEN] = wp[k * 16 : (k + 1) * 16, :]

    @pl.when(core == 1)
    def _():
        fill(wk, wo, wu, 1)
        rows = [g1[...].astype(F32), g2[...].astype(F32), g3[...].astype(F32)]
        head = jnp.concatenate(rows + [jnp.zeros((5, 96), F32)], axis=0)
        tail = jnp.concatenate([table[...].astype(F32), jnp.zeros((7, 48), F32)], axis=0)
        tail = jnp.concatenate([tail, jnp.zeros((8, 48), F32)], axis=1)
        both = jnp.concatenate([head, tail], axis=0)
        slab_a[192:208, :] = jnp.concatenate(
            [both, jnp.zeros((16, D - 96), F32)], axis=1
        ).astype(BF)


def copies(pairs, sem):
    for src, dst in pairs:
        pltpu.make_async_copy(src, dst, sem).start()


def landed(buffer, sem):
    pltpu.make_async_copy(buffer, buffer, sem).wait()


def fetch_a(ids, pieces, spots, wqk, wvo, extra, sems):
    b, core = ids[0], ids[2]
    for cflip, m, array, entry in spots:
        src = pieces[array].at[entry]
        c, j = core ^ cflip, b ^ m
        row = pl.multiple_of(j * 96, 96)
        copies([(src.at[pl.ds(0, 96)], wqk.at[c, pl.ds(row, 96)])], sems.at[0])
        copies([(src.at[pl.ds(96, 96)], wvo.at[c, pl.ds(row, 96)])], sems.at[1])
        copies([(src.at[pl.ds(192, 16)], extra.at[c, j])], sems.at[2])


def fetch_wide(ids, pieces, spots, wgu, sems):
    b, y, core = ids[0], ids[1], ids[2]
    for yflip, cflip, m, array, entry in spots:
        src = pieces[array].at[entry]
        c, yy, j = core ^ cflip, y ^ yflip, b ^ m
        row = pl.multiple_of(j * 96, 96)
        for k in range(4):
            tile = wgu.at[c, yy, pl.ds(row, 96), pl.ds(k * 256, 256)]
            copies([(src.at[pl.ds(k * 96, 96)], tile)], sems.at[2 * yy + c])


def fetch_deep(ids, pieces, spots, wd, sem):
    b, y, core = ids[0], ids[1], ids[2]
    for yflip, cflip, m, array, entry in spots:
        src = pieces[array].at[entry]
        low = pl.multiple_of((b ^ m) * 256 + (2 * (y ^ yflip) + (core ^ cflip)) * 64, 64)
        for k in range(3):
            tile = wd.at[pl.ds(low, 64), pl.ds(k * 256, 256)]
            copies([(src.at[pl.ds(384 + k * 64, 64)], tile)], sem)


def head_masks():
    low_lane = lax.broadcasted_iota(jnp.int32, (DLEN, DLEN), 1) < DH
    return low_lane


def both_heads(pair, low_lane):
    zero = jnp.zeros_like(pair)
    return jnp.concatenate(
        [jnp.where(low_lane, pair, zero), jnp.where(low_lane, zero, pair)], axis=0
    )


PAIRS_OF_HEADS = [
    (m, p, slice(m * DLEN, (m + 1) * DLEN), slice(p * DLEN, (p + 1) * DLEN))
    for m in range(MICRO)
    for p in range(H // 2)
]


def attention_forward_kernel(direct, spots, ids, x, mask, onehot, *refs):
    if direct:
        count = 1 + max(spot[2] for spot in spots)
        pieces, refs = refs[:count], refs[count:]
        qkv, attended, weights, first, n1, n2, gains, wproj, wqk_out, wvo_out = refs[:10]
        wqk, wvo, extra, bias, scores, sems = refs[10:]
        fetch_a(ids, pieces, spots, wqk, wvo, extra, sems)
        landed(extra, sems.at[2])
        lane = lax.broadcasted_iota(jnp.int32, (8, D), 1)
        all_gains = jnp.zeros((8, D), F32)
        flat = jnp.zeros((8, D), F32)
        for j in range(SHARDS):
            block = extra[1, j].astype(F32)
            all_gains += pltpu.roll(jnp.where(lane < 96, block[0:8], 0.0), j * 96, 1)
            flat += pltpu.roll(jnp.where(lane < 48, block[8:16], 0.0), j * 48, 1)
            for k in range(6):
                wproj[j * 96 + k * 16 : j * 96 + (k + 1) * 16, :] = extra[
                    0, j, :, k * DLEN : (k + 1) * DLEN
                ]
        gains[...] = all_gains
        flat = flat[0:1, : BUCKETS * H]
    else:
        gains, flat_in, wqk, wvo = refs[:4]
        qkv, attended, weights, first, n1, n2, bias, scores = refs[4:]
        flat = flat_in[...].astype(F32)
    entry = lax.broadcasted_iota(jnp.int32, (16, BUCKETS * H), 1)
    head = lax.broadcasted_iota(jnp.int32, (16, BUCKETS * H), 0)
    by_head = jnp.where(entry % H == head, jnp.broadcast_to(flat, entry.shape), 0.0)
    offsets = dot(by_head.astype(BF), onehot[...])
    for h in range(H):
        row = jnp.broadcast_to(offsets[h : h + 1, :], (DLEN, 2 * DLEN))
        rolled = pltpu.roll(row, DLEN + 1, 1, stride=1, stride_axis=0)
        bias[h // 2, (h % 2) * DLEN : (h % 2 + 1) * DLEN, :] = rolled[:, :DLEN]
    tokens = x[...].astype(F32)
    normed = (tokens * norm_scale(tokens) * gains[0:1, :]).astype(BF)
    n1[...] = normed
    if direct:
        landed(wqk, sems.at[0])
        copies([(wqk, wqk_out)], sems.at[0])
        landed(wvo, sems.at[1])
        copies([(wvo, wvo_out)], sems.at[1])
    qkv[0] = dot(normed, wqk[0]).astype(BF)
    qkv[1] = dot(normed, wqk[1]).astype(BF)
    qkv[2] = dot(normed, wvo[0]).astype(BF)
    low_lane = head_masks()
    for i, (m, p, rows, lanes) in enumerate(PAIRS_OF_HEADS):
        scores[i] = dot_nt(both_heads(qkv[0, rows, lanes], low_lane), qkv[1, rows, lanes])
    for i, (m, p, rows, lanes) in enumerate(PAIRS_OF_HEADS):
        hidden = jnp.concatenate([mask[m], mask[m]], axis=0)
        biased = scores[i] + bias[p] + hidden
        shifted = jnp.exp(biased - jnp.max(biased, axis=-1, keepdims=True))
        weights[m, p] = (shifted / jnp.sum(shifted, axis=-1, keepdims=True)).astype(BF)
    for i, (m, p, rows, lanes) in enumerate(PAIRS_OF_HEADS):
        mixed = dot(weights[m, p], qkv[2, rows, lanes])
        attended[rows, lanes] = jnp.where(low_lane, mixed[:DLEN], mixed[DLEN:]).astype(BF)
    x1 = tokens + dot(attended[...], wvo[1])
    first[...] = x1
    n2[...] = (x1 * norm_scale(x1) * gains[1:2, :]).astype(BF)
    if direct:
        landed(wqk, sems.at[0])
        landed(wvo, sems.at[1])


def gelu_parts(gate):
    c0, c1 = math.sqrt(2.0 / math.pi), 0.044715
    square = gate * gate
    bent = jnp.tanh(c0 * gate * (1.0 + c1 * square))
    value = 0.5 * gate * (1.0 + bent)
    slope = 0.5 * (1.0 + bent) + 0.5 * gate * (1.0 - bent * bent) * (
        c0 * (1.0 + 3.0 * c1 * square)
    )
    return value, slope


def ffn_forward_kernel(direct, spots, ids, first, n2, gains, wproj, *refs):
    if direct:
        count = 1 + max(spot[3] for spot in spots)
        pieces, refs = refs[:count], refs[count:]
        second, n3, vectors, gelu_out, slope_out, hidden_out = refs[1:7]
        wgu, wd, gelu_kept, slope_kept, hidden, sems = refs[7:]
        fetch_wide(ids, pieces, spots, wgu, sems)
        fetch_deep(ids, pieces, spots, wd, sems.at[4])
    else:
        wgu, wd, second, n3, vectors, gelu_kept, slope_kept, hidden = refs
    normed = n2[...]
    for half in range(2):
        lanes = slice(half * HALF, (half + 1) * HALF)
        if direct:
            landed(wgu.at[0, half], sems.at[2 * half])
            landed(wgu.at[1, half], sems.at[2 * half + 1])
        gate = dot(normed, wgu[0, half])
        up = dot(normed, wgu[1, half])
        value, slope = gelu_parts(gate)
        gelu_kept[half] = value.astype(BF)
        slope_kept[half] = (up * slope).astype(BF)
        hidden[:, lanes] = (value * up).astype(BF)
        if direct:
            copies([(gelu_kept.at[half], gelu_out.at[half])], sems.at[2 * half])
            copies([(slope_kept.at[half], slope_out.at[half])], sems.at[2 * half + 1])
    if direct:
        landed(wd, sems.at[4])
        copies([(hidden, hidden_out)], sems.at[4])
    total = first[...] + dot(hidden[...], wd[...])
    second[...] = total
    normed_three = (total * norm_scale(total) * gains[2:3, :]).astype(BF)
    n3[...] = normed_three
    vectors[...] = dot(normed_three, wproj[...]).astype(BF)
    if direct:
        for half in range(2):
            landed(gelu_kept.at[half], sems.at[2 * half])
            landed(slope_kept.at[half], sems.at[2 * half + 1])
        landed(hidden, sems.at[4])


def count_kernel(ids, picks, counts):
    spots = lax.broadcasted_iota(jnp.int32, (DLEN, DLEN), 0)

    def one(j):
        for m in range(MICRO):
            total = jnp.zeros((DLEN, DLEN), F32)
            for t in range(picks.shape[2]):
                total += jnp.where(spots == picks[m, j, t : t + 1, :], 1.0, 0.0)
            counts[m, j] = total

    steps(picks.shape[1], one)


def block_of(others, m):
    return others[m % 2].at[m // 2] if len(others) == 2 else others[0].at[m]


def group_sums(values):
    lane = lax.broadcasted_iota(jnp.int32, values.shape, 1)
    shift = 1
    while shift < QLEN:
        ahead = pltpu.roll(values, DLEN - shift, 1)
        behind = pltpu.roll(values, shift, 1)
        values = values + jnp.where((lane & shift) == 0, ahead, behind)
        shift *= 2
    return values


def similarity_kernel(direct, count, ids, own, counts, share, *refs):
    others, (soft, score, best) = refs[:-3], refs[-3:]
    b, is_query = ids[0], ids[3]
    scale = DLEN**-0.5

    def one(m):
        j = (b ^ m) if direct else m
        for micro in range(MICRO):
            rows = slice(micro * DLEN, (micro + 1) * DLEN)
            mine, theirs = own[rows, :], block_of(others, m)[rows, :]
            doc = jnp.where(is_query == 1, theirs, mine)
            query = jnp.where(is_query == 1, mine, theirs)
            times = counts[micro, j]
            sim = dot_nt(doc, query) * scale
            peak = jnp.max(jnp.where(times > 0, sim, -jnp.inf), axis=0, keepdims=True)
            mass = jnp.where(times > 0, times * jnp.exp(jnp.minimum(sim - peak, 0.0)), 0.0)
            total = jnp.sum(mass, axis=0, keepdims=True)
            soft[micro, j] = mass / total
            best[micro, pl.ds(j, 1), :] = peak + jnp.log(total)

    steps(count, one)
    for micro in range(MICRO):
        score[micro] = group_sums(best[micro] * share[micro])


def vector_grad_kernel(
    direct, count, ids, soft, share, sharp, target, score, scores, *refs
):
    others, (grad, weight, total) = refs[:-3], refs[-3:]
    b, is_query = ids[0], ids[3]
    scale = DLEN**-0.5

    @pl.when(is_query == 1)
    def _():
        for micro in range(MICRO):
            logits = score[micro] * sharp[micro]
            raised = jnp.exp(logits - jnp.max(logits, axis=0, keepdims=True))
            odds = raised / jnp.sum(raised, axis=0, keepdims=True)
            doc = lax.broadcasted_iota(jnp.int32, (count, DLEN), 0)
            hit = jnp.where(target[micro] == doc, 1.0, 0.0)
            weight[micro] = (odds - hit) * sharp[micro] * share[micro] * scale

    @pl.when(is_query == 0)
    def _():
        for micro in range(MICRO):
            sharpness = sharp[micro]
            logits = scores[:, micro] * sharpness[None]
            peak = jnp.max(logits, axis=0)
            norm = jnp.sum(jnp.exp(logits - peak[None]), axis=0)
            odds = jnp.exp(score[micro] * sharpness - peak) / norm
            hit = jnp.where(target[micro] == b, 1.0, 0.0)
            weight[micro] = (odds - hit) * sharpness * share[micro] * scale

    total[...] = jnp.zeros_like(total)

    def one(m):
        j = (b ^ m) if direct else m
        for micro in range(MICRO):
            rows = slice(micro * DLEN, (micro + 1) * DLEN)
            dense = soft[micro, j] * weight[micro, pl.ds(j, 1), :]
            upper = dense.astype(BF)
            lower = (dense - upper.astype(F32)).astype(BF)
            theirs = block_of(others, m)[rows, :]

            @pl.when(is_query == 1)
            def _():
                total[rows, :] += dot_tn(upper, theirs) + dot_tn(lower, theirs)

            @pl.when(is_query == 0)
            def _():
                total[rows, :] += dot(upper, theirs) + dot(lower, theirs)

    steps(count, one)
    grad[...] = total[...].astype(BF)


def ffn_backward_kernel(direct, spots, ids, dvec, second, n2, n3, gains, wproj, *refs):
    if direct:
        hidden_in, gelu_in, slope_in = refs[:3]
        count = 1 + max(spot[3] for spot in spots)
        pieces, refs = refs[3 : 3 + count], refs[3 + count :]
        dx2_out, grad_proj, grad_gain, dgu, *outs = refs[:14]
        wd, hidden, gelu_kept, slope_kept, grad_down, quarters, sems = refs[14:]
        fetch_deep(ids, pieces, spots, wd, sems.at[0])
        copies([(slope_in, slope_kept)], sems.at[1])
        copies([(gelu_in, gelu_kept)], sems.at[2])
        copies([(hidden_in, hidden)], sems.at[3])
    else:
        wd, hidden, gelu_kept, slope_kept, dx2_out, grad_proj, grad_gain, dgu, dy_out = refs
    b, y, core = ids[0], ids[1], ids[2]
    dvectors = dvec[...]
    grad_proj[...] = dot_tn(n3[...], dvectors)
    dn3 = dot_nt(dvectors, wproj[...])
    dx2, dgain3 = norm_backward(second[...], gains[2:3, :], dn3)
    dx2_out[...] = dx2
    grad_gain[...] = dgain3
    dy = dx2.astype(BF)
    if direct:
        landed(wd, sems.at[0])
    dh = dot_nt(dy, wd[...])
    if direct:
        landed(slope_kept, sems.at[1])
        landed(gelu_kept, sems.at[2])
    for half in range(2):
        part = dh[:, half * HALF : (half + 1) * HALF]
        dgu[0, half] = (part * slope_kept[half].astype(F32)).astype(BF)
        dgu[1, half] = (part * gelu_kept[half].astype(F32)).astype(BF)
    if not direct:
        dy_out[...] = dy
        return
    landed(hidden, sems.at[3])
    for j in range(SHARDS):
        down = dot_tn(hidden[:, j * 256 : (j + 1) * 256], dy).astype(BF)
        for part in range(4):
            grad_down[j, part] = down[part * 64 : (part + 1) * 64, :]
    normed = n2[...]
    for cflip in (1, 0):
        for yflip in (1, 0):
            place = cflip * 2 + yflip
            c, yy = core ^ cflip, y ^ yflip
            piece = dot_tn(normed, dgu[c, yy]).astype(BF)
            for j in range(SHARDS):
                m = b ^ j
                for k in range(4):
                    quarters[place, m, k * 96 : (k + 1) * 96, :] = piece[
                        j * 96 : (j + 1) * 96, k * 256 : (k + 1) * 256
                    ]
                down = grad_down[j, 2 * yy + c]
                for k in range(3):
                    quarters[place, m, 384 + k * 64 : 384 + (k + 1) * 64, :] = down[
                        :, k * 256 : (k + 1) * 256
                    ]
            if yflip:
                parts = outs[2 + 4 * cflip : 6 + 4 * cflip]
                for (m, _), out in zip(PAIRS_F, parts):
                    copies([(quarters.at[place, pl.ds(m, 2)], out)], sems.at[place])
            else:
                copies([(quarters.at[place], outs[cflip])], sems.at[place])
    for place in range(4):
        landed(quarters.at[place], sems.at[place])


def middle_backward_kernel(direct, spots, ids, dx2, first, dgu, gains, *refs):
    if direct:
        count = 1 + max(spot[3] for spot in spots)
        pieces, refs = refs[:count], refs[count:]
        wvo_in, dx1_out, dattended, grad_gain, wgu, wout, sems = refs
        fetch_wide(ids, pieces, spots, wgu, sems)
        copies([(wvo_in.at[1], wout)], sems.at[4])
    else:
        wgu, wvo, dx1_out, dattended, grad_gain = refs
        wout = wvo.at[1]
    dn2 = jnp.zeros((ROWS, D), F32)
    for half in range(2):
        for c in range(2):
            if direct:
                landed(wgu.at[c, half], sems.at[half * 2 + c])
            dn2 = dn2 + dot_nt(dgu[c, half], wgu[c, half])
    back, dgain2 = norm_backward(first[...], gains[1:2, :], dn2)
    dx1 = dx2[...] + back
    dx1_out[...] = dx1
    grad_gain[...] = dgain2
    if direct:
        landed(wout, sems.at[4])
    dattended[...] = dot_nt(dx1.astype(BF), wout[...]).astype(BF)


def attention_backward_kernel(
    direct,
    ids,
    grad_first,
    dattended,
    x,
    n1,
    attended,
    weights,
    qkv,
    gains,
    bucket,
    grad_proj,
    grad_gain2,
    grad_gain3,
    *refs,
):
    if direct:
        wqk_in, wvo_in, grad_in, own_out, other_out = refs[:5]
        wqk, wvo, own, other, left, right, dqk, extra, *refs = refs[5:]
        copies([(wvo_in.at[0], wvo.at[0])], refs[-1].at[0])
        copies([(wqk_in, wqk)], refs[-1].at[1])
    else:
        wqk, wvo, small, grad_in, dqkv_out, da_out, left, right, dqk, *refs = refs
    diag, bias_grad, dshares, scaled, queries, douts, *rest = refs
    b, core = ids[0], ids[2]
    dx1 = grad_first[...]
    da = dx1.astype(BF)
    low_lane = head_masks()
    row_at = lax.broadcasted_iota(jnp.int32, (DLEN, MICRO * DLEN), 0)
    lane_at = lax.broadcasted_iota(jnp.int32, (DLEN, MICRO * DLEN), 1)
    mirror = jnp.where(row_at == DLEN - 1 - lane_at % DLEN, 1.0, 0.0).astype(BF)
    diag[...] = jnp.zeros_like(diag)
    for i, (m, p, rows, lanes) in enumerate(PAIRS_OF_HEADS):
        queries[i] = both_heads(qkv[0, rows, lanes], low_lane)
        douts[i] = both_heads(dattended[rows, lanes], low_lane)
    for i, (m, p, rows, lanes) in enumerate(PAIRS_OF_HEADS):
        dshares[i] = dot_nt(douts[i], qkv[2, rows, lanes])
        right[0, rows, lanes] = dot_tn(weights[m, p], douts[i]).astype(BF)
    for i, (m, p, rows, lanes) in enumerate(PAIRS_OF_HEADS):
        wide = weights[m, p].astype(F32)
        dshare = dshares[i]
        centre = jnp.sum(wide * dshare, axis=-1, keepdims=True)
        scaled[i] = (wide * (dshare - centre)).astype(BF)
    for i, (m, p, rows, lanes) in enumerate(PAIRS_OF_HEADS):
        dq = dot(scaled[i], qkv[1, rows, lanes])
        dqk[0, rows, lanes] = jnp.where(low_lane, dq[:DLEN], dq[DLEN:]).astype(BF)
        dqk[1, rows, lanes] = dot_tn(scaled[i], queries[i]).astype(BF)
    for h in range(H):
        part = slice((h % 2) * DLEN, (h % 2 + 1) * DLEN)
        both = jnp.concatenate([scaled[m * (H // 2) + h // 2, part] for m in range(MICRO)], axis=0)
        turned = dot(mirror, both)
        wider = jnp.concatenate([turned, jnp.zeros_like(turned)], axis=1)
        rolled = pltpu.roll(wider, 0, 1, stride=1, stride_axis=0)
        diag[h : h + 1, :] = jnp.sum(rolled, axis=0, keepdims=True)
    bias_grad[...] = lax.dot_general(
        bucket[...],
        diag[...],
        (((1,), (1,)), ((), ())),
        precision=HIGHEST,
        preferred_element_type=F32,
    )
    if direct:
        sems = rest[0]
        landed(wvo.at[0], sems.at[0])
        landed(wqk, sems.at[1])
    dn1 = dot_nt(dqk[0], wqk[0]) + dot_nt(dqk[1], wqk[1]) + dot_nt(right[0], wvo[0])
    dx, dgain1 = norm_backward(x[...].astype(F32), gains[0:1, :], dn1)
    grad_in[...] = dx1 + dx
    right[1] = da
    left[0] = n1[...]
    left[1] = attended[...]
    all_gains = jnp.concatenate(
        [dgain1, grad_gain2[...], grad_gain3[...], jnp.zeros((5, D), F32)], axis=0
    )
    if not direct:
        small[0:8, :] = all_gains
        small[8:40, :] = jnp.concatenate(
            [bias_grad[...], jnp.zeros((BUCKETS, D - DLEN), F32)], axis=1
        )
        dqkv_out[0] = dqk[0]
        dqkv_out[1] = dqk[1]
        dqkv_out[2] = right[0]
        da_out[...] = da
        return
    per_shard = BUCKETS // SHARDS
    for j in range(SHARDS):
        for k in range(6):
            extra[0, j, :, k * DLEN : (k + 1) * DLEN] = grad_proj[
                j * 96 + k * 16 : j * 96 + (k + 1) * 16, :
            ]
        extra[1, j] = jnp.zeros((16, D), F32)
        extra[1, j, 0:8, :] = pltpu.roll(all_gains, (D - j * 96) % D, 1)
        extra[1, j, 8 : 8 + per_shard, 0:DLEN] = bias_grad[j * per_shard : (j + 1) * per_shard, :]
    for flip, out, target in ((1, other, other_out), (0, own, own_out)):
        c = core ^ flip
        top = dot_tn(n1[...], dqk[c]).astype(BF)
        bottom = dot_tn(left[c], right[c]).astype(BF)
        for j in range(SHARDS):
            m = b ^ j
            out[m, 0:96, :] = top[j * 96 : (j + 1) * 96, :]
            out[m, 96:192, :] = bottom[j * 96 : (j + 1) * 96, :]
            out[m, 192:208, :] = extra[c, j].astype(BF)
        copies([(out, target)], sems.at[flip])
    landed(other, sems.at[1])
    landed(own, sems.at[0])


def finish_wide_kernel(ids, near, far, twin, far_twin, token, grad_g, grad_u, grad_d):
    y, core = ids[1], ids[2]
    for yy in range(2):
        for c in range(2):

            @pl.when((y == yy) & (core == c))
            def _():
                for yflip, cflip, part in ((0, 0, near), (1, 0, far), (0, 1, twin), (1, 1, far_twin)):
                    half, rank = yy ^ yflip, c ^ cflip
                    out = grad_u if rank else grad_g
                    for k in range(4):
                        start = half * HALF + k * 256
                        out[:, start : start + 256] = part[0, k * 96 : (k + 1) * 96, :].astype(F32)
                    low = (2 * half + rank) * 64
                    for k in range(3):
                        grad_d[low : low + 64, k * 256 : (k + 1) * 256] = part[
                            0, 384 + k * 64 : 384 + (k + 1) * 64, :
                        ].astype(F32)


def finish_narrow_kernel(
    ids, near, twin, grad_q, grad_k, grad_v, grad_o, grad_p, grad_1, grad_2, grad_3, table
):
    core = ids[2]
    for c in range(2):

        @pl.when(core == c)
        def _():
            low, high = (twin, near) if c else (near, twin)
            grad_q[...] = low[0, 0:96, :].astype(F32)
            grad_k[...] = high[0, 0:96, :].astype(F32)
            grad_v[...] = low[0, 96:192, :].astype(F32)
            grad_o[...] = high[0, 96:192, :].astype(F32)
            for k in range(6):
                grad_p[k * 16 : (k + 1) * 16, :] = low[
                    0, 192:208, k * DLEN : (k + 1) * DLEN
                ].astype(F32)
            rows = high[0, 192:208, :].astype(F32)
            grad_1[...] = rows[0:1, :96]
            grad_2[...] = rows[1:2, :96]
            grad_3[...] = rows[2:3, :96]
            block = jnp.where(lax.broadcasted_iota(jnp.int32, (8, DLEN), 1) < H, rows[8:16, :DLEN], 0.0)
            line = block[0:1]
            for i in range(1, BUCKETS // SHARDS):
                line += pltpu.roll(block, i * H, 1)[i : i + 1]
            table[...] = line[:, : BUCKETS // SHARDS * H]


def local(
    hidden_in,
    norm1_gain,
    w_query,
    w_key,
    w_value,
    w_out,
    rel_table,
    norm2_gain,
    w_gate,
    w_up,
    w_down,
    norm3_gain,
    w_proj,
    query_lengths,
    keyword_request_mask,
    targets,
    candidates,
):
    streams = lax.axis_size("stream")
    shards = lax.axis_size("batch")
    pairs = streams // 2
    direct = shards == SHARDS and pairs == 2
    b = lax.axis_index("batch")
    s = lax.axis_index("stream")
    y, core = s // pairs, s % pairs
    is_query = s < pairs
    ids = jnp.stack([b, y, core, is_query.astype(jnp.int32)]).astype(jnp.int32)

    def swap(block, yflip, cflip, m):
        route = []
        for source in range(streams):
            target = ((source // pairs) ^ yflip) * pairs + ((source % pairs) ^ cflip)
            for j in range(shards):
                route.append((source * shards + j, target * shards + (j ^ m)))
        return lax.ppermute(block, EVERY, route)

    fence = lax.optimization_barrier
    first_core = core == 0
    spots_a = spots_f = None
    if direct:
        lines = [part.reshape(1, -1) for part in (norm1_gain, norm2_gain, norm3_gain, rel_table)]
        slab_a, slab_f = call(
            pack_kernel,
            "pack",
            ids,
            [w_query, w_key, w_value, w_out, w_gate, w_up, w_down, w_proj, *lines],
            [((PIECE_A, D), BF), ((PIECE_F, 256), BF)],
        )

        def join(*parts):
            return jnp.concatenate(parts)

        def along_x(part):
            return swap(part, 0, 0, 1)

        def along_y(part):
            return swap(part, 1, 0, 0)

        def along_z(part):
            return swap(part, 0, 0, 2)

        def along_zz(part):
            return swap(part, 0, 0, 4)

        def other_core(part):
            return swap(part, 0, 1, 0)

        f0, a0 = slab_f[None], slab_a[None]
        token = jnp.zeros((8, DLEN), F32)
        f1, y0, f4 = along_x(f0), along_y(f0), along_zz(f0)
        a0, token = fence((a0, tick(token)))
        a1, a2 = along_x(a0), along_z(a0)

        f1, y0, f4, token = fence((f1, y0, f4, token))
        f14, f04, token = fence((join(f1, f4), join(f0, f4), token))
        f5, y14, f26 = along_x(f4), along_y(f14), along_z(f04)
        a1, a2, token = fence((a1, a2, tick(token)))
        a3, a4 = along_x(a2), along_zz(a0)

        f5, y14, f26, token = fence((f5, y14, f26, token))
        f526, a012, token = fence((join(f5, f26), join(a0, a1, a2), token))
        f37, y526, ta012 = along_x(f26), along_y(f526), other_core(a012)
        a3, a4, token = fence((a3, a4, tick(token)))
        a34, token = fence((join(a3, a4), token))
        a5, a6 = along_x(a4), along_z(a4)

        f37, ta012, token = fence((f37, ta012, token))
        f37, a34, token = fence((f37, a34, token))
        y37, ta34 = along_y(f37), other_core(a34)
        a5, a6, ta34, token = fence((a5, a6, ta34, tick(token)))
        f_all, a56, token = fence((join(f0, f14, f526, f37), join(a5, a6), token))
        a7, ta56, tf_all = along_x(a6), other_core(a56), other_core(f_all)
        a7, ta56, token = fence((a7, ta56, tick(token)))
        y014, token = fence((join(y0, y14), token))
        ta7, ty014 = other_core(a7), other_core(y014)
        a7, ta7, token = fence((a7, ta7, token))
        order_f = (0, 1, 4, 5, 2, 6, 3, 7)
        groups_a = [
            (0, (a012, (0, 1, 2)), (a34, (3, 4)), (a56, (5, 6)), (a7, (7,))),
            (1, (ta012, (0, 1, 2)), (ta34, (3, 4)), (ta56, (5, 6)), (ta7, (7,))),
        ]
        pieces_a, spots_a, pieces_f, spots_f = [], [], [], []
        for cflip, *group in groups_a:
            for part, flips in group:
                spots_a += [(cflip, m, len(pieces_a), i) for i, m in enumerate(flips)]
                pieces_a.append(part)
    else:

        def whole(part):
            return lax.all_gather(part, "batch", axis=0, tiled=True)

        wqk = jnp.stack([whole(w_query), whole(w_key)])
        wvo = jnp.stack([whole(w_value), whole(w_out)])
        gate_up = jnp.stack([whole(w_gate), whole(w_up)])
        wgu = jnp.transpose(gate_up.reshape(2, D, 2, HALF), (0, 2, 1, 3))
        wd = whole(w_down)
        wproj = whole(w_proj)
        gain_rows = [whole(gain) for gain in (norm1_gain, norm2_gain, norm3_gain)]
        gains = jnp.pad(jnp.stack(gain_rows).astype(F32), ((0, 5), (0, 0)))
        table = whole(rel_table).reshape(1, BUCKETS * H)

    micro_count = hidden_in.shape[0]
    slot = jnp.arange(DLEN)
    pair_lengths = lax.dynamic_index_in_dim(query_lengths, core, 1, keepdims=False)
    pair_keyword = lax.dynamic_index_in_dim(keyword_request_mask, core, 1, keepdims=False)
    pair_targets = lax.dynamic_index_in_dim(targets, core, 1, keepdims=False)

    def by_slot(values):
        blocks = values.reshape(micro_count, shards, GROUPS)
        own = lax.dynamic_slice_in_dim(blocks, b, 1, 1)
        blocks = jnp.where(is_query, jnp.broadcast_to(own, blocks.shape), blocks)
        return jnp.repeat(blocks, QLEN, axis=2)

    length_slots = by_slot(pair_lengths)
    valid_slots = (slot % QLEN)[None, None, :] < length_slots
    share = jnp.where(valid_slots, 1.0 / length_slots.astype(F32), 0.0)
    sharp = jnp.where(by_slot(pair_keyword) == 1, 20.0, 10.0).astype(F32)
    target_slots = by_slot(pair_targets)
    own_valid = lax.dynamic_slice_in_dim(valid_slots, b, 1, 1)
    same = (slot[:, None] // QLEN) == (slot[None, :] // QLEN)
    mask = jnp.where(is_query & ~(same[None] & own_valid), -1000000000.0, 0.0).astype(F32)

    small = 16 if direct else 48
    picked = lax.dynamic_index_in_dim(candidates, core, 1, keepdims=False)[:, 0]
    picked = picked.reshape(micro_count, shards, DLEN, picked.shape[-1])
    picked = jnp.transpose(picked, (0, 1, 3, 2))
    received = lax.all_to_all(picked, "batch", split_axis=1, concat_axis=1, tiled=True)
    picks = jnp.where(is_query, received, picked)
    (counts,) = call(
        count_kernel,
        "count",
        ids,
        [picks],
        [((micro_count, shards, DLEN, DLEN), F32)],
        limit=small,
    )

    onehot = bucket_onehot()
    by_entry = jnp.asarray(np.repeat(onehot.T, H, axis=0), BF)
    x = hidden_in[:, 0].reshape(ROWS, D)
    row_bf, row_f32 = ((ROWS, D), BF), ((ROWS, D), F32)
    qkv_shape, weight_shape = ((3, ROWS, D), BF), ((MICRO, H // 2, ROWS, DLEN), BF)
    pair_weights = ((2, D, D), BF)
    gain_rows = ((8, D), F32)
    proj_shape = ((D, DLEN), BF)
    kept = [qkv_shape, row_bf, weight_shape, row_f32, row_bf, row_bf]
    bias_shape, score_shape = ((H // 2, ROWS, DLEN), F32), ((H, ROWS, DLEN), F32)
    result = call(
        functools.partial(attention_forward_kernel, direct, spots_a),
        "attention_forward",
        ids,
        [x, mask, by_entry] + ([] if direct else [gains, table, wqk, wvo]),
        kept + ([gain_rows, proj_shape] if direct else []),
        ([pair_weights, pair_weights, ((2, SHARDS, 16, D), BF)] if direct else [])
        + [bias_shape, score_shape],
        far=pieces_a if direct else [],
        far_outs=[pair_weights, pair_weights] if direct else [],
        sems=3 if direct else 0,
        flops=2 * ROWS * D * D * 4,
    )
    qkv, attended, weights, first, n1, n2 = result[:6]
    if direct:
        gains, wproj, wqk, wvo = result[6:]
    first, counts, share, sharp, target_slots = fence((first, counts, share, sharp, target_slots))
    if direct:
        y526, tf_all, ty014, first, token = fence((y526, tf_all, ty014, first, token))
        ty526 = other_core(y526)
        y37, ty526, token = fence((y37, ty526, tick(token)))
        near, twin = ((f_all, order_f),), ((tf_all, order_f),)
        far = ((y014, (0, 1, 4)), (y526, (5, 2, 6)), (y37, (3, 7)))
        far_twin = ((ty014, (0, 1, 4)), (ty526, (5, 2, 6)), (other_core(y37), (3, 7)))
        for yflip, cflip, group in ((0, 0, near), (0, 1, twin), (1, 0, far), (1, 1, far_twin)):
            for part, flips in group:
                spots_f += [(yflip, cflip, m, len(pieces_f), i) for i, m in enumerate(flips)]
                pieces_f.append(part)
    wide_bf, deep_bf = ((2, ROWS, HALF), BF), ((ROWS, FF), BF)
    wgu_shape, wd_shape = ((2, 2, D, HALF), BF), ((FF, D), BF)
    lasting = [wide_bf, wide_bf, deep_bf]
    result = call(
        functools.partial(ffn_forward_kernel, direct, spots_f),
        "ffn_forward",
        ids,
        [first, n2, gains, wproj] + ([] if direct else [wgu, wd]),
        [row_f32, row_bf, ((ROWS, DLEN), BF)] + ([] if direct else lasting),
        [wgu_shape, wd_shape] + lasting if direct else [],
        far=[*pieces_f, token] if direct else [],
        far_outs=lasting if direct else [],
        sems=5 if direct else 0,
        flops=2 * ROWS * D * FF * 3,
    )
    second, n3, vectors, gelu_kept, slope_kept, hidden = result

    if direct:
        even = jnp.stack([swap(vectors, 1, 0, m) for m in (0, 2, 4, 6)])
        others = [even, swap(even, 0, 0, 1)]
    else:
        route = [(i, (i + pairs) % streams) for i in range(streams)]
        arrived = lax.ppermute(vectors, "stream", route)
        others = [lax.all_gather(arrived, "batch", axis=0)]
    block_f32 = ((micro_count, shards, DLEN, DLEN), F32)
    line_f32 = ((micro_count, shards, DLEN), F32)
    soft, score = call(
        functools.partial(similarity_kernel, direct, shards),
        "similarity",
        ids,
        [vectors, counts, share, *others],
        [block_f32, line_f32],
        [line_f32],
        limit=small,
    )
    if direct:
        blocks = jnp.broadcast_to(score[None], (shards,) + score.shape)
        scores = lax.all_to_all(blocks, "batch", split_axis=0, concat_axis=0, tiled=True)
    else:
        scores = lax.all_gather(score, "batch", axis=0)
    (dvec,) = call(
        functools.partial(vector_grad_kernel, direct, shards),
        "vector_grad",
        ids,
        [soft, share, sharp, target_slots, score, scores, *others],
        [((ROWS, DLEN), BF)],
        [line_f32, ((ROWS, DLEN), F32)],
        limit=small,
    )

    gain_row = ((1, D), F32)
    proj_f32 = ((D, DLEN), F32)
    dgu_shape = ((2, 2, ROWS, HALF), BF)
    quarter = ((SHARDS, PIECE_F, 256), BF)
    saved = [hidden, gelu_kept, slope_kept]
    result = call(
        functools.partial(ffn_backward_kernel, direct, spots_f),
        "ffn_backward",
        ids,
        [dvec, second, n2, n3, gains, wproj] + ([] if direct else [wd, *saved]),
        [row_f32, proj_f32, gain_row, dgu_shape] + ([] if direct else [row_bf]),
        [wd_shape, deep_bf, wide_bf, wide_bf, ((SHARDS, 4, 64, D), BF), ((4, *quarter[0]), BF)]
        if direct
        else [],
        far=[*saved, *pieces_f] if direct else [],
        far_outs=[quarter] * 2 + [((2, PIECE_F, 256), BF)] * 8 if direct else [],
        sems=4 if direct else 0,
        flops=2 * ROWS * D * FF * 4,
    )
    dx2, grad_proj, grad_gain, dgu = result[:4]
    if direct:
        f_own, f_twin, *f_far = result[4:]
    else:
        dy = result[4]

    if direct:
        def far_sum(i):
            return [[(f_far[i], n), (c_far[i], n)] for n in range(2)]

        c_far = [other_core(part) for part in f_far[4:]]
        c_far[0], f_twin, dgu = fence((c_far[0], f_twin, dgu))
        twin = other_core(f_twin)
        (sent_67,) = add_up(ids, far_sum(0))
        sent_67, dgu = fence((sent_67, dgu))
        y67 = along_y(sent_67)
    middle_in = [dx2, first, dgu, gains]
    dx1, dattended, grad_gain2 = call(
        functools.partial(middle_backward_kernel, direct, spots_f),
        "middle_backward",
        ids,
        middle_in + ([] if direct else [wgu, wvo]),
        [row_f32, row_bf, gain_row],
        [wgu_shape, ((D, D), BF)] if direct else [],
        far=[*pieces_f, wvo] if direct else [],
        sems=5 if direct else 0,
        flops=ROUND_FLOPS,
    )
    if direct:
        *c_far[1:], twin, dattended = fence((*c_far[1:], twin, dattended))
        sent_23, sent_45, sent_01 = add_up(ids, far_sum(1), far_sum(2), far_sum(3))
        sent_23, sent_45, sent_01, dattended = fence((sent_23, sent_45, sent_01, dattended))
        y23 = along_y(sent_23)
    two_rows = ((2, ROWS, D), BF)
    slab_out = ((SHARDS, PIECE_A, D), BF)
    blocks_bf = ((H, ROWS, DLEN), BF)
    result = call(
        functools.partial(attention_backward_kernel, direct),
        "attention_backward",
        ids,
        [dx1, dattended, x, n1, attended, weights, qkv, gains, jnp.asarray(onehot.T)]
        + [grad_proj, grad_gain2, grad_gain]
        + ([] if direct else [wqk, wvo]),
        [row_f32] if direct else [((40, D), F32), row_f32, qkv_shape, row_bf],
        ([pair_weights, pair_weights, slab_out, slab_out] if direct else [])
        + [two_rows, two_rows, two_rows]
        + ([((2, SHARDS, 16, D), F32)] if direct else [])
        + [((DLEN, 2 * DLEN), F32), ((BUCKETS, DLEN), F32)]
        + [score_shape, blocks_bf, blocks_bf, blocks_bf],
        far=[wqk, wvo] if direct else [],
        far_outs=[slab_out, slab_out] if direct else [],
        sems=2 if direct else 0,
        flops=2 * ROWS * D * D * 7,
    )

    if direct:
        input_grad, a_own, a_other = result

        def own_f(m, *more):
            return [(base_f, m), *more]

        def own_a(m, *more):
            return [(base_a, m), *more]

        y67, a_own, a_other = fence((y67, a_own, a_other))
        token = jnp.ones((8, DLEN), F32)
        twin_a = other_core(a_other)
        (out_7,) = add_up(ids, [[(f_own, 7), (twin, 7), (y67, 1)]])
        out_7, sent_45, twin, token = fence((out_7, sent_45, twin, token))
        x7, y45 = along_x(out_7), along_y(sent_45)

        twin_a, token = fence((twin_a, token))
        base_a, out_a37, out_a51 = base_up(ids, a_own, twin_a, (3, 7), (5, 1))
        out_a37, token = fence((out_a37, token))
        xa37 = along_x(out_a37)
        token = tick(token)

        (base_f,) = base_up(ids, f_own, twin)
        y23, x7, base_f, token = fence((y23, x7, base_f, token))
        out_3, out_6 = add_up(
            ids, [own_f(3, (y23, 1))], [own_f(6, (y67, 0), (x7, 0))]
        )
        out_3, out_6, sent_01, token = fence((out_3, out_6, sent_01, token))
        x3, z6, y01 = along_x(out_3), along_z(out_6), along_y(sent_01)

        xa37, token = fence((xa37, token))
        out_a6, out_a2 = add_up(ids, [own_a(6, (xa37, 1))], [own_a(2, (xa37, 0))])
        out_a6, out_a2, out_a51, token = fence((out_a6, out_a2, out_a51, token))
        za6, xa51 = along_z(out_a6), along_x(out_a51)
        token = tick(token)

        y45, x3, token = fence((y45, x3, token))
        out_5, out_2 = add_up(ids, [own_f(5, (y45, 1))], [own_f(2, (y23, 0), (x3, 0))])
        out_5, out_2, token = fence((out_5, out_2, token))
        x5, z2 = along_x(out_5), along_z(out_2)

        za6, xa51, token = fence((za6, xa51, token))
        (out_a4,) = add_up(ids, [own_a(4, (xa51, 0), (za6, 0))])
        out_a4, out_a2, token = fence((out_a4, out_a2, token))
        za4, za2 = along_zz(out_a4), along_z(out_a2)
        token = tick(token)

        x5, z6, token = fence((x5, z6, token))
        (out_4,) = add_up(ids, [own_f(4, (y45, 0), (x5, 0), (z6, 0))])
        out_4, token = fence((out_4, token))
        z4 = along_zz(out_4)
        y01, token = fence((y01, token))
        (out_1,) = add_up(ids, [own_f(1, (y01, 1))])
        out_1, token = fence((out_1, token))
        x1 = along_x(out_1)

        za4, za2, token = fence((za4, za2, token))
        (part_a,) = add_up(ids, [own_a(0, (xa51, 1), (za2, 0), (za4, 0))])
        part_a, token = fence((part_a, token))
        ya = along_y(part_a)
        token = tick(token)

        z2, x1, z4, token = fence((z2, x1, z4, token))
        (mine_f,) = add_up(ids, [own_f(0, (y01, 0), (x1, 0), (z2, 0), (z4, 0))])
        mine_f, token = fence((mine_f, token))
        far, twin_f = along_y(mine_f), other_core(mine_f)

        ya, token = fence((ya, token))
        (mine_a,) = add_up(ids, [[(part_a, 0), (ya, 0)]])
        mine_a, token = fence((mine_a, token))
        twin_a = other_core(mine_a)
        far, twin_f, token = fence((far, twin_f, token))
        far_twin_f = other_core(far)
        shard_f32, wide_f32 = ((96, D), F32), ((96, FF), F32)
        grad_g, grad_u, grad_d = call(
            finish_wide_kernel,
            "finish_wide",
            ids,
            [mine_f, far, twin_f, far_twin_f],
            [wide_f32, wide_f32, ((256, D), F32)],
            far=[token],
            limit=24,
        )
        grad_q, grad_k, grad_v, grad_o, grad_p, *small = call(
            finish_narrow_kernel,
            "finish_narrow",
            ids,
            [mine_a, twin_a],
            [shard_f32] * 4 + [((96, DLEN), F32), ((1, 96), F32), ((1, 96), F32), ((1, 96), F32)]
            + [((1, 48), F32)],
            limit=24,
        )
        grad_n1, grad_n2, grad_n3, grad_table = [row.reshape(-1) for row in small]
    else:
        small, input_grad, dqkv, da = result

        def summed(part):
            part = lax.psum_scatter(part, "batch", scatter_dimension=0, tiled=True)
            return lax.psum(part, "stream")

        grad_q, grad_k, grad_v = [summed(dot_tn(n1, dqkv[i])) for i in range(3)]
        grad_o = summed(dot_tn(attended, da))
        grad_g, grad_u = [
            summed(jnp.concatenate([dot_tn(n2, dgu[i, half]) for half in range(2)], axis=1))
            for i in range(2)
        ]
        grad_d = summed(dot_tn(hidden, dy))
        grad_p = summed(grad_proj)
        grad_n1, grad_n2, grad_n3 = [summed(small[i]) for i in range(3)]
        flat = lax.psum(small[8 : 8 + BUCKETS, :H].reshape(-1), EVERY)
        share_rows = flat.shape[0] // shards
        grad_table = lax.dynamic_slice_in_dim(flat, b * share_rows, share_rows, 0)

    vectors_out = vectors.reshape(micro_count, DLEN, DLEN)[:, None]
    grad_hidden = input_grad.reshape(micro_count, DLEN, D)[:, None]
    return (
        vectors_out,
        grad_hidden,
        grad_n1,
        grad_q,
        grad_k,
        grad_v,
        grad_o,
        grad_table,
        grad_n2,
        grad_g,
        grad_u,
        grad_d,
        grad_n3,
        grad_p,
    )


def solution(mesh):
    rows, lines = P("batch", None), P("batch")
    spread = P(None, "stream", "batch", None)
    return jax.shard_map(
        local,
        mesh=mesh,
        in_specs=(spread, lines, rows, rows, rows, rows, lines, lines, rows, rows, rows, lines, rows)
        + (P(), P(), P(), P(None, None, "batch", None, None)),
        out_specs=(spread, spread, lines, rows, rows, rows, rows, lines, lines)
        + (rows, rows, rows, lines, rows),
        check_vma=False,
    )
```

```python
import functools
import math

import jax
import jax.numpy as jnp
import numpy as np
from jax import lax
from jax.experimental import pallas as pl
from jax.experimental.pallas import tpu as pltpu
from jax.sharding import PartitionSpec as P

H = 12
DH = 64
BUCKETS = 32
MAX_DIST = 128
DLEN = 128
QLEN = 32
GROUPS = DLEN // QLEN
MICRO = 2
ROWS = MICRO * DLEN
D = 768
FF = 2048
HALF = FF // 2
SHARDS = 8
PIECE_A = 208
PIECE_F = 576
FIRST_A, REST_A = (3, 7), (6, 2, 5, 1, 4, 0)
GROUPS_F = ((6, 7, 2, 3), (4, 5, 0, 1))

EPSILON = 1e-06
HIGHEST = lax.Precision.HIGHEST
BF = jnp.bfloat16
F32 = jnp.float32
EVERY = ("stream", "batch")
MIB = 2**20
ROUND_FLOPS = 5 * 10**10


def distance_bucket(distance):
    half_count = BUCKETS // 2
    exact_count = half_count // 2
    if distance < exact_count:
        return distance
    grown = exact_count + int(
        math.floor(
            math.log(distance / exact_count)
            / math.log(MAX_DIST / exact_count)
            * (half_count - exact_count)
            + 1e-09
        )
    )
    return min(grown, half_count - 1)


def bucket_onehot():
    table = np.zeros((2 * DLEN, BUCKETS), np.float32)
    for o in range(2 * DLEN - 1):
        offset = o - (DLEN - 1)
        table[o, distance_bucket(abs(offset)) + (BUCKETS // 2 if offset > 0 else 0)] = 1.0
    return table


def norm_scale(values):
    return lax.rsqrt(jnp.mean(values * values, axis=-1, keepdims=True) + EPSILON)


def norm_backward(values, gain, grad):
    scale = norm_scale(values)
    pulled = gain * grad
    inner = jnp.mean(values * pulled, axis=-1, keepdims=True)
    back = scale * pulled - values * (scale * scale * scale * inner)
    return back, jnp.sum(grad * values * scale, axis=0, keepdims=True)


def dot(left, right):
    return jnp.dot(left, right, preferred_element_type=F32)


def dot_nt(left, right):
    return lax.dot_general(left, right, (((1,), (1,)), ((), ())), preferred_element_type=F32)


def dot_tn(left, right):
    return lax.dot_general(left, right, (((0,), (0,)), ((), ())), preferred_element_type=F32)


def steps(count, body):
    if count <= 16:
        for i in range(count):
            body(i)
    else:

        @pl.loop(0, count)
        def _(i):
            body(i)


VMEM = pl.BlockSpec(memory_space=pltpu.VMEM)
SMEM = pl.BlockSpec(memory_space=pltpu.SMEM)
HBM = pl.BlockSpec(memory_space=pltpu.HBM)


def positions():
    pairs = lax.axis_size("stream") // 2
    stream = lax.axis_index("stream")
    return lax.axis_index("batch"), stream // pairs, stream % pairs, jnp.where(stream < pairs, 1, 0)


def body_kernel(kernel, lazy, counts, *refs):
    parts = []
    for count in counts:
        parts.append(refs[:count])
        refs = refs[count:]
    arrays, far, outs, far_outs, held, made, scratch = parts
    in_sems, out_sems = refs
    for i, (array, place) in enumerate(zip(arrays, held)):
        pltpu.make_async_copy(array, place, in_sems.at[i]).start()
    sent = set()

    def ready():
        for i, (array, place) in enumerate(zip(arrays, held)):
            pltpu.make_async_copy(array, place, in_sems.at[i]).wait()

    def send(*results):
        for i in results:
            sent.add(i)
            pltpu.make_async_copy(made[i], outs[i], out_sems.at[i]).start()

    if not lazy:
        ready()
    kernel((*positions(), ready, send), *held, *far, *made, *far_outs, *scratch)
    send(*(i for i in range(len(outs)) if i not in sent))
    for i, (place, out) in enumerate(zip(made, outs)):
        pltpu.make_async_copy(place, out, out_sems.at[i]).wait()


def near_kernel(kernel, *refs):
    kernel(positions(), *refs)


def call(
    kernel,
    name,
    arrays,
    outs,
    scratch=(),
    far=(),
    far_outs=(),
    sems=0,
    flops=0,
    limit=59,
    near=False,
    lazy=False,
):
    shapes = [jax.ShapeDtypeStruct(s, t) for s, t in (*outs, *far_outs)]
    moved = sum(math.prod(s.shape) * s.dtype.itemsize for s in shapes)
    moved += sum(math.prod(a.shape) * a.dtype.itemsize for a in (*arrays, *far))
    spaces = [pltpu.VMEM(s, t) for s, t in scratch]
    if sems:
        spaces.append(pltpu.SemaphoreType.DMA((sems,)))
    kind = VMEM if near else HBM
    if near:
        body = functools.partial(near_kernel, kernel)
    else:
        counts = (len(arrays), len(far), len(outs), len(far_outs))
        counts += (len(arrays), len(outs), len(spaces))
        body = functools.partial(body_kernel, kernel, lazy, counts)
        spaces = (
            [pltpu.VMEM(a.shape, a.dtype) for a in arrays]
            + [pltpu.VMEM(s, t) for s, t in outs]
            + spaces
            + [pltpu.SemaphoreType.DMA((max(1, len(part)),)) for part in (arrays, outs)]
        )
    return pl.pallas_call(
        body,
        name=name,
        out_shape=shapes,
        in_specs=[kind] * len(arrays) + [HBM] * len(far),
        out_specs=[kind] * len(outs) + [HBM] * len(far_outs),
        scratch_shapes=spaces,
        compiler_params=pltpu.CompilerParams(vmem_limit_bytes=limit * MIB),
        cost_estimate=pl.CostEstimate(flops=flops, bytes_accessed=moved, transcendentals=0),
    )(*arrays, *far)


def tick_kernel(token, out):
    pass


def tick(token):
    return pl.pallas_call(
        tick_kernel,
        name="tick",
        in_specs=[HBM],
        out_specs=HBM,
        out_shape=jax.ShapeDtypeStruct(token.shape, token.dtype),
        input_output_aliases={0: 0},
        cost_estimate=pl.CostEstimate(flops=ROUND_FLOPS, bytes_accessed=0, transcendentals=0),
    )(token)


def add_kernel(plan, near, far, ids, *refs):
    near, far, refs = refs[:near], refs[near : near + far], refs[near + far :]
    outs, refs = refs[: len(plan)], refs[len(plan) :]
    held, sems = (refs[:-1], refs[-1]) if far else ((), None)
    place = 0
    for entries in plan:
        for terms in entries:
            for is_far, array, entry in terms:
                if is_far:
                    copies([(far[array].at[entry], held[place])], sems.at[place])
                    place += 1
    place = 0
    for out, entries in zip(outs, plan):
        for i, terms in enumerate(entries):
            total = None
            for is_far, array, entry in terms:
                if is_far:
                    landed(held[place], sems.at[place])
                    part = held[place][...].astype(F32)
                    place += 1
                else:
                    part = near[array][entry].astype(F32)
                total = part if total is None else total + part
            out[i] = total.astype(BF)


def base_kernel(picks, ids, own, rest, out, left, right, sems):
    for i, m in enumerate(picks):
        copies([(own.at[m], left.at[i]), (rest.at[i], right.at[i])], sems.at[i])
    for i in range(len(picks)):
        landed(left.at[i], sems.at[i])
        landed(right.at[i], sems.at[i])
        left[i] = (left[i].astype(F32) + right[i].astype(F32)).astype(BF)
        copies([(left.at[i], out.at[i])], sems.at[i])
    for i in range(len(picks)):
        landed(left.at[i], sems.at[i])


def base_up(own, rest, picks):
    shape = (rest.shape, BF)
    (base,) = call(
        functools.partial(base_kernel, tuple(picks)),
        "base_up",
        [],
        [],
        [shape, shape],
        far=[own, rest],
        far_outs=[shape],
        sems=len(picks),
    )
    return base


def add_up(*outputs, limit=24):
    known = ([], [])
    plan, flat, shapes = [], [], []
    for entries in outputs:
        plan.append([])
        for terms in entries:
            plan[-1].append([])
            for array, entry in terms:
                is_far = int(array.shape[0] > 4)
                arrays = known[is_far]
                found = [i for i, other in enumerate(arrays) if other is array]
                if not found:
                    arrays.append(array)
                    found = [len(arrays) - 1]
                if is_far:
                    flat.append((array.shape[1:], BF))
                plan[-1][-1].append((is_far, found[0], entry))
        shapes.append(((len(entries), *entries[0][0][0].shape[1:]), BF))
    return call(
        functools.partial(add_kernel, plan, len(known[0]), len(known[1])),
        "add_up",
        known[0],
        shapes,
        flat,
        far=known[1],
        sems=len(flat),
        limit=limit,
        near=True,
    )


def pack_kernel(ids, wq, wk, wv, wo, wg, wu, wd, wp, g1, g2, g3, table, slab_a, slab_f):
    y, core = ids[1], ids[2]

    def fill(top, bottom, wide, rank):
        slab_a[0:96, :] = top[...]
        slab_a[96:192, :] = bottom[...]
        for yy in range(2):

            @pl.when(y == yy)
            def _():
                for k in range(4):
                    start = yy * HALF + k * 256
                    slab_f[k * 96 : (k + 1) * 96, :] = wide[:, start : start + 256]
                row = (2 * yy + rank) * 64
                for k in range(3):
                    slab_f[384 + k * 64 : 384 + (k + 1) * 64, :] = wd[
                        row : row + 64, k * 256 : (k + 1) * 256
                    ]

    @pl.when(core == 0)
    def _():
        fill(wq, wv, wg, 0)
        for k in range(6):
            slab_a[192:208, k * DLEN : (k + 1) * DLEN] = wp[k * 16 : (k + 1) * 16, :]

    @pl.when(core == 1)
    def _():
        fill(wk, wo, wu, 1)
        rows = [g1[...].astype(F32), g2[...].astype(F32), g3[...].astype(F32)]
        head = jnp.concatenate(rows + [jnp.zeros((5, 96), F32)], axis=0)
        tail = jnp.concatenate([table[...].astype(F32), jnp.zeros((7, 48), F32)], axis=0)
        tail = jnp.concatenate([tail, jnp.zeros((8, 48), F32)], axis=1)
        both = jnp.concatenate([head, tail], axis=0)
        slab_a[192:208, :] = jnp.concatenate(
            [both, jnp.zeros((16, D - 96), F32)], axis=1
        ).astype(BF)


def copies(pairs, sem):
    for src, dst in pairs:
        pltpu.make_async_copy(src, dst, sem).start()


def landed(buffer, sem):
    pltpu.make_async_copy(buffer, buffer, sem).wait()


def fetch_a(ids, pieces, spots, wqk, wvo, extra, sems):
    b, core = ids[0], ids[2]
    for cflip, m, array, entry in spots:
        src = pieces[array].at[entry]
        c, j = core ^ cflip, b ^ m
        row = pl.multiple_of(j * 96, 96)
        copies([(src.at[pl.ds(0, 96)], wqk.at[c, pl.ds(row, 96)])], sems.at[0])
        copies([(src.at[pl.ds(96, 96)], wvo.at[c, pl.ds(row, 96)])], sems.at[1])
        copies([(src.at[pl.ds(192, 16)], extra.at[c, j])], sems.at[2])


def fetch_wide(ids, pieces, spots, wgu, sems):
    b, y, core = ids[0], ids[1], ids[2]
    for yflip, cflip, m, array, entry in spots:
        src = pieces[array].at[entry]
        c, yy, j = core ^ cflip, y ^ yflip, b ^ m
        row = pl.multiple_of(j * 96, 96)
        for k in range(4):
            tile = wgu.at[c, yy, pl.ds(row, 96), pl.ds(k * 256, 256)]
            copies([(src.at[pl.ds(k * 96, 96)], tile)], sems.at[2 * yy + c])


def fetch_deep(ids, pieces, spots, wd, sem):
    b, y, core = ids[0], ids[1], ids[2]
    for yflip, cflip, m, array, entry in spots:
        src = pieces[array].at[entry]
        low = pl.multiple_of((b ^ m) * 256 + (2 * (y ^ yflip) + (core ^ cflip)) * 64, 64)
        for k in range(3):
            tile = wd.at[pl.ds(low, 64), pl.ds(k * 256, 256)]
            copies([(src.at[pl.ds(384 + k * 64, 64)], tile)], sem)


def head_masks():
    low_lane = lax.broadcasted_iota(jnp.int32, (DLEN, DLEN), 1) < DH
    return low_lane


def both_heads(pair, low_lane):
    zero = jnp.zeros_like(pair)
    return jnp.concatenate(
        [jnp.where(low_lane, pair, zero), jnp.where(low_lane, zero, pair)], axis=0
    )


PAIRS_OF_HEADS = [
    (m, p, slice(m * DLEN, (m + 1) * DLEN), slice(p * DLEN, (p + 1) * DLEN))
    for m in range(MICRO)
    for p in range(H // 2)
]


def attention_forward_kernel(direct, spots, ids, x, mask, onehot, *refs):
    if direct:
        count = 1 + max(spot[2] for spot in spots)
        pieces, refs = refs[:count], refs[count:]
        qkv, attended, weights, first, n1, n2, gains, wproj, wqk_out, wvo_out = refs[:10]
        wqk, wvo, extra, bias, scores, sems = refs[10:]
        fetch_a(ids, pieces, spots, wqk, wvo, extra, sems)
        ids[4]()
        landed(extra, sems.at[2])
        lane = lax.broadcasted_iota(jnp.int32, (8, D), 1)
        all_gains = jnp.zeros((8, D), F32)
        flat = jnp.zeros((8, D), F32)
        for j in range(SHARDS):
            block = extra[1, j].astype(F32)
            all_gains += pltpu.roll(jnp.where(lane < 96, block[0:8], 0.0), j * 96, 1)
            flat += pltpu.roll(jnp.where(lane < 48, block[8:16], 0.0), j * 48, 1)
            for k in range(6):
                wproj[j * 96 + k * 16 : j * 96 + (k + 1) * 16, :] = extra[
                    0, j, :, k * DLEN : (k + 1) * DLEN
                ]
        gains[...] = all_gains
        flat = flat[0:1, : BUCKETS * H]
    else:
        ids[4]()
        gains, flat_in, wqk, wvo = refs[:4]
        qkv, attended, weights, first, n1, n2, bias, scores = refs[4:]
        flat = flat_in[...].astype(F32)
    entry = lax.broadcasted_iota(jnp.int32, (16, BUCKETS * H), 1)
    head = lax.broadcasted_iota(jnp.int32, (16, BUCKETS * H), 0)
    by_head = jnp.where(entry % H == head, jnp.broadcast_to(flat, entry.shape), 0.0)
    offsets = dot(by_head.astype(BF), onehot[...])
    for h in range(H):
        row = jnp.broadcast_to(offsets[h : h + 1, :], (DLEN, 2 * DLEN))
        rolled = pltpu.roll(row, DLEN + 1, 1, stride=1, stride_axis=0)
        bias[h // 2, (h % 2) * DLEN : (h % 2 + 1) * DLEN, :] = rolled[:, :DLEN]
    tokens = x[...].astype(F32)
    normed = (tokens * norm_scale(tokens) * gains[0:1, :]).astype(BF)
    n1[...] = normed
    if direct:
        landed(wqk, sems.at[0])
        copies([(wqk, wqk_out)], sems.at[0])
        landed(wvo, sems.at[1])
        copies([(wvo, wvo_out)], sems.at[1])
    qkv[0] = dot(normed, wqk[0]).astype(BF)
    qkv[1] = dot(normed, wqk[1]).astype(BF)
    qkv[2] = dot(normed, wvo[0]).astype(BF)
    ids[5](0, 4)
    low_lane = head_masks()
    for i, (m, p, rows, lanes) in enumerate(PAIRS_OF_HEADS):
        scores[i] = dot_nt(both_heads(qkv[0, rows, lanes], low_lane), qkv[1, rows, lanes])
    for i, (m, p, rows, lanes) in enumerate(PAIRS_OF_HEADS):
        hidden = jnp.concatenate([mask[m], mask[m]], axis=0)
        biased = scores[i] + bias[p] + hidden
        shifted = jnp.exp(biased - jnp.max(biased, axis=-1, keepdims=True))
        weights[m, p] = (shifted / jnp.sum(shifted, axis=-1, keepdims=True)).astype(BF)
    for i, (m, p, rows, lanes) in enumerate(PAIRS_OF_HEADS):
        mixed = dot(weights[m, p], qkv[2, rows, lanes])
        attended[rows, lanes] = jnp.where(low_lane, mixed[:DLEN], mixed[DLEN:]).astype(BF)
    x1 = tokens + dot(attended[...], wvo[1])
    first[...] = x1
    n2[...] = (x1 * norm_scale(x1) * gains[1:2, :]).astype(BF)
    if direct:
        landed(wqk, sems.at[0])
        landed(wvo, sems.at[1])


def gelu_parts(gate):
    c0, c1 = math.sqrt(2.0 / math.pi), 0.044715
    square = gate * gate
    bent = jnp.tanh(c0 * gate * (1.0 + c1 * square))
    value = 0.5 * gate * (1.0 + bent)
    slope = 0.5 * (1.0 + bent) + 0.5 * gate * (1.0 - bent * bent) * (
        c0 * (1.0 + 3.0 * c1 * square)
    )
    return value, slope


def ffn_forward_kernel(direct, spots, ids, first, n2, gains, wproj, *refs):
    if direct:
        count = 1 + max(spot[3] for spot in spots)
        pieces, refs = refs[:count], refs[count:]
        second, n3, vectors, gelu_out, slope_out, hidden_out = refs[1:7]
        wgu, wd, gelu_kept, slope_kept, hidden, sems = refs[7:]
        fetch_wide(ids, pieces, spots, wgu, sems)
        fetch_deep(ids, pieces, spots, wd, sems.at[4])
    else:
        wgu, wd, second, n3, vectors, gelu_kept, slope_kept, hidden = refs
    ids[4]()
    normed = n2[...]
    for half in range(2):
        lanes = slice(half * HALF, (half + 1) * HALF)
        if direct:
            landed(wgu.at[0, half], sems.at[2 * half])
            landed(wgu.at[1, half], sems.at[2 * half + 1])
        gate = dot(normed, wgu[0, half])
        up = dot(normed, wgu[1, half])
        value, slope = gelu_parts(gate)
        gelu_kept[half] = value.astype(BF)
        slope_kept[half] = (up * slope).astype(BF)
        hidden[:, lanes] = (value * up).astype(BF)
        if direct:
            copies([(gelu_kept.at[half], gelu_out.at[half])], sems.at[2 * half])
            copies([(slope_kept.at[half], slope_out.at[half])], sems.at[2 * half + 1])
    if direct:
        landed(wd, sems.at[4])
        copies([(hidden, hidden_out)], sems.at[4])
    total = first[...] + dot(hidden[...], wd[...])
    second[...] = total
    normed_three = (total * norm_scale(total) * gains[2:3, :]).astype(BF)
    n3[...] = normed_three
    vectors[...] = dot(normed_three, wproj[...]).astype(BF)
    if direct:
        for half in range(2):
            landed(gelu_kept.at[half], sems.at[2 * half])
            landed(slope_kept.at[half], sems.at[2 * half + 1])
        landed(hidden, sems.at[4])


def count_kernel(ids, picks, counts):
    spots = lax.broadcasted_iota(jnp.int32, (DLEN, DLEN), 0)

    def one(j):
        for m in range(MICRO):
            total = jnp.zeros((DLEN, DLEN), F32)
            for t in range(picks.shape[2]):
                total += jnp.where(spots == picks[m, j, t : t + 1, :], 1.0, 0.0)
            counts[m, j] = total

    steps(picks.shape[1], one)


def block_of(others, m):
    return others[m % 2].at[m // 2] if len(others) == 2 else others[0].at[m]


def group_sums(values):
    lane = lax.broadcasted_iota(jnp.int32, values.shape, 1)
    shift = 1
    while shift < QLEN:
        ahead = pltpu.roll(values, DLEN - shift, 1)
        behind = pltpu.roll(values, shift, 1)
        values = values + jnp.where((lane & shift) == 0, ahead, behind)
        shift *= 2
    return values


def similarity_kernel(direct, count, ids, own, counts, share, *refs):
    others, (soft, score, best) = refs[:-3], refs[-3:]
    b, is_query = ids[0], ids[3]
    scale = DLEN**-0.5

    def one(m):
        j = (b ^ m) if direct else m
        for micro in range(MICRO):
            rows = slice(micro * DLEN, (micro + 1) * DLEN)
            mine, theirs = own[rows, :], block_of(others, m)[rows, :]
            doc = jnp.where(is_query == 1, theirs, mine)
            query = jnp.where(is_query == 1, mine, theirs)
            times = counts[micro, j]
            sim = dot_nt(doc, query) * scale
            peak = jnp.max(jnp.where(times > 0, sim, -jnp.inf), axis=0, keepdims=True)
            mass = jnp.where(times > 0, times * jnp.exp(jnp.minimum(sim - peak, 0.0)), 0.0)
            total = jnp.sum(mass, axis=0, keepdims=True)
            soft[micro, j] = mass / total
            best[micro, pl.ds(j, 1), :] = peak + jnp.log(total)

    steps(count, one)
    for micro in range(MICRO):
        score[micro] = group_sums(best[micro] * share[micro])


def vector_grad_kernel(
    direct, count, ids, soft, share, sharp, target, score, scores, *refs
):
    others, (grad, weight, total) = refs[:-3], refs[-3:]
    b, is_query = ids[0], ids[3]
    scale = DLEN**-0.5

    @pl.when(is_query == 1)
    def _():
        for micro in range(MICRO):
            logits = score[micro] * sharp[micro]
            raised = jnp.exp(logits - jnp.max(logits, axis=0, keepdims=True))
            odds = raised / jnp.sum(raised, axis=0, keepdims=True)
            doc = lax.broadcasted_iota(jnp.int32, (count, DLEN), 0)
            hit = jnp.where(target[micro] == doc, 1.0, 0.0)
            weight[micro] = (odds - hit) * sharp[micro] * share[micro] * scale

    @pl.when(is_query == 0)
    def _():
        for micro in range(MICRO):
            sharpness = sharp[micro]
            logits = scores[:, micro] * sharpness[None]
            peak = jnp.max(logits, axis=0)
            norm = jnp.sum(jnp.exp(logits - peak[None]), axis=0)
            odds = jnp.exp(score[micro] * sharpness - peak) / norm
            hit = jnp.where(target[micro] == b, 1.0, 0.0)
            weight[micro] = (odds - hit) * sharpness * share[micro] * scale

    total[...] = jnp.zeros_like(total)

    def one(m):
        j = (b ^ m) if direct else m
        for micro in range(MICRO):
            rows = slice(micro * DLEN, (micro + 1) * DLEN)
            dense = soft[micro, j] * weight[micro, pl.ds(j, 1), :]
            upper = dense.astype(BF)
            lower = (dense - upper.astype(F32)).astype(BF)
            theirs = block_of(others, m)[rows, :]

            @pl.when(is_query == 1)
            def _():
                total[rows, :] += dot_tn(upper, theirs) + dot_tn(lower, theirs)

            @pl.when(is_query == 0)
            def _():
                total[rows, :] += dot(upper, theirs) + dot(lower, theirs)

    steps(count, one)
    grad[...] = total[...].astype(BF)


def ffn_backward_kernel(direct, spots, ids, dvec, second, n2, n3, gains, wproj, *refs):
    if direct:
        hidden_in, gelu_in, slope_in = refs[:3]
        count = 1 + max(spot[3] for spot in spots)
        pieces, refs = refs[3 : 3 + count], refs[3 + count :]
        dx2_out, grad_proj, grad_gain, dgu, *outs = refs[:10]
        wd, hidden, gelu_kept, slope_kept, grad_down, quarters, sems = refs[10:]
        fetch_deep(ids, pieces, spots, wd, sems.at[0])
        copies([(slope_in, slope_kept)], sems.at[1])
        copies([(gelu_in, gelu_kept)], sems.at[2])
        copies([(hidden_in, hidden)], sems.at[3])
    else:
        wd, hidden, gelu_kept, slope_kept, dx2_out, grad_proj, grad_gain, dgu, dy_out = refs
    b, y, core, _, ready, send = ids
    ready()
    dvectors = dvec[...]
    dn3 = dot_nt(dvectors, wproj[...])
    dx2, dgain3 = norm_backward(second[...], gains[2:3, :], dn3)
    dx2_out[...] = dx2
    grad_gain[...] = dgain3
    grad_proj[...] = dot_tn(n3[...], dvectors)
    send(0, 1, 2)
    dy = dx2.astype(BF)
    if direct:
        landed(wd, sems.at[0])
    dh = dot_nt(dy, wd[...])
    if direct:
        landed(slope_kept, sems.at[1])
        landed(gelu_kept, sems.at[2])
    for half in range(2):
        part = dh[:, half * HALF : (half + 1) * HALF]
        dgu[0, half] = (part * slope_kept[half].astype(F32)).astype(BF)
        dgu[1, half] = (part * gelu_kept[half].astype(F32)).astype(BF)
    send(3)
    if not direct:
        dy_out[...] = dy
        return
    landed(hidden, sems.at[3])
    for j in range(SHARDS):
        down = dot_tn(hidden[:, j * 256 : (j + 1) * 256], dy).astype(BF)
        for part in range(4):
            grad_down[j, part] = down[part * 64 : (part + 1) * 64, :]
    normed = n2[...]
    for cflip in (1, 0):
        for yflip in (1, 0):
            place = cflip * 2 + yflip
            c, yy = core ^ cflip, y ^ yflip
            piece = dot_tn(normed, dgu[c, yy]).astype(BF)
            for j in range(SHARDS):
                m = b ^ j
                for k in range(4):
                    quarters[place, m, k * 96 : (k + 1) * 96, :] = piece[
                        j * 96 : (j + 1) * 96, k * 256 : (k + 1) * 256
                    ]
                down = grad_down[j, 2 * yy + c]
                for k in range(3):
                    quarters[place, m, 384 + k * 64 : 384 + (k + 1) * 64, :] = down[
                        :, k * 256 : (k + 1) * 256
                    ]
            if yflip:
                for group, out in zip(GROUPS_F, outs[2 + 2 * cflip : 4 + 2 * cflip]):
                    pairs = [(quarters.at[place, m], out.at[i]) for i, m in enumerate(group)]
                    copies(pairs, sems.at[place])
            else:
                copies([(quarters.at[place], outs[cflip])], sems.at[place])
    for place in range(4):
        landed(quarters.at[place], sems.at[place])


def middle_backward_kernel(direct, spots, ids, dx2, first, dgu, gains, *refs):
    if direct:
        count = 1 + max(spot[3] for spot in spots)
        pieces, refs = refs[:count], refs[count:]
        wvo_in, dx1_out, dattended, grad_gain, wgu, wout, sems = refs
        fetch_wide(ids, pieces, spots, wgu, sems)
        copies([(wvo_in.at[1], wout)], sems.at[4])
    else:
        wgu, wvo, dx1_out, dattended, grad_gain = refs
        wout = wvo.at[1]
    ids[4]()
    dn2 = jnp.zeros((ROWS, D), F32)
    for half in range(2):
        for c in range(2):
            if direct:
                landed(wgu.at[c, half], sems.at[half * 2 + c])
            dn2 = dn2 + dot_nt(dgu[c, half], wgu[c, half])
    back, dgain2 = norm_backward(first[...], gains[1:2, :], dn2)
    dx1 = dx2[...] + back
    dx1_out[...] = dx1
    grad_gain[...] = dgain2
    if direct:
        landed(wout, sems.at[4])
    dattended[...] = dot_nt(dx1.astype(BF), wout[...]).astype(BF)


def attention_backward_kernel(
    direct,
    ids,
    grad_first,
    dattended,
    x,
    n1,
    attended,
    weights,
    qkv,
    gains,
    bucket,
    grad_proj,
    grad_gain2,
    grad_gain3,
    *refs,
):
    if direct:
        wqk_in, wvo_in, grad_in, own_out, first_out, rest_out = refs[:6]
        wqk, wvo, own, other, left, right, dqk, extra, *refs = refs[6:]
        copies([(wvo_in.at[0], wvo.at[0])], refs[-1].at[0])
        copies([(wqk_in, wqk)], refs[-1].at[1])
    else:
        wqk, wvo, small, grad_in, dqkv_out, da_out, left, right, dqk, *refs = refs
    diag, bias_grad, dshares, scaled, queries, douts, *rest = refs
    b, core = ids[0], ids[2]
    ids[4]()
    dx1 = grad_first[...]
    da = dx1.astype(BF)
    low_lane = head_masks()
    row_at = lax.broadcasted_iota(jnp.int32, (DLEN, MICRO * DLEN), 0)
    lane_at = lax.broadcasted_iota(jnp.int32, (DLEN, MICRO * DLEN), 1)
    mirror = jnp.where(row_at == DLEN - 1 - lane_at % DLEN, 1.0, 0.0).astype(BF)
    diag[...] = jnp.zeros_like(diag)
    for i, (m, p, rows, lanes) in enumerate(PAIRS_OF_HEADS):
        queries[i] = both_heads(qkv[0, rows, lanes], low_lane)
        douts[i] = both_heads(dattended[rows, lanes], low_lane)
    for i, (m, p, rows, lanes) in enumerate(PAIRS_OF_HEADS):
        dshares[i] = dot_nt(douts[i], qkv[2, rows, lanes])
        right[0, rows, lanes] = dot_tn(weights[m, p], douts[i]).astype(BF)
    for i, (m, p, rows, lanes) in enumerate(PAIRS_OF_HEADS):
        wide = weights[m, p].astype(F32)
        dshare = dshares[i]
        centre = jnp.sum(wide * dshare, axis=-1, keepdims=True)
        scaled[i] = (wide * (dshare - centre)).astype(BF)
    for i, (m, p, rows, lanes) in enumerate(PAIRS_OF_HEADS):
        dq = dot(scaled[i], qkv[1, rows, lanes])
        dqk[0, rows, lanes] = jnp.where(low_lane, dq[:DLEN], dq[DLEN:]).astype(BF)
        dqk[1, rows, lanes] = dot_tn(scaled[i], queries[i]).astype(BF)
    for h in range(H):
        part = slice((h % 2) * DLEN, (h % 2 + 1) * DLEN)
        both = jnp.concatenate([scaled[m * (H // 2) + h // 2, part] for m in range(MICRO)], axis=0)
        turned = dot(mirror, both)
        wider = jnp.concatenate([turned, jnp.zeros_like(turned)], axis=1)
        rolled = pltpu.roll(wider, 0, 1, stride=1, stride_axis=0)
        diag[h : h + 1, :] = jnp.sum(rolled, axis=0, keepdims=True)
    bias_grad[...] = lax.dot_general(
        bucket[...],
        diag[...],
        (((1,), (1,)), ((), ())),
        precision=HIGHEST,
        preferred_element_type=F32,
    )
    if direct:
        sems = rest[0]
        landed(wvo.at[0], sems.at[0])
        landed(wqk, sems.at[1])
    dn1 = dot_nt(dqk[0], wqk[0]) + dot_nt(dqk[1], wqk[1]) + dot_nt(right[0], wvo[0])
    dx, dgain1 = norm_backward(x[...].astype(F32), gains[0:1, :], dn1)
    grad_in[...] = dx1 + dx
    right[1] = da
    left[0] = n1[...]
    left[1] = attended[...]
    all_gains = jnp.concatenate(
        [dgain1, grad_gain2[...], grad_gain3[...], jnp.zeros((5, D), F32)], axis=0
    )
    if not direct:
        small[0:8, :] = all_gains
        small[8:40, :] = jnp.concatenate(
            [bias_grad[...], jnp.zeros((BUCKETS, D - DLEN), F32)], axis=1
        )
        dqkv_out[0] = dqk[0]
        dqkv_out[1] = dqk[1]
        dqkv_out[2] = right[0]
        da_out[...] = da
        return
    per_shard = BUCKETS // SHARDS
    for j in range(SHARDS):
        for k in range(6):
            extra[0, j, :, k * DLEN : (k + 1) * DLEN] = grad_proj[
                j * 96 + k * 16 : j * 96 + (k + 1) * 16, :
            ]
        extra[1, j] = jnp.zeros((16, D), F32)
        extra[1, j, 0:8, :] = pltpu.roll(all_gains, (D - j * 96) % D, 1)
        extra[1, j, 8 : 8 + per_shard, 0:DLEN] = bias_grad[j * per_shard : (j + 1) * per_shard, :]
    for flip, out in ((1, other), (0, own)):
        c = core ^ flip
        top = dot_tn(n1[...], dqk[c]).astype(BF)
        bottom = dot_tn(left[c], right[c]).astype(BF)
        for j in range(SHARDS):
            m = b ^ j
            out[m, 0:96, :] = top[j * 96 : (j + 1) * 96, :]
            out[m, 96:192, :] = bottom[j * 96 : (j + 1) * 96, :]
            out[m, 192:208, :] = extra[c, j].astype(BF)
        if flip:
            pairs = [(other.at[m], first_out.at[i]) for i, m in enumerate(FIRST_A)]
            pairs += [(other.at[m], rest_out.at[i]) for i, m in enumerate(REST_A)]
            copies(pairs, sems.at[1])
        else:
            copies([(own, own_out)], sems.at[0])
    landed(other, sems.at[1])
    landed(own, sems.at[0])


def finish_wide_kernel(ids, near, far, twin, far_twin, token, grad_g, grad_u, grad_d):
    y, core = ids[1], ids[2]
    for yy in range(2):
        for c in range(2):

            @pl.when((y == yy) & (core == c))
            def _():
                for yflip, cflip, part in ((0, 0, near), (1, 0, far), (0, 1, twin), (1, 1, far_twin)):
                    half, rank = yy ^ yflip, c ^ cflip
                    out = grad_u if rank else grad_g
                    for k in range(4):
                        start = half * HALF + k * 256
                        out[:, start : start + 256] = part[0, k * 96 : (k + 1) * 96, :].astype(F32)
                    low = (2 * half + rank) * 64
                    for k in range(3):
                        grad_d[low : low + 64, k * 256 : (k + 1) * 256] = part[
                            0, 384 + k * 64 : 384 + (k + 1) * 64, :
                        ].astype(F32)


def finish_narrow_kernel(
    ids, near, twin, grad_q, grad_k, grad_v, grad_o, grad_p, grad_1, grad_2, grad_3, table
):
    core = ids[2]
    for c in range(2):

        @pl.when(core == c)
        def _():
            low, high = (twin, near) if c else (near, twin)
            grad_q[...] = low[0, 0:96, :].astype(F32)
            grad_k[...] = high[0, 0:96, :].astype(F32)
            grad_v[...] = low[0, 96:192, :].astype(F32)
            grad_o[...] = high[0, 96:192, :].astype(F32)
            for k in range(6):
                grad_p[k * 16 : (k + 1) * 16, :] = low[
                    0, 192:208, k * DLEN : (k + 1) * DLEN
                ].astype(F32)
            rows = high[0, 192:208, :].astype(F32)
            grad_1[...] = rows[0:1, :96]
            grad_2[...] = rows[1:2, :96]
            grad_3[...] = rows[2:3, :96]
            block = jnp.where(lax.broadcasted_iota(jnp.int32, (8, DLEN), 1) < H, rows[8:16, :DLEN], 0.0)
            line = block[0:1]
            for i in range(1, BUCKETS // SHARDS):
                line += pltpu.roll(block, i * H, 1)[i : i + 1]
            table[...] = line[:, : BUCKETS // SHARDS * H]


def local(
    hidden_in,
    norm1_gain,
    w_query,
    w_key,
    w_value,
    w_out,
    rel_table,
    norm2_gain,
    w_gate,
    w_up,
    w_down,
    norm3_gain,
    w_proj,
    query_lengths,
    keyword_request_mask,
    targets,
    candidates,
):
    streams = lax.axis_size("stream")
    shards = lax.axis_size("batch")
    pairs = streams // 2
    direct = shards == SHARDS and pairs == 2
    b = lax.axis_index("batch")
    s = lax.axis_index("stream")
    y, core = s // pairs, s % pairs
    is_query = s < pairs

    def swap(block, yflip, cflip, m):
        route = []
        for source in range(streams):
            target = ((source // pairs) ^ yflip) * pairs + ((source % pairs) ^ cflip)
            for j in range(shards):
                route.append((source * shards + j, target * shards + (j ^ m)))
        return lax.ppermute(block, EVERY, route)

    fence = lax.optimization_barrier
    first_core = core == 0
    spots_a = spots_f = None
    if direct:
        lines = [part.reshape(1, -1) for part in (norm1_gain, norm2_gain, norm3_gain, rel_table)]
        slab_a, slab_f = call(
            pack_kernel,
            "pack",
            [w_query, w_key, w_value, w_out, w_gate, w_up, w_down, w_proj, *lines],
            [((PIECE_A, D), BF), ((PIECE_F, 256), BF)],
        )

        def join(*parts):
            return jnp.concatenate(parts)

        def along_x(part):
            return swap(part, 0, 0, 1)

        def along_y(part):
            return swap(part, 1, 0, 0)

        def along_z(part):
            return swap(part, 0, 0, 2)

        def along_zz(part):
            return swap(part, 0, 0, 4)

        def other_core(part):
            return swap(part, 0, 1, 0)

        f0, a0 = slab_f[None], slab_a[None]
        token = jnp.zeros((8, DLEN), F32)
        f4, f2, y0, f1, a1 = along_zz(f0), along_z(f0), along_y(f0), along_x(f0), along_x(a0)
        token = tick(token)
        f4, f2, y0, f1, a1, a0, token = fence((f4, f2, y0, f1, a1, a0, token))
        f42, f142, token = fence((join(f4, f2), join(f1, f4, f2), token))
        y142, f53, f6, a4, a2 = (
            along_y(f142),
            along_x(f42),
            along_z(f4),
            along_zz(a0),
            along_z(a0),
        )
        token = tick(token)
        f53, f6, token = fence((f53, f6, token))
        f65, token = fence((join(f6, f53[0:1]), token))
        f7 = along_x(f6)

        a4, a2, token = fence((a4, a2, token))
        a42, a0142, token = fence((join(a4, a2), join(a0, a1, a4, a2), token))
        a53, a6, ta0142 = along_x(a42), along_z(a4), other_core(a0142)

        y142, f65, token = fence((y142, f65, token))
        y65 = along_y(f65)

        f7, ta0142, token = fence((f7, ta0142, token))
        f37, f_all, token = fence((join(f53[1:2], f7), join(f0, f142, f65, f53[1:2], f7), token))
        tf_all = other_core(f_all)

        a6, token = fence((a6, token))
        a7 = along_x(a6)
        y65, f37, token = fence((y65, f37, token))
        y37 = along_y(f37)

        a53, a7, token = fence((a53, a7, token))
        a5367, y_most, token = fence((join(a53, a6, a7), join(y0, y142, y65), token))
        ta5367, ty_most = other_core(a5367), other_core(y_most)
        token = tick(token)
        a5367, ta5367, y37, tf_all, token = fence((a5367, ta5367, y37, tf_all, token))
        ty37 = other_core(y37)

        a5367, token = fence((a5367, token))
        order_f = (0, 1, 4, 2, 6, 5, 3, 7)
        groups_a = [
            (0, (a0142, (0, 1, 4, 2)), (a5367, (5, 3, 6, 7))),
            (1, (ta0142, (0, 1, 4, 2)), (ta5367, (5, 3, 6, 7))),
        ]
        pieces_a, spots_a, pieces_f, spots_f = [], [], [], []
        for cflip, *group in groups_a:
            for part, flips in group:
                spots_a += [(cflip, m, len(pieces_a), i) for i, m in enumerate(flips)]
                pieces_a.append(part)
    else:

        def whole(part):
            return lax.all_gather(part, "batch", axis=0, tiled=True)

        wqk = jnp.stack([whole(w_query), whole(w_key)])
        wvo = jnp.stack([whole(w_value), whole(w_out)])
        gate_up = jnp.stack([whole(w_gate), whole(w_up)])
        wgu = jnp.transpose(gate_up.reshape(2, D, 2, HALF), (0, 2, 1, 3))
        wd = whole(w_down)
        wproj = whole(w_proj)
        gain_rows = [whole(gain) for gain in (norm1_gain, norm2_gain, norm3_gain)]
        gains = jnp.pad(jnp.stack(gain_rows).astype(F32), ((0, 5), (0, 0)))
        table = whole(rel_table).reshape(1, BUCKETS * H)

    micro_count = hidden_in.shape[0]
    slot = jnp.arange(DLEN)
    pair_lengths = lax.dynamic_index_in_dim(query_lengths, core, 1, keepdims=False)
    pair_keyword = lax.dynamic_index_in_dim(keyword_request_mask, core, 1, keepdims=False)
    pair_targets = lax.dynamic_index_in_dim(targets, core, 1, keepdims=False)

    def by_slot(values):
        blocks = values.reshape(micro_count, shards, GROUPS)
        own = lax.dynamic_slice_in_dim(blocks, b, 1, 1)
        blocks = jnp.where(is_query, jnp.broadcast_to(own, blocks.shape), blocks)
        return jnp.repeat(blocks, QLEN, axis=2)

    length_slots = by_slot(pair_lengths)
    valid_slots = (slot % QLEN)[None, None, :] < length_slots
    share = jnp.where(valid_slots, 1.0 / length_slots.astype(F32), 0.0)
    sharp = jnp.where(by_slot(pair_keyword) == 1, 20.0, 10.0).astype(F32)
    target_slots = by_slot(pair_targets)
    own_valid = lax.dynamic_slice_in_dim(valid_slots, b, 1, 1)
    same = (slot[:, None] // QLEN) == (slot[None, :] // QLEN)
    mask = jnp.where(is_query & ~(same[None] & own_valid), -1000000000.0, 0.0).astype(F32)

    small = 16 if direct else 48
    picked = lax.dynamic_index_in_dim(candidates, core, 1, keepdims=False)[:, 0]
    picked = picked.reshape(micro_count, shards, DLEN, picked.shape[-1])
    picked = jnp.transpose(picked, (0, 1, 3, 2))
    received = lax.all_to_all(picked, "batch", split_axis=1, concat_axis=1, tiled=True)
    picks = jnp.where(is_query, received, picked)
    (counts,) = call(
        count_kernel,
        "count",
        [picks],
        [((micro_count, shards, DLEN, DLEN), F32)],
        limit=small,
    )

    onehot = bucket_onehot()
    by_entry = jnp.asarray(np.repeat(onehot.T, H, axis=0), BF)
    x = hidden_in[:, 0].reshape(ROWS, D)
    row_bf, row_f32 = ((ROWS, D), BF), ((ROWS, D), F32)
    qkv_shape, weight_shape = ((3, ROWS, D), BF), ((MICRO, H // 2, ROWS, DLEN), BF)
    pair_weights = ((2, D, D), BF)
    gain_rows = ((8, D), F32)
    proj_shape = ((D, DLEN), BF)
    kept = [qkv_shape, row_bf, weight_shape, row_f32, row_bf, row_bf]
    bias_shape, score_shape = ((H // 2, ROWS, DLEN), F32), ((H, ROWS, DLEN), F32)
    result = call(
        functools.partial(attention_forward_kernel, direct, spots_a),
        "attention_forward",
        [x, mask, by_entry] + ([] if direct else [gains, table, wqk, wvo]),
        kept + ([gain_rows, proj_shape] if direct else []),
        ([pair_weights, pair_weights, ((2, SHARDS, 16, D), BF)] if direct else [])
        + [bias_shape, score_shape],
        far=pieces_a if direct else [],
        far_outs=[pair_weights, pair_weights] if direct else [],
        sems=3 if direct else 0,
        flops=2 * ROWS * D * D * 4,
        lazy=True,
    )
    qkv, attended, weights, first, n1, n2 = result[:6]
    if direct:
        gains, wproj, wqk, wvo = result[6:]
    first, counts, share, sharp, target_slots = fence((first, counts, share, sharp, target_slots))
    if direct:
        ty37, ty_most, first, token = fence((ty37, ty_most, first, token))
        near, twin = ((f_all, order_f),), ((tf_all, order_f),)
        far = ((y_most, order_f[:6]), (y37, order_f[6:]))
        far_twin = ((ty_most, order_f[:6]), (ty37, order_f[6:]))
        for yflip, cflip, group in ((0, 0, near), (0, 1, twin), (1, 0, far), (1, 1, far_twin)):
            for part, flips in group:
                spots_f += [(yflip, cflip, m, len(pieces_f), i) for i, m in enumerate(flips)]
                pieces_f.append(part)
    wide_bf, deep_bf = ((2, ROWS, HALF), BF), ((ROWS, FF), BF)
    wgu_shape, wd_shape = ((2, 2, D, HALF), BF), ((FF, D), BF)
    lasting = [wide_bf, wide_bf, deep_bf]
    result = call(
        functools.partial(ffn_forward_kernel, direct, spots_f),
        "ffn_forward",
        [first, n2, gains, wproj] + ([] if direct else [wgu, wd]),
        [row_f32, row_bf, ((ROWS, DLEN), BF)] + ([] if direct else lasting),
        [wgu_shape, wd_shape] + lasting if direct else [],
        far=[*pieces_f, token] if direct else [],
        far_outs=lasting if direct else [],
        sems=5 if direct else 0,
        flops=2 * ROWS * D * FF * 3,
        lazy=True,
    )
    second, n3, vectors, gelu_kept, slope_kept, hidden = result

    if direct:
        even = jnp.stack([swap(vectors, 1, 0, m) for m in (0, 2, 4, 6)])
        others = [even, swap(even, 0, 0, 1)]
    else:
        route = [(i, (i + pairs) % streams) for i in range(streams)]
        arrived = lax.ppermute(vectors, "stream", route)
        others = [lax.all_gather(arrived, "batch", axis=0)]
    block_f32 = ((micro_count, shards, DLEN, DLEN), F32)
    line_f32 = ((micro_count, shards, DLEN), F32)
    soft, score = call(
        functools.partial(similarity_kernel, direct, shards),
        "similarity",
        [vectors, counts, share, *others],
        [block_f32, line_f32],
        [line_f32],
        limit=small,
    )
    if direct:
        blocks = jnp.broadcast_to(score[None], (shards,) + score.shape)
        scores = lax.all_to_all(blocks, "batch", split_axis=0, concat_axis=0, tiled=True)
    else:
        scores = lax.all_gather(score, "batch", axis=0)
    (dvec,) = call(
        functools.partial(vector_grad_kernel, direct, shards),
        "vector_grad",
        [soft, share, sharp, target_slots, score, scores, *others],
        [((ROWS, DLEN), BF)],
        [line_f32, ((ROWS, DLEN), F32)],
        limit=small,
    )

    gain_row = ((1, D), F32)
    proj_f32 = ((D, DLEN), F32)
    dgu_shape = ((2, 2, ROWS, HALF), BF)
    quarter = ((SHARDS, PIECE_F, 256), BF)
    saved = [hidden, gelu_kept, slope_kept]
    result = call(
        functools.partial(ffn_backward_kernel, direct, spots_f),
        "ffn_backward",
        [dvec, second, n2, n3, gains, wproj] + ([] if direct else [wd, *saved]),
        [row_f32, proj_f32, gain_row, dgu_shape] + ([] if direct else [row_bf]),
        [wd_shape, deep_bf, wide_bf, wide_bf, ((SHARDS, 4, 64, D), BF), ((4, *quarter[0]), BF)]
        if direct
        else [],
        far=[*saved, *pieces_f] if direct else [],
        far_outs=[quarter] * 2 + [((4, PIECE_F, 256), BF)] * 4 if direct else [],
        sems=4 if direct else 0,
        flops=2 * ROWS * D * FF * 4,
        lazy=True,
    )
    dx2, grad_proj, grad_gain, dgu = result[:4]
    if direct:
        f_own, f_twin, *f_far = result[4:]
    else:
        dy = result[4]

    if direct:
        def own_f(m, *more):
            return [(base_f, m), *more]

        def far_sum(i):
            return [[(f_far[i], n), (c_far[i], n)] for n in range(4)]

        c_far = [other_core(part) for part in f_far[2:]]
        c_far[0], f_twin, dgu = fence((c_far[0], f_twin, dgu))
        twin = other_core(f_twin)
        (sent_a,) = add_up(far_sum(0))
        sent_a, dgu = fence((sent_a, dgu))
        y_a = along_y(sent_a)
    middle_in = [dx2, first, dgu, gains]
    dx1, dattended, grad_gain2 = call(
        functools.partial(middle_backward_kernel, direct, spots_f),
        "middle_backward",
        middle_in + ([] if direct else [wgu, wvo]),
        [row_f32, row_bf, gain_row],
        [wgu_shape, ((D, D), BF)] if direct else [],
        far=[*pieces_f, wvo] if direct else [],
        sems=5 if direct else 0,
        flops=ROUND_FLOPS,
        lazy=True,
    )
    if direct:
        *c_far[1:], twin, dattended = fence((*c_far[1:], twin, dattended))
        (sent_b,) = add_up(far_sum(1))
        base_f = base_up(f_own, twin, range(SHARDS))
        sent_b, base_f, dattended = fence((sent_b, base_f, dattended))
    two_rows = ((2, ROWS, D), BF)
    slab_out = ((SHARDS, PIECE_A, D), BF)
    blocks_bf = ((H, ROWS, DLEN), BF)
    result = call(
        functools.partial(attention_backward_kernel, direct),
        "attention_backward",
        [dx1, dattended, x, n1, attended, weights, qkv, gains, jnp.asarray(onehot.T)]
        + [grad_proj, grad_gain2, grad_gain]
        + ([] if direct else [wqk, wvo]),
        [row_f32] if direct else [((40, D), F32), row_f32, qkv_shape, row_bf],
        ([pair_weights, pair_weights, slab_out, slab_out] if direct else [])
        + [two_rows, two_rows, two_rows]
        + ([((2, SHARDS, 16, D), F32)] if direct else [])
        + [((DLEN, 2 * DLEN), F32), ((BUCKETS, DLEN), F32)]
        + [score_shape, blocks_bf, blocks_bf, blocks_bf],
        far=[wqk, wvo] if direct else [],
        far_outs=[slab_out] + [((count, PIECE_A, D), BF) for count in (2, 6)] if direct else [],
        sems=2 if direct else 0,
        flops=2 * ROWS * D * D * 7,
        lazy=True,
    )

    if direct:
        input_grad, a_own, a_first, a_rest = result

        def own_a(m, *more):
            return [(base_a, REST_A.index(m)), *more]

        y_a, sent_b, a_own, a_first, a_rest = fence((y_a, sent_b, a_own, a_first, a_rest))
        token = jnp.ones((8, DLEN), F32)
        y_b, c_first = along_y(sent_b), other_core(a_first)
        (out_73,) = add_up([own_f(7, (y_a, 1)), own_f(3, (y_a, 3))])
        out_73, token = fence((out_73, token))
        x73 = along_x(out_73)
        token = tick(token)
        c_first, a_rest, token = fence((c_first, a_rest, token))
        (out_a37,) = add_up([[(a_own, m), (c_first, i)] for i, m in enumerate(FIRST_A)], limit=59)
        out_a37, a_rest, token = fence((out_a37, a_rest, token))
        xa37, c_rest = along_x(out_a37), other_core(a_rest)
        token = tick(token)
        c_rest, token = fence((c_rest, token))
        base_a = base_up(a_own, c_rest, REST_A)
        x73, base_a, token = fence((x73, base_a, token))
        (out_62,) = add_up([own_f(6, (y_a, 0), (x73, 0)), own_f(2, (y_a, 2), (x73, 1))])
        out_62, token = fence((out_62, token))
        z62 = along_z(out_62)

        xa37, token = fence((xa37, token))
        out_a51, out_a62 = add_up(
            [own_a(5), own_a(1)], [own_a(6, (xa37, 1)), own_a(2, (xa37, 0))]
        )
        out_a62, token = fence((out_a62, token))
        za62 = along_z(out_a62)

        y_b, token = fence((y_b, token))
        out_5, out_1 = add_up([own_f(5, (y_b, 1))], [own_f(1, (y_b, 3))])
        out_5, token = fence((out_5, token))
        x5 = along_x(out_5)

        x5, z62, token = fence((x5, z62, token))
        (out_4,) = add_up([own_f(4, (y_b, 0), (x5, 0), (z62, 0))])
        out_4, out_a51, out_1, token = fence((out_4, out_a51, out_1, token))
        x1, xa51, z4 = along_x(out_1), along_x(out_a51), along_zz(out_4)

        za62, xa51, token = fence((za62, xa51, token))
        (out_a4,) = add_up([own_a(4, (xa51, 0), (za62, 0))])
        out_a4, token = fence((out_a4, token))
        za4 = along_zz(out_a4)

        x1, z4, token = fence((x1, z4, token))
        (mine_f,) = add_up([own_f(0, (y_b, 2), (x1, 0), (z62, 1), (z4, 0))])
        mine_f, token = fence((mine_f, token))
        far, twin_f = along_y(mine_f), other_core(mine_f)

        za4, token = fence((za4, token))
        (part_a,) = add_up([own_a(0, (xa51, 1), (za62, 1), (za4, 0))])
        part_a, token = fence((part_a, token))
        ya = along_y(part_a)

        far, twin_f, token = fence((far, twin_f, token))
        far_twin_f = other_core(far)
        ya, token = fence((ya, token))
        (mine_a,) = add_up([[(part_a, 0), (ya, 0)]])
        mine_a, far_twin_f, token = fence((mine_a, far_twin_f, token))
        twin_a = other_core(mine_a)
        shard_f32, wide_f32 = ((96, D), F32), ((96, FF), F32)
        grad_g, grad_u, grad_d = call(
            finish_wide_kernel,
            "finish_wide",
            [mine_f, far, twin_f, far_twin_f],
            [wide_f32, wide_f32, ((256, D), F32)],
            far=[token],
            limit=24,
            near=True,
        )
        grad_q, grad_k, grad_v, grad_o, grad_p, *small = call(
            finish_narrow_kernel,
            "finish_narrow",
            [mine_a, twin_a],
            [shard_f32] * 4 + [((96, DLEN), F32), ((1, 96), F32), ((1, 96), F32), ((1, 96), F32)]
            + [((1, 48), F32)],
            limit=24,
            near=True,
        )
        grad_n1, grad_n2, grad_n3, grad_table = [row.reshape(-1) for row in small]
    else:
        small, input_grad, dqkv, da = result

        def summed(part):
            part = lax.psum_scatter(part, "batch", scatter_dimension=0, tiled=True)
            return lax.psum(part, "stream")

        grad_q, grad_k, grad_v = [summed(dot_tn(n1, dqkv[i])) for i in range(3)]
        grad_o = summed(dot_tn(attended, da))
        grad_g, grad_u = [
            summed(jnp.concatenate([dot_tn(n2, dgu[i, half]) for half in range(2)], axis=1))
            for i in range(2)
        ]
        grad_d = summed(dot_tn(hidden, dy))
        grad_p = summed(grad_proj)
        grad_n1, grad_n2, grad_n3 = [summed(small[i]) for i in range(3)]
        flat = lax.psum(small[8 : 8 + BUCKETS, :H].reshape(-1), EVERY)
        share_rows = flat.shape[0] // shards
        grad_table = lax.dynamic_slice_in_dim(flat, b * share_rows, share_rows, 0)

    vectors_out = vectors.reshape(micro_count, DLEN, DLEN)[:, None]
    grad_hidden = input_grad.reshape(micro_count, DLEN, D)[:, None]
    return (
        vectors_out,
        grad_hidden,
        grad_n1,
        grad_q,
        grad_k,
        grad_v,
        grad_o,
        grad_table,
        grad_n2,
        grad_g,
        grad_u,
        grad_d,
        grad_n3,
        grad_p,
    )


def solution(mesh):
    rows, lines = P("batch", None), P("batch")
    spread = P(None, "stream", "batch", None)
    return jax.shard_map(
        local,
        mesh=mesh,
        in_specs=(spread, lines, rows, rows, rows, rows, lines, lines, rows, rows, rows, lines, rows)
        + (P(), P(), P(), P(None, None, "batch", None, None)),
        out_specs=(spread, spread, lines, rows, rows, rows, rows, lines, lines)
        + (rows, rows, rows, lines, rows),
        check_vma=False,
    )
```

```python
import functools
import math

import jax
import jax.numpy as jnp
import numpy as np
from jax import lax
from jax.experimental import pallas as pl
from jax.experimental.pallas import tpu as pltpu
from jax.sharding import PartitionSpec as P

H = 12
DH = 64
BUCKETS = 32
MAX_DIST = 128
DLEN = 128
QLEN = 32
GROUPS = DLEN // QLEN
MICRO = 2
ROWS = MICRO * DLEN
D = 768
FF = 2048
HALF = FF // 2
SHARDS = 8
PIECE_A = 208
PIECE_F = 576
FIRST_A, REST_A = (3, 7), (6, 2, 5, 1, 4, 0)
GROUPS_F = ((6, 7, 2, 3), (4, 5, 0, 1))

EPSILON = 1e-06
HIGHEST = lax.Precision.HIGHEST
BF = jnp.bfloat16
F32 = jnp.float32
EVERY = ("stream", "batch")
MIB = 2**20
ROUND_FLOPS = 5 * 10**10


def distance_bucket(distance):
    half_count = BUCKETS // 2
    exact_count = half_count // 2
    if distance < exact_count:
        return distance
    grown = exact_count + int(
        math.floor(
            math.log(distance / exact_count)
            / math.log(MAX_DIST / exact_count)
            * (half_count - exact_count)
            + 1e-09
        )
    )
    return min(grown, half_count - 1)


def bucket_onehot():
    table = np.zeros((2 * DLEN, BUCKETS), np.float32)
    for o in range(2 * DLEN - 1):
        offset = o - (DLEN - 1)
        table[o, distance_bucket(abs(offset)) + (BUCKETS // 2 if offset > 0 else 0)] = 1.0
    return table


def norm_scale(values):
    return lax.rsqrt(jnp.mean(values * values, axis=-1, keepdims=True) + EPSILON)


def norm_backward(values, gain, grad):
    scale = norm_scale(values)
    pulled = gain * grad
    inner = jnp.mean(values * pulled, axis=-1, keepdims=True)
    back = scale * pulled - values * (scale * scale * scale * inner)
    return back, jnp.sum(grad * values * scale, axis=0, keepdims=True)


def dot(left, right):
    return jnp.dot(left, right, preferred_element_type=F32)


def dot_nt(left, right):
    return lax.dot_general(left, right, (((1,), (1,)), ((), ())), preferred_element_type=F32)


def dot_tn(left, right):
    return lax.dot_general(left, right, (((0,), (0,)), ((), ())), preferred_element_type=F32)


def steps(count, body):
    if count <= 16:
        for i in range(count):
            body(i)
    else:

        @pl.loop(0, count)
        def _(i):
            body(i)


VMEM = pl.BlockSpec(memory_space=pltpu.VMEM)
SMEM = pl.BlockSpec(memory_space=pltpu.SMEM)
HBM = pl.BlockSpec(memory_space=pltpu.HBM)


def positions():
    pairs = lax.axis_size("stream") // 2
    stream = lax.axis_index("stream")
    return lax.axis_index("batch"), stream // pairs, stream % pairs, jnp.where(stream < pairs, 1, 0)


def body_kernel(kernel, lazy, counts, *refs):
    parts = []
    for count in counts:
        parts.append(refs[:count])
        refs = refs[count:]
    arrays, far, outs, far_outs, held, made, scratch = parts
    in_sems, out_sems = refs
    for i, (array, place) in enumerate(zip(arrays, held)):
        pltpu.make_async_copy(array, place, in_sems.at[i]).start()
    sent = set()

    def ready():
        for i, (array, place) in enumerate(zip(arrays, held)):
            pltpu.make_async_copy(array, place, in_sems.at[i]).wait()

    def send(*results):
        for i in results:
            sent.add(i)
            pltpu.make_async_copy(made[i], outs[i], out_sems.at[i]).start()

    if not lazy:
        ready()
    kernel((*positions(), ready, send), *held, *far, *made, *far_outs, *scratch)
    send(*(i for i in range(len(outs)) if i not in sent))
    for i, (place, out) in enumerate(zip(made, outs)):
        pltpu.make_async_copy(place, out, out_sems.at[i]).wait()


def near_kernel(kernel, *refs):
    kernel(positions(), *refs)


def call(
    kernel,
    name,
    arrays,
    outs,
    scratch=(),
    far=(),
    far_outs=(),
    sems=0,
    flops=0,
    limit=59,
    near=False,
    lazy=False,
):
    shapes = [jax.ShapeDtypeStruct(s, t) for s, t in (*outs, *far_outs)]
    moved = sum(math.prod(s.shape) * s.dtype.itemsize for s in shapes)
    moved += sum(math.prod(a.shape) * a.dtype.itemsize for a in (*arrays, *far))
    spaces = [pltpu.VMEM(s, t) for s, t in scratch]
    if sems:
        spaces.append(pltpu.SemaphoreType.DMA((sems,)))
    kind = VMEM if near else HBM
    if near:
        body = functools.partial(near_kernel, kernel)
    else:
        counts = (len(arrays), len(far), len(outs), len(far_outs))
        counts += (len(arrays), len(outs), len(spaces))
        body = functools.partial(body_kernel, kernel, lazy, counts)
        spaces = (
            [pltpu.VMEM(a.shape, a.dtype) for a in arrays]
            + [pltpu.VMEM(s, t) for s, t in outs]
            + spaces
            + [pltpu.SemaphoreType.DMA((max(1, len(part)),)) for part in (arrays, outs)]
        )
    return pl.pallas_call(
        body,
        name=name,
        out_shape=shapes,
        in_specs=[kind] * len(arrays) + [HBM] * len(far),
        out_specs=[kind] * len(outs) + [HBM] * len(far_outs),
        scratch_shapes=spaces,
        compiler_params=pltpu.CompilerParams(vmem_limit_bytes=limit * MIB),
        cost_estimate=pl.CostEstimate(flops=flops, bytes_accessed=moved, transcendentals=0),
    )(*arrays, *far)


def tick_kernel(token, out):
    pass


def tick(token):
    return pl.pallas_call(
        tick_kernel,
        name="tick",
        in_specs=[HBM],
        out_specs=HBM,
        out_shape=jax.ShapeDtypeStruct(token.shape, token.dtype),
        input_output_aliases={0: 0},
        cost_estimate=pl.CostEstimate(flops=ROUND_FLOPS, bytes_accessed=0, transcendentals=0),
    )(token)


def add_kernel(plan, near, far, ids, *refs):
    near, far, refs = refs[:near], refs[near : near + far], refs[near + far :]
    outs, refs = refs[: len(plan)], refs[len(plan) :]
    held, sems = (refs[:-1], refs[-1]) if far else ((), None)
    place = 0
    for entries in plan:
        for terms in entries:
            for is_far, array, entry in terms:
                if is_far:
                    copies([(far[array].at[entry], held[place])], sems.at[place])
                    place += 1
    place = 0
    for out, entries in zip(outs, plan):
        for i, terms in enumerate(entries):
            total = None
            for is_far, array, entry in terms:
                if is_far:
                    landed(held[place], sems.at[place])
                    part = held[place][...].astype(F32)
                    place += 1
                else:
                    part = near[array][entry].astype(F32)
                total = part if total is None else total + part
            out[i] = total.astype(BF)


def base_kernel(picks, ids, own, rest, out, left, right, sems):
    for i, m in enumerate(picks):
        copies([(own.at[m], left.at[i]), (rest.at[i], right.at[i])], sems.at[i])
    for i in range(len(picks)):
        landed(left.at[i], sems.at[i])
        landed(right.at[i], sems.at[i])
        left[i] = (left[i].astype(F32) + right[i].astype(F32)).astype(BF)
        copies([(left.at[i], out.at[i])], sems.at[i])
    for i in range(len(picks)):
        landed(left.at[i], sems.at[i])


def base_up(own, rest, picks):
    shape = (rest.shape, BF)
    (base,) = call(
        functools.partial(base_kernel, tuple(picks)),
        "base_up",
        [],
        [],
        [shape, shape],
        far=[own, rest],
        far_outs=[shape],
        sems=len(picks),
    )
    return base


def add_up(*outputs, limit=24):
    known = ([], [])
    plan, flat, shapes = [], [], []
    for entries in outputs:
        plan.append([])
        for terms in entries:
            plan[-1].append([])
            for array, entry in terms:
                is_far = int(array.shape[0] > 4)
                arrays = known[is_far]
                found = [i for i, other in enumerate(arrays) if other is array]
                if not found:
                    arrays.append(array)
                    found = [len(arrays) - 1]
                if is_far:
                    flat.append((array.shape[1:], BF))
                plan[-1][-1].append((is_far, found[0], entry))
        shapes.append(((len(entries), *entries[0][0][0].shape[1:]), BF))
    return call(
        functools.partial(add_kernel, plan, len(known[0]), len(known[1])),
        "add_up",
        known[0],
        shapes,
        flat,
        far=known[1],
        sems=len(flat),
        limit=limit,
        near=True,
    )


def pack_kernel(ids, wq, wk, wv, wo, wg, wu, wd, wp, g1, g2, g3, table, slab_a, slab_f):
    y, core = ids[1], ids[2]

    def fill(top, bottom, wide, rank):
        slab_a[0:96, :] = top[...]
        slab_a[96:192, :] = bottom[...]
        for yy in range(2):

            @pl.when(y == yy)
            def _():
                for k in range(4):
                    start = yy * HALF + k * 256
                    slab_f[k * 96 : (k + 1) * 96, :] = wide[:, start : start + 256]
                row = (2 * yy + rank) * 64
                for k in range(3):
                    slab_f[384 + k * 64 : 384 + (k + 1) * 64, :] = wd[
                        row : row + 64, k * 256 : (k + 1) * 256
                    ]

    @pl.when(core == 0)
    def _():
        fill(wq, wv, wg, 0)
        for k in range(6):
            slab_a[192:208, k * DLEN : (k + 1) * DLEN] = wp[k * 16 : (k + 1) * 16, :]

    @pl.when(core == 1)
    def _():
        fill(wk, wo, wu, 1)
        rows = [g1[...].astype(F32), g2[...].astype(F32), g3[...].astype(F32)]
        head = jnp.concatenate(rows + [jnp.zeros((5, 96), F32)], axis=0)
        tail = jnp.concatenate([table[...].astype(F32), jnp.zeros((7, 48), F32)], axis=0)
        tail = jnp.concatenate([tail, jnp.zeros((8, 48), F32)], axis=1)
        both = jnp.concatenate([head, tail], axis=0)
        slab_a[192:208, :] = jnp.concatenate(
            [both, jnp.zeros((16, D - 96), F32)], axis=1
        ).astype(BF)


def copies(pairs, sem):
    for src, dst in pairs:
        pltpu.make_async_copy(src, dst, sem).start()


def landed(buffer, sem):
    pltpu.make_async_copy(buffer, buffer, sem).wait()


def fetch_a(ids, pieces, spots, wqk, wvo, extra, sems):
    b, core = ids[0], ids[2]
    for cflip, m, array, entry in spots:
        src = pieces[array].at[entry]
        c, j = core ^ cflip, b ^ m
        row = pl.multiple_of(j * 96, 96)
        copies([(src.at[pl.ds(0, 96)], wqk.at[c, pl.ds(row, 96)])], sems.at[0])
        copies([(src.at[pl.ds(96, 96)], wvo.at[c, pl.ds(row, 96)])], sems.at[1])
        copies([(src.at[pl.ds(192, 16)], extra.at[c, j])], sems.at[2])


def fetch_wide(ids, pieces, spots, wgu, sems):
    b, y, core = ids[0], ids[1], ids[2]
    for yflip, cflip, m, array, entry in spots:
        src = pieces[array].at[entry]
        c, yy, j = core ^ cflip, y ^ yflip, b ^ m
        row = pl.multiple_of(j * 96, 96)
        for k in range(4):
            tile = wgu.at[c, yy, pl.ds(row, 96), pl.ds(k * 256, 256)]
            copies([(src.at[pl.ds(k * 96, 96)], tile)], sems.at[2 * yy + c])


def fetch_deep(ids, pieces, spots, wd, sem):
    b, y, core = ids[0], ids[1], ids[2]
    for yflip, cflip, m, array, entry in spots:
        src = pieces[array].at[entry]
        low = pl.multiple_of((b ^ m) * 256 + (2 * (y ^ yflip) + (core ^ cflip)) * 64, 64)
        for k in range(3):
            tile = wd.at[pl.ds(low, 64), pl.ds(k * 256, 256)]
            copies([(src.at[pl.ds(384 + k * 64, 64)], tile)], sem)


def head_masks():
    low_lane = lax.broadcasted_iota(jnp.int32, (DLEN, DLEN), 1) < DH
    return low_lane


def both_heads(pair, low_lane):
    zero = jnp.zeros_like(pair)
    return jnp.concatenate(
        [jnp.where(low_lane, pair, zero), jnp.where(low_lane, zero, pair)], axis=0
    )


PAIRS_OF_HEADS = [
    (m, p, slice(m * DLEN, (m + 1) * DLEN), slice(p * DLEN, (p + 1) * DLEN))
    for m in range(MICRO)
    for p in range(H // 2)
]


def attention_forward_kernel(direct, spots, ids, x, mask, onehot, *refs):
    if direct:
        count = 1 + max(spot[2] for spot in spots)
        pieces, refs = refs[:count], refs[count:]
        qkv, attended, weights, first, n1, n2, gains, wproj, wqk_out, wvo_out = refs[:10]
        wqk, wvo, extra, bias, scores, sems = refs[10:]
        fetch_a(ids, pieces, spots, wqk, wvo, extra, sems)
        ids[4]()
        landed(extra, sems.at[2])
        lane = lax.broadcasted_iota(jnp.int32, (8, D), 1)
        all_gains = jnp.zeros((8, D), F32)
        flat = jnp.zeros((8, D), F32)
        for j in range(SHARDS):
            block = extra[1, j].astype(F32)
            all_gains += pltpu.roll(jnp.where(lane < 96, block[0:8], 0.0), j * 96, 1)
            flat += pltpu.roll(jnp.where(lane < 48, block[8:16], 0.0), j * 48, 1)
            for k in range(6):
                wproj[j * 96 + k * 16 : j * 96 + (k + 1) * 16, :] = extra[
                    0, j, :, k * DLEN : (k + 1) * DLEN
                ]
        gains[...] = all_gains
        flat = flat[0:1, : BUCKETS * H]
    else:
        ids[4]()
        gains, flat_in, wqk, wvo = refs[:4]
        qkv, attended, weights, first, n1, n2, bias, scores = refs[4:]
        flat = flat_in[...].astype(F32)
    entry = lax.broadcasted_iota(jnp.int32, (16, BUCKETS * H), 1)
    head = lax.broadcasted_iota(jnp.int32, (16, BUCKETS * H), 0)
    by_head = jnp.where(entry % H == head, jnp.broadcast_to(flat, entry.shape), 0.0)
    offsets = dot(by_head.astype(BF), onehot[...])
    for h in range(H):
        row = jnp.broadcast_to(offsets[h : h + 1, :], (DLEN, 2 * DLEN))
        rolled = pltpu.roll(row, DLEN + 1, 1, stride=1, stride_axis=0)
        bias[h // 2, (h % 2) * DLEN : (h % 2 + 1) * DLEN, :] = rolled[:, :DLEN]
    tokens = x[...].astype(F32)
    normed = (tokens * norm_scale(tokens) * gains[0:1, :]).astype(BF)
    n1[...] = normed
    if direct:
        landed(wqk, sems.at[0])
        copies([(wqk, wqk_out)], sems.at[0])
        landed(wvo, sems.at[1])
        copies([(wvo, wvo_out)], sems.at[1])
    qkv[0] = dot(normed, wqk[0]).astype(BF)
    qkv[1] = dot(normed, wqk[1]).astype(BF)
    qkv[2] = dot(normed, wvo[0]).astype(BF)
    ids[5](0, 4)
    low_lane = head_masks()
    for i, (m, p, rows, lanes) in enumerate(PAIRS_OF_HEADS):
        scores[i] = dot_nt(both_heads(qkv[0, rows, lanes], low_lane), qkv[1, rows, lanes])
    for i, (m, p, rows, lanes) in enumerate(PAIRS_OF_HEADS):
        hidden = jnp.concatenate([mask[m], mask[m]], axis=0)
        biased = scores[i] + bias[p] + hidden
        shifted = jnp.exp(biased - jnp.max(biased, axis=-1, keepdims=True))
        weights[m, p] = (shifted / jnp.sum(shifted, axis=-1, keepdims=True)).astype(BF)
    for i, (m, p, rows, lanes) in enumerate(PAIRS_OF_HEADS):
        mixed = dot(weights[m, p], qkv[2, rows, lanes])
        attended[rows, lanes] = jnp.where(low_lane, mixed[:DLEN], mixed[DLEN:]).astype(BF)
    x1 = tokens + dot(attended[...], wvo[1])
    first[...] = x1
    n2[...] = (x1 * norm_scale(x1) * gains[1:2, :]).astype(BF)
    if direct:
        landed(wqk, sems.at[0])
        landed(wvo, sems.at[1])


def gelu_parts(gate):
    c0, c1 = math.sqrt(2.0 / math.pi), 0.044715
    square = gate * gate
    bent = jnp.tanh(c0 * gate * (1.0 + c1 * square))
    value = 0.5 * gate * (1.0 + bent)
    slope = 0.5 * (1.0 + bent) + 0.5 * gate * (1.0 - bent * bent) * (
        c0 * (1.0 + 3.0 * c1 * square)
    )
    return value, slope


def ffn_forward_kernel(direct, spots, ids, first, n2, gains, wproj, *refs):
    if direct:
        count = 1 + max(spot[3] for spot in spots)
        pieces, refs = refs[:count], refs[count:]
        second, n3, vectors, gelu_out, slope_out, hidden_out = refs[1:7]
        wgu, wd, gelu_kept, slope_kept, hidden, sems = refs[7:]
        fetch_wide(ids, pieces, spots, wgu, sems)
        fetch_deep(ids, pieces, spots, wd, sems.at[4])
    else:
        wgu, wd, second, n3, vectors, gelu_kept, slope_kept, hidden = refs
    ids[4]()
    normed = n2[...]
    for step in range(2):
        half = (ids[1] ^ step) if direct else step
        if direct:
            landed(wgu.at[0, half], sems.at[2 * half])
            landed(wgu.at[1, half], sems.at[2 * half + 1])
        gate = dot(normed, wgu[0, half])
        up = dot(normed, wgu[1, half])
        value, slope = gelu_parts(gate)
        gelu_kept[half] = value.astype(BF)
        slope_kept[half] = (up * slope).astype(BF)
        hidden[half] = (value * up).astype(BF)
        if direct:
            copies([(gelu_kept.at[half], gelu_out.at[half])], sems.at[2 * half])
            copies([(slope_kept.at[half], slope_out.at[half])], sems.at[2 * half + 1])
    if direct:
        landed(wd, sems.at[4])
        copies([(hidden, hidden_out)], sems.at[4])
    total = first[...] + dot(hidden[0], wd[:HALF, :]) + dot(hidden[1], wd[HALF:, :])
    second[...] = total
    normed_three = (total * norm_scale(total) * gains[2:3, :]).astype(BF)
    n3[...] = normed_three
    vectors[...] = dot(normed_three, wproj[...]).astype(BF)
    if direct:
        for half in range(2):
            landed(gelu_kept.at[half], sems.at[2 * half])
            landed(slope_kept.at[half], sems.at[2 * half + 1])
        landed(hidden, sems.at[4])


def count_kernel(ids, picks, counts):
    spots = lax.broadcasted_iota(jnp.int32, (DLEN, DLEN), 0)

    def one(j):
        for m in range(MICRO):
            total = jnp.zeros((DLEN, DLEN), F32)
            for t in range(picks.shape[2]):
                total += jnp.where(spots == picks[m, j, t : t + 1, :], 1.0, 0.0)
            counts[m, j] = total

    steps(picks.shape[1], one)


def block_of(others, m):
    return others[m % 2].at[m // 2] if len(others) == 2 else others[0].at[m]


def group_sums(values):
    lane = lax.broadcasted_iota(jnp.int32, values.shape, 1)
    shift = 1
    while shift < QLEN:
        ahead = pltpu.roll(values, DLEN - shift, 1)
        behind = pltpu.roll(values, shift, 1)
        values = values + jnp.where((lane & shift) == 0, ahead, behind)
        shift *= 2
    return values


def similarity_kernel(direct, count, ids, own, counts, share, *refs):
    others, (soft, score, best) = refs[:-3], refs[-3:]
    b, is_query = ids[0], ids[3]
    scale = DLEN**-0.5

    def one(m):
        j = (b ^ m) if direct else m
        for micro in range(MICRO):
            rows = slice(micro * DLEN, (micro + 1) * DLEN)
            mine, theirs = own[rows, :], block_of(others, m)[rows, :]
            doc = jnp.where(is_query == 1, theirs, mine)
            query = jnp.where(is_query == 1, mine, theirs)
            times = counts[micro, j]
            sim = dot_nt(doc, query) * scale
            peak = jnp.max(jnp.where(times > 0, sim, -jnp.inf), axis=0, keepdims=True)
            mass = jnp.where(times > 0, times * jnp.exp(jnp.minimum(sim - peak, 0.0)), 0.0)
            total = jnp.sum(mass, axis=0, keepdims=True)
            soft[micro, j] = mass / total
            best[micro, pl.ds(j, 1), :] = peak + jnp.log(total)

    steps(count, one)
    for micro in range(MICRO):
        score[micro] = group_sums(best[micro] * share[micro])


def vector_grad_kernel(
    direct, count, ids, soft, share, sharp, target, score, scores, *refs
):
    others, (grad, weight, total) = refs[:-3], refs[-3:]
    b, is_query = ids[0], ids[3]
    scale = DLEN**-0.5

    @pl.when(is_query == 1)
    def _():
        for micro in range(MICRO):
            logits = score[micro] * sharp[micro]
            raised = jnp.exp(logits - jnp.max(logits, axis=0, keepdims=True))
            odds = raised / jnp.sum(raised, axis=0, keepdims=True)
            doc = lax.broadcasted_iota(jnp.int32, (count, DLEN), 0)
            hit = jnp.where(target[micro] == doc, 1.0, 0.0)
            weight[micro] = (odds - hit) * sharp[micro] * share[micro] * scale

    @pl.when(is_query == 0)
    def _():
        for micro in range(MICRO):
            sharpness = sharp[micro]
            logits = scores[:, micro] * sharpness[None]
            peak = jnp.max(logits, axis=0)
            norm = jnp.sum(jnp.exp(logits - peak[None]), axis=0)
            odds = jnp.exp(score[micro] * sharpness - peak) / norm
            hit = jnp.where(target[micro] == b, 1.0, 0.0)
            weight[micro] = (odds - hit) * sharpness * share[micro] * scale

    def parts(m, micro):
        j = (b ^ m) if direct else m
        dense = soft[micro, j] * weight[micro, pl.ds(j, 1), :]
        upper = dense.astype(BF)
        lower = (dense - upper.astype(F32)).astype(BF)
        return upper, lower, block_of(others, m)[micro * DLEN : (micro + 1) * DLEN, :]

    for flag, product in ((1, dot_tn), (0, dot)):

        @pl.when(is_query == flag)
        def _():
            for micro in range(MICRO):
                rows = slice(micro * DLEN, (micro + 1) * DLEN)
                if count <= 16:
                    sums = []
                    for m in range(count):
                        upper, lower, theirs = parts(m, micro)
                        sums.append(product(upper, theirs) + product(lower, theirs))
                    grad[rows, :] = sum(sums[1:], sums[0]).astype(BF)
                else:
                    total[rows, :] = jnp.zeros((DLEN, DLEN), F32)

                    @pl.loop(0, count)
                    def _(m):
                        upper, lower, theirs = parts(m, micro)
                        total[rows, :] += product(upper, theirs) + product(lower, theirs)

                    grad[rows, :] = total[rows, :].astype(BF)


def ffn_backward_kernel(direct, spots, ids, dvec, second, n2, n3, gains, wproj, *refs):
    if direct:
        hidden_in, gelu_in, slope_in = refs[:3]
        count = 1 + max(spot[3] for spot in spots)
        pieces, refs = refs[3 : 3 + count], refs[3 + count :]
        dx2_out, grad_proj, grad_gain, dgu, *outs = refs[:10]
        wd, hidden, gelu_kept, slope_kept, grad_down, quarters, sems = refs[10:]
        fetch_deep(ids, pieces, spots, wd, sems.at[0])
        copies([(slope_in, slope_kept)], sems.at[1])
        copies([(gelu_in, gelu_kept)], sems.at[2])
        copies([(hidden_in, hidden)], sems.at[3])
    else:
        wd, hidden, gelu_kept, slope_kept, dx2_out, grad_proj, grad_gain, dgu, dy_out = refs
    b, y, core, _, ready, send = ids
    ready()
    dvectors = dvec[...]
    dn3 = dot_nt(dvectors, wproj[...])
    dx2, dgain3 = norm_backward(second[...], gains[2:3, :], dn3)
    dx2_out[...] = dx2
    grad_gain[...] = dgain3
    grad_proj[...] = dot_tn(n3[...], dvectors)
    send(0, 1, 2)
    dy = dx2.astype(BF)
    if direct:
        landed(wd, sems.at[0])
    dh = dot_nt(dy, wd[...])
    if direct:
        landed(slope_kept, sems.at[1])
        landed(gelu_kept, sems.at[2])
    for half in range(2):
        part = dh[:, half * HALF : (half + 1) * HALF]
        dgu[0, half] = (part * slope_kept[half].astype(F32)).astype(BF)
        dgu[1, half] = (part * gelu_kept[half].astype(F32)).astype(BF)
    send(3)
    if not direct:
        dy_out[...] = dy
        return
    landed(hidden, sems.at[3])
    for j in range(SHARDS):
        place = (j % 4) * 256
        down = dot_tn(hidden[j // 4, :, place : place + 256], dy).astype(BF)
        for part in range(4):
            grad_down[j, part] = down[part * 64 : (part + 1) * 64, :]
    normed = n2[...]
    for cflip in (1, 0):
        for yflip in (1, 0):
            place = cflip * 2 + yflip
            c, yy = core ^ cflip, y ^ yflip
            piece = dot_tn(normed, dgu[c, yy]).astype(BF)
            for j in range(SHARDS):
                m = b ^ j
                for k in range(4):
                    quarters[place, m, k * 96 : (k + 1) * 96, :] = piece[
                        j * 96 : (j + 1) * 96, k * 256 : (k + 1) * 256
                    ]
                down = grad_down[j, 2 * yy + c]
                for k in range(3):
                    quarters[place, m, 384 + k * 64 : 384 + (k + 1) * 64, :] = down[
                        :, k * 256 : (k + 1) * 256
                    ]
            if yflip:
                for group, out in zip(GROUPS_F, outs[2 + 2 * cflip : 4 + 2 * cflip]):
                    pairs = [(quarters.at[place, m], out.at[i]) for i, m in enumerate(group)]
                    copies(pairs, sems.at[place])
            else:
                copies([(quarters.at[place], outs[cflip])], sems.at[place])
    for place in range(4):
        landed(quarters.at[place], sems.at[place])


def middle_backward_kernel(direct, spots, ids, dx2, first, dgu, gains, *refs):
    if direct:
        count = 1 + max(spot[3] for spot in spots)
        pieces, refs = refs[:count], refs[count:]
        wvo_in, dx1_out, dattended, grad_gain, wgu, wout, sems = refs
        fetch_wide(ids, pieces, spots, wgu, sems)
        copies([(wvo_in.at[1], wout)], sems.at[4])
    else:
        wgu, wvo, dx1_out, dattended, grad_gain = refs
        wout = wvo.at[1]
    ids[4]()
    dn2 = jnp.zeros((ROWS, D), F32)
    for half in range(2):
        for c in range(2):
            if direct:
                landed(wgu.at[c, half], sems.at[half * 2 + c])
            dn2 = dn2 + dot_nt(dgu[c, half], wgu[c, half])
    back, dgain2 = norm_backward(first[...], gains[1:2, :], dn2)
    dx1 = dx2[...] + back
    dx1_out[...] = dx1
    grad_gain[...] = dgain2
    if direct:
        landed(wout, sems.at[4])
    dattended[...] = dot_nt(dx1.astype(BF), wout[...]).astype(BF)


def attention_backward_kernel(
    direct,
    ids,
    grad_first,
    dattended,
    x,
    n1,
    attended,
    weights,
    qkv,
    gains,
    bucket,
    grad_proj,
    grad_gain2,
    grad_gain3,
    *refs,
):
    if direct:
        wqk_in, wvo_in, grad_in, *outs = refs[:7]
        wqk, wvo, own, other, left, right, dqk, extra, *refs = refs[7:]
        copies([(wvo_in.at[0], wvo.at[0])], refs[-1].at[0])
        copies([(wqk_in, wqk)], refs[-1].at[1])
    else:
        wqk, wvo, small, grad_in, dqkv_out, da_out, left, right, dqk, *refs = refs
    diag, bias_grad, dshares, scaled, queries, douts, *rest = refs
    b, core = ids[0], ids[2]
    ids[4]()
    dx1 = grad_first[...]
    da = dx1.astype(BF)
    low_lane = head_masks()
    row_at = lax.broadcasted_iota(jnp.int32, (DLEN, MICRO * DLEN), 0)
    lane_at = lax.broadcasted_iota(jnp.int32, (DLEN, MICRO * DLEN), 1)
    mirror = jnp.where(row_at == DLEN - 1 - lane_at % DLEN, 1.0, 0.0).astype(BF)
    diag[...] = jnp.zeros_like(diag)
    for i, (m, p, rows, lanes) in enumerate(PAIRS_OF_HEADS):
        queries[i] = both_heads(qkv[0, rows, lanes], low_lane)
        douts[i] = both_heads(dattended[rows, lanes], low_lane)
    for i, (m, p, rows, lanes) in enumerate(PAIRS_OF_HEADS):
        dshares[i] = dot_nt(douts[i], qkv[2, rows, lanes])
        right[0, rows, lanes] = dot_tn(weights[m, p], douts[i]).astype(BF)
    for i, (m, p, rows, lanes) in enumerate(PAIRS_OF_HEADS):
        wide = weights[m, p].astype(F32)
        dshare = dshares[i]
        centre = jnp.sum(wide * dshare, axis=-1, keepdims=True)
        scaled[i] = (wide * (dshare - centre)).astype(BF)
    for i, (m, p, rows, lanes) in enumerate(PAIRS_OF_HEADS):
        dq = dot(scaled[i], qkv[1, rows, lanes])
        dqk[0, rows, lanes] = jnp.where(low_lane, dq[:DLEN], dq[DLEN:]).astype(BF)
        dqk[1, rows, lanes] = dot_tn(scaled[i], queries[i]).astype(BF)
    for h in range(H):
        part = slice((h % 2) * DLEN, (h % 2 + 1) * DLEN)
        both = jnp.concatenate([scaled[m * (H // 2) + h // 2, part] for m in range(MICRO)], axis=0)
        turned = dot(mirror, both)
        wider = jnp.concatenate([turned, jnp.zeros_like(turned)], axis=1)
        rolled = pltpu.roll(wider, 0, 1, stride=1, stride_axis=0)
        diag[h : h + 1, :] = jnp.sum(rolled, axis=0, keepdims=True)
    bias_grad[...] = lax.dot_general(
        bucket[...],
        diag[...],
        (((1,), (1,)), ((), ())),
        precision=HIGHEST,
        preferred_element_type=F32,
    )
    if direct:
        sems = rest[0]
        landed(wvo.at[0], sems.at[0])
        landed(wqk, sems.at[1])
    dn1 = dot_nt(dqk[0], wqk[0]) + dot_nt(dqk[1], wqk[1]) + dot_nt(right[0], wvo[0])
    dx, dgain1 = norm_backward(x[...].astype(F32), gains[0:1, :], dn1)
    grad_in[...] = dx1 + dx
    right[1] = da
    left[0] = n1[...]
    left[1] = attended[...]
    all_gains = jnp.concatenate(
        [dgain1, grad_gain2[...], grad_gain3[...], jnp.zeros((5, D), F32)], axis=0
    )
    if not direct:
        small[0:8, :] = all_gains
        small[8:40, :] = jnp.concatenate(
            [bias_grad[...], jnp.zeros((BUCKETS, D - DLEN), F32)], axis=1
        )
        dqkv_out[0] = dqk[0]
        dqkv_out[1] = dqk[1]
        dqkv_out[2] = right[0]
        da_out[...] = da
        return
    per_shard = BUCKETS // SHARDS
    for j in range(SHARDS):
        for k in range(6):
            extra[0, j, :, k * DLEN : (k + 1) * DLEN] = grad_proj[
                j * 96 + k * 16 : j * 96 + (k + 1) * 16, :
            ]
        extra[1, j] = jnp.zeros((16, D), F32)
        extra[1, j, 0:8, :] = pltpu.roll(all_gains, (D - j * 96) % D, 1)
        extra[1, j, 8 : 8 + per_shard, 0:DLEN] = bias_grad[j * per_shard : (j + 1) * per_shard, :]
    for flip, out in ((1, other), (0, own)):
        c = core ^ flip
        top = dot_tn(n1[...], dqk[c]).astype(BF)
        bottom = dot_tn(left[c], right[c]).astype(BF)
        for j in range(SHARDS):
            m = b ^ j
            out[m, 0:96, :] = top[j * 96 : (j + 1) * 96, :]
            out[m, 96:192, :] = bottom[j * 96 : (j + 1) * 96, :]
            out[m, 192:208, :] = extra[c, j].astype(BF)
        for group, target in zip((FIRST_A, REST_A), outs[2 * flip : 2 * flip + 2]):
            copies([(out.at[m], target.at[i]) for i, m in enumerate(group)], sems.at[flip])
    landed(other, sems.at[1])
    landed(own, sems.at[0])


def finish_wide_kernel(ids, near, far, twin, far_twin, token, grad_g, grad_u, grad_d):
    y, core = ids[1], ids[2]
    for yy in range(2):
        for c in range(2):

            @pl.when((y == yy) & (core == c))
            def _():
                for yflip, cflip, part in ((0, 0, near), (1, 0, far), (0, 1, twin), (1, 1, far_twin)):
                    half, rank = yy ^ yflip, c ^ cflip
                    out = grad_u if rank else grad_g
                    for k in range(4):
                        start = half * HALF + k * 256
                        out[:, start : start + 256] = part[0, k * 96 : (k + 1) * 96, :].astype(F32)
                    low = (2 * half + rank) * 64
                    for k in range(3):
                        grad_d[low : low + 64, k * 256 : (k + 1) * 256] = part[
                            0, 384 + k * 64 : 384 + (k + 1) * 64, :
                        ].astype(F32)


def finish_narrow_kernel(
    ids, near, twin, grad_q, grad_k, grad_v, grad_o, grad_p, grad_1, grad_2, grad_3, table
):
    core = ids[2]
    for c in range(2):

        @pl.when(core == c)
        def _():
            low, high = (twin, near) if c else (near, twin)
            grad_q[...] = low[0, 0:96, :].astype(F32)
            grad_k[...] = high[0, 0:96, :].astype(F32)
            grad_v[...] = low[0, 96:192, :].astype(F32)
            grad_o[...] = high[0, 96:192, :].astype(F32)
            for k in range(6):
                grad_p[k * 16 : (k + 1) * 16, :] = low[
                    0, 192:208, k * DLEN : (k + 1) * DLEN
                ].astype(F32)
            rows = high[0, 192:208, :].astype(F32)
            grad_1[...] = rows[0:1, :96]
            grad_2[...] = rows[1:2, :96]
            grad_3[...] = rows[2:3, :96]
            block = jnp.where(lax.broadcasted_iota(jnp.int32, (8, DLEN), 1) < H, rows[8:16, :DLEN], 0.0)
            line = block[0:1]
            for i in range(1, BUCKETS // SHARDS):
                line += pltpu.roll(block, i * H, 1)[i : i + 1]
            table[...] = line[:, : BUCKETS // SHARDS * H]


def local(
    hidden_in,
    norm1_gain,
    w_query,
    w_key,
    w_value,
    w_out,
    rel_table,
    norm2_gain,
    w_gate,
    w_up,
    w_down,
    norm3_gain,
    w_proj,
    query_lengths,
    keyword_request_mask,
    targets,
    candidates,
):
    streams = lax.axis_size("stream")
    shards = lax.axis_size("batch")
    pairs = streams // 2
    direct = shards == SHARDS and pairs == 2
    b = lax.axis_index("batch")
    s = lax.axis_index("stream")
    y, core = s // pairs, s % pairs
    is_query = s < pairs

    def swap(block, yflip, cflip, m):
        route = []
        for source in range(streams):
            target = ((source // pairs) ^ yflip) * pairs + ((source % pairs) ^ cflip)
            for j in range(shards):
                route.append((source * shards + j, target * shards + (j ^ m)))
        return lax.ppermute(block, EVERY, route)

    micro_count = hidden_in.shape[0]
    slot = jnp.arange(DLEN)
    pair_lengths = lax.dynamic_index_in_dim(query_lengths, core, 1, keepdims=False)
    pair_keyword = lax.dynamic_index_in_dim(keyword_request_mask, core, 1, keepdims=False)
    pair_targets = lax.dynamic_index_in_dim(targets, core, 1, keepdims=False)

    def by_slot(values):
        blocks = values.reshape(micro_count, shards, GROUPS)
        own = lax.dynamic_slice_in_dim(blocks, b, 1, 1)
        blocks = jnp.where(is_query, jnp.broadcast_to(own, blocks.shape), blocks)
        return jnp.repeat(blocks, QLEN, axis=2)

    length_slots = by_slot(pair_lengths)
    valid_slots = (slot % QLEN)[None, None, :] < length_slots
    share = jnp.where(valid_slots, 1.0 / length_slots.astype(F32), 0.0)
    sharp = jnp.where(by_slot(pair_keyword) == 1, 20.0, 10.0).astype(F32)
    target_slots = by_slot(pair_targets)
    own_valid = lax.dynamic_slice_in_dim(valid_slots, b, 1, 1)
    same = (slot[:, None] // QLEN) == (slot[None, :] // QLEN)
    mask = jnp.where(is_query & ~(same[None] & own_valid), -1000000000.0, 0.0).astype(F32)

    small = 16 if direct else 48
    picked = lax.dynamic_index_in_dim(candidates, core, 1, keepdims=False)[:, 0]
    picked = picked.reshape(micro_count, shards, DLEN, picked.shape[-1])
    picked = jnp.transpose(picked, (0, 1, 3, 2))
    received = lax.all_to_all(picked, "batch", split_axis=1, concat_axis=1, tiled=True)
    picks = jnp.where(is_query, received, picked)
    (counts,) = call(
        count_kernel,
        "count",
        [picks],
        [((micro_count, shards, DLEN, DLEN), F32)],
        limit=small,
    )

    fence = lax.optimization_barrier
    first_core = core == 0
    spots_a = spots_f = None
    if direct:
        lines = [part.reshape(1, -1) for part in (norm1_gain, norm2_gain, norm3_gain, rel_table)]
        slab_a, slab_f = call(
            pack_kernel,
            "pack",
            [w_query, w_key, w_value, w_out, w_gate, w_up, w_down, w_proj, *lines],
            [((PIECE_A, D), BF), ((PIECE_F, 256), BF)],
        )

        def join(*parts):
            return jnp.concatenate(parts)

        def along_x(part):
            return swap(part, 0, 0, 1)

        def along_y(part):
            return swap(part, 1, 0, 0)

        def along_z(part):
            return swap(part, 0, 0, 2)

        def along_zz(part):
            return swap(part, 0, 0, 4)

        def other_core(part):
            return swap(part, 0, 1, 0)

        f0, a0 = slab_f[None], slab_a[None]
        token = jnp.zeros((8, DLEN), F32)
        f4, f2, y0, f1, a1 = along_zz(f0), along_z(f0), along_y(f0), along_x(f0), along_x(a0)
        token = tick(token)
        f4, f2, y0, f1, a1, a0, token = fence((f4, f2, y0, f1, a1, a0, token))
        f42, f142, token = fence((join(f4, f2), join(f1, f4, f2), token))
        y142, f53, f6, a4, a2 = (
            along_y(f142),
            along_x(f42),
            along_z(f4),
            along_zz(a0),
            along_z(a0),
        )
        token = tick(token)
        f53, f6, counts, mask, share, sharp, target_slots, token = fence(
            (f53, f6, counts, mask, share, sharp, target_slots, token)
        )
        f65, token = fence((join(f6, f53[0:1]), token))
        f7 = along_x(f6)

        a2, token = fence((a2, token))
        a3 = along_x(a2)
        a4, token = fence((a4, token))
        a5, a6 = along_x(a4), along_z(a4)

        y142, f65, token = fence((y142, f65, token))
        y65 = along_y(f65)

        f7, token = fence((f7, token))
        f37, f_all, token = fence((join(f53[1:2], f7), join(f0, f142, f65, f53[1:2], f7), token))
        f_all, token = fence((f_all, token))
        tf_all = other_core(f_all)

        a6, token = fence((a6, token))
        a7 = along_x(a6)
        a0142, token = fence((join(a0, a1, a4, a2), token))
        ta0142 = other_core(a0142)
        y65, f37, token = fence((y65, f37, token))
        y37, ty65 = along_y(f37), other_core(y65)
        token = tick(token)
        a3, a5, tf_all, ta0142, token = fence((a3, a5, tf_all, ta0142, token))
        a536, y_first, token = fence((join(a5, a3, a6), join(y0, y142), token))
        ta536, ty_first = other_core(a536), other_core(y_first)
        a7, token = fence((a7, token))
        ta7 = other_core(a7)
        token = tick(token)
        y37, ta536, ta7, token = fence((y37, ta536, ta7, token))
        ty37 = other_core(y37)

        order_f = (0, 1, 4, 2, 6, 5, 3, 7)
        groups_a = [
            (0, (a0142, (0, 1, 4, 2)), (a536, (5, 3, 6)), (a7, (7,))),
            (1, (ta0142, (0, 1, 4, 2)), (ta536, (5, 3, 6)), (ta7, (7,))),
        ]
        pieces_a, spots_a, pieces_f, spots_f = [], [], [], []
        for cflip, *group in groups_a:
            for part, flips in group:
                spots_a += [(cflip, m, len(pieces_a), i) for i, m in enumerate(flips)]
                pieces_a.append(part)
    else:

        def whole(part):
            return lax.all_gather(part, "batch", axis=0, tiled=True)

        wqk = jnp.stack([whole(w_query), whole(w_key)])
        wvo = jnp.stack([whole(w_value), whole(w_out)])
        gate_up = jnp.stack([whole(w_gate), whole(w_up)])
        wgu = jnp.transpose(gate_up.reshape(2, D, 2, HALF), (0, 2, 1, 3))
        wd = whole(w_down)
        wproj = whole(w_proj)
        gain_rows = [whole(gain) for gain in (norm1_gain, norm2_gain, norm3_gain)]
        gains = jnp.pad(jnp.stack(gain_rows).astype(F32), ((0, 5), (0, 0)))
        table = whole(rel_table).reshape(1, BUCKETS * H)

    onehot = bucket_onehot()
    by_entry = jnp.asarray(np.repeat(onehot.T, H, axis=0), BF)
    x = hidden_in[:, 0].reshape(ROWS, D)
    row_bf, row_f32 = ((ROWS, D), BF), ((ROWS, D), F32)
    qkv_shape, weight_shape = ((3, ROWS, D), BF), ((MICRO, H // 2, ROWS, DLEN), BF)
    pair_weights = ((2, D, D), BF)
    gain_rows = ((8, D), F32)
    proj_shape = ((D, DLEN), BF)
    kept = [qkv_shape, row_bf, weight_shape, row_f32, row_bf, row_bf]
    bias_shape, score_shape = ((H // 2, ROWS, DLEN), F32), ((H, ROWS, DLEN), F32)
    result = call(
        functools.partial(attention_forward_kernel, direct, spots_a),
        "attention_forward",
        [x, mask, by_entry] + ([] if direct else [gains, table, wqk, wvo]),
        kept + ([gain_rows, proj_shape] if direct else []),
        ([pair_weights, pair_weights, ((2, SHARDS, 16, D), BF)] if direct else [])
        + [bias_shape, score_shape],
        far=pieces_a if direct else [],
        far_outs=[pair_weights, pair_weights] if direct else [],
        sems=3 if direct else 0,
        flops=2 * ROWS * D * D * 4,
        lazy=True,
    )
    qkv, attended, weights, first, n1, n2 = result[:6]
    if direct:
        gains, wproj, wqk, wvo = result[6:]
    first, counts, share, sharp, target_slots = fence((first, counts, share, sharp, target_slots))
    if direct:
        ty_first, ty65, ty37, first, token = fence((ty_first, ty65, ty37, first, token))
        near, twin = ((f_all, order_f),), ((tf_all, order_f),)
        far = ((y_first, order_f[:4]), (y65, order_f[4:6]), (y37, order_f[6:]))
        far_twin = ((ty_first, order_f[:4]), (ty65, order_f[4:6]), (ty37, order_f[6:]))
        for yflip, cflip, group in ((0, 0, near), (0, 1, twin), (1, 0, far), (1, 1, far_twin)):
            for part, flips in group:
                spots_f += [(yflip, cflip, m, len(pieces_f), i) for i, m in enumerate(flips)]
                pieces_f.append(part)
    wide_bf = ((2, ROWS, HALF), BF)
    wgu_shape, wd_shape = ((2, 2, D, HALF), BF), ((FF, D), BF)
    lasting = [wide_bf, wide_bf, wide_bf]
    result = call(
        functools.partial(ffn_forward_kernel, direct, spots_f),
        "ffn_forward",
        [first, n2, gains, wproj] + ([] if direct else [wgu, wd]),
        [row_f32, row_bf, ((ROWS, DLEN), BF)] + ([] if direct else lasting),
        [wgu_shape, wd_shape] + lasting if direct else [],
        far=[*pieces_f, token] if direct else [],
        far_outs=lasting if direct else [],
        sems=5 if direct else 0,
        flops=2 * ROWS * D * FF * 3,
        lazy=True,
    )
    second, n3, vectors, gelu_kept, slope_kept, hidden = result

    if direct:
        even = jnp.stack([swap(vectors, 1, 0, m) for m in (0, 2, 4, 6)])
        others = [even, swap(even, 0, 0, 1)]
    else:
        route = [(i, (i + pairs) % streams) for i in range(streams)]
        arrived = lax.ppermute(vectors, "stream", route)
        others = [lax.all_gather(arrived, "batch", axis=0)]
    block_f32 = ((micro_count, shards, DLEN, DLEN), F32)
    line_f32 = ((micro_count, shards, DLEN), F32)
    soft, score = call(
        functools.partial(similarity_kernel, direct, shards),
        "similarity",
        [vectors, counts, share, *others],
        [block_f32, line_f32],
        [line_f32],
        limit=small,
        near=True,
    )
    if direct:
        blocks = jnp.broadcast_to(score[None], (shards,) + score.shape)
        scores = lax.all_to_all(blocks, "batch", split_axis=0, concat_axis=0, tiled=True)
    else:
        scores = lax.all_gather(score, "batch", axis=0)
    (dvec,) = call(
        functools.partial(vector_grad_kernel, direct, shards),
        "vector_grad",
        [soft, share, sharp, target_slots, score, scores, *others],
        [((ROWS, DLEN), BF)],
        [line_f32, ((ROWS, DLEN), F32)],
        limit=small,
        near=True,
    )

    gain_row = ((1, D), F32)
    proj_f32 = ((D, DLEN), F32)
    dgu_shape = ((2, 2, ROWS, HALF), BF)
    quarter = ((SHARDS, PIECE_F, 256), BF)
    saved = [hidden, gelu_kept, slope_kept]
    result = call(
        functools.partial(ffn_backward_kernel, direct, spots_f),
        "ffn_backward",
        [dvec, second, n2, n3, gains, wproj] + ([] if direct else [wd, *saved]),
        [row_f32, proj_f32, gain_row, dgu_shape] + ([] if direct else [row_bf]),
        [wd_shape, wide_bf, wide_bf, wide_bf, ((SHARDS, 4, 64, D), BF), ((4, *quarter[0]), BF)]
        if direct
        else [],
        far=[*saved, *pieces_f] if direct else [],
        far_outs=[quarter] * 2 + [((4, PIECE_F, 256), BF)] * 4 if direct else [],
        sems=4 if direct else 0,
        flops=2 * ROWS * D * FF * 4,
        lazy=True,
    )
    dx2, grad_proj, grad_gain, dgu = result[:4]
    if direct:
        f_own, f_twin, *f_far = result[4:]
    else:
        dy = result[4]

    if direct:
        def own_f(m, *more):
            return [(base_f, m), *more]

        def far_sum(i):
            return [[(f_far[i], n), (c_far[i], n)] for n in range(4)]

        c_far = [other_core(part) for part in f_far[2:]]
        c_far[0], f_twin, dgu = fence((c_far[0], f_twin, dgu))
        twin = other_core(f_twin)
        (sent_a,) = add_up(far_sum(0))
        sent_a, dgu = fence((sent_a, dgu))
        y_a = along_y(sent_a)
    middle_in = [dx2, first, dgu, gains]
    dx1, dattended, grad_gain2 = call(
        functools.partial(middle_backward_kernel, direct, spots_f),
        "middle_backward",
        middle_in + ([] if direct else [wgu, wvo]),
        [row_f32, row_bf, gain_row],
        [wgu_shape, ((D, D), BF)] if direct else [],
        far=[*pieces_f, wvo] if direct else [],
        sems=5 if direct else 0,
        flops=ROUND_FLOPS,
        lazy=True,
    )
    if direct:
        *c_far[1:], twin, dattended = fence((*c_far[1:], twin, dattended))
        (sent_b,) = add_up(far_sum(1))
        base_f = base_up(f_own, twin, range(SHARDS))
        sent_b, base_f, dattended = fence((sent_b, base_f, dattended))
    two_rows = ((2, ROWS, D), BF)
    slab_out = ((SHARDS, PIECE_A, D), BF)
    blocks_bf = ((H, ROWS, DLEN), BF)
    result = call(
        functools.partial(attention_backward_kernel, direct),
        "attention_backward",
        [dx1, dattended, x, n1, attended, weights, qkv, gains, jnp.asarray(onehot.T)]
        + [grad_proj, grad_gain2, grad_gain]
        + ([] if direct else [wqk, wvo]),
        [row_f32] if direct else [((40, D), F32), row_f32, qkv_shape, row_bf],
        ([pair_weights, pair_weights, slab_out, slab_out] if direct else [])
        + [two_rows, two_rows, two_rows]
        + ([((2, SHARDS, 16, D), F32)] if direct else [])
        + [((DLEN, 2 * DLEN), F32), ((BUCKETS, DLEN), F32)]
        + [score_shape, blocks_bf, blocks_bf, blocks_bf],
        far=[wqk, wvo] if direct else [],
        far_outs=[((count, PIECE_A, D), BF) for count in (2, 6, 2, 6)] if direct else [],
        sems=2 if direct else 0,
        flops=2 * ROWS * D * D * 7,
        lazy=True,
    )

    if direct:
        input_grad, o_first, o_rest, a_first, a_rest = result

        def own_a(m, *more):
            return [(base_a, REST_A.index(m)), *more]

        o_first, o_rest, a_first, a_rest = fence((o_first, o_rest, a_first, a_rest))
        token = jnp.ones((8, DLEN), F32)
        c_first = other_core(a_first)
        c_first, a_rest, token = fence((c_first, a_rest, token))
        (out_a37,) = add_up([[(o_first, i), (c_first, i)] for i in range(2)])
        out_a37, a_rest, token = fence((out_a37, a_rest, token))
        xa37, c_rest = along_x(out_a37), other_core(a_rest)

        y_a, sent_b, token = fence((y_a, sent_b, token))
        y_b = along_y(sent_b)
        (out_73,) = add_up([own_f(7, (y_a, 1)), own_f(3, (y_a, 3))])
        out_73, token = fence((out_73, token))
        x73 = along_x(out_73)
        token = tick(token)
        c_rest, token = fence((c_rest, token))
        base_a = base_up(o_rest, c_rest, range(len(REST_A)))
        x73, base_a, token = fence((x73, base_a, token))
        (out_62,) = add_up([own_f(6, (y_a, 0), (x73, 0)), own_f(2, (y_a, 2), (x73, 1))])
        out_62, token = fence((out_62, token))
        z62 = along_z(out_62)

        xa37, token = fence((xa37, token))
        out_a51, out_a62 = add_up(
            [own_a(5), own_a(1)], [own_a(6, (xa37, 1)), own_a(2, (xa37, 0))]
        )
        out_a62, token = fence((out_a62, token))
        za62 = along_z(out_a62)

        y_b, token = fence((y_b, token))
        out_5, out_1 = add_up([own_f(5, (y_b, 1))], [own_f(1, (y_b, 3))])
        out_5, token = fence((out_5, token))
        x5 = along_x(out_5)

        x5, z62, token = fence((x5, z62, token))
        (out_4,) = add_up([own_f(4, (y_b, 0), (x5, 0), (z62, 0))])
        out_4, out_a51, out_1, token = fence((out_4, out_a51, out_1, token))
        x1, xa51, z4 = along_x(out_1), along_x(out_a51), along_zz(out_4)

        za62, xa51, token = fence((za62, xa51, token))
        (out_a4,) = add_up([own_a(4, (xa51, 0), (za62, 0))])
        out_a4, token = fence((out_a4, token))
        za4 = along_zz(out_a4)

        x1, z4, token = fence((x1, z4, token))
        (mine_f,) = add_up([own_f(0, (y_b, 2), (x1, 0), (z62, 1), (z4, 0))])
        mine_f, token = fence((mine_f, token))
        far, twin_f = along_y(mine_f), other_core(mine_f)

        za4, token = fence((za4, token))
        (part_a,) = add_up([own_a(0, (xa51, 1), (za62, 1), (za4, 0))])
        part_a, token = fence((part_a, token))
        ya = along_y(part_a)

        far, twin_f, token = fence((far, twin_f, token))
        far_twin_f = other_core(far)
        ya, token = fence((ya, token))
        (mine_a,) = add_up([[(part_a, 0), (ya, 0)]])
        mine_a, far_twin_f, token = fence((mine_a, far_twin_f, token))
        twin_a = other_core(mine_a)
        shard_f32, wide_f32 = ((96, D), F32), ((96, FF), F32)
        grad_g, grad_u, grad_d = call(
            finish_wide_kernel,
            "finish_wide",
            [mine_f, far, twin_f, far_twin_f],
            [wide_f32, wide_f32, ((256, D), F32)],
            far=[token],
            limit=24,
            near=True,
        )
        grad_q, grad_k, grad_v, grad_o, grad_p, *small = call(
            finish_narrow_kernel,
            "finish_narrow",
            [mine_a, twin_a],
            [shard_f32] * 4 + [((96, DLEN), F32), ((1, 96), F32), ((1, 96), F32), ((1, 96), F32)]
            + [((1, 48), F32)],
            limit=24,
            near=True,
        )
        grad_n1, grad_n2, grad_n3, grad_table = [row.reshape(-1) for row in small]
    else:
        small, input_grad, dqkv, da = result

        def summed(part):
            part = lax.psum_scatter(part, "batch", scatter_dimension=0, tiled=True)
            return lax.psum(part, "stream")

        grad_q, grad_k, grad_v = [summed(dot_tn(n1, dqkv[i])) for i in range(3)]
        grad_o = summed(dot_tn(attended, da))
        grad_g, grad_u = [
            summed(jnp.concatenate([dot_tn(n2, dgu[i, half]) for half in range(2)], axis=1))
            for i in range(2)
        ]
        grad_d = summed(jnp.concatenate([dot_tn(hidden[half], dy) for half in range(2)]))
        grad_p = summed(grad_proj)
        grad_n1, grad_n2, grad_n3 = [summed(small[i]) for i in range(3)]
        flat = lax.psum(small[8 : 8 + BUCKETS, :H].reshape(-1), EVERY)
        share_rows = flat.shape[0] // shards
        grad_table = lax.dynamic_slice_in_dim(flat, b * share_rows, share_rows, 0)

    vectors_out = vectors.reshape(micro_count, DLEN, DLEN)[:, None]
    grad_hidden = input_grad.reshape(micro_count, DLEN, D)[:, None]
    return (
        vectors_out,
        grad_hidden,
        grad_n1,
        grad_q,
        grad_k,
        grad_v,
        grad_o,
        grad_table,
        grad_n2,
        grad_g,
        grad_u,
        grad_d,
        grad_n3,
        grad_p,
    )


def solution(mesh):
    rows, lines = P("batch", None), P("batch")
    spread = P(None, "stream", "batch", None)
    return jax.shard_map(
        local,
        mesh=mesh,
        in_specs=(spread, lines, rows, rows, rows, rows, lines, lines, rows, rows, rows, lines, rows)
        + (P(), P(), P(), P(None, None, "batch", None, None)),
        out_specs=(spread, spread, lines, rows, rows, rows, rows, lines, lines)
        + (rows, rows, rows, lines, rows),
        check_vma=False,
    )
```

```python
import functools
import math

import jax
import jax.numpy as jnp
import numpy as np
from jax import lax
from jax.experimental import pallas as pl
from jax.experimental.pallas import tpu as pltpu
from jax.sharding import PartitionSpec as P

H = 12
DH = 64
BUCKETS = 32
MAX_DIST = 128
DLEN = 128
QLEN = 32
GROUPS = DLEN // QLEN
MICRO = 2
ROWS = MICRO * DLEN
D = 768
FF = 2048
HALF = FF // 2
SHARDS = 8
PIECE_A = 208
PIECE_F = 576
FIRST_A, REST_A = (3, 7), (6, 2, 5, 1, 4, 0)
GROUPS_F = ((6, 7, 2, 3), (4, 5, 0, 1))

EPSILON = 1e-06
HIGHEST = lax.Precision.HIGHEST
BF = jnp.bfloat16
F32 = jnp.float32
EVERY = ("stream", "batch")
MIB = 2**20
ROUND_FLOPS = 5 * 10**10


def distance_bucket(distance):
    half_count = BUCKETS // 2
    exact_count = half_count // 2
    if distance < exact_count:
        return distance
    grown = exact_count + int(
        math.floor(
            math.log(distance / exact_count)
            / math.log(MAX_DIST / exact_count)
            * (half_count - exact_count)
            + 1e-09
        )
    )
    return min(grown, half_count - 1)


def bucket_onehot():
    table = np.zeros((2 * DLEN, BUCKETS), np.float32)
    for o in range(2 * DLEN - 1):
        offset = o - (DLEN - 1)
        table[o, distance_bucket(abs(offset)) + (BUCKETS // 2 if offset > 0 else 0)] = 1.0
    return table


def norm_scale(values):
    return lax.rsqrt(jnp.mean(values * values, axis=-1, keepdims=True) + EPSILON)


def norm_backward(values, gain, grad):
    scale = norm_scale(values)
    pulled = gain * grad
    inner = jnp.mean(values * pulled, axis=-1, keepdims=True)
    back = scale * pulled - values * (scale * scale * scale * inner)
    return back, jnp.sum(grad * values * scale, axis=0, keepdims=True)


def dot(left, right):
    return jnp.dot(left, right, preferred_element_type=F32)


def dot_nt(left, right):
    return lax.dot_general(left, right, (((1,), (1,)), ((), ())), preferred_element_type=F32)


def dot_tn(left, right):
    return lax.dot_general(left, right, (((0,), (0,)), ((), ())), preferred_element_type=F32)


def steps(count, body):
    if count <= 16:
        for i in range(count):
            body(i)
    else:

        @pl.loop(0, count)
        def _(i):
            body(i)


VMEM = pl.BlockSpec(memory_space=pltpu.VMEM)
SMEM = pl.BlockSpec(memory_space=pltpu.SMEM)
HBM = pl.BlockSpec(memory_space=pltpu.HBM)


def positions():
    pairs = lax.axis_size("stream") // 2
    stream = lax.axis_index("stream")
    return lax.axis_index("batch"), stream // pairs, stream % pairs, jnp.where(stream < pairs, 1, 0)


def body_kernel(kernel, lazy, counts, *refs):
    parts = []
    for count in counts:
        parts.append(refs[:count])
        refs = refs[count:]
    arrays, far, outs, far_outs, held, made, scratch = parts
    in_sems, out_sems = refs
    for i, (array, place) in enumerate(zip(arrays, held)):
        pltpu.make_async_copy(array, place, in_sems.at[i]).start()
    sent = set()

    def ready():
        for i, (array, place) in enumerate(zip(arrays, held)):
            pltpu.make_async_copy(array, place, in_sems.at[i]).wait()

    def send(*results):
        for i in results:
            sent.add(i)
            pltpu.make_async_copy(made[i], outs[i], out_sems.at[i]).start()

    if not lazy:
        ready()
    kernel((*positions(), ready, send), *held, *far, *made, *far_outs, *scratch)
    send(*(i for i in range(len(outs)) if i not in sent))
    for i, (place, out) in enumerate(zip(made, outs)):
        pltpu.make_async_copy(place, out, out_sems.at[i]).wait()


def near_kernel(kernel, *refs):
    kernel(positions(), *refs)


def call(
    kernel,
    name,
    arrays,
    outs,
    scratch=(),
    far=(),
    far_outs=(),
    sems=0,
    flops=0,
    limit=59,
    near=False,
    lazy=False,
):
    shapes = [jax.ShapeDtypeStruct(s, t) for s, t in (*outs, *far_outs)]
    moved = sum(math.prod(s.shape) * s.dtype.itemsize for s in shapes)
    moved += sum(math.prod(a.shape) * a.dtype.itemsize for a in (*arrays, *far))
    spaces = [pltpu.VMEM(s, t) for s, t in scratch]
    if sems:
        spaces.append(pltpu.SemaphoreType.DMA((sems,)))
    kind = VMEM if near else HBM
    if near:
        body = functools.partial(near_kernel, kernel)
    else:
        counts = (len(arrays), len(far), len(outs), len(far_outs))
        counts += (len(arrays), len(outs), len(spaces))
        body = functools.partial(body_kernel, kernel, lazy, counts)
        spaces = (
            [pltpu.VMEM(a.shape, a.dtype) for a in arrays]
            + [pltpu.VMEM(s, t) for s, t in outs]
            + spaces
            + [pltpu.SemaphoreType.DMA((max(1, len(part)),)) for part in (arrays, outs)]
        )
    return pl.pallas_call(
        body,
        name=name,
        out_shape=shapes,
        in_specs=[kind] * len(arrays) + [HBM] * len(far),
        out_specs=[kind] * len(outs) + [HBM] * len(far_outs),
        scratch_shapes=spaces,
        compiler_params=pltpu.CompilerParams(vmem_limit_bytes=limit * MIB),
        cost_estimate=pl.CostEstimate(flops=flops, bytes_accessed=moved, transcendentals=0),
    )(*arrays, *far)


def tick_kernel(token, out):
    pass


def tick(token):
    return pl.pallas_call(
        tick_kernel,
        name="tick",
        in_specs=[HBM],
        out_specs=HBM,
        out_shape=jax.ShapeDtypeStruct(token.shape, token.dtype),
        input_output_aliases={0: 0},
        cost_estimate=pl.CostEstimate(flops=ROUND_FLOPS, bytes_accessed=0, transcendentals=0),
    )(token)


def add_kernel(plan, near, far, ids, *refs):
    near, far, refs = refs[:near], refs[near : near + far], refs[near + far :]
    outs, refs = refs[: len(plan)], refs[len(plan) :]
    held, sems = (refs[:-1], refs[-1]) if far else ((), None)
    place = 0
    for entries in plan:
        for terms in entries:
            for is_far, array, entry in terms:
                if is_far:
                    copies([(far[array].at[entry], held[place])], sems.at[place])
                    place += 1
    place = 0
    for out, entries in zip(outs, plan):
        for i, terms in enumerate(entries):
            total = None
            for is_far, array, entry in terms:
                if is_far:
                    landed(held[place], sems.at[place])
                    part = held[place][...].astype(F32)
                    place += 1
                else:
                    part = near[array][entry].astype(F32)
                total = part if total is None else total + part
            out[i] = total.astype(BF)


def base_kernel(picks, whole, ids, own, rest, out, left, right, sems):
    for i, m in enumerate(picks):
        part = rest.at[m if whole else i]
        copies([(own.at[m], left.at[i]), (part, right.at[i])], sems.at[i])
    for i in range(len(picks)):
        landed(left.at[i], sems.at[i])
        landed(right.at[i], sems.at[i])
        left[i] = (left[i].astype(F32) + right[i].astype(F32)).astype(BF)
        copies([(left.at[i], out.at[i])], sems.at[i])
    for i in range(len(picks)):
        landed(left.at[i], sems.at[i])


def base_up(own, rest, picks):
    picks = tuple(picks)
    shape = ((len(picks), *rest.shape[1:]), BF)
    (base,) = call(
        functools.partial(base_kernel, picks, rest.shape[0] > len(picks)),
        "base_up",
        [],
        [],
        [shape, shape],
        far=[own, rest],
        far_outs=[shape],
        sems=len(picks),
    )
    return base


def add_up(*outputs, limit=24):
    known = ([], [])
    plan, flat, shapes = [], [], []
    for entries in outputs:
        plan.append([])
        for terms in entries:
            plan[-1].append([])
            for array, entry in terms:
                is_far = int(array.shape[0] > 4)
                arrays = known[is_far]
                found = [i for i, other in enumerate(arrays) if other is array]
                if not found:
                    arrays.append(array)
                    found = [len(arrays) - 1]
                if is_far:
                    flat.append((array.shape[1:], BF))
                plan[-1][-1].append((is_far, found[0], entry))
        shapes.append(((len(entries), *entries[0][0][0].shape[1:]), BF))
    return call(
        functools.partial(add_kernel, plan, len(known[0]), len(known[1])),
        "add_up",
        known[0],
        shapes,
        flat,
        far=known[1],
        sems=len(flat),
        limit=limit,
        near=True,
    )


def pack_kernel(ids, wq, wk, wv, wo, wg, wu, wd, wp, g1, g2, g3, table, slab_a, slab_f):
    y, core = ids[1], ids[2]

    def fill(top, bottom, wide, rank):
        slab_a[0:96, :] = top[...]
        slab_a[96:192, :] = bottom[...]
        for yy in range(2):

            @pl.when(y == yy)
            def _():
                for k in range(4):
                    start = yy * HALF + k * 256
                    slab_f[k * 96 : (k + 1) * 96, :] = wide[:, start : start + 256]
                row = (2 * yy + rank) * 64
                for k in range(3):
                    slab_f[384 + k * 64 : 384 + (k + 1) * 64, :] = wd[
                        row : row + 64, k * 256 : (k + 1) * 256
                    ]

    @pl.when(core == 0)
    def _():
        fill(wq, wv, wg, 0)
        for k in range(6):
            slab_a[192:208, k * DLEN : (k + 1) * DLEN] = wp[k * 16 : (k + 1) * 16, :]

    @pl.when(core == 1)
    def _():
        fill(wk, wo, wu, 1)
        rows = [g1[...].astype(F32), g2[...].astype(F32), g3[...].astype(F32)]
        head = jnp.concatenate(rows + [jnp.zeros((5, 96), F32)], axis=0)
        tail = jnp.concatenate([table[...].astype(F32), jnp.zeros((7, 48), F32)], axis=0)
        tail = jnp.concatenate([tail, jnp.zeros((8, 48), F32)], axis=1)
        both = jnp.concatenate([head, tail], axis=0)
        slab_a[192:208, :] = jnp.concatenate(
            [both, jnp.zeros((16, D - 96), F32)], axis=1
        ).astype(BF)


def copies(pairs, sem):
    for src, dst in pairs:
        pltpu.make_async_copy(src, dst, sem).start()


def landed(buffer, sem):
    pltpu.make_async_copy(buffer, buffer, sem).wait()


def fetch_a(ids, pieces, spots, wqk, wvo, extra, sems):
    b, core = ids[0], ids[2]
    for cflip, m, array, entry in spots:
        src = pieces[array].at[entry]
        c, j = core ^ cflip, b ^ m
        row = pl.multiple_of(j * 96, 96)
        copies([(src.at[pl.ds(0, 96)], wqk.at[c, pl.ds(row, 96)])], sems.at[0])
        copies([(src.at[pl.ds(96, 96)], wvo.at[c, pl.ds(row, 96)])], sems.at[1])
        copies([(src.at[pl.ds(192, 16)], extra.at[c, j])], sems.at[2])


def fetch_wide(ids, pieces, spots, wgu, sems):
    b, y, core = ids[0], ids[1], ids[2]
    for yflip, cflip, m, array, entry in spots:
        src = pieces[array].at[entry]
        c, yy, j = core ^ cflip, y ^ yflip, b ^ m
        row = pl.multiple_of(j * 96, 96)
        for k in range(4):
            tile = wgu.at[c, yy, pl.ds(row, 96), pl.ds(k * 256, 256)]
            copies([(src.at[pl.ds(k * 96, 96)], tile)], sems.at[2 * yy + c])


def fetch_deep(ids, pieces, spots, wd, sem):
    b, y, core = ids[0], ids[1], ids[2]
    for yflip, cflip, m, array, entry in spots:
        src = pieces[array].at[entry]
        low = pl.multiple_of((b ^ m) * 256 + (2 * (y ^ yflip) + (core ^ cflip)) * 64, 64)
        for k in range(3):
            tile = wd.at[pl.ds(low, 64), pl.ds(k * 256, 256)]
            copies([(src.at[pl.ds(384 + k * 64, 64)], tile)], sem)


def head_masks():
    low_lane = lax.broadcasted_iota(jnp.int32, (DLEN, DLEN), 1) < DH
    return low_lane


def both_heads(pair, low_lane):
    zero = jnp.zeros_like(pair)
    return jnp.concatenate(
        [jnp.where(low_lane, pair, zero), jnp.where(low_lane, zero, pair)], axis=0
    )


PAIRS_OF_HEADS = [
    (m, p, slice(m * DLEN, (m + 1) * DLEN), slice(p * DLEN, (p + 1) * DLEN))
    for m in range(MICRO)
    for p in range(H // 2)
]


def attention_forward_kernel(direct, spots, ids, x, mask, onehot, *refs):
    if direct:
        count = 1 + max(spot[2] for spot in spots)
        pieces, refs = refs[:count], refs[count:]
        qkv, attended, weights, first, n1, n2, gains, wproj, wqk_out, wvo_out = refs[:10]
        wqk, wvo, extra, bias, scores, sems = refs[10:]
        fetch_a(ids, pieces, spots, wqk, wvo, extra, sems)
        ids[4]()
        landed(extra, sems.at[2])
        lane = lax.broadcasted_iota(jnp.int32, (8, D), 1)
        all_gains = jnp.zeros((8, D), F32)
        flat = jnp.zeros((8, D), F32)
        for j in range(SHARDS):
            block = extra[1, j].astype(F32)
            all_gains += pltpu.roll(jnp.where(lane < 96, block[0:8], 0.0), j * 96, 1)
            flat += pltpu.roll(jnp.where(lane < 48, block[8:16], 0.0), j * 48, 1)
            for k in range(6):
                wproj[j * 96 + k * 16 : j * 96 + (k + 1) * 16, :] = extra[
                    0, j, :, k * DLEN : (k + 1) * DLEN
                ]
        gains[...] = all_gains
        ids[5](6, 7)
        flat = flat[0:1, : BUCKETS * H]
    else:
        ids[4]()
        gains, flat_in, wqk, wvo = refs[:4]
        qkv, attended, weights, first, n1, n2, bias, scores = refs[4:]
        flat = flat_in[...].astype(F32)
    entry = lax.broadcasted_iota(jnp.int32, (16, BUCKETS * H), 1)
    head = lax.broadcasted_iota(jnp.int32, (16, BUCKETS * H), 0)
    by_head = jnp.where(entry % H == head, jnp.broadcast_to(flat, entry.shape), 0.0)
    offsets = dot(by_head.astype(BF), onehot[...])
    for h in range(H):
        row = jnp.broadcast_to(offsets[h : h + 1, :], (DLEN, 2 * DLEN))
        rolled = pltpu.roll(row, DLEN + 1, 1, stride=1, stride_axis=0)
        bias[h // 2, (h % 2) * DLEN : (h % 2 + 1) * DLEN, :] = rolled[:, :DLEN]
    tokens = x[...].astype(F32)
    normed = (tokens * norm_scale(tokens) * gains[0:1, :]).astype(BF)
    n1[...] = normed
    if direct:
        landed(wqk, sems.at[0])
        copies([(wqk, wqk_out)], sems.at[0])
        landed(wvo, sems.at[1])
        copies([(wvo, wvo_out)], sems.at[1])
    qkv[0] = dot(normed, wqk[0]).astype(BF)
    qkv[1] = dot(normed, wqk[1]).astype(BF)
    qkv[2] = dot(normed, wvo[0]).astype(BF)
    ids[5](0, 4)
    low_lane = head_masks()
    for i, (m, p, rows, lanes) in enumerate(PAIRS_OF_HEADS):
        scores[i] = dot_nt(both_heads(qkv[0, rows, lanes], low_lane), qkv[1, rows, lanes])
    for i, (m, p, rows, lanes) in enumerate(PAIRS_OF_HEADS):
        hidden = jnp.concatenate([mask[m], mask[m]], axis=0)
        biased = scores[i] + bias[p] + hidden
        shifted = jnp.exp(biased - jnp.max(biased, axis=-1, keepdims=True))
        weights[m, p] = (shifted / jnp.sum(shifted, axis=-1, keepdims=True)).astype(BF)
    ids[5](2)
    for i, (m, p, rows, lanes) in enumerate(PAIRS_OF_HEADS):
        mixed = dot(weights[m, p], qkv[2, rows, lanes])
        attended[rows, lanes] = jnp.where(low_lane, mixed[:DLEN], mixed[DLEN:]).astype(BF)
    ids[5](1)
    x1 = tokens + dot(attended[...], wvo[1])
    first[...] = x1
    ids[5](3)
    n2[...] = (x1 * norm_scale(x1) * gains[1:2, :]).astype(BF)
    if direct:
        landed(wqk, sems.at[0])
        landed(wvo, sems.at[1])


def gelu_parts(gate):
    c0, c1 = math.sqrt(2.0 / math.pi), 0.044715
    square = gate * gate
    bent = jnp.tanh(c0 * gate * (1.0 + c1 * square))
    value = 0.5 * gate * (1.0 + bent)
    slope = 0.5 * (1.0 + bent) + 0.5 * gate * (1.0 - bent * bent) * (
        c0 * (1.0 + 3.0 * c1 * square)
    )
    return value, slope


def ffn_forward_kernel(direct, spots, ids, first, n2, gains, wproj, *refs):
    if direct:
        count = 1 + max(spot[3] for spot in spots)
        pieces, refs = refs[:count], refs[count:]
        second, n3, vectors, gelu_out, slope_out, hidden_out = refs[1:7]
        wgu, wd, gelu_kept, slope_kept, hidden, sems = refs[7:]
        fetch_wide(ids, pieces, spots, wgu, sems)
    else:
        wgu, wd, second, n3, vectors, gelu_kept, slope_kept, hidden = refs
    ids[4]()
    normed = n2[...]
    for step in range(2):
        half = (ids[1] ^ step) if direct else step
        if direct:
            landed(wgu.at[0, half], sems.at[2 * half])
            landed(wgu.at[1, half], sems.at[2 * half + 1])
        gate = dot(normed, wgu[0, half])
        up = dot(normed, wgu[1, half])
        value, slope = gelu_parts(gate)
        gelu_kept[half] = value.astype(BF)
        slope_kept[half] = (up * slope).astype(BF)
        hidden[half] = (value * up).astype(BF)
        if direct and step == 0:
            fetch_deep(ids, pieces, spots, wd, sems.at[4])
        if direct:
            copies([(gelu_kept.at[half], gelu_out.at[half])], sems.at[2 * half])
            copies([(slope_kept.at[half], slope_out.at[half])], sems.at[2 * half + 1])
    if direct:
        landed(wd, sems.at[4])
        copies([(hidden, hidden_out)], sems.at[4])
    total = first[...] + dot(hidden[0], wd[:HALF, :]) + dot(hidden[1], wd[HALF:, :])
    second[...] = total
    ids[5](0)
    normed_three = (total * norm_scale(total) * gains[2:3, :]).astype(BF)
    n3[...] = normed_three
    ids[5](1)
    vectors[...] = dot(normed_three, wproj[...]).astype(BF)
    if direct:
        for half in range(2):
            landed(gelu_kept.at[half], sems.at[2 * half])
            landed(slope_kept.at[half], sems.at[2 * half + 1])
        landed(hidden, sems.at[4])


def count_kernel(ids, picks, counts):
    spots = lax.broadcasted_iota(jnp.int32, (DLEN, DLEN), 0)

    def one(j):
        for m in range(MICRO):
            total = jnp.zeros((DLEN, DLEN), F32)
            for t in range(picks.shape[2]):
                total += jnp.where(spots == picks[m, j, t : t + 1, :], 1.0, 0.0)
            counts[m, j] = total

    steps(picks.shape[1], one)


def block_of(others, m):
    return others[m % 2].at[m // 2] if len(others) == 2 else others[0].at[m]


def group_sums(values):
    lane = lax.broadcasted_iota(jnp.int32, values.shape, 1)
    shift = 1
    while shift < QLEN:
        ahead = pltpu.roll(values, DLEN - shift, 1)
        behind = pltpu.roll(values, shift, 1)
        values = values + jnp.where((lane & shift) == 0, ahead, behind)
        shift *= 2
    return values


def similarity_kernel(direct, count, ids, own, counts, share, *refs):
    others, (soft, score, best) = refs[:-3], refs[-3:]
    b, is_query = ids[0], ids[3]
    scale = DLEN**-0.5

    def one(m):
        j = (b ^ m) if direct else m
        for micro in range(MICRO):
            rows = slice(micro * DLEN, (micro + 1) * DLEN)
            mine, theirs = own[rows, :], block_of(others, m)[rows, :]
            doc = jnp.where(is_query == 1, theirs, mine)
            query = jnp.where(is_query == 1, mine, theirs)
            times = counts[micro, j]
            sim = dot_nt(doc, query) * scale
            peak = jnp.max(jnp.where(times > 0, sim, -jnp.inf), axis=0, keepdims=True)
            mass = jnp.where(times > 0, times * jnp.exp(jnp.minimum(sim - peak, 0.0)), 0.0)
            total = jnp.sum(mass, axis=0, keepdims=True)
            soft[micro, j] = mass / total
            best[micro, pl.ds(j, 1), :] = peak + jnp.log(total)

    steps(count, one)
    for micro in range(MICRO):
        score[micro] = group_sums(best[micro] * share[micro])


def vector_grad_kernel(
    direct, count, ids, soft, share, sharp, target, score, scores, *refs
):
    others, (grad, weight, total) = refs[:-3], refs[-3:]
    b, is_query = ids[0], ids[3]
    scale = DLEN**-0.5

    @pl.when(is_query == 1)
    def _():
        for micro in range(MICRO):
            logits = score[micro] * sharp[micro]
            raised = jnp.exp(logits - jnp.max(logits, axis=0, keepdims=True))
            odds = raised / jnp.sum(raised, axis=0, keepdims=True)
            doc = lax.broadcasted_iota(jnp.int32, (count, DLEN), 0)
            hit = jnp.where(target[micro] == doc, 1.0, 0.0)
            weight[micro] = (odds - hit) * sharp[micro] * share[micro] * scale

    @pl.when(is_query == 0)
    def _():
        for micro in range(MICRO):
            sharpness = sharp[micro]
            logits = scores[:, micro] * sharpness[None]
            peak = jnp.max(logits, axis=0)
            norm = jnp.sum(jnp.exp(logits - peak[None]), axis=0)
            odds = jnp.exp(score[micro] * sharpness - peak) / norm
            hit = jnp.where(target[micro] == b, 1.0, 0.0)
            weight[micro] = (odds - hit) * sharpness * share[micro] * scale

    def parts(m, micro):
        j = (b ^ m) if direct else m
        dense = soft[micro, j] * weight[micro, pl.ds(j, 1), :]
        upper = dense.astype(BF)
        lower = (dense - upper.astype(F32)).astype(BF)
        return upper, lower, block_of(others, m)[micro * DLEN : (micro + 1) * DLEN, :]

    for flag, product in ((1, dot_tn), (0, dot)):

        @pl.when(is_query == flag)
        def _():
            for micro in range(MICRO):
                rows = slice(micro * DLEN, (micro + 1) * DLEN)
                if count <= 16:
                    sums = []
                    for m in range(count):
                        upper, lower, theirs = parts(m, micro)
                        sums.append(product(upper, theirs) + product(lower, theirs))
                    grad[rows, :] = sum(sums[1:], sums[0]).astype(BF)
                else:
                    total[rows, :] = jnp.zeros((DLEN, DLEN), F32)

                    @pl.loop(0, count)
                    def _(m):
                        upper, lower, theirs = parts(m, micro)
                        total[rows, :] += product(upper, theirs) + product(lower, theirs)

                    grad[rows, :] = total[rows, :].astype(BF)


def ffn_backward_kernel(direct, spots, ids, dvec, second, n2, n3, gains, wproj, *refs):
    if direct:
        hidden_in, gelu_in, slope_in = refs[:3]
        count = 1 + max(spot[3] for spot in spots)
        pieces, refs = refs[3 : 3 + count], refs[3 + count :]
        dx2_out, grad_proj, grad_gain, dgu, *outs = refs[:10]
        wd, hidden, gelu_kept, slope_kept, grad_down, quarters, sems = refs[10:]
        fetch_deep(ids, pieces, spots, wd, sems.at[0])
        copies([(slope_in, slope_kept)], sems.at[1])
        copies([(gelu_in, gelu_kept)], sems.at[2])
        copies([(hidden_in, hidden)], sems.at[3])
    else:
        wd, hidden, gelu_kept, slope_kept, dx2_out, grad_proj, grad_gain, dgu, dy_out = refs
    b, y, core, _, ready, send = ids
    ready()
    dvectors = dvec[...]
    dn3 = dot_nt(dvectors, wproj[...])
    dx2, dgain3 = norm_backward(second[...], gains[2:3, :], dn3)
    dx2_out[...] = dx2
    grad_gain[...] = dgain3
    grad_proj[...] = dot_tn(n3[...], dvectors)
    send(0, 1, 2)
    dy = dx2.astype(BF)
    if direct:
        landed(wd, sems.at[0])
    dh = dot_nt(dy, wd[...])
    if direct:
        landed(slope_kept, sems.at[1])
        landed(gelu_kept, sems.at[2])
    for half in range(2):
        part = dh[:, half * HALF : (half + 1) * HALF]
        dgu[0, half] = (part * slope_kept[half].astype(F32)).astype(BF)
        dgu[1, half] = (part * gelu_kept[half].astype(F32)).astype(BF)
    send(3)
    if not direct:
        dy_out[...] = dy
        return
    landed(hidden, sems.at[3])
    normed = n2[...]
    wide_rows, deep_rows = pl.ds(0, 384), pl.ds(384, 192)

    def leave(place, rows):
        if place % 2:
            for group, out in zip(GROUPS_F, outs[1 + place : 3 + place]):
                for i, m in enumerate(group):
                    copies([(quarters.at[place, m, rows], out.at[i, rows])], sems.at[place])
        else:
            copies([(quarters.at[place, :, rows], outs[place // 2].at[:, rows])], sems.at[place])

    for place in (3, 2, 1, 0):
        c, yy = core ^ (place // 2), y ^ (place % 2)
        piece = dot_tn(normed, dgu[c, yy]).astype(BF)
        for j in range(SHARDS):
            for k in range(4):
                quarters[place, b ^ j, k * 96 : (k + 1) * 96, :] = piece[
                    j * 96 : (j + 1) * 96, k * 256 : (k + 1) * 256
                ]
        leave(place, wide_rows)
    for j in range(SHARDS):
        start = (j % 4) * 256
        down = dot_tn(hidden[j // 4, :, start : start + 256], dy).astype(BF)
        for part in range(4):
            grad_down[j, part] = down[part * 64 : (part + 1) * 64, :]
    for place in (3, 2, 1, 0):
        c, yy = core ^ (place // 2), y ^ (place % 2)
        for j in range(SHARDS):
            down = grad_down[j, 2 * yy + c]
            for k in range(3):
                quarters[place, b ^ j, 384 + k * 64 : 384 + (k + 1) * 64, :] = down[
                    :, k * 256 : (k + 1) * 256
                ]
        leave(place, deep_rows)
    for place in range(4):
        landed(quarters.at[place], sems.at[place])


def middle_backward_kernel(direct, spots, ids, dx2, first, dgu, gains, *refs):
    if direct:
        count = 1 + max(spot[3] for spot in spots)
        pieces, refs = refs[:count], refs[count:]
        wvo_in, dx1_out, dattended, grad_gain, wgu, wout, sems = refs
        fetch_wide(ids, pieces, spots, wgu, sems)
        copies([(wvo_in.at[1], wout)], sems.at[4])
    else:
        wgu, wvo, dx1_out, dattended, grad_gain = refs
        wout = wvo.at[1]
    ids[4]()
    dn2 = jnp.zeros((ROWS, D), F32)
    for half in range(2):
        for c in range(2):
            if direct:
                landed(wgu.at[c, half], sems.at[half * 2 + c])
            dn2 = dn2 + dot_nt(dgu[c, half], wgu[c, half])
    back, dgain2 = norm_backward(first[...], gains[1:2, :], dn2)
    dx1 = dx2[...] + back
    dx1_out[...] = dx1
    grad_gain[...] = dgain2
    ids[5](0, 2)
    if direct:
        landed(wout, sems.at[4])
    dattended[...] = dot_nt(dx1.astype(BF), wout[...]).astype(BF)


def attention_backward_kernel(
    direct,
    ids,
    grad_first,
    dattended,
    x,
    n1,
    attended,
    weights,
    qkv,
    gains,
    bucket,
    grad_proj,
    grad_gain2,
    grad_gain3,
    *refs,
):
    if direct:
        wqk_in, wvo_in, grad_in, *outs = refs[:7]
        wqk, wvo, own, other, left, right, dqk, extra, *refs = refs[7:]
        copies([(wvo_in.at[0], wvo.at[0])], refs[-1].at[0])
        copies([(wqk_in, wqk)], refs[-1].at[1])
    else:
        wqk, wvo, small, grad_in, dqkv_out, da_out, left, right, dqk, *refs = refs
    diag, bias_grad, dshares, scaled, queries, douts, *rest = refs
    b, core = ids[0], ids[2]
    ids[4]()
    dx1 = grad_first[...]
    da = dx1.astype(BF)
    low_lane = head_masks()
    row_at = lax.broadcasted_iota(jnp.int32, (DLEN, MICRO * DLEN), 0)
    lane_at = lax.broadcasted_iota(jnp.int32, (DLEN, MICRO * DLEN), 1)
    mirror = jnp.where(row_at == DLEN - 1 - lane_at % DLEN, 1.0, 0.0).astype(BF)
    diag[...] = jnp.zeros_like(diag)
    for i, (m, p, rows, lanes) in enumerate(PAIRS_OF_HEADS):
        queries[i] = both_heads(qkv[0, rows, lanes], low_lane)
        douts[i] = both_heads(dattended[rows, lanes], low_lane)
    for i, (m, p, rows, lanes) in enumerate(PAIRS_OF_HEADS):
        dshares[i] = dot_nt(douts[i], qkv[2, rows, lanes])
        right[0, rows, lanes] = dot_tn(weights[m, p], douts[i]).astype(BF)
    for i, (m, p, rows, lanes) in enumerate(PAIRS_OF_HEADS):
        wide = weights[m, p].astype(F32)
        dshare = dshares[i]
        centre = jnp.sum(wide * dshare, axis=-1, keepdims=True)
        scaled[i] = (wide * (dshare - centre)).astype(BF)
    for i, (m, p, rows, lanes) in enumerate(PAIRS_OF_HEADS):
        dq = dot(scaled[i], qkv[1, rows, lanes])
        dqk[0, rows, lanes] = jnp.where(low_lane, dq[:DLEN], dq[DLEN:]).astype(BF)
        dqk[1, rows, lanes] = dot_tn(scaled[i], queries[i]).astype(BF)
    for h in range(H):
        part = slice((h % 2) * DLEN, (h % 2 + 1) * DLEN)
        both = jnp.concatenate([scaled[m * (H // 2) + h // 2, part] for m in range(MICRO)], axis=0)
        turned = dot(mirror, both)
        wider = jnp.concatenate([turned, jnp.zeros_like(turned)], axis=1)
        rolled = pltpu.roll(wider, 0, 1, stride=1, stride_axis=0)
        diag[h : h + 1, :] = jnp.sum(rolled, axis=0, keepdims=True)
    bias_grad[...] = lax.dot_general(
        bucket[...],
        diag[...],
        (((1,), (1,)), ((), ())),
        precision=HIGHEST,
        preferred_element_type=F32,
    )
    if direct:
        sems = rest[0]
        landed(wvo.at[0], sems.at[0])
        landed(wqk, sems.at[1])
    dn1 = dot_nt(dqk[0], wqk[0]) + dot_nt(dqk[1], wqk[1]) + dot_nt(right[0], wvo[0])
    dx, dgain1 = norm_backward(x[...].astype(F32), gains[0:1, :], dn1)
    grad_in[...] = dx1 + dx
    if direct:
        ids[5](0)
    right[1] = da
    left[0] = n1[...]
    left[1] = attended[...]
    all_gains = jnp.concatenate(
        [dgain1, grad_gain2[...], grad_gain3[...], jnp.zeros((5, D), F32)], axis=0
    )
    if not direct:
        small[0:8, :] = all_gains
        small[8:40, :] = jnp.concatenate(
            [bias_grad[...], jnp.zeros((BUCKETS, D - DLEN), F32)], axis=1
        )
        dqkv_out[0] = dqk[0]
        dqkv_out[1] = dqk[1]
        dqkv_out[2] = right[0]
        da_out[...] = da
        return
    per_shard = BUCKETS // SHARDS
    for j in range(SHARDS):
        for k in range(6):
            extra[0, j, :, k * DLEN : (k + 1) * DLEN] = grad_proj[
                j * 96 + k * 16 : j * 96 + (k + 1) * 16, :
            ]
        extra[1, j] = jnp.zeros((16, D), F32)
        extra[1, j, 0:8, :] = pltpu.roll(all_gains, (D - j * 96) % D, 1)
        extra[1, j, 8 : 8 + per_shard, 0:DLEN] = bias_grad[j * per_shard : (j + 1) * per_shard, :]
    for flip, out in ((1, other), (0, own)):
        c = core ^ flip
        top = dot_tn(n1[...], dqk[c]).astype(BF)
        bottom = dot_tn(left[c], right[c]).astype(BF)
        for j in range(SHARDS):
            m = b ^ j
            out[m, 0:96, :] = top[j * 96 : (j + 1) * 96, :]
            out[m, 96:192, :] = bottom[j * 96 : (j + 1) * 96, :]
            out[m, 192:208, :] = extra[c, j].astype(BF)
        for group, target in zip((FIRST_A, REST_A), outs[2 * flip : 2 * flip + 2]):
            copies([(out.at[m], target.at[i]) for i, m in enumerate(group)], sems.at[flip])
    landed(other, sems.at[1])
    landed(own, sems.at[0])


def finish_wide_kernel(ids, near, far, twin, far_twin, token, grad_g, grad_u, grad_d):
    y, core = ids[1], ids[2]
    for yy in range(2):
        for c in range(2):

            @pl.when((y == yy) & (core == c))
            def _():
                for yflip, cflip, part in ((0, 0, near), (1, 0, far), (0, 1, twin), (1, 1, far_twin)):
                    half, rank = yy ^ yflip, c ^ cflip
                    out = grad_u if rank else grad_g
                    for k in range(4):
                        start = half * HALF + k * 256
                        out[:, start : start + 256] = part[0, k * 96 : (k + 1) * 96, :].astype(F32)
                    low = (2 * half + rank) * 64
                    for k in range(3):
                        grad_d[low : low + 64, k * 256 : (k + 1) * 256] = part[
                            0, 384 + k * 64 : 384 + (k + 1) * 64, :
                        ].astype(F32)


def finish_narrow_kernel(
    ids, near, twin, grad_q, grad_k, grad_v, grad_o, grad_p, grad_1, grad_2, grad_3, table
):
    core = ids[2]
    for c in range(2):

        @pl.when(core == c)
        def _():
            low, high = (twin, near) if c else (near, twin)
            grad_q[...] = low[0, 0:96, :].astype(F32)
            grad_k[...] = high[0, 0:96, :].astype(F32)
            grad_v[...] = low[0, 96:192, :].astype(F32)
            grad_o[...] = high[0, 96:192, :].astype(F32)
            for k in range(6):
                grad_p[k * 16 : (k + 1) * 16, :] = low[
                    0, 192:208, k * DLEN : (k + 1) * DLEN
                ].astype(F32)
            rows = high[0, 192:208, :].astype(F32)
            grad_1[...] = rows[0:1, :96]
            grad_2[...] = rows[1:2, :96]
            grad_3[...] = rows[2:3, :96]
            block = jnp.where(lax.broadcasted_iota(jnp.int32, (8, DLEN), 1) < H, rows[8:16, :DLEN], 0.0)
            line = block[0:1]
            for i in range(1, BUCKETS // SHARDS):
                line += pltpu.roll(block, i * H, 1)[i : i + 1]
            table[...] = line[:, : BUCKETS // SHARDS * H]


def local(
    hidden_in,
    norm1_gain,
    w_query,
    w_key,
    w_value,
    w_out,
    rel_table,
    norm2_gain,
    w_gate,
    w_up,
    w_down,
    norm3_gain,
    w_proj,
    query_lengths,
    keyword_request_mask,
    targets,
    candidates,
):
    streams = lax.axis_size("stream")
    shards = lax.axis_size("batch")
    pairs = streams // 2
    direct = shards == SHARDS and pairs == 2
    b = lax.axis_index("batch")
    s = lax.axis_index("stream")
    y, core = s // pairs, s % pairs
    is_query = s < pairs

    def swap(block, yflip, cflip, m):
        route = []
        for source in range(streams):
            target = ((source // pairs) ^ yflip) * pairs + ((source % pairs) ^ cflip)
            for j in range(shards):
                route.append((source * shards + j, target * shards + (j ^ m)))
        return lax.ppermute(block, EVERY, route)

    micro_count = hidden_in.shape[0]
    slot = jnp.arange(DLEN)
    pair_lengths = lax.dynamic_index_in_dim(query_lengths, core, 1, keepdims=False)
    pair_keyword = lax.dynamic_index_in_dim(keyword_request_mask, core, 1, keepdims=False)
    pair_targets = lax.dynamic_index_in_dim(targets, core, 1, keepdims=False)

    def by_slot(values):
        blocks = values.reshape(micro_count, shards, GROUPS)
        own = lax.dynamic_slice_in_dim(blocks, b, 1, 1)
        blocks = jnp.where(is_query, jnp.broadcast_to(own, blocks.shape), blocks)
        return jnp.repeat(blocks, QLEN, axis=2)

    length_slots = by_slot(pair_lengths)
    valid_slots = (slot % QLEN)[None, None, :] < length_slots
    share = jnp.where(valid_slots, 1.0 / length_slots.astype(F32), 0.0)
    sharp = jnp.where(by_slot(pair_keyword) == 1, 20.0, 10.0).astype(F32)
    target_slots = by_slot(pair_targets)
    own_valid = lax.dynamic_slice_in_dim(valid_slots, b, 1, 1)
    same = (slot[:, None] // QLEN) == (slot[None, :] // QLEN)
    mask = jnp.where(is_query & ~(same[None] & own_valid), -1000000000.0, 0.0).astype(F32)

    small = 16 if direct else 48
    picked = lax.dynamic_index_in_dim(candidates, core, 1, keepdims=False)[:, 0]
    picked = picked.reshape(micro_count, shards, DLEN, picked.shape[-1])
    picked = jnp.transpose(picked, (0, 1, 3, 2))
    received = lax.all_to_all(picked, "batch", split_axis=1, concat_axis=1, tiled=True)
    picks = jnp.where(is_query, received, picked)
    (counts,) = call(
        count_kernel,
        "count",
        [picks],
        [((micro_count, shards, DLEN, DLEN), F32)],
        limit=small,
    )

    fence = lax.optimization_barrier
    first_core = core == 0
    spots_a = spots_f = None
    if direct:
        lines = [part.reshape(1, -1) for part in (norm1_gain, norm2_gain, norm3_gain, rel_table)]
        slab_a, slab_f = call(
            pack_kernel,
            "pack",
            [w_query, w_key, w_value, w_out, w_gate, w_up, w_down, w_proj, *lines],
            [((PIECE_A, D), BF), ((PIECE_F, 256), BF)],
        )

        def join(*parts):
            return jnp.concatenate(parts)

        def along_x(part):
            return swap(part, 0, 0, 1)

        def along_y(part):
            return swap(part, 1, 0, 0)

        def along_z(part):
            return swap(part, 0, 0, 2)

        def along_zz(part):
            return swap(part, 0, 0, 4)

        def other_core(part):
            return swap(part, 0, 1, 0)

        f0, a0 = slab_f[None], slab_a[None]
        token = jnp.zeros((8, DLEN), F32)
        f4, f2, y0, f1, a1 = along_zz(f0), along_z(f0), along_y(f0), along_x(f0), along_x(a0)
        token = tick(token)
        f4, f2, y0, f1, a1, a0, token = fence((f4, f2, y0, f1, a1, a0, token))
        f42, f142, token = fence((join(f4, f2), join(f1, f4, f2), token))
        y142, f53, f6, a4, a2 = (
            along_y(f142),
            along_x(f42),
            along_z(f4),
            along_zz(a0),
            along_z(a0),
        )
        token = tick(token)
        f53, f6, counts, mask, share, sharp, target_slots, token = fence(
            (f53, f6, counts, mask, share, sharp, target_slots, token)
        )
        f65, token = fence((join(f6, f53[0:1]), token))
        f7 = along_x(f6)

        a2, token = fence((a2, token))
        a3 = along_x(a2)
        a4, token = fence((a4, token))
        a5, a6 = along_x(a4), along_z(a4)

        y142, f65, token = fence((y142, f65, token))
        y65 = along_y(f65)

        f7, token = fence((f7, token))
        f37, f_all, token = fence((join(f53[1:2], f7), join(f0, f142, f65, f53[1:2], f7), token))
        f_all, token = fence((f_all, token))
        tf_all = other_core(f_all)

        a6, token = fence((a6, token))
        a7 = along_x(a6)
        a0142, token = fence((join(a0, a1, a4, a2), token))
        ta0142 = other_core(a0142)
        y65, f37, token = fence((y65, f37, token))
        y37, ty65 = along_y(f37), other_core(y65)
        token = tick(token)
        a3, a5, tf_all, ta0142, token = fence((a3, a5, tf_all, ta0142, token))
        a536, y_first, token = fence((join(a5, a3, a6), join(y0, y142), token))
        ta536, ty_first = other_core(a536), other_core(y_first)
        a7, token = fence((a7, token))
        ta7 = other_core(a7)
        token = tick(token)
        y37, ta536, ta7, token = fence((y37, ta536, ta7, token))
        ty37 = other_core(y37)

        order_f = (0, 1, 4, 2, 6, 5, 3, 7)
        groups_a = [
            (0, (a0142, (0, 1, 4, 2)), (a536, (5, 3, 6)), (a7, (7,))),
            (1, (ta0142, (0, 1, 4, 2)), (ta536, (5, 3, 6)), (ta7, (7,))),
        ]
        pieces_a, spots_a, pieces_f, spots_f = [], [], [], []
        for cflip, *group in groups_a:
            for part, flips in group:
                spots_a += [(cflip, m, len(pieces_a), i) for i, m in enumerate(flips)]
                pieces_a.append(part)
    else:

        def whole(part):
            return lax.all_gather(part, "batch", axis=0, tiled=True)

        wqk = jnp.stack([whole(w_query), whole(w_key)])
        wvo = jnp.stack([whole(w_value), whole(w_out)])
        gate_up = jnp.stack([whole(w_gate), whole(w_up)])
        wgu = jnp.transpose(gate_up.reshape(2, D, 2, HALF), (0, 2, 1, 3))
        wd = whole(w_down)
        wproj = whole(w_proj)
        gain_rows = [whole(gain) for gain in (norm1_gain, norm2_gain, norm3_gain)]
        gains = jnp.pad(jnp.stack(gain_rows).astype(F32), ((0, 5), (0, 0)))
        table = whole(rel_table).reshape(1, BUCKETS * H)

    onehot = bucket_onehot()
    by_entry = jnp.asarray(np.repeat(onehot.T, H, axis=0), BF)
    x = hidden_in[:, 0].reshape(ROWS, D)
    row_bf, row_f32 = ((ROWS, D), BF), ((ROWS, D), F32)
    qkv_shape, weight_shape = ((3, ROWS, D), BF), ((MICRO, H // 2, ROWS, DLEN), BF)
    pair_weights = ((2, D, D), BF)
    gain_rows = ((8, D), F32)
    proj_shape = ((D, DLEN), BF)
    kept = [qkv_shape, row_bf, weight_shape, row_f32, row_bf, row_bf]
    bias_shape, score_shape = ((H // 2, ROWS, DLEN), F32), ((H, ROWS, DLEN), F32)
    result = call(
        functools.partial(attention_forward_kernel, direct, spots_a),
        "attention_forward",
        [x, mask, by_entry] + ([] if direct else [gains, table, wqk, wvo]),
        kept + ([gain_rows, proj_shape] if direct else []),
        ([pair_weights, pair_weights, ((2, SHARDS, 16, D), BF)] if direct else [])
        + [bias_shape, score_shape],
        far=pieces_a if direct else [],
        far_outs=[pair_weights, pair_weights] if direct else [],
        sems=3 if direct else 0,
        flops=2 * ROWS * D * D * 4,
        lazy=True,
    )
    qkv, attended, weights, first, n1, n2 = result[:6]
    if direct:
        gains, wproj, wqk, wvo = result[6:]
    first, counts, share, sharp, target_slots = fence((first, counts, share, sharp, target_slots))
    if direct:
        ty_first, ty65, ty37, first, token = fence((ty_first, ty65, ty37, first, token))
        near, twin = ((f_all, order_f),), ((tf_all, order_f),)
        far = ((y_first, order_f[:4]), (y65, order_f[4:6]), (y37, order_f[6:]))
        far_twin = ((ty_first, order_f[:4]), (ty65, order_f[4:6]), (ty37, order_f[6:]))
        for yflip, cflip, group in ((0, 0, near), (0, 1, twin), (1, 0, far), (1, 1, far_twin)):
            for part, flips in group:
                spots_f += [(yflip, cflip, m, len(pieces_f), i) for i, m in enumerate(flips)]
                pieces_f.append(part)
    wide_bf = ((2, ROWS, HALF), BF)
    wgu_shape, wd_shape = ((2, 2, D, HALF), BF), ((FF, D), BF)
    lasting = [wide_bf, wide_bf, wide_bf]
    result = call(
        functools.partial(ffn_forward_kernel, direct, spots_f),
        "ffn_forward",
        [first, n2, gains, wproj] + ([] if direct else [wgu, wd]),
        [row_f32, row_bf, ((ROWS, DLEN), BF)] + ([] if direct else lasting),
        [wgu_shape, wd_shape] + lasting if direct else [],
        far=[*pieces_f, token] if direct else [],
        far_outs=lasting if direct else [],
        sems=5 if direct else 0,
        flops=2 * ROWS * D * FF * 3,
        lazy=True,
    )
    second, n3, vectors, gelu_kept, slope_kept, hidden = result

    if direct:
        even = jnp.stack([swap(vectors, 1, 0, m) for m in (0, 2, 4, 6)])
        others = [even, swap(even, 0, 0, 1)]
    else:
        route = [(i, (i + pairs) % streams) for i in range(streams)]
        arrived = lax.ppermute(vectors, "stream", route)
        others = [lax.all_gather(arrived, "batch", axis=0)]
    block_f32 = ((micro_count, shards, DLEN, DLEN), F32)
    line_f32 = ((micro_count, shards, DLEN), F32)
    soft, score = call(
        functools.partial(similarity_kernel, direct, shards),
        "similarity",
        [vectors, counts, share, *others],
        [block_f32, line_f32],
        [line_f32],
        limit=small,
        near=True,
    )
    if direct:
        blocks = jnp.broadcast_to(score[None], (shards,) + score.shape)
        scores = lax.all_to_all(blocks, "batch", split_axis=0, concat_axis=0, tiled=True)
    else:
        scores = lax.all_gather(score, "batch", axis=0)
    (dvec,) = call(
        functools.partial(vector_grad_kernel, direct, shards),
        "vector_grad",
        [soft, share, sharp, target_slots, score, scores, *others],
        [((ROWS, DLEN), BF)],
        [line_f32, ((ROWS, DLEN), F32)],
        limit=small,
        near=True,
    )

    gain_row = ((1, D), F32)
    proj_f32 = ((D, DLEN), F32)
    dgu_shape = ((2, 2, ROWS, HALF), BF)
    quarter = ((SHARDS, PIECE_F, 256), BF)
    saved = [hidden, gelu_kept, slope_kept]
    result = call(
        functools.partial(ffn_backward_kernel, direct, spots_f),
        "ffn_backward",
        [dvec, second, n2, n3, gains, wproj] + ([] if direct else [wd, *saved]),
        [row_f32, proj_f32, gain_row, dgu_shape] + ([] if direct else [row_bf]),
        [wd_shape, wide_bf, wide_bf, wide_bf, ((SHARDS, 4, 64, D), BF), ((4, *quarter[0]), BF)]
        if direct
        else [],
        far=[*saved, *pieces_f] if direct else [],
        far_outs=[quarter] * 2 + [((4, PIECE_F, 256), BF)] * 4 if direct else [],
        sems=4 if direct else 0,
        flops=2 * ROWS * D * FF * 4,
        lazy=True,
    )
    dx2, grad_proj, grad_gain, dgu = result[:4]
    if direct:
        f_own, f_twin, *f_far = result[4:]
    else:
        dy = result[4]

    if direct:
        def own_f(m, *more):
            group = 0 if m in GROUPS_F[0] else 1
            return [(base_f[group], GROUPS_F[group].index(m)), *more]

        def far_sum(i):
            return [[(f_far[i], n), (c_far[i], n)] for n in range(4)]

        c_far = [other_core(part) for part in f_far[2:]]
        c_far[0], f_twin, dgu = fence((c_far[0], f_twin, dgu))
        twin = other_core(f_twin)
        (sent_a,) = add_up(far_sum(0))
        sent_a, dgu = fence((sent_a, dgu))
        y_a = along_y(sent_a)
    middle_in = [dx2, first, dgu, gains]
    dx1, dattended, grad_gain2 = call(
        functools.partial(middle_backward_kernel, direct, spots_f),
        "middle_backward",
        middle_in + ([] if direct else [wgu, wvo]),
        [row_f32, row_bf, gain_row],
        [wgu_shape, ((D, D), BF)] if direct else [],
        far=[*pieces_f, wvo] if direct else [],
        sems=5 if direct else 0,
        flops=ROUND_FLOPS,
        lazy=True,
    )
    if direct:
        *c_far[1:], twin, dattended = fence((*c_far[1:], twin, dattended))
        (sent_b,) = add_up(far_sum(1))
        base_f = [base_up(f_own, twin, GROUPS_F[0])]
        sent_b, base_f[0], dattended = fence((sent_b, base_f[0], dattended))
    two_rows = ((2, ROWS, D), BF)
    slab_out = ((SHARDS, PIECE_A, D), BF)
    blocks_bf = ((H, ROWS, DLEN), BF)
    result = call(
        functools.partial(attention_backward_kernel, direct),
        "attention_backward",
        [dx1, dattended, x, n1, attended, weights, qkv, gains, jnp.asarray(onehot.T)]
        + [grad_proj, grad_gain2, grad_gain]
        + ([] if direct else [wqk, wvo]),
        [row_f32] if direct else [((40, D), F32), row_f32, qkv_shape, row_bf],
        ([pair_weights, pair_weights, slab_out, slab_out] if direct else [])
        + [two_rows, two_rows, two_rows]
        + ([((2, SHARDS, 16, D), F32)] if direct else [])
        + [((DLEN, 2 * DLEN), F32), ((BUCKETS, DLEN), F32)]
        + [score_shape, blocks_bf, blocks_bf, blocks_bf],
        far=[wqk, wvo] if direct else [],
        far_outs=[((count, PIECE_A, D), BF) for count in (2, 6, 2, 6)] if direct else [],
        sems=2 if direct else 0,
        flops=2 * ROWS * D * D * 7,
        lazy=True,
    )

    if direct:
        input_grad, o_first, o_rest, a_first, a_rest = result

        def own_a(m, *more):
            return [(base_a, REST_A.index(m)), *more]

        o_first, o_rest, a_first, a_rest = fence((o_first, o_rest, a_first, a_rest))
        token = jnp.ones((8, DLEN), F32)
        c_first = other_core(a_first)
        c_first, a_rest, token = fence((c_first, a_rest, token))
        (out_a37,) = add_up([[(o_first, i), (c_first, i)] for i in range(2)])
        out_a37, a_rest, token = fence((out_a37, a_rest, token))
        xa37, c_rest = along_x(out_a37), other_core(a_rest)

        y_a, sent_b, token = fence((y_a, sent_b, token))
        y_b = along_y(sent_b)
        (out_73,) = add_up([own_f(7, (y_a, 1)), own_f(3, (y_a, 3))])
        out_73, token = fence((out_73, token))
        x73 = along_x(out_73)
        token = tick(token)
        c_rest, token = fence((c_rest, token))
        base_a = base_up(o_rest, c_rest, range(len(REST_A)))
        base_f.append(base_up(f_own, twin, GROUPS_F[1]))
        x73, base_a, base_f[1], token = fence((x73, base_a, base_f[1], token))
        (out_62,) = add_up([own_f(6, (y_a, 0), (x73, 0)), own_f(2, (y_a, 2), (x73, 1))])
        out_62, token = fence((out_62, token))
        z62 = along_z(out_62)

        xa37, token = fence((xa37, token))
        out_a51, out_a62 = add_up(
            [own_a(5), own_a(1)], [own_a(6, (xa37, 1)), own_a(2, (xa37, 0))]
        )
        out_a62, token = fence((out_a62, token))
        za62 = along_z(out_a62)

        y_b, token = fence((y_b, token))
        out_5, out_1 = add_up([own_f(5, (y_b, 1))], [own_f(1, (y_b, 3))])
        out_5, token = fence((out_5, token))
        x5 = along_x(out_5)

        x5, z62, token = fence((x5, z62, token))
        (out_4,) = add_up([own_f(4, (y_b, 0), (x5, 0), (z62, 0))])
        out_4, out_a51, out_1, token = fence((out_4, out_a51, out_1, token))
        x1, xa51, z4 = along_x(out_1), along_x(out_a51), along_zz(out_4)

        za62, xa51, token = fence((za62, xa51, token))
        (out_a4,) = add_up([own_a(4, (xa51, 0), (za62, 0))])
        out_a4, token = fence((out_a4, token))
        za4 = along_zz(out_a4)

        x1, z4, token = fence((x1, z4, token))
        (mine_f,) = add_up([own_f(0, (y_b, 2), (x1, 0), (z62, 1), (z4, 0))])
        mine_f, token = fence((mine_f, token))
        far, twin_f = along_y(mine_f), other_core(mine_f)

        za4, token = fence((za4, token))
        (part_a,) = add_up([own_a(0, (xa51, 1), (za62, 1), (za4, 0))])
        part_a, token = fence((part_a, token))
        ya = along_y(part_a)

        far, twin_f, token = fence((far, twin_f, token))
        far_twin_f = other_core(far)
        ya, token = fence((ya, token))
        (mine_a,) = add_up([[(part_a, 0), (ya, 0)]])
        mine_a, far_twin_f, token = fence((mine_a, far_twin_f, token))
        twin_a = other_core(mine_a)
        shard_f32, wide_f32 = ((96, D), F32), ((96, FF), F32)
        grad_g, grad_u, grad_d = call(
            finish_wide_kernel,
            "finish_wide",
            [mine_f, far, twin_f, far_twin_f],
            [wide_f32, wide_f32, ((256, D), F32)],
            far=[token],
            limit=24,
            near=True,
        )
        grad_q, grad_k, grad_v, grad_o, grad_p, *small = call(
            finish_narrow_kernel,
            "finish_narrow",
            [mine_a, twin_a],
            [shard_f32] * 4 + [((96, DLEN), F32), ((1, 96), F32), ((1, 96), F32), ((1, 96), F32)]
            + [((1, 48), F32)],
            limit=24,
            near=True,
        )
        grad_n1, grad_n2, grad_n3, grad_table = [row.reshape(-1) for row in small]
    else:
        small, input_grad, dqkv, da = result

        def summed(part):
            part = lax.psum_scatter(part, "batch", scatter_dimension=0, tiled=True)
            return lax.psum(part, "stream")

        grad_q, grad_k, grad_v = [summed(dot_tn(n1, dqkv[i])) for i in range(3)]
        grad_o = summed(dot_tn(attended, da))
        grad_g, grad_u = [
            summed(jnp.concatenate([dot_tn(n2, dgu[i, half]) for half in range(2)], axis=1))
            for i in range(2)
        ]
        grad_d = summed(jnp.concatenate([dot_tn(hidden[half], dy) for half in range(2)]))
        grad_p = summed(grad_proj)
        grad_n1, grad_n2, grad_n3 = [summed(small[i]) for i in range(3)]
        flat = lax.psum(small[8 : 8 + BUCKETS, :H].reshape(-1), EVERY)
        share_rows = flat.shape[0] // shards
        grad_table = lax.dynamic_slice_in_dim(flat, b * share_rows, share_rows, 0)

    vectors_out = vectors.reshape(micro_count, DLEN, DLEN)[:, None]
    grad_hidden = input_grad.reshape(micro_count, DLEN, D)[:, None]
    return (
        vectors_out,
        grad_hidden,
        grad_n1,
        grad_q,
        grad_k,
        grad_v,
        grad_o,
        grad_table,
        grad_n2,
        grad_g,
        grad_u,
        grad_d,
        grad_n3,
        grad_p,
    )


def solution(mesh):
    rows, lines = P("batch", None), P("batch")
    spread = P(None, "stream", "batch", None)
    return jax.shard_map(
        local,
        mesh=mesh,
        in_specs=(spread, lines, rows, rows, rows, rows, lines, lines, rows, rows, rows, lines, rows)
        + (P(), P(), P(), P(None, None, "batch", None, None)),
        out_specs=(spread, spread, lines, rows, rows, rows, rows, lines, lines)
        + (rows, rows, rows, lines, rows),
        check_vma=False,
    )
```

```python
import functools
import math

import jax
import jax.numpy as jnp
import numpy as np
from jax import lax
from jax.experimental import pallas as pl
from jax.experimental.pallas import tpu as pltpu
from jax.sharding import PartitionSpec as P

H = 12
DH = 64
BUCKETS = 32
MAX_DIST = 128
DLEN = 128
QLEN = 32
GROUPS = DLEN // QLEN
MICRO = 2
ROWS = MICRO * DLEN
D = 768
FF = 2048
HALF = FF // 2
SHARDS = 8
PIECE_A = 208
PIECE_F = 576
FIRST_A, REST_A = (3, 7), (6, 2, 5, 1, 4, 0)
GROUPS_F = ((6, 7, 2, 3), (4, 5, 0, 1))

EPSILON = 1e-06
HIGHEST = lax.Precision.HIGHEST
BF = jnp.bfloat16
F32 = jnp.float32
EVERY = ("stream", "batch")
MIB = 2**20
ROUND_FLOPS = 5 * 10**10


def distance_bucket(distance):
    half_count = BUCKETS // 2
    exact_count = half_count // 2
    if distance < exact_count:
        return distance
    grown = exact_count + int(
        math.floor(
            math.log(distance / exact_count)
            / math.log(MAX_DIST / exact_count)
            * (half_count - exact_count)
            + 1e-09
        )
    )
    return min(grown, half_count - 1)


def bucket_onehot():
    table = np.zeros((2 * DLEN, BUCKETS), np.float32)
    for o in range(2 * DLEN - 1):
        offset = o - (DLEN - 1)
        table[o, distance_bucket(abs(offset)) + (BUCKETS // 2 if offset > 0 else 0)] = 1.0
    return table


def norm_scale(values):
    return lax.rsqrt(jnp.mean(values * values, axis=-1, keepdims=True) + EPSILON)


def norm_backward(values, gain, grad):
    scale = norm_scale(values)
    pulled = gain * grad
    inner = jnp.mean(values * pulled, axis=-1, keepdims=True)
    back = scale * pulled - values * (scale * scale * scale * inner)
    return back, jnp.sum(grad * values * scale, axis=0, keepdims=True)


def dot(left, right):
    return jnp.dot(left, right, preferred_element_type=F32)


def dot_nt(left, right):
    return lax.dot_general(left, right, (((1,), (1,)), ((), ())), preferred_element_type=F32)


def dot_tn(left, right):
    return lax.dot_general(left, right, (((0,), (0,)), ((), ())), preferred_element_type=F32)


def steps(count, body):
    if count <= 16:
        for i in range(count):
            body(i)
    else:

        @pl.loop(0, count)
        def _(i):
            body(i)


VMEM = pl.BlockSpec(memory_space=pltpu.VMEM)
SMEM = pl.BlockSpec(memory_space=pltpu.SMEM)
HBM = pl.BlockSpec(memory_space=pltpu.HBM)


def positions():
    pairs = lax.axis_size("stream") // 2
    stream = lax.axis_index("stream")
    return lax.axis_index("batch"), stream // pairs, stream % pairs, jnp.where(stream < pairs, 1, 0)


def body_kernel(kernel, lazy, counts, *refs):
    parts = []
    for count in counts:
        parts.append(refs[:count])
        refs = refs[count:]
    arrays, far, outs, far_outs, held, made, scratch = parts
    in_sems, out_sems = refs
    for i, (array, place) in enumerate(zip(arrays, held)):
        pltpu.make_async_copy(array, place, in_sems.at[i]).start()
    sent = set()

    def ready():
        for i, (array, place) in enumerate(zip(arrays, held)):
            pltpu.make_async_copy(array, place, in_sems.at[i]).wait()

    def send(*results):
        for i in results:
            sent.add(i)
            pltpu.make_async_copy(made[i], outs[i], out_sems.at[i]).start()

    if not lazy:
        ready()
    kernel((*positions(), ready, send), *held, *far, *made, *far_outs, *scratch)
    send(*(i for i in range(len(outs)) if i not in sent))
    for i, (place, out) in enumerate(zip(made, outs)):
        pltpu.make_async_copy(place, out, out_sems.at[i]).wait()


def near_kernel(kernel, *refs):
    kernel(positions(), *refs)


def call(
    kernel,
    name,
    arrays,
    outs,
    scratch=(),
    far=(),
    far_outs=(),
    sems=0,
    flops=0,
    limit=59,
    near=False,
    lazy=False,
):
    shapes = [jax.ShapeDtypeStruct(s, t) for s, t in (*outs, *far_outs)]
    moved = sum(math.prod(s.shape) * s.dtype.itemsize for s in shapes)
    moved += sum(math.prod(a.shape) * a.dtype.itemsize for a in (*arrays, *far))
    spaces = [pltpu.VMEM(s, t) for s, t in scratch]
    if sems:
        spaces.append(pltpu.SemaphoreType.DMA((sems,)))
    kind = VMEM if near else HBM
    if near:
        body = functools.partial(near_kernel, kernel)
    else:
        counts = (len(arrays), len(far), len(outs), len(far_outs))
        counts += (len(arrays), len(outs), len(spaces))
        body = functools.partial(body_kernel, kernel, lazy, counts)
        spaces = (
            [pltpu.VMEM(a.shape, a.dtype) for a in arrays]
            + [pltpu.VMEM(s, t) for s, t in outs]
            + spaces
            + [pltpu.SemaphoreType.DMA((max(1, len(part)),)) for part in (arrays, outs)]
        )
    return pl.pallas_call(
        body,
        name=name,
        out_shape=shapes,
        in_specs=[kind] * len(arrays) + [HBM] * len(far),
        out_specs=[kind] * len(outs) + [HBM] * len(far_outs),
        scratch_shapes=spaces,
        compiler_params=pltpu.CompilerParams(vmem_limit_bytes=limit * MIB),
        cost_estimate=pl.CostEstimate(flops=flops, bytes_accessed=moved, transcendentals=0),
    )(*arrays, *far)


def tick_kernel(token, out):
    pass


def tick(token):
    return pl.pallas_call(
        tick_kernel,
        name="tick",
        in_specs=[HBM],
        out_specs=HBM,
        out_shape=jax.ShapeDtypeStruct(token.shape, token.dtype),
        input_output_aliases={0: 0},
        cost_estimate=pl.CostEstimate(flops=ROUND_FLOPS, bytes_accessed=0, transcendentals=0),
    )(token)


def add_kernel(plan, near, far, ids, *refs):
    near, far, refs = refs[:near], refs[near : near + far], refs[near + far :]
    outs, refs = refs[: len(plan)], refs[len(plan) :]
    held, sems = (refs[:-1], refs[-1]) if far else ((), None)
    place = 0
    for entries in plan:
        for terms in entries:
            for is_far, array, entry in terms:
                if is_far:
                    copies([(far[array].at[entry], held[place])], sems.at[place])
                    place += 1
    place = 0
    for out, entries in zip(outs, plan):
        for i, terms in enumerate(entries):
            total = None
            for is_far, array, entry in terms:
                if is_far:
                    landed(held[place], sems.at[place])
                    part = held[place][...].astype(F32)
                    place += 1
                else:
                    part = near[array][entry].astype(F32)
                total = part if total is None else total + part
            out[i] = total.astype(BF)


def base_kernel(picks, whole, ids, own, rest, out, left, right, sems):
    for i, m in enumerate(picks):
        part = rest.at[m if whole else i]
        copies([(own.at[m], left.at[i]), (part, right.at[i])], sems.at[i])
    for i in range(len(picks)):
        landed(left.at[i], sems.at[i])
        landed(right.at[i], sems.at[i])
        left[i] = (left[i].astype(F32) + right[i].astype(F32)).astype(BF)
        copies([(left.at[i], out.at[i])], sems.at[i])
    for i in range(len(picks)):
        landed(left.at[i], sems.at[i])


def base_up(own, rest, picks):
    picks = tuple(picks)
    shape = ((len(picks), *rest.shape[1:]), BF)
    (base,) = call(
        functools.partial(base_kernel, picks, rest.shape[0] > len(picks)),
        "base_up",
        [],
        [],
        [shape, shape],
        far=[own, rest],
        far_outs=[shape],
        sems=len(picks),
    )
    return base


def add_up(*outputs, limit=24):
    known = ([], [])
    plan, flat, shapes = [], [], []
    for entries in outputs:
        plan.append([])
        for terms in entries:
            plan[-1].append([])
            for array, entry in terms:
                is_far = int(array.shape[0] > 4)
                arrays = known[is_far]
                found = [i for i, other in enumerate(arrays) if other is array]
                if not found:
                    arrays.append(array)
                    found = [len(arrays) - 1]
                if is_far:
                    flat.append((array.shape[1:], BF))
                plan[-1][-1].append((is_far, found[0], entry))
        shapes.append(((len(entries), *entries[0][0][0].shape[1:]), BF))
    return call(
        functools.partial(add_kernel, plan, len(known[0]), len(known[1])),
        "add_up",
        known[0],
        shapes,
        flat,
        far=known[1],
        sems=len(flat),
        limit=limit,
        near=True,
    )


def pack_kernel(ids, g1, g2, g3, table, wq, wk, wv, wo, wg, wu, wd, wp, slab_a, slab_f, sems):
    y, core, ready, send = ids[1], ids[2], ids[4], ids[5]

    def fill(top, bottom, wide, rank):
        for yy in range(2):

            @pl.when(y == yy)
            def _():
                pairs = []
                for k in range(4):
                    lanes = pl.ds(yy * HALF + k * 256, 256)
                    pairs.append((wide.at[:, lanes], slab_f.at[pl.ds(k * 96, 96)]))
                rows = pl.ds((2 * yy + rank) * 64, 64)
                for k in range(3):
                    part = wd.at[rows, pl.ds(k * 256, 256)]
                    pairs.append((part, slab_f.at[pl.ds(384 + k * 64, 64)]))
                copies(pairs, sems.at[0])

        pairs = [(top, slab_a.at[pl.ds(0, 96)]), (bottom, slab_a.at[pl.ds(96, 96)])]
        copies(pairs, sems.at[1])

    @pl.when(core == 0)
    def _():
        fill(wq, wv, wg, 0)
        for k in range(6):
            place = slab_a.at[pl.ds(192, 16), pl.ds(k * DLEN, DLEN)]
            copies([(wp.at[pl.ds(k * 16, 16)], place)], sems.at[1])

    @pl.when(core == 1)
    def _():
        fill(wk, wo, wu, 1)

    ready()
    landed(slab_f, sems.at[0])
    send(1)

    @pl.when(core == 0)
    def _():
        landed(slab_a, sems.at[1])

    @pl.when(core == 1)
    def _():
        rows = [g1[...].astype(F32), g2[...].astype(F32), g3[...].astype(F32)]
        head = jnp.concatenate(rows + [jnp.zeros((5, 96), F32)], axis=0)
        tail = jnp.concatenate([table[...].astype(F32), jnp.zeros((7, 48), F32)], axis=0)
        tail = jnp.concatenate([tail, jnp.zeros((8, 48), F32)], axis=1)
        both = jnp.concatenate([head, tail], axis=0)
        slab_a[192:208, :] = jnp.concatenate(
            [both, jnp.zeros((16, D - 96), F32)], axis=1
        ).astype(BF)
        landed(slab_a.at[pl.ds(0, 192)], sems.at[1])


def copies(pairs, sem):
    for src, dst in pairs:
        pltpu.make_async_copy(src, dst, sem).start()


def landed(buffer, sem):
    pltpu.make_async_copy(buffer, buffer, sem).wait()


def fetch_a(ids, pieces, spots, wqk, wvo, extra, sems):
    b, core = ids[0], ids[2]
    for cflip, m, array, entry in spots:
        src = pieces[array].at[entry]
        c, j = core ^ cflip, b ^ m
        row = pl.multiple_of(j * 96, 96)
        copies([(src.at[pl.ds(0, 96)], wqk.at[c, pl.ds(row, 96)])], sems.at[0])
        copies([(src.at[pl.ds(96, 96)], wvo.at[c, pl.ds(row, 96)])], sems.at[1])
        copies([(src.at[pl.ds(192, 16)], extra.at[c, j])], sems.at[2])


def fetch_wide(ids, pieces, spots, wgu, sems):
    b, y, core = ids[0], ids[1], ids[2]
    for yflip, cflip, m, array, entry in spots:
        src = pieces[array].at[entry]
        c, yy, j = core ^ cflip, y ^ yflip, b ^ m
        row = pl.multiple_of(j * 96, 96)
        for k in range(4):
            tile = wgu.at[c, yy, pl.ds(row, 96), pl.ds(k * 256, 256)]
            copies([(src.at[pl.ds(k * 96, 96)], tile)], sems.at[2 * yy + c])


def fetch_deep(ids, pieces, spots, wd, sem):
    b, y, core = ids[0], ids[1], ids[2]
    for yflip, cflip, m, array, entry in spots:
        src = pieces[array].at[entry]
        low = pl.multiple_of((b ^ m) * 256 + (2 * (y ^ yflip) + (core ^ cflip)) * 64, 64)
        for k in range(3):
            tile = wd.at[pl.ds(low, 64), pl.ds(k * 256, 256)]
            copies([(src.at[pl.ds(384 + k * 64, 64)], tile)], sem)


def head_masks():
    low_lane = lax.broadcasted_iota(jnp.int32, (DLEN, DLEN), 1) < DH
    return low_lane


def both_heads(pair, low_lane):
    zero = jnp.zeros_like(pair)
    return jnp.concatenate(
        [jnp.where(low_lane, pair, zero), jnp.where(low_lane, zero, pair)], axis=0
    )


PAIRS_OF_HEADS = [
    (m, p, slice(m * DLEN, (m + 1) * DLEN), slice(p * DLEN, (p + 1) * DLEN))
    for m in range(MICRO)
    for p in range(H // 2)
]


def attention_forward_kernel(direct, spots, ids, x, mask, onehot, *refs):
    if direct:
        count = 1 + max(spot[2] for spot in spots)
        pieces, refs = refs[:count], refs[count:]
        qkv, attended, weights, first, n1, n2, gains, wproj, wqk_out, wvo_out = refs[:10]
        wqk, wvo, extra, bias, scores, sems = refs[10:]
        fetch_a(ids, pieces, spots, wqk, wvo, extra, sems)
        ids[4]()
        landed(extra, sems.at[2])
        lane = lax.broadcasted_iota(jnp.int32, (8, D), 1)
        all_gains = jnp.zeros((8, D), F32)
        flat = jnp.zeros((8, D), F32)
        for j in range(SHARDS):
            block = extra[1, j].astype(F32)
            all_gains += pltpu.roll(jnp.where(lane < 96, block[0:8], 0.0), j * 96, 1)
            flat += pltpu.roll(jnp.where(lane < 48, block[8:16], 0.0), j * 48, 1)
            for k in range(6):
                wproj[j * 96 + k * 16 : j * 96 + (k + 1) * 16, :] = extra[
                    0, j, :, k * DLEN : (k + 1) * DLEN
                ]
        gains[...] = all_gains
        ids[5](6, 7)
        flat = flat[0:1, : BUCKETS * H]
    else:
        ids[4]()
        gains, flat_in, wqk, wvo = refs[:4]
        qkv, attended, weights, first, n1, n2, bias, scores = refs[4:]
        flat = flat_in[...].astype(F32)
    entry = lax.broadcasted_iota(jnp.int32, (16, BUCKETS * H), 1)
    head = lax.broadcasted_iota(jnp.int32, (16, BUCKETS * H), 0)
    by_head = jnp.where(entry % H == head, jnp.broadcast_to(flat, entry.shape), 0.0)
    offsets = dot(by_head.astype(BF), onehot[...])
    for h in range(H):
        row = jnp.broadcast_to(offsets[h : h + 1, :], (DLEN, 2 * DLEN))
        rolled = pltpu.roll(row, DLEN + 1, 1, stride=1, stride_axis=0)
        bias[h // 2, (h % 2) * DLEN : (h % 2 + 1) * DLEN, :] = rolled[:, :DLEN]
    tokens = x[...].astype(F32)
    normed = (tokens * norm_scale(tokens) * gains[0:1, :]).astype(BF)
    n1[...] = normed
    if direct:
        landed(wqk, sems.at[0])
        copies([(wqk, wqk_out)], sems.at[0])
        landed(wvo, sems.at[1])
        copies([(wvo, wvo_out)], sems.at[1])
    qkv[0] = dot(normed, wqk[0]).astype(BF)
    qkv[1] = dot(normed, wqk[1]).astype(BF)
    qkv[2] = dot(normed, wvo[0]).astype(BF)
    ids[5](0, 4)
    low_lane = head_masks()
    for i, (m, p, rows, lanes) in enumerate(PAIRS_OF_HEADS):
        scores[i] = dot_nt(both_heads(qkv[0, rows, lanes], low_lane), qkv[1, rows, lanes])
    for i, (m, p, rows, lanes) in enumerate(PAIRS_OF_HEADS):
        hidden = jnp.concatenate([mask[m], mask[m]], axis=0)
        biased = scores[i] + bias[p] + hidden
        shifted = jnp.exp(biased - jnp.max(biased, axis=-1, keepdims=True))
        weights[m, p] = (shifted / jnp.sum(shifted, axis=-1, keepdims=True)).astype(BF)
    ids[5](2)
    for i, (m, p, rows, lanes) in enumerate(PAIRS_OF_HEADS):
        mixed = dot(weights[m, p], qkv[2, rows, lanes])
        attended[rows, lanes] = jnp.where(low_lane, mixed[:DLEN], mixed[DLEN:]).astype(BF)
    ids[5](1)
    x1 = tokens + dot(attended[...], wvo[1])
    first[...] = x1
    ids[5](3)
    n2[...] = (x1 * norm_scale(x1) * gains[1:2, :]).astype(BF)
    if direct:
        landed(wqk, sems.at[0])
        landed(wvo, sems.at[1])


def gelu_parts(gate):
    c0, c1 = math.sqrt(2.0 / math.pi), 0.044715
    square = gate * gate
    bent = jnp.tanh(c0 * gate * (1.0 + c1 * square))
    value = 0.5 * gate * (1.0 + bent)
    slope = 0.5 * (1.0 + bent) + 0.5 * gate * (1.0 - bent * bent) * (
        c0 * (1.0 + 3.0 * c1 * square)
    )
    return value, slope


def ffn_forward_kernel(direct, spots, ids, first, n2, gains, wproj, *refs):
    if direct:
        count = 1 + max(spot[3] for spot in spots)
        pieces, refs = refs[:count], refs[count:]
        second, n3, vectors, gelu_out, slope_out, hidden_out = refs[1:7]
        wgu, wd, gelu_kept, slope_kept, hidden, sems = refs[7:]
        fetch_wide(ids, pieces, spots, wgu, sems)
    else:
        wgu, wd, second, n3, vectors, gelu_kept, slope_kept, hidden = refs
    ids[4]()
    normed = n2[...]
    for step in range(2):
        half = (ids[1] ^ step) if direct else step
        if direct:
            landed(wgu.at[0, half], sems.at[2 * half])
            landed(wgu.at[1, half], sems.at[2 * half + 1])
        gate = dot(normed, wgu[0, half])
        up = dot(normed, wgu[1, half])
        value, slope = gelu_parts(gate)
        gelu_kept[half] = value.astype(BF)
        slope_kept[half] = (up * slope).astype(BF)
        hidden[half] = (value * up).astype(BF)
        if direct and step == 0:
            fetch_deep(ids, pieces, spots, wd, sems.at[4])
        if direct:
            copies([(gelu_kept.at[half], gelu_out.at[half])], sems.at[2 * half])
            copies([(slope_kept.at[half], slope_out.at[half])], sems.at[2 * half + 1])
    if direct:
        landed(wd, sems.at[4])
        copies([(hidden, hidden_out)], sems.at[4])
    total = first[...] + dot(hidden[0], wd[:HALF, :]) + dot(hidden[1], wd[HALF:, :])
    second[...] = total
    ids[5](0)
    normed_three = (total * norm_scale(total) * gains[2:3, :]).astype(BF)
    n3[...] = normed_three
    ids[5](1)
    vectors[...] = dot(normed_three, wproj[...]).astype(BF)
    if direct:
        for half in range(2):
            landed(gelu_kept.at[half], sems.at[2 * half])
            landed(slope_kept.at[half], sems.at[2 * half + 1])
        landed(hidden, sems.at[4])


def count_kernel(ids, picks, counts):
    spots = lax.broadcasted_iota(jnp.int32, (DLEN, DLEN), 0)

    def one(j):
        for m in range(MICRO):
            total = jnp.zeros((DLEN, DLEN), F32)
            for t in range(picks.shape[2]):
                total += jnp.where(spots == picks[m, j, t : t + 1, :], 1.0, 0.0)
            counts[m, j] = total

    steps(picks.shape[1], one)


def block_of(others, m):
    return others[m % 2].at[m // 2] if len(others) == 2 else others[0].at[m]


def group_sums(values):
    lane = lax.broadcasted_iota(jnp.int32, values.shape, 1)
    shift = 1
    while shift < QLEN:
        ahead = pltpu.roll(values, DLEN - shift, 1)
        behind = pltpu.roll(values, shift, 1)
        values = values + jnp.where((lane & shift) == 0, ahead, behind)
        shift *= 2
    return values


def similarity_kernel(direct, count, ids, own, counts, share, *refs):
    others, (soft, score, best) = refs[:-3], refs[-3:]
    b, is_query = ids[0], ids[3]
    scale = DLEN**-0.5

    def one(m):
        j = (b ^ m) if direct else m
        for micro in range(MICRO):
            rows = slice(micro * DLEN, (micro + 1) * DLEN)
            mine, theirs = own[0, rows, :], block_of(others, m)[rows, :]
            doc = jnp.where(is_query == 1, theirs, mine)
            query = jnp.where(is_query == 1, mine, theirs)
            times = counts[micro, j]
            sim = dot_nt(doc, query) * scale
            peak = jnp.max(jnp.where(times > 0, sim, -jnp.inf), axis=0, keepdims=True)
            mass = jnp.where(times > 0, times * jnp.exp(jnp.minimum(sim - peak, 0.0)), 0.0)
            total = jnp.sum(mass, axis=0, keepdims=True)
            soft[micro, j] = mass / total
            best[micro, pl.ds(j, 1), :] = peak + jnp.log(total)

    steps(count, one)
    for micro in range(MICRO):
        score[micro] = group_sums(best[micro] * share[micro])


def vector_grad_kernel(
    direct, count, ids, soft, share, sharp, target, score, scores, *refs
):
    others, (grad, weight, total) = refs[:-3], refs[-3:]
    b, is_query = ids[0], ids[3]
    scale = DLEN**-0.5

    @pl.when(is_query == 1)
    def _():
        for micro in range(MICRO):
            logits = score[micro] * sharp[micro]
            raised = jnp.exp(logits - jnp.max(logits, axis=0, keepdims=True))
            odds = raised / jnp.sum(raised, axis=0, keepdims=True)
            doc = lax.broadcasted_iota(jnp.int32, (count, DLEN), 0)
            hit = jnp.where(target[micro] == doc, 1.0, 0.0)
            weight[micro] = (odds - hit) * sharp[micro] * share[micro] * scale

    @pl.when(is_query == 0)
    def _():
        for micro in range(MICRO):
            sharpness = sharp[micro]
            logits = scores[:, micro] * sharpness[None]
            peak = jnp.max(logits, axis=0)
            norm = jnp.sum(jnp.exp(logits - peak[None]), axis=0)
            odds = jnp.exp(score[micro] * sharpness - peak) / norm
            hit = jnp.where(target[micro] == b, 1.0, 0.0)
            weight[micro] = (odds - hit) * sharpness * share[micro] * scale

    def parts(m, micro):
        j = (b ^ m) if direct else m
        dense = soft[micro, j] * weight[micro, pl.ds(j, 1), :]
        upper = dense.astype(BF)
        lower = (dense - upper.astype(F32)).astype(BF)
        return upper, lower, block_of(others, m)[micro * DLEN : (micro + 1) * DLEN, :]

    for flag, product in ((1, dot_tn), (0, dot)):

        @pl.when(is_query == flag)
        def _():
            for micro in range(MICRO):
                rows = slice(micro * DLEN, (micro + 1) * DLEN)
                if count <= 16:
                    sums = []
                    for m in range(count):
                        upper, lower, theirs = parts(m, micro)
                        sums.append(product(upper, theirs) + product(lower, theirs))
                    grad[rows, :] = sum(sums[1:], sums[0]).astype(BF)
                else:
                    total[rows, :] = jnp.zeros((DLEN, DLEN), F32)

                    @pl.loop(0, count)
                    def _(m):
                        upper, lower, theirs = parts(m, micro)
                        total[rows, :] += product(upper, theirs) + product(lower, theirs)

                    grad[rows, :] = total[rows, :].astype(BF)


def ffn_backward_kernel(direct, spots, ids, dvec, second, n2, n3, gains, wproj, *refs):
    if direct:
        hidden_in, gelu_in, slope_in = refs[:3]
        count = 1 + max(spot[3] for spot in spots)
        pieces, refs = refs[3 : 3 + count], refs[3 + count :]
        dx2_out, grad_proj, grad_gain, dgu, *outs = refs[:10]
        wd, hidden, gelu_kept, slope_kept, grad_down, quarters, sems = refs[10:]
        fetch_deep(ids, pieces, spots, wd, sems.at[0])
        copies([(slope_in, slope_kept)], sems.at[1])
        copies([(gelu_in, gelu_kept)], sems.at[2])
        copies([(hidden_in, hidden)], sems.at[3])
    else:
        wd, hidden, gelu_kept, slope_kept, dx2_out, grad_proj, grad_gain, dgu, dy_out = refs
    b, y, core, _, ready, send = ids
    ready()
    dvectors = dvec[...]
    dn3 = dot_nt(dvectors, wproj[...])
    dx2, dgain3 = norm_backward(second[...], gains[2:3, :], dn3)
    dx2_out[...] = dx2
    grad_gain[...] = dgain3
    grad_proj[...] = dot_tn(n3[...], dvectors)
    send(0, 1, 2)
    dy = dx2.astype(BF)
    if direct:
        landed(wd, sems.at[0])
    dh = dot_nt(dy, wd[...])
    if direct:
        landed(slope_kept, sems.at[1])
        landed(gelu_kept, sems.at[2])
    for half in range(2):
        part = dh[:, half * HALF : (half + 1) * HALF]
        dgu[0, half] = (part * slope_kept[half].astype(F32)).astype(BF)
        dgu[1, half] = (part * gelu_kept[half].astype(F32)).astype(BF)
    send(3)
    if not direct:
        dy_out[...] = dy
        return
    landed(hidden, sems.at[3])
    normed = n2[...]
    wide_rows, deep_rows = pl.ds(0, 384), pl.ds(384, 192)

    def leave(place, rows):
        if place % 2:
            for group, out in zip(GROUPS_F, outs[1 + place : 3 + place]):
                for i, m in enumerate(group):
                    copies([(quarters.at[place, m, rows], out.at[i, rows])], sems.at[place])
        else:
            copies([(quarters.at[place, :, rows], outs[place // 2].at[:, rows])], sems.at[place])

    for place in (3, 2, 1, 0):
        c, yy = core ^ (place // 2), y ^ (place % 2)
        piece = dot_tn(normed, dgu[c, yy]).astype(BF)
        for j in range(SHARDS):
            for k in range(4):
                quarters[place, b ^ j, k * 96 : (k + 1) * 96, :] = piece[
                    j * 96 : (j + 1) * 96, k * 256 : (k + 1) * 256
                ]
        leave(place, wide_rows)
    for j in range(SHARDS):
        start = (j % 4) * 256
        down = dot_tn(hidden[j // 4, :, start : start + 256], dy).astype(BF)
        for part in range(4):
            grad_down[j, part] = down[part * 64 : (part + 1) * 64, :]
    for place in (3, 2, 1, 0):
        c, yy = core ^ (place // 2), y ^ (place % 2)
        for j in range(SHARDS):
            down = grad_down[j, 2 * yy + c]
            for k in range(3):
                quarters[place, b ^ j, 384 + k * 64 : 384 + (k + 1) * 64, :] = down[
                    :, k * 256 : (k + 1) * 256
                ]
        leave(place, deep_rows)
    for place in range(4):
        landed(quarters.at[place], sems.at[place])


def middle_backward_kernel(direct, spots, ids, dx2, first, dgu, gains, *refs):
    if direct:
        count = 1 + max(spot[3] for spot in spots)
        pieces, refs = refs[:count], refs[count:]
        wvo_in, dx1_out, dattended, grad_gain, wgu, wout, sems = refs
        fetch_wide(ids, pieces, spots, wgu, sems)
        copies([(wvo_in.at[1], wout)], sems.at[4])
    else:
        wgu, wvo, dx1_out, dattended, grad_gain = refs
        wout = wvo.at[1]
    ids[4]()
    dn2 = jnp.zeros((ROWS, D), F32)
    for half in range(2):
        for c in range(2):
            if direct:
                landed(wgu.at[c, half], sems.at[half * 2 + c])
            dn2 = dn2 + dot_nt(dgu[c, half], wgu[c, half])
    back, dgain2 = norm_backward(first[...], gains[1:2, :], dn2)
    dx1 = dx2[...] + back
    dx1_out[...] = dx1
    grad_gain[...] = dgain2
    ids[5](0, 2)
    if direct:
        landed(wout, sems.at[4])
    dattended[...] = dot_nt(dx1.astype(BF), wout[...]).astype(BF)


def attention_backward_kernel(
    direct,
    ids,
    grad_first,
    dattended,
    x,
    n1,
    attended,
    weights,
    qkv,
    gains,
    bucket,
    grad_proj,
    grad_gain2,
    grad_gain3,
    *refs,
):
    if direct:
        wqk_in, wvo_in, grad_in, *outs = refs[:7]
        wqk, wvo, own, other, left, right, dqk, extra, *refs = refs[7:]
        copies([(wvo_in.at[0], wvo.at[0])], refs[-1].at[0])
        copies([(wqk_in, wqk)], refs[-1].at[1])
    else:
        wqk, wvo, small, grad_in, dqkv_out, da_out, left, right, dqk, *refs = refs
    diag, bias_grad, dshares, scaled, queries, douts, *rest = refs
    b, core = ids[0], ids[2]
    ids[4]()
    dx1 = grad_first[...]
    da = dx1.astype(BF)
    low_lane = head_masks()
    row_at = lax.broadcasted_iota(jnp.int32, (DLEN, MICRO * DLEN), 0)
    lane_at = lax.broadcasted_iota(jnp.int32, (DLEN, MICRO * DLEN), 1)
    mirror = jnp.where(row_at == DLEN - 1 - lane_at % DLEN, 1.0, 0.0).astype(BF)
    diag[...] = jnp.zeros_like(diag)
    for i, (m, p, rows, lanes) in enumerate(PAIRS_OF_HEADS):
        queries[i] = both_heads(qkv[0, rows, lanes], low_lane)
        douts[i] = both_heads(dattended[rows, lanes], low_lane)
    for i, (m, p, rows, lanes) in enumerate(PAIRS_OF_HEADS):
        dshares[i] = dot_nt(douts[i], qkv[2, rows, lanes])
        right[0, rows, lanes] = dot_tn(weights[m, p], douts[i]).astype(BF)
    for i, (m, p, rows, lanes) in enumerate(PAIRS_OF_HEADS):
        wide = weights[m, p].astype(F32)
        dshare = dshares[i]
        centre = jnp.sum(wide * dshare, axis=-1, keepdims=True)
        scaled[i] = (wide * (dshare - centre)).astype(BF)
    for i, (m, p, rows, lanes) in enumerate(PAIRS_OF_HEADS):
        dq = dot(scaled[i], qkv[1, rows, lanes])
        dqk[0, rows, lanes] = jnp.where(low_lane, dq[:DLEN], dq[DLEN:]).astype(BF)
        dqk[1, rows, lanes] = dot_tn(scaled[i], queries[i]).astype(BF)
    for h in range(H):
        part = slice((h % 2) * DLEN, (h % 2 + 1) * DLEN)
        both = jnp.concatenate([scaled[m * (H // 2) + h // 2, part] for m in range(MICRO)], axis=0)
        turned = dot(mirror, both)
        wider = jnp.concatenate([turned, jnp.zeros_like(turned)], axis=1)
        rolled = pltpu.roll(wider, 0, 1, stride=1, stride_axis=0)
        diag[h : h + 1, :] = jnp.sum(rolled, axis=0, keepdims=True)
    bias_grad[...] = lax.dot_general(
        bucket[...],
        diag[...],
        (((1,), (1,)), ((), ())),
        precision=HIGHEST,
        preferred_element_type=F32,
    )
    if direct:
        sems = rest[0]
        landed(wvo.at[0], sems.at[0])
        landed(wqk, sems.at[1])
    dn1 = dot_nt(dqk[0], wqk[0]) + dot_nt(dqk[1], wqk[1]) + dot_nt(right[0], wvo[0])
    dx, dgain1 = norm_backward(x[...].astype(F32), gains[0:1, :], dn1)
    grad_in[...] = dx1 + dx
    if direct:
        ids[5](0)
    right[1] = da
    left[0] = n1[...]
    left[1] = attended[...]
    all_gains = jnp.concatenate(
        [dgain1, grad_gain2[...], grad_gain3[...], jnp.zeros((5, D), F32)], axis=0
    )
    if not direct:
        small[0:8, :] = all_gains
        small[8:40, :] = jnp.concatenate(
            [bias_grad[...], jnp.zeros((BUCKETS, D - DLEN), F32)], axis=1
        )
        dqkv_out[0] = dqk[0]
        dqkv_out[1] = dqk[1]
        dqkv_out[2] = right[0]
        da_out[...] = da
        return
    per_shard = BUCKETS // SHARDS
    for j in range(SHARDS):
        for k in range(6):
            extra[0, j, :, k * DLEN : (k + 1) * DLEN] = grad_proj[
                j * 96 + k * 16 : j * 96 + (k + 1) * 16, :
            ]
        extra[1, j] = jnp.zeros((16, D), F32)
        extra[1, j, 0:8, :] = pltpu.roll(all_gains, (D - j * 96) % D, 1)
        extra[1, j, 8 : 8 + per_shard, 0:DLEN] = bias_grad[j * per_shard : (j + 1) * per_shard, :]
    for flip, out in ((1, other), (0, own)):
        c = core ^ flip
        top = dot_tn(n1[...], dqk[c]).astype(BF)
        bottom = dot_tn(left[c], right[c]).astype(BF)
        for j in range(SHARDS):
            m = b ^ j
            out[m, 0:96, :] = top[j * 96 : (j + 1) * 96, :]
            out[m, 96:192, :] = bottom[j * 96 : (j + 1) * 96, :]
            out[m, 192:208, :] = extra[c, j].astype(BF)
        for group, target in zip((FIRST_A, REST_A), outs[2 * flip : 2 * flip + 2]):
            copies([(out.at[m], target.at[i]) for i, m in enumerate(group)], sems.at[flip])
    landed(other, sems.at[1])
    landed(own, sems.at[0])


def finish_wide_kernel(ids, near, far, twin, far_twin, token, grad_g, grad_u, grad_d):
    y, core = ids[1], ids[2]
    for yy in range(2):
        for c in range(2):

            @pl.when((y == yy) & (core == c))
            def _():
                for yflip, cflip, part in ((0, 0, near), (1, 0, far), (0, 1, twin), (1, 1, far_twin)):
                    half, rank = yy ^ yflip, c ^ cflip
                    out = grad_u if rank else grad_g
                    for k in range(4):
                        start = half * HALF + k * 256
                        out[:, start : start + 256] = part[0, k * 96 : (k + 1) * 96, :].astype(F32)
                    low = (2 * half + rank) * 64
                    for k in range(3):
                        grad_d[low : low + 64, k * 256 : (k + 1) * 256] = part[
                            0, 384 + k * 64 : 384 + (k + 1) * 64, :
                        ].astype(F32)


def finish_narrow_kernel(
    ids, near, near_far, twin, twin_far, grad_q, grad_k, grad_v, grad_o, grad_p, grad_1, grad_2, grad_3, table
):
    core = ids[2]
    for c in range(2):

        @pl.when(core == c)
        def _():
            pairs = [(near, near_far), (twin, twin_far)]
            low, high = pairs[::-1] if c else pairs

            def summed(pair, rows):
                return pair[0][0, rows, :].astype(F32) + pair[1][0, rows, :].astype(F32)

            grad_q[...] = summed(low, slice(0, 96))
            grad_k[...] = summed(high, slice(0, 96))
            grad_v[...] = summed(low, slice(96, 192))
            grad_o[...] = summed(high, slice(96, 192))
            packed = summed(low, slice(192, 208))
            for k in range(6):
                grad_p[k * 16 : (k + 1) * 16, :] = packed[:, k * DLEN : (k + 1) * DLEN]
            rows = summed(high, slice(192, 208))
            grad_1[...] = rows[0:1, :96]
            grad_2[...] = rows[1:2, :96]
            grad_3[...] = rows[2:3, :96]
            block = jnp.where(lax.broadcasted_iota(jnp.int32, (8, DLEN), 1) < H, rows[8:16, :DLEN], 0.0)
            line = block[0:1]
            for i in range(1, BUCKETS // SHARDS):
                line += pltpu.roll(block, i * H, 1)[i : i + 1]
            table[...] = line[:, : BUCKETS // SHARDS * H]


def local(
    hidden_in,
    norm1_gain,
    w_query,
    w_key,
    w_value,
    w_out,
    rel_table,
    norm2_gain,
    w_gate,
    w_up,
    w_down,
    norm3_gain,
    w_proj,
    query_lengths,
    keyword_request_mask,
    targets,
    candidates,
):
    streams = lax.axis_size("stream")
    shards = lax.axis_size("batch")
    pairs = streams // 2
    direct = shards == SHARDS and pairs == 2
    b = lax.axis_index("batch")
    s = lax.axis_index("stream")
    y, core = s // pairs, s % pairs
    is_query = s < pairs

    def swap(block, yflip, cflip, m):
        route = []
        for source in range(streams):
            target = ((source // pairs) ^ yflip) * pairs + ((source % pairs) ^ cflip)
            for j in range(shards):
                route.append((source * shards + j, target * shards + (j ^ m)))
        return lax.ppermute(block, EVERY, route)

    micro_count = hidden_in.shape[0]
    slot = jnp.arange(DLEN)
    pair_lengths = lax.dynamic_index_in_dim(query_lengths, core, 1, keepdims=False)
    pair_keyword = lax.dynamic_index_in_dim(keyword_request_mask, core, 1, keepdims=False)
    pair_targets = lax.dynamic_index_in_dim(targets, core, 1, keepdims=False)

    def by_slot(values):
        blocks = values.reshape(micro_count, shards, GROUPS)
        own = lax.dynamic_slice_in_dim(blocks, b, 1, 1)
        blocks = jnp.where(is_query, jnp.broadcast_to(own, blocks.shape), blocks)
        return jnp.repeat(blocks, QLEN, axis=2)

    length_slots = by_slot(pair_lengths)
    valid_slots = (slot % QLEN)[None, None, :] < length_slots
    share = jnp.where(valid_slots, 1.0 / length_slots.astype(F32), 0.0)
    sharp = jnp.where(by_slot(pair_keyword) == 1, 20.0, 10.0).astype(F32)
    target_slots = by_slot(pair_targets)
    own_valid = lax.dynamic_slice_in_dim(valid_slots, b, 1, 1)
    same = (slot[:, None] // QLEN) == (slot[None, :] // QLEN)
    mask = jnp.where(is_query & ~(same[None] & own_valid), -1000000000.0, 0.0).astype(F32)

    small = 16 if direct else 48
    picked = lax.dynamic_index_in_dim(candidates, core, 1, keepdims=False)[:, 0]
    picked = picked.reshape(micro_count, shards, DLEN, picked.shape[-1])
    picked = jnp.transpose(picked, (0, 1, 3, 2))
    received = lax.all_to_all(picked, "batch", split_axis=1, concat_axis=1, tiled=True)
    picks = jnp.where(is_query, received, picked)
    (counts,) = call(
        count_kernel,
        "count",
        [picks],
        [((micro_count, shards, DLEN, DLEN), F32)],
        limit=small,
    )

    fence = lax.optimization_barrier
    first_core = core == 0
    spots_a = spots_f = None
    if direct:
        lines = [part.reshape(1, -1) for part in (norm1_gain, norm2_gain, norm3_gain, rel_table)]
        slab_a, slab_f = call(
            pack_kernel,
            "pack",
            lines,
            [((PIECE_A, D), BF), ((PIECE_F, 256), BF)],
            far=[w_query, w_key, w_value, w_out, w_gate, w_up, w_down, w_proj],
            sems=2,
            lazy=True,
        )

        def join(*parts):
            return jnp.concatenate(parts)

        def along_x(part):
            return swap(part, 0, 0, 1)

        def along_y(part):
            return swap(part, 1, 0, 0)

        def along_z(part):
            return swap(part, 0, 0, 2)

        def along_zz(part):
            return swap(part, 0, 0, 4)

        def other_core(part):
            return swap(part, 0, 1, 0)

        f0, a0 = slab_f[None], slab_a[None]
        token = jnp.zeros((8, DLEN), F32)
        f4, f2, y0, f1, a1 = along_zz(f0), along_z(f0), along_y(f0), along_x(f0), along_x(a0)
        token = tick(token)
        f4, f2, y0, f1, a1, a0, token = fence((f4, f2, y0, f1, a1, a0, token))
        f42, f142, token = fence((join(f4, f2), join(f1, f4, f2), token))
        y142, f53, f6, a4, a2 = (
            along_y(f142),
            along_x(f42),
            along_z(f4),
            along_zz(a0),
            along_z(a0),
        )
        token = tick(token)
        f53, f6, counts, mask, share, sharp, target_slots, token = fence(
            (f53, f6, counts, mask, share, sharp, target_slots, token)
        )
        f65, token = fence((join(f6, f53[0:1]), token))
        f7 = along_x(f6)

        a2, token = fence((a2, token))
        a3 = along_x(a2)
        a4, token = fence((a4, token))
        a5, a6 = along_x(a4), along_z(a4)

        y142, f65, token = fence((y142, f65, token))
        y65 = along_y(f65)

        f7, token = fence((f7, token))
        f37, f_all, token = fence((join(f53[1:2], f7), join(f0, f142, f65, f53[1:2], f7), token))
        f_all, token = fence((f_all, token))
        tf_all = other_core(f_all)

        a6, token = fence((a6, token))
        a7 = along_x(a6)
        a0142, token = fence((join(a0, a1, a4, a2), token))
        ta0142 = other_core(a0142)
        y65, f37, token = fence((y65, f37, token))
        y37, ty65 = along_y(f37), other_core(y65)
        token = tick(token)
        a3, a5, tf_all, ta0142, token = fence((a3, a5, tf_all, ta0142, token))
        a536, y_first, token = fence((join(a5, a3, a6), join(y0, y142), token))
        ta536, ty_first = other_core(a536), other_core(y_first)
        a7, token = fence((a7, token))
        ta7 = other_core(a7)
        token = tick(token)
        y37, ta536, ta7, token = fence((y37, ta536, ta7, token))
        ty37 = other_core(y37)

        order_f = (0, 1, 4, 2, 6, 5, 3, 7)
        groups_a = [
            (0, (a0142, (0, 1, 4, 2)), (a536, (5, 3, 6)), (a7, (7,))),
            (1, (ta0142, (0, 1, 4, 2)), (ta536, (5, 3, 6)), (ta7, (7,))),
        ]
        pieces_a, spots_a, pieces_f, spots_f = [], [], [], []
        for cflip, *group in groups_a:
            for part, flips in group:
                spots_a += [(cflip, m, len(pieces_a), i) for i, m in enumerate(flips)]
                pieces_a.append(part)
    else:

        def whole(part):
            return lax.all_gather(part, "batch", axis=0, tiled=True)

        wqk = jnp.stack([whole(w_query), whole(w_key)])
        wvo = jnp.stack([whole(w_value), whole(w_out)])
        gate_up = jnp.stack([whole(w_gate), whole(w_up)])
        wgu = jnp.transpose(gate_up.reshape(2, D, 2, HALF), (0, 2, 1, 3))
        wd = whole(w_down)
        wproj = whole(w_proj)
        gain_rows = [whole(gain) for gain in (norm1_gain, norm2_gain, norm3_gain)]
        gains = jnp.pad(jnp.stack(gain_rows).astype(F32), ((0, 5), (0, 0)))
        table = whole(rel_table).reshape(1, BUCKETS * H)

    onehot = bucket_onehot()
    by_entry = jnp.asarray(np.repeat(onehot.T, H, axis=0), BF)
    x = hidden_in[:, 0].reshape(ROWS, D)
    row_bf, row_f32 = ((ROWS, D), BF), ((ROWS, D), F32)
    qkv_shape, weight_shape = ((3, ROWS, D), BF), ((MICRO, H // 2, ROWS, DLEN), BF)
    pair_weights = ((2, D, D), BF)
    gain_rows = ((8, D), F32)
    proj_shape = ((D, DLEN), BF)
    kept = [qkv_shape, row_bf, weight_shape, row_f32, row_bf, row_bf]
    bias_shape, score_shape = ((H // 2, ROWS, DLEN), F32), ((H, ROWS, DLEN), F32)
    result = call(
        functools.partial(attention_forward_kernel, direct, spots_a),
        "attention_forward",
        [x, mask, by_entry] + ([] if direct else [gains, table, wqk, wvo]),
        kept + ([gain_rows, proj_shape] if direct else []),
        ([pair_weights, pair_weights, ((2, SHARDS, 16, D), BF)] if direct else [])
        + [bias_shape, score_shape],
        far=pieces_a if direct else [],
        far_outs=[pair_weights, pair_weights] if direct else [],
        sems=3 if direct else 0,
        flops=2 * ROWS * D * D * 4,
        lazy=True,
    )
    qkv, attended, weights, first, n1, n2 = result[:6]
    if direct:
        gains, wproj, wqk, wvo = result[6:]
    first, counts, share, sharp, target_slots = fence((first, counts, share, sharp, target_slots))
    if direct:
        ty_first, ty65, ty37, first, token = fence((ty_first, ty65, ty37, first, token))
        near, twin = ((f_all, order_f),), ((tf_all, order_f),)
        far = ((y_first, order_f[:4]), (y65, order_f[4:6]), (y37, order_f[6:]))
        far_twin = ((ty_first, order_f[:4]), (ty65, order_f[4:6]), (ty37, order_f[6:]))
        for yflip, cflip, group in ((0, 0, near), (0, 1, twin), (1, 0, far), (1, 1, far_twin)):
            for part, flips in group:
                spots_f += [(yflip, cflip, m, len(pieces_f), i) for i, m in enumerate(flips)]
                pieces_f.append(part)
    wide_bf = ((2, ROWS, HALF), BF)
    wgu_shape, wd_shape = ((2, 2, D, HALF), BF), ((FF, D), BF)
    lasting = [wide_bf, wide_bf, wide_bf]
    result = call(
        functools.partial(ffn_forward_kernel, direct, spots_f),
        "ffn_forward",
        [first, n2, gains, wproj] + ([] if direct else [wgu, wd]),
        [row_f32, row_bf, ((ROWS, DLEN), BF)] + ([] if direct else lasting),
        [wgu_shape, wd_shape] + lasting if direct else [],
        far=[*pieces_f, token] if direct else [],
        far_outs=lasting if direct else [],
        sems=5 if direct else 0,
        flops=2 * ROWS * D * FF * 3,
        lazy=True,
    )
    second, n3, vectors, gelu_kept, slope_kept, hidden = result

    if direct:
        even = jnp.stack([swap(vectors, 1, 0, m) for m in (0, 2, 4, 6)])
        odd = swap(even, 0, 0, 1)
        own, odd = fence((jnp.stack([vectors, vectors]), odd))
        others = [even, odd]
    else:
        route = [(i, (i + pairs) % streams) for i in range(streams)]
        arrived = lax.ppermute(vectors, "stream", route)
        others = [lax.all_gather(arrived, "batch", axis=0)]
    block_f32 = ((micro_count, shards, DLEN, DLEN), F32)
    line_f32 = ((micro_count, shards, DLEN), F32)
    soft, score = call(
        functools.partial(similarity_kernel, direct, shards),
        "similarity",
        [own if direct else vectors[None], counts, share, *others],
        [block_f32, line_f32],
        [line_f32],
        limit=small,
        near=True,
    )
    if direct:
        blocks = jnp.broadcast_to(score[None], (shards,) + score.shape)
        scores = lax.all_to_all(blocks, "batch", split_axis=0, concat_axis=0, tiled=True)
    else:
        scores = lax.all_gather(score, "batch", axis=0)
    (dvec,) = call(
        functools.partial(vector_grad_kernel, direct, shards),
        "vector_grad",
        [soft, share, sharp, target_slots, score, scores, *others],
        [((ROWS, DLEN), BF)],
        [line_f32, ((ROWS, DLEN), F32)],
        limit=small,
        near=True,
    )

    gain_row = ((1, D), F32)
    proj_f32 = ((D, DLEN), F32)
    dgu_shape = ((2, 2, ROWS, HALF), BF)
    quarter = ((SHARDS, PIECE_F, 256), BF)
    saved = [hidden, gelu_kept, slope_kept]
    result = call(
        functools.partial(ffn_backward_kernel, direct, spots_f),
        "ffn_backward",
        [dvec, second, n2, n3, gains, wproj] + ([] if direct else [wd, *saved]),
        [row_f32, proj_f32, gain_row, dgu_shape] + ([] if direct else [row_bf]),
        [wd_shape, wide_bf, wide_bf, wide_bf, ((SHARDS, 4, 64, D), BF), ((4, *quarter[0]), BF)]
        if direct
        else [],
        far=[*saved, *pieces_f] if direct else [],
        far_outs=[quarter] * 2 + [((4, PIECE_F, 256), BF)] * 4 if direct else [],
        sems=4 if direct else 0,
        flops=2 * ROWS * D * FF * 4,
        lazy=True,
    )
    dx2, grad_proj, grad_gain, dgu = result[:4]
    if direct:
        f_own, f_twin, *f_far = result[4:]
    else:
        dy = result[4]

    if direct:
        def own_f(m, *more):
            group = 0 if m in GROUPS_F[0] else 1
            return [(base_f[group], GROUPS_F[group].index(m)), *more]

        def far_sum(i):
            return [[(f_far[i], n), (c_far[i], n)] for n in range(4)]

        c_far = [other_core(part) for part in f_far[2:]]
        c_far[0], f_twin, dgu = fence((c_far[0], f_twin, dgu))
        twin = other_core(f_twin)
        (sent_a,) = add_up(far_sum(0))
        sent_a, dgu = fence((sent_a, dgu))
        y_a = along_y(sent_a)
    middle_in = [dx2, first, dgu, gains]
    dx1, dattended, grad_gain2 = call(
        functools.partial(middle_backward_kernel, direct, spots_f),
        "middle_backward",
        middle_in + ([] if direct else [wgu, wvo]),
        [row_f32, row_bf, gain_row],
        [wgu_shape, ((D, D), BF)] if direct else [],
        far=[*pieces_f, wvo] if direct else [],
        sems=5 if direct else 0,
        flops=ROUND_FLOPS,
        lazy=True,
    )
    if direct:
        *c_far[1:], twin, dattended = fence((*c_far[1:], twin, dattended))
        (sent_b,) = add_up(far_sum(1))
        base_f = [base_up(f_own, twin, GROUPS_F[0])]
        sent_b, base_f[0], dattended = fence((sent_b, base_f[0], dattended))
    two_rows = ((2, ROWS, D), BF)
    slab_out = ((SHARDS, PIECE_A, D), BF)
    blocks_bf = ((H, ROWS, DLEN), BF)
    result = call(
        functools.partial(attention_backward_kernel, direct),
        "attention_backward",
        [dx1, dattended, x, n1, attended, weights, qkv, gains, jnp.asarray(onehot.T)]
        + [grad_proj, grad_gain2, grad_gain]
        + ([] if direct else [wqk, wvo]),
        [row_f32] if direct else [((40, D), F32), row_f32, qkv_shape, row_bf],
        ([pair_weights, pair_weights, slab_out, slab_out] if direct else [])
        + [two_rows, two_rows, two_rows]
        + ([((2, SHARDS, 16, D), F32)] if direct else [])
        + [((DLEN, 2 * DLEN), F32), ((BUCKETS, DLEN), F32)]
        + [score_shape, blocks_bf, blocks_bf, blocks_bf],
        far=[wqk, wvo] if direct else [],
        far_outs=[((count, PIECE_A, D), BF) for count in (2, 6, 2, 6)] if direct else [],
        sems=2 if direct else 0,
        flops=2 * ROWS * D * D * 7,
        lazy=True,
    )

    if direct:
        input_grad, o_first, o_rest, a_first, a_rest = result

        def own_a(m, *more):
            return [(base_a, REST_A.index(m)), *more]

        o_first, o_rest, a_first, a_rest = fence((o_first, o_rest, a_first, a_rest))
        token = jnp.ones((8, DLEN), F32)
        c_first = other_core(a_first)
        c_first, a_rest, token = fence((c_first, a_rest, token))
        (out_a37,) = add_up([[(o_first, i), (c_first, i)] for i in range(2)])
        out_a37, a_rest, token = fence((out_a37, a_rest, token))
        xa37, c_rest = along_x(out_a37), other_core(a_rest)

        y_a, sent_b, token = fence((y_a, sent_b, token))
        y_b = along_y(sent_b)
        (out_73,) = add_up([own_f(7, (y_a, 1)), own_f(3, (y_a, 3))])
        out_73, token = fence((out_73, token))
        x73 = along_x(out_73)
        token = tick(token)
        c_rest, token = fence((c_rest, token))
        base_a = base_up(o_rest, c_rest, range(len(REST_A)))
        base_f.append(base_up(f_own, twin, GROUPS_F[1]))
        x73, base_a, base_f[1], token = fence((x73, base_a, base_f[1], token))
        (out_62,) = add_up([own_f(6, (y_a, 0), (x73, 0)), own_f(2, (y_a, 2), (x73, 1))])
        out_62, token = fence((out_62, token))
        z62 = along_z(out_62)

        xa37, token = fence((xa37, token))
        out_a51, out_a62 = add_up(
            [own_a(5), own_a(1)], [own_a(6, (xa37, 1)), own_a(2, (xa37, 0))]
        )
        out_a62, token = fence((out_a62, token))
        za62 = along_z(out_a62)

        y_b, token = fence((y_b, token))
        out_5, out_1 = add_up([own_f(5, (y_b, 1))], [own_f(1, (y_b, 3))])
        out_5, token = fence((out_5, token))
        x5 = along_x(out_5)

        x5, z62, token = fence((x5, z62, token))
        (out_4,) = add_up([own_f(4, (y_b, 0), (x5, 0), (z62, 0))])
        out_4, out_a51, out_1, token = fence((out_4, out_a51, out_1, token))
        x1, xa51, z4 = along_x(out_1), along_x(out_a51), along_zz(out_4)

        za62, xa51, token = fence((za62, xa51, token))
        (out_a4,) = add_up([own_a(4, (xa51, 0), (za62, 0))])
        out_a4, token = fence((out_a4, token))
        za4 = along_zz(out_a4)

        x1, z4, token = fence((x1, z4, token))
        (mine_f,) = add_up([own_f(0, (y_b, 2), (x1, 0), (z62, 1), (z4, 0))])
        mine_f, token = fence((mine_f, token))
        far, twin_f = along_y(mine_f), other_core(mine_f)

        za4, token = fence((za4, token))
        (part_a,) = add_up([own_a(0, (xa51, 1), (za62, 1), (za4, 0))])
        part_a, token = fence((part_a, token))
        ya, twin_part = along_y(part_a), other_core(part_a)

        far, twin_f, token = fence((far, twin_f, token))
        far_twin_f = other_core(far)
        ya, far_twin_f, twin_part, token = fence((ya, far_twin_f, twin_part, token))
        twin_ya = other_core(ya)
        shard_f32, wide_f32 = ((96, D), F32), ((96, FF), F32)
        grad_g, grad_u, grad_d = call(
            finish_wide_kernel,
            "finish_wide",
            [mine_f, far, twin_f, far_twin_f],
            [wide_f32, wide_f32, ((256, D), F32)],
            far=[token],
            limit=24,
            near=True,
        )
        grad_q, grad_k, grad_v, grad_o, grad_p, *small = call(
            finish_narrow_kernel,
            "finish_narrow",
            [part_a, ya, twin_part, twin_ya],
            [shard_f32] * 4 + [((96, DLEN), F32), ((1, 96), F32), ((1, 96), F32), ((1, 96), F32)]
            + [((1, 48), F32)],
            limit=24,
            near=True,
        )
        grad_n1, grad_n2, grad_n3, grad_table = [row.reshape(-1) for row in small]
    else:
        small, input_grad, dqkv, da = result

        def summed(part):
            part = lax.psum_scatter(part, "batch", scatter_dimension=0, tiled=True)
            return lax.psum(part, "stream")

        grad_q, grad_k, grad_v = [summed(dot_tn(n1, dqkv[i])) for i in range(3)]
        grad_o = summed(dot_tn(attended, da))
        grad_g, grad_u = [
            summed(jnp.concatenate([dot_tn(n2, dgu[i, half]) for half in range(2)], axis=1))
            for i in range(2)
        ]
        grad_d = summed(jnp.concatenate([dot_tn(hidden[half], dy) for half in range(2)]))
        grad_p = summed(grad_proj)
        grad_n1, grad_n2, grad_n3 = [summed(small[i]) for i in range(3)]
        flat = lax.psum(small[8 : 8 + BUCKETS, :H].reshape(-1), EVERY)
        share_rows = flat.shape[0] // shards
        grad_table = lax.dynamic_slice_in_dim(flat, b * share_rows, share_rows, 0)

    vectors_out = vectors.reshape(micro_count, DLEN, DLEN)[:, None]
    grad_hidden = input_grad.reshape(micro_count, DLEN, D)[:, None]
    return (
        vectors_out,
        grad_hidden,
        grad_n1,
        grad_q,
        grad_k,
        grad_v,
        grad_o,
        grad_table,
        grad_n2,
        grad_g,
        grad_u,
        grad_d,
        grad_n3,
        grad_p,
    )


def solution(mesh):
    rows, lines = P("batch", None), P("batch")
    spread = P(None, "stream", "batch", None)
    return jax.shard_map(
        local,
        mesh=mesh,
        in_specs=(spread, lines, rows, rows, rows, rows, lines, lines, rows, rows, rows, lines, rows)
        + (P(), P(), P(), P(None, None, "batch", None, None)),
        out_specs=(spread, spread, lines, rows, rows, rows, rows, lines, lines)
        + (rows, rows, rows, lines, rows),
        check_vma=False,
    )
```

```python
import functools
import math

import jax
import jax.numpy as jnp
import numpy as np
from jax import lax
from jax.experimental import pallas as pl
from jax.experimental.pallas import tpu as pltpu
from jax.sharding import PartitionSpec as P

H = 12
DH = 64
BUCKETS = 32
MAX_DIST = 128
DLEN = 128
QLEN = 32
GROUPS = DLEN // QLEN
MICRO = 2
ROWS = MICRO * DLEN
D = 768
FF = 2048
HALF = FF // 2
SHARDS = 8
PIECE_A = 208
PIECE_F = 576
FIRST_A, REST_A = (3, 7), (6, 2, 5, 1, 4, 0)
GROUPS_F = ((6, 7, 2, 3), (4, 5, 0, 1))

EPSILON = 1e-06
HIGHEST = lax.Precision.HIGHEST
BF = jnp.bfloat16
F32 = jnp.float32
EVERY = ("stream", "batch")
MIB = 2**20
ROUND_FLOPS = 5 * 10**10


def distance_bucket(distance):
    half_count = BUCKETS // 2
    exact_count = half_count // 2
    if distance < exact_count:
        return distance
    grown = exact_count + int(
        math.floor(
            math.log(distance / exact_count)
            / math.log(MAX_DIST / exact_count)
            * (half_count - exact_count)
            + 1e-09
        )
    )
    return min(grown, half_count - 1)


def bucket_onehot():
    table = np.zeros((2 * DLEN, BUCKETS), np.float32)
    for o in range(2 * DLEN - 1):
        offset = o - (DLEN - 1)
        table[o, distance_bucket(abs(offset)) + (BUCKETS // 2 if offset > 0 else 0)] = 1.0
    return table


def norm_scale(values):
    return lax.rsqrt(jnp.mean(values * values, axis=-1, keepdims=True) + EPSILON)


def norm_backward(values, gain, grad):
    scale = norm_scale(values)
    pulled = gain * grad
    inner = jnp.mean(values * pulled, axis=-1, keepdims=True)
    back = scale * pulled - values * (scale * scale * scale * inner)
    return back, jnp.sum(grad * values * scale, axis=0, keepdims=True)


def dot(left, right):
    return jnp.dot(left, right, preferred_element_type=F32)


def dot_nt(left, right):
    return lax.dot_general(left, right, (((1,), (1,)), ((), ())), preferred_element_type=F32)


def dot_tn(left, right):
    return lax.dot_general(left, right, (((0,), (0,)), ((), ())), preferred_element_type=F32)


def steps(count, body):
    if count <= 16:
        for i in range(count):
            body(i)
    else:

        @pl.loop(0, count)
        def _(i):
            body(i)


VMEM = pl.BlockSpec(memory_space=pltpu.VMEM)
SMEM = pl.BlockSpec(memory_space=pltpu.SMEM)
HBM = pl.BlockSpec(memory_space=pltpu.HBM)


def positions():
    pairs = lax.axis_size("stream") // 2
    stream = lax.axis_index("stream")
    return lax.axis_index("batch"), stream // pairs, stream % pairs, jnp.where(stream < pairs, 1, 0)


def body_kernel(kernel, lazy, counts, *refs):
    parts = []
    for count in counts:
        parts.append(refs[:count])
        refs = refs[count:]
    arrays, far, outs, far_outs, held, made, scratch = parts
    in_sems, out_sems = refs
    for i, (array, place) in enumerate(zip(arrays, held)):
        pltpu.make_async_copy(array, place, in_sems.at[i]).start()
    sent = set()

    def ready():
        for i, (array, place) in enumerate(zip(arrays, held)):
            pltpu.make_async_copy(array, place, in_sems.at[i]).wait()

    def send(*results):
        for i in results:
            sent.add(i)
            pltpu.make_async_copy(made[i], outs[i], out_sems.at[i]).start()

    if not lazy:
        ready()
    kernel((*positions(), ready, send), *held, *far, *made, *far_outs, *scratch)
    send(*(i for i in range(len(outs)) if i not in sent))
    for i, (place, out) in enumerate(zip(made, outs)):
        pltpu.make_async_copy(place, out, out_sems.at[i]).wait()


def near_kernel(kernel, *refs):
    kernel(positions(), *refs)


def call(
    kernel,
    name,
    arrays,
    outs,
    scratch=(),
    far=(),
    far_outs=(),
    sems=0,
    flops=0,
    limit=59,
    near=False,
    lazy=False,
):
    shapes = [jax.ShapeDtypeStruct(s, t) for s, t in (*outs, *far_outs)]
    moved = sum(math.prod(s.shape) * s.dtype.itemsize for s in shapes)
    moved += sum(math.prod(a.shape) * a.dtype.itemsize for a in (*arrays, *far))
    spaces = [pltpu.VMEM(s, t) for s, t in scratch]
    if sems:
        spaces.append(pltpu.SemaphoreType.DMA((sems,)))
    kind = VMEM if near else HBM
    if near:
        body = functools.partial(near_kernel, kernel)
    else:
        counts = (len(arrays), len(far), len(outs), len(far_outs))
        counts += (len(arrays), len(outs), len(spaces))
        body = functools.partial(body_kernel, kernel, lazy, counts)
        spaces = (
            [pltpu.VMEM(a.shape, a.dtype) for a in arrays]
            + [pltpu.VMEM(s, t) for s, t in outs]
            + spaces
            + [pltpu.SemaphoreType.DMA((max(1, len(part)),)) for part in (arrays, outs)]
        )
    return pl.pallas_call(
        body,
        name=name,
        out_shape=shapes,
        in_specs=[kind] * len(arrays) + [HBM] * len(far),
        out_specs=[kind] * len(outs) + [HBM] * len(far_outs),
        scratch_shapes=spaces,
        compiler_params=pltpu.CompilerParams(vmem_limit_bytes=limit * MIB),
        cost_estimate=pl.CostEstimate(flops=flops, bytes_accessed=moved, transcendentals=0),
    )(*arrays, *far)


def tick_kernel(token, out):
    pass


def tick(token):
    return pl.pallas_call(
        tick_kernel,
        name="tick",
        in_specs=[HBM],
        out_specs=HBM,
        out_shape=jax.ShapeDtypeStruct(token.shape, token.dtype),
        input_output_aliases={0: 0},
        cost_estimate=pl.CostEstimate(flops=ROUND_FLOPS, bytes_accessed=0, transcendentals=0),
    )(token)


def add_kernel(plan, near, far, ids, *refs):
    near, far, refs = refs[:near], refs[near : near + far], refs[near + far :]
    outs, refs = refs[: len(plan)], refs[len(plan) :]
    held, sems = (refs[:-1], refs[-1]) if far else ((), None)
    place = 0
    for entries in plan:
        for terms in entries:
            for is_far, array, entry in terms:
                if is_far:
                    copies([(far[array].at[entry], held[place])], sems.at[place])
                    place += 1
    place = 0
    for out, entries in zip(outs, plan):
        for i, terms in enumerate(entries):
            total = None
            for is_far, array, entry in terms:
                if is_far:
                    landed(held[place], sems.at[place])
                    part = held[place][...].astype(F32)
                    place += 1
                else:
                    part = near[array][entry].astype(F32)
                total = part if total is None else total + part
            out[i] = total.astype(BF)


def base_kernel(picks, whole, ids, own, rest, out, left, right, sems):
    for i, m in enumerate(picks):
        part = rest.at[m if whole else i]
        copies([(own.at[m], left.at[i]), (part, right.at[i])], sems.at[i])
    for i in range(len(picks)):
        landed(left.at[i], sems.at[i])
        landed(right.at[i], sems.at[i])
        left[i] = (left[i].astype(F32) + right[i].astype(F32)).astype(BF)
        copies([(left.at[i], out.at[i])], sems.at[i])
    for i in range(len(picks)):
        landed(left.at[i], sems.at[i])


def base_up(own, rest, picks):
    picks = tuple(picks)
    shape = ((len(picks), *rest.shape[1:]), BF)
    (base,) = call(
        functools.partial(base_kernel, picks, rest.shape[0] > len(picks)),
        "base_up",
        [],
        [],
        [shape, shape],
        far=[own, rest],
        far_outs=[shape],
        sems=len(picks),
    )
    return base


def add_up(*outputs, limit=24):
    known = ([], [])
    plan, flat, shapes = [], [], []
    for entries in outputs:
        plan.append([])
        for terms in entries:
            plan[-1].append([])
            for array, entry in terms:
                is_far = int(array.shape[0] > 4)
                arrays = known[is_far]
                found = [i for i, other in enumerate(arrays) if other is array]
                if not found:
                    arrays.append(array)
                    found = [len(arrays) - 1]
                if is_far:
                    flat.append((array.shape[1:], BF))
                plan[-1][-1].append((is_far, found[0], entry))
        shapes.append(((len(entries), *entries[0][0][0].shape[1:]), BF))
    return call(
        functools.partial(add_kernel, plan, len(known[0]), len(known[1])),
        "add_up",
        known[0],
        shapes,
        flat,
        far=known[1],
        sems=len(flat),
        limit=limit,
        near=True,
    )


def pack_kernel(ids, g1, g2, g3, table, wq, wk, wv, wo, wg, wu, wd, wp, slab_a, slab_f, sems):
    y, core, ready, send = ids[1], ids[2], ids[4], ids[5]

    def fill(top, bottom, wide, rank):
        for yy in range(2):

            @pl.when(y == yy)
            def _():
                pairs = []
                for k in range(4):
                    lanes = pl.ds(yy * HALF + k * 256, 256)
                    pairs.append((wide.at[:, lanes], slab_f.at[pl.ds(k * 96, 96)]))
                rows = pl.ds((2 * yy + rank) * 64, 64)
                for k in range(3):
                    part = wd.at[rows, pl.ds(k * 256, 256)]
                    pairs.append((part, slab_f.at[pl.ds(384 + k * 64, 64)]))
                copies(pairs, sems.at[0])

        pairs = [(top, slab_a.at[pl.ds(0, 96)]), (bottom, slab_a.at[pl.ds(96, 96)])]
        copies(pairs, sems.at[1])

    @pl.when(core == 0)
    def _():
        fill(wq, wv, wg, 0)
        for k in range(6):
            place = slab_a.at[pl.ds(192, 16), pl.ds(k * DLEN, DLEN)]
            copies([(wp.at[pl.ds(k * 16, 16)], place)], sems.at[1])

    @pl.when(core == 1)
    def _():
        fill(wk, wo, wu, 1)

    ready()
    landed(slab_f, sems.at[0])
    send(1)

    @pl.when(core == 0)
    def _():
        landed(slab_a, sems.at[1])

    @pl.when(core == 1)
    def _():
        rows = [g1[...].astype(F32), g2[...].astype(F32), g3[...].astype(F32)]
        head = jnp.concatenate(rows + [jnp.zeros((5, 96), F32)], axis=0)
        tail = jnp.concatenate([table[...].astype(F32), jnp.zeros((7, 48), F32)], axis=0)
        tail = jnp.concatenate([tail, jnp.zeros((8, 48), F32)], axis=1)
        both = jnp.concatenate([head, tail], axis=0)
        slab_a[192:208, :] = jnp.concatenate(
            [both, jnp.zeros((16, D - 96), F32)], axis=1
        ).astype(BF)
        landed(slab_a.at[pl.ds(0, 192)], sems.at[1])


def copies(pairs, sem):
    for src, dst in pairs:
        pltpu.make_async_copy(src, dst, sem).start()


def landed(buffer, sem):
    pltpu.make_async_copy(buffer, buffer, sem).wait()


def fetch_a(ids, pieces, spots, wqk, wvo, extra, sems):
    b, core = ids[0], ids[2]
    for cflip, m, array, entry in spots:
        src = pieces[array].at[entry]
        c, j = core ^ cflip, b ^ m
        row = pl.multiple_of(j * 96, 96)
        copies([(src.at[pl.ds(0, 96)], wqk.at[c, pl.ds(row, 96)])], sems.at[0])
        copies([(src.at[pl.ds(96, 96)], wvo.at[c, pl.ds(row, 96)])], sems.at[1])
        copies([(src.at[pl.ds(192, 16)], extra.at[c, j])], sems.at[2])


def fetch_wide(ids, pieces, spots, wgu, sems):
    b, y, core = ids[0], ids[1], ids[2]
    for yflip, cflip, m, array, entry in spots:
        src = pieces[array].at[entry]
        c, yy, j = core ^ cflip, y ^ yflip, b ^ m
        row = pl.multiple_of(j * 96, 96)
        for k in range(4):
            tile = wgu.at[c, yy, pl.ds(row, 96), pl.ds(k * 256, 256)]
            copies([(src.at[pl.ds(k * 96, 96)], tile)], sems.at[2 * yy + c])


def fetch_deep(ids, pieces, spots, wd, sem):
    b, y, core = ids[0], ids[1], ids[2]
    for yflip, cflip, m, array, entry in spots:
        src = pieces[array].at[entry]
        low = pl.multiple_of((b ^ m) * 256 + (2 * (y ^ yflip) + (core ^ cflip)) * 64, 64)
        for k in range(3):
            tile = wd.at[pl.ds(low, 64), pl.ds(k * 256, 256)]
            copies([(src.at[pl.ds(384 + k * 64, 64)], tile)], sem)


def head_masks():
    low_lane = lax.broadcasted_iota(jnp.int32, (DLEN, DLEN), 1) < DH
    return low_lane


def both_heads(pair, low_lane):
    zero = jnp.zeros_like(pair)
    return jnp.concatenate(
        [jnp.where(low_lane, pair, zero), jnp.where(low_lane, zero, pair)], axis=0
    )


PAIRS_OF_HEADS = [
    (m, p, slice(m * DLEN, (m + 1) * DLEN), slice(p * DLEN, (p + 1) * DLEN))
    for m in range(MICRO)
    for p in range(H // 2)
]


def attention_forward_kernel(direct, spots, ids, x, mask, onehot, *refs):
    if direct:
        count = 1 + max(spot[2] for spot in spots)
        pieces, refs = refs[:count], refs[count:]
        qkv, attended, weights, first, n1, n2, gains, wproj, wqk_out, wvo_out = refs[:10]
        wqk, wvo, extra, bias, scores, sems = refs[10:]
        fetch_a(ids, pieces, spots, wqk, wvo, extra, sems)
        ids[4]()
        landed(extra, sems.at[2])
        lane = lax.broadcasted_iota(jnp.int32, (8, D), 1)
        all_gains = jnp.zeros((8, D), F32)
        flat = jnp.zeros((8, D), F32)
        for j in range(SHARDS):
            block = extra[1, j].astype(F32)
            all_gains += pltpu.roll(jnp.where(lane < 96, block[0:8], 0.0), j * 96, 1)
            flat += pltpu.roll(jnp.where(lane < 48, block[8:16], 0.0), j * 48, 1)
            for k in range(6):
                wproj[j * 96 + k * 16 : j * 96 + (k + 1) * 16, :] = extra[
                    0, j, :, k * DLEN : (k + 1) * DLEN
                ]
        gains[...] = all_gains
        ids[5](6, 7)
        flat = flat[0:1, : BUCKETS * H]
    else:
        ids[4]()
        gains, flat_in, wqk, wvo = refs[:4]
        qkv, attended, weights, first, n1, n2, bias, scores = refs[4:]
        flat = flat_in[...].astype(F32)
    entry = lax.broadcasted_iota(jnp.int32, (16, BUCKETS * H), 1)
    head = lax.broadcasted_iota(jnp.int32, (16, BUCKETS * H), 0)
    by_head = jnp.where(entry % H == head, jnp.broadcast_to(flat, entry.shape), 0.0)
    offsets = dot(by_head.astype(BF), onehot[...])
    for h in range(H):
        row = jnp.broadcast_to(offsets[h : h + 1, :], (DLEN, 2 * DLEN))
        rolled = pltpu.roll(row, DLEN + 1, 1, stride=1, stride_axis=0)
        bias[h // 2, (h % 2) * DLEN : (h % 2 + 1) * DLEN, :] = rolled[:, :DLEN]
    tokens = x[...].astype(F32)
    normed = (tokens * norm_scale(tokens) * gains[0:1, :]).astype(BF)
    n1[...] = normed
    if direct:
        landed(wqk, sems.at[0])
        copies([(wqk, wqk_out)], sems.at[0])
        landed(wvo, sems.at[1])
        copies([(wvo, wvo_out)], sems.at[1])
    qkv[0] = dot(normed, wqk[0]).astype(BF)
    qkv[1] = dot(normed, wqk[1]).astype(BF)
    qkv[2] = dot(normed, wvo[0]).astype(BF)
    ids[5](0, 4)
    low_lane = head_masks()
    for i, (m, p, rows, lanes) in enumerate(PAIRS_OF_HEADS):
        scores[i] = dot_nt(both_heads(qkv[0, rows, lanes], low_lane), qkv[1, rows, lanes])
    for i, (m, p, rows, lanes) in enumerate(PAIRS_OF_HEADS):
        hidden = jnp.concatenate([mask[m], mask[m]], axis=0)
        biased = scores[i] + bias[p] + hidden
        shifted = jnp.exp(biased - jnp.max(biased, axis=-1, keepdims=True))
        weights[m, p] = (shifted / jnp.sum(shifted, axis=-1, keepdims=True)).astype(BF)
    ids[5](2)
    for i, (m, p, rows, lanes) in enumerate(PAIRS_OF_HEADS):
        mixed = dot(weights[m, p], qkv[2, rows, lanes])
        attended[rows, lanes] = jnp.where(low_lane, mixed[:DLEN], mixed[DLEN:]).astype(BF)
    ids[5](1)
    x1 = tokens + dot(attended[...], wvo[1])
    first[...] = x1
    ids[5](3)
    n2[...] = (x1 * norm_scale(x1) * gains[1:2, :]).astype(BF)
    if direct:
        landed(wqk, sems.at[0])
        landed(wvo, sems.at[1])


def gelu_parts(gate):
    c0, c1 = math.sqrt(2.0 / math.pi), 0.044715
    square = gate * gate
    bent = jnp.tanh(c0 * gate * (1.0 + c1 * square))
    value = 0.5 * gate * (1.0 + bent)
    slope = 0.5 * (1.0 + bent) + 0.5 * gate * (1.0 - bent * bent) * (
        c0 * (1.0 + 3.0 * c1 * square)
    )
    return value, slope


def ffn_forward_kernel(direct, spots, ids, first, n2, gains, wproj, *refs):
    if direct:
        count = 1 + max(spot[3] for spot in spots)
        pieces, refs = refs[:count], refs[count:]
        second, n3, vectors, gelu_out, slope_out, hidden_out = refs[1:7]
        wgu, wd, gelu_kept, slope_kept, hidden, sems = refs[7:]
        fetch_wide(ids, pieces, spots, wgu, sems)
    else:
        wgu, wd, second, n3, vectors, gelu_kept, slope_kept, hidden = refs
    ids[4]()
    normed = n2[...]
    for step in range(2):
        half = (ids[1] ^ step) if direct else step
        if direct:
            landed(wgu.at[0, half], sems.at[2 * half])
            landed(wgu.at[1, half], sems.at[2 * half + 1])
        gate = dot(normed, wgu[0, half])
        up = dot(normed, wgu[1, half])
        value, slope = gelu_parts(gate)
        gelu_kept[half] = value.astype(BF)
        slope_kept[half] = (up * slope).astype(BF)
        hidden[half] = (value * up).astype(BF)
        if direct and step == 0:
            fetch_deep(ids, pieces, spots, wd, sems.at[4])
        if direct:
            copies([(gelu_kept.at[half], gelu_out.at[half])], sems.at[2 * half])
            copies([(slope_kept.at[half], slope_out.at[half])], sems.at[2 * half + 1])
    if direct:
        landed(wd, sems.at[4])
        copies([(hidden, hidden_out)], sems.at[4])
    total = first[...] + dot(hidden[0], wd[:HALF, :]) + dot(hidden[1], wd[HALF:, :])
    second[...] = total
    ids[5](0)
    normed_three = (total * norm_scale(total) * gains[2:3, :]).astype(BF)
    n3[...] = normed_three
    ids[5](1)
    vectors[...] = dot(normed_three, wproj[...]).astype(BF)
    if direct:
        for half in range(2):
            landed(gelu_kept.at[half], sems.at[2 * half])
            landed(slope_kept.at[half], sems.at[2 * half + 1])
        landed(hidden, sems.at[4])


def count_kernel(ids, picks, counts):
    spots = lax.broadcasted_iota(jnp.int32, (DLEN, DLEN), 0)

    def one(j):
        for m in range(MICRO):
            total = jnp.zeros((DLEN, DLEN), F32)
            for t in range(picks.shape[2]):
                total += jnp.where(spots == picks[m, j, t : t + 1, :], 1.0, 0.0)
            counts[m, j] = total

    steps(picks.shape[1], one)


def block_of(others, m):
    return others[m % 2].at[m // 2] if len(others) == 2 else others[0].at[m]


def group_sums(values):
    lane = lax.broadcasted_iota(jnp.int32, values.shape, 1)
    shift = 1
    while shift < QLEN:
        ahead = pltpu.roll(values, DLEN - shift, 1)
        behind = pltpu.roll(values, shift, 1)
        values = values + jnp.where((lane & shift) == 0, ahead, behind)
        shift *= 2
    return values


def similarity_kernel(direct, count, ids, own, counts, share, *refs):
    others, (soft, score, best) = refs[:-3], refs[-3:]
    b, is_query = ids[0], ids[3]
    scale = DLEN**-0.5

    def one(m):
        j = (b ^ m) if direct else m
        for micro in range(MICRO):
            rows = slice(micro * DLEN, (micro + 1) * DLEN)
            mine, theirs = own[0, rows, :], block_of(others, m)[rows, :]
            doc = jnp.where(is_query == 1, theirs, mine)
            query = jnp.where(is_query == 1, mine, theirs)
            times = counts[micro, j]
            sim = dot_nt(doc, query) * scale
            peak = jnp.max(jnp.where(times > 0, sim, -jnp.inf), axis=0, keepdims=True)
            mass = jnp.where(times > 0, times * jnp.exp(jnp.minimum(sim - peak, 0.0)), 0.0)
            total = jnp.sum(mass, axis=0, keepdims=True)
            soft[micro, j] = mass / total
            best[micro, pl.ds(j, 1), :] = peak + jnp.log(total)

    steps(count, one)
    for micro in range(MICRO):
        score[micro] = group_sums(best[micro] * share[micro])


def vector_grad_kernel(
    direct, count, ids, soft, share, sharp, target, score, scores, *refs
):
    others, (grad, weight, total) = refs[:-3], refs[-3:]
    b, is_query = ids[0], ids[3]
    scale = DLEN**-0.5

    @pl.when(is_query == 1)
    def _():
        for micro in range(MICRO):
            logits = score[micro] * sharp[micro]
            raised = jnp.exp(logits - jnp.max(logits, axis=0, keepdims=True))
            odds = raised / jnp.sum(raised, axis=0, keepdims=True)
            doc = lax.broadcasted_iota(jnp.int32, (count, DLEN), 0)
            hit = jnp.where(target[micro] == doc, 1.0, 0.0)
            weight[micro] = (odds - hit) * sharp[micro] * share[micro] * scale

    @pl.when(is_query == 0)
    def _():
        for micro in range(MICRO):
            sharpness = sharp[micro]
            logits = scores[:, micro] * sharpness[None]
            peak = jnp.max(logits, axis=0)
            norm = jnp.sum(jnp.exp(logits - peak[None]), axis=0)
            odds = jnp.exp(score[micro] * sharpness - peak) / norm
            hit = jnp.where(target[micro] == b, 1.0, 0.0)
            weight[micro] = (odds - hit) * sharpness * share[micro] * scale

    def parts(m, micro):
        j = (b ^ m) if direct else m
        dense = soft[micro, j] * weight[micro, pl.ds(j, 1), :]
        upper = dense.astype(BF)
        lower = (dense - upper.astype(F32)).astype(BF)
        return upper, lower, block_of(others, m)[micro * DLEN : (micro + 1) * DLEN, :]

    for flag, product in ((1, dot_tn), (0, dot)):

        @pl.when(is_query == flag)
        def _():
            for micro in range(MICRO):
                rows = slice(micro * DLEN, (micro + 1) * DLEN)
                if count <= 16:
                    sums = []
                    for m in range(count):
                        upper, lower, theirs = parts(m, micro)
                        sums.append(product(upper, theirs) + product(lower, theirs))
                    grad[rows, :] = sum(sums[1:], sums[0]).astype(BF)
                else:
                    total[rows, :] = jnp.zeros((DLEN, DLEN), F32)

                    @pl.loop(0, count)
                    def _(m):
                        upper, lower, theirs = parts(m, micro)
                        total[rows, :] += product(upper, theirs) + product(lower, theirs)

                    grad[rows, :] = total[rows, :].astype(BF)


def ffn_backward_kernel(direct, spots, ids, dvec, second, n2, n3, gains, wproj, *refs):
    if direct:
        hidden_in, gelu_in, slope_in = refs[:3]
        count = 1 + max(spot[3] for spot in spots)
        pieces, refs = refs[3 : 3 + count], refs[3 + count :]
        dx2_out, grad_proj, grad_gain, dgu, *outs = refs[:10]
        wd, hidden, gelu_kept, slope_kept, grad_down, quarters, sems = refs[10:]
        fetch_deep(ids, pieces, spots, wd, sems.at[0])
        copies([(slope_in, slope_kept)], sems.at[1])
        copies([(gelu_in, gelu_kept)], sems.at[2])
        copies([(hidden_in, hidden)], sems.at[3])
    else:
        wd, hidden, gelu_kept, slope_kept, dx2_out, grad_proj, grad_gain, dgu, dy_out = refs
    b, y, core, _, ready, send = ids
    ready()
    dvectors = dvec[...]
    dn3 = dot_nt(dvectors, wproj[...])
    dx2, dgain3 = norm_backward(second[...], gains[2:3, :], dn3)
    dx2_out[...] = dx2
    grad_gain[...] = dgain3
    send(0, 2)
    grad_proj[...] = dot_tn(n3[...], dvectors)
    send(1)
    dy = dx2.astype(BF)
    if direct:
        landed(wd, sems.at[0])
    dh = dot_nt(dy, wd[...])
    if direct:
        landed(slope_kept, sems.at[1])
        landed(gelu_kept, sems.at[2])
    for half in range(2):
        part = dh[:, half * HALF : (half + 1) * HALF]
        dgu[0, half] = (part * slope_kept[half].astype(F32)).astype(BF)
        dgu[1, half] = (part * gelu_kept[half].astype(F32)).astype(BF)
    send(3)
    if not direct:
        dy_out[...] = dy
        return
    landed(hidden, sems.at[3])
    normed = n2[...]
    wide_rows, deep_rows = pl.ds(0, 384), pl.ds(384, 192)

    def leave(place, rows):
        if place % 2:
            for group, out in zip(GROUPS_F, outs[1 + place : 3 + place]):
                for i, m in enumerate(group):
                    copies([(quarters.at[place, m, rows], out.at[i, rows])], sems.at[place])
        else:
            copies([(quarters.at[place, :, rows], outs[place // 2].at[:, rows])], sems.at[place])

    for place in (3, 2, 1, 0):
        c, yy = core ^ (place // 2), y ^ (place % 2)
        piece = dot_tn(normed, dgu[c, yy]).astype(BF)
        for j in range(SHARDS):
            for k in range(4):
                quarters[place, b ^ j, k * 96 : (k + 1) * 96, :] = piece[
                    j * 96 : (j + 1) * 96, k * 256 : (k + 1) * 256
                ]
        leave(place, wide_rows)
    for j in range(SHARDS):
        start = (j % 4) * 256
        down = dot_tn(hidden[j // 4, :, start : start + 256], dy).astype(BF)
        for part in range(4):
            grad_down[j, part] = down[part * 64 : (part + 1) * 64, :]
    for place in (3, 2, 1, 0):
        c, yy = core ^ (place // 2), y ^ (place % 2)
        for j in range(SHARDS):
            down = grad_down[j, 2 * yy + c]
            for k in range(3):
                quarters[place, b ^ j, 384 + k * 64 : 384 + (k + 1) * 64, :] = down[
                    :, k * 256 : (k + 1) * 256
                ]
        leave(place, deep_rows)
    for place in range(4):
        landed(quarters.at[place], sems.at[place])


def middle_backward_kernel(direct, spots, ids, dx2, first, dgu, gains, *refs):
    if direct:
        count = 1 + max(spot[3] for spot in spots)
        pieces, refs = refs[:count], refs[count:]
        wvo_in, dx1_out, dattended, grad_gain, wgu, wout, sems = refs
        fetch_wide(ids, pieces, spots, wgu, sems)
        copies([(wvo_in.at[1], wout)], sems.at[4])
    else:
        wgu, wvo, dx1_out, dattended, grad_gain = refs
        wout = wvo.at[1]
    ids[4]()
    dn2 = jnp.zeros((ROWS, D), F32)
    for half in range(2):
        for c in range(2):
            if direct:
                landed(wgu.at[c, half], sems.at[half * 2 + c])
            dn2 = dn2 + dot_nt(dgu[c, half], wgu[c, half])
    back, dgain2 = norm_backward(first[...], gains[1:2, :], dn2)
    dx1 = dx2[...] + back
    dx1_out[...] = dx1
    grad_gain[...] = dgain2
    ids[5](0, 2)
    if direct:
        landed(wout, sems.at[4])
    dattended[...] = dot_nt(dx1.astype(BF), wout[...]).astype(BF)


def attention_backward_kernel(
    direct,
    ids,
    grad_first,
    dattended,
    x,
    n1,
    attended,
    weights,
    qkv,
    gains,
    bucket,
    grad_proj,
    grad_gain2,
    grad_gain3,
    *refs,
):
    if direct:
        wqk_in, wvo_in, grad_in, *outs = refs[:7]
        wqk, wvo, own, other, left, right, dqk, extra, *refs = refs[7:]
        copies([(wvo_in.at[0], wvo.at[0])], refs[-1].at[0])
        copies([(wqk_in, wqk)], refs[-1].at[1])
    else:
        wqk, wvo, small, grad_in, dqkv_out, da_out, left, right, dqk, *refs = refs
    diag, bias_grad, dshares, scaled, queries, douts, *rest = refs
    b, core = ids[0], ids[2]
    ids[4]()
    dx1 = grad_first[...]
    da = dx1.astype(BF)
    low_lane = head_masks()
    row_at = lax.broadcasted_iota(jnp.int32, (DLEN, MICRO * DLEN), 0)
    lane_at = lax.broadcasted_iota(jnp.int32, (DLEN, MICRO * DLEN), 1)
    mirror = jnp.where(row_at == DLEN - 1 - lane_at % DLEN, 1.0, 0.0).astype(BF)
    diag[...] = jnp.zeros_like(diag)
    for i, (m, p, rows, lanes) in enumerate(PAIRS_OF_HEADS):
        queries[i] = both_heads(qkv[0, rows, lanes], low_lane)
        douts[i] = both_heads(dattended[rows, lanes], low_lane)
    for i, (m, p, rows, lanes) in enumerate(PAIRS_OF_HEADS):
        dshares[i] = dot_nt(douts[i], qkv[2, rows, lanes])
        right[0, rows, lanes] = dot_tn(weights[m, p], douts[i]).astype(BF)
    for i, (m, p, rows, lanes) in enumerate(PAIRS_OF_HEADS):
        wide = weights[m, p].astype(F32)
        dshare = dshares[i]
        centre = jnp.sum(wide * dshare, axis=-1, keepdims=True)
        scaled[i] = (wide * (dshare - centre)).astype(BF)
    for i, (m, p, rows, lanes) in enumerate(PAIRS_OF_HEADS):
        dq = dot(scaled[i], qkv[1, rows, lanes])
        dqk[0, rows, lanes] = jnp.where(low_lane, dq[:DLEN], dq[DLEN:]).astype(BF)
        dqk[1, rows, lanes] = dot_tn(scaled[i], queries[i]).astype(BF)
    for h in range(H):
        part = slice((h % 2) * DLEN, (h % 2 + 1) * DLEN)
        both = jnp.concatenate([scaled[m * (H // 2) + h // 2, part] for m in range(MICRO)], axis=0)
        turned = dot(mirror, both)
        wider = jnp.concatenate([turned, jnp.zeros_like(turned)], axis=1)
        rolled = pltpu.roll(wider, 0, 1, stride=1, stride_axis=0)
        diag[h : h + 1, :] = jnp.sum(rolled, axis=0, keepdims=True)
    bias_grad[...] = lax.dot_general(
        bucket[...],
        diag[...],
        (((1,), (1,)), ((), ())),
        precision=HIGHEST,
        preferred_element_type=F32,
    )
    if direct:
        sems = rest[0]
        landed(wvo.at[0], sems.at[0])
        landed(wqk, sems.at[1])
    dn1 = dot_nt(dqk[0], wqk[0]) + dot_nt(dqk[1], wqk[1]) + dot_nt(right[0], wvo[0])
    dx, dgain1 = norm_backward(x[...].astype(F32), gains[0:1, :], dn1)
    grad_in[...] = dx1 + dx
    if direct:
        ids[5](0)
    right[1] = da
    left[0] = n1[...]
    left[1] = attended[...]
    all_gains = jnp.concatenate(
        [dgain1, grad_gain2[...], grad_gain3[...], jnp.zeros((5, D), F32)], axis=0
    )
    if not direct:
        small[0:8, :] = all_gains
        small[8:40, :] = jnp.concatenate(
            [bias_grad[...], jnp.zeros((BUCKETS, D - DLEN), F32)], axis=1
        )
        dqkv_out[0] = dqk[0]
        dqkv_out[1] = dqk[1]
        dqkv_out[2] = right[0]
        da_out[...] = da
        return
    per_shard = BUCKETS // SHARDS
    for j in range(SHARDS):
        for k in range(6):
            extra[0, j, :, k * DLEN : (k + 1) * DLEN] = grad_proj[
                j * 96 + k * 16 : j * 96 + (k + 1) * 16, :
            ]
        extra[1, j] = jnp.zeros((16, D), F32)
        extra[1, j, 0:8, :] = pltpu.roll(all_gains, (D - j * 96) % D, 1)
        extra[1, j, 8 : 8 + per_shard, 0:DLEN] = bias_grad[j * per_shard : (j + 1) * per_shard, :]
    for flip, out in ((1, other), (0, own)):
        c = core ^ flip
        top = dot_tn(n1[...], dqk[c]).astype(BF)
        bottom = dot_tn(left[c], right[c]).astype(BF)
        for j in range(SHARDS):
            m = b ^ j
            out[m, 0:96, :] = top[j * 96 : (j + 1) * 96, :]
            out[m, 96:192, :] = bottom[j * 96 : (j + 1) * 96, :]
            out[m, 192:208, :] = extra[c, j].astype(BF)
        for group, target in zip((FIRST_A, REST_A), outs[2 * flip : 2 * flip + 2]):
            copies([(out.at[m], target.at[i]) for i, m in enumerate(group)], sems.at[flip])
    landed(other, sems.at[1])
    landed(own, sems.at[0])


def finish_wide_kernel(ids, near, far, twin, far_twin, token, grad_g, grad_u, grad_d):
    y, core = ids[1], ids[2]
    for yy in range(2):
        for c in range(2):

            @pl.when((y == yy) & (core == c))
            def _():
                for yflip, cflip, part in ((0, 0, near), (1, 0, far), (0, 1, twin), (1, 1, far_twin)):
                    half, rank = yy ^ yflip, c ^ cflip
                    out = grad_u if rank else grad_g
                    for k in range(4):
                        start = half * HALF + k * 256
                        out[:, start : start + 256] = part[0, k * 96 : (k + 1) * 96, :].astype(F32)
                    low = (2 * half + rank) * 64
                    for k in range(3):
                        grad_d[low : low + 64, k * 256 : (k + 1) * 256] = part[
                            0, 384 + k * 64 : 384 + (k + 1) * 64, :
                        ].astype(F32)


def finish_narrow_kernel(
    ids, near, near_far, twin, twin_far, grad_q, grad_k, grad_v, grad_o, grad_p, grad_1, grad_2, grad_3, table
):
    core = ids[2]
    for c in range(2):

        @pl.when(core == c)
        def _():
            pairs = [(near, near_far), (twin, twin_far)]
            low, high = pairs[::-1] if c else pairs

            def summed(pair, rows):
                return pair[0][0, rows, :].astype(F32) + pair[1][0, rows, :].astype(F32)

            grad_q[...] = summed(low, slice(0, 96))
            grad_k[...] = summed(high, slice(0, 96))
            grad_v[...] = summed(low, slice(96, 192))
            grad_o[...] = summed(high, slice(96, 192))
            packed = summed(low, slice(192, 208))
            for k in range(6):
                grad_p[k * 16 : (k + 1) * 16, :] = packed[:, k * DLEN : (k + 1) * DLEN]
            rows = summed(high, slice(192, 208))
            grad_1[...] = rows[0:1, :96]
            grad_2[...] = rows[1:2, :96]
            grad_3[...] = rows[2:3, :96]
            block = jnp.where(lax.broadcasted_iota(jnp.int32, (8, DLEN), 1) < H, rows[8:16, :DLEN], 0.0)
            line = block[0:1]
            for i in range(1, BUCKETS // SHARDS):
                line += pltpu.roll(block, i * H, 1)[i : i + 1]
            table[...] = line[:, : BUCKETS // SHARDS * H]


def local(
    hidden_in,
    norm1_gain,
    w_query,
    w_key,
    w_value,
    w_out,
    rel_table,
    norm2_gain,
    w_gate,
    w_up,
    w_down,
    norm3_gain,
    w_proj,
    query_lengths,
    keyword_request_mask,
    targets,
    candidates,
):
    streams = lax.axis_size("stream")
    shards = lax.axis_size("batch")
    pairs = streams // 2
    direct = shards == SHARDS and pairs == 2
    b = lax.axis_index("batch")
    s = lax.axis_index("stream")
    y, core = s // pairs, s % pairs
    is_query = s < pairs

    def swap(block, yflip, cflip, m):
        route = []
        for source in range(streams):
            target = ((source // pairs) ^ yflip) * pairs + ((source % pairs) ^ cflip)
            for j in range(shards):
                route.append((source * shards + j, target * shards + (j ^ m)))
        return lax.ppermute(block, EVERY, route)

    micro_count = hidden_in.shape[0]
    slot = jnp.arange(DLEN)
    pair_lengths = lax.dynamic_index_in_dim(query_lengths, core, 1, keepdims=False)
    pair_keyword = lax.dynamic_index_in_dim(keyword_request_mask, core, 1, keepdims=False)
    pair_targets = lax.dynamic_index_in_dim(targets, core, 1, keepdims=False)

    def by_slot(values):
        blocks = values.reshape(micro_count, shards, GROUPS)
        own = lax.dynamic_slice_in_dim(blocks, b, 1, 1)
        blocks = jnp.where(is_query, jnp.broadcast_to(own, blocks.shape), blocks)
        return jnp.repeat(blocks, QLEN, axis=2)

    length_slots = by_slot(pair_lengths)
    valid_slots = (slot % QLEN)[None, None, :] < length_slots
    share = jnp.where(valid_slots, 1.0 / length_slots.astype(F32), 0.0)
    sharp = jnp.where(by_slot(pair_keyword) == 1, 20.0, 10.0).astype(F32)
    target_slots = by_slot(pair_targets)
    own_valid = lax.dynamic_slice_in_dim(valid_slots, b, 1, 1)
    same = (slot[:, None] // QLEN) == (slot[None, :] // QLEN)
    mask = jnp.where(is_query & ~(same[None] & own_valid), -1000000000.0, 0.0).astype(F32)

    small = 16 if direct else 48
    picked = lax.dynamic_index_in_dim(candidates, core, 1, keepdims=False)[:, 0]
    picked = picked.reshape(micro_count, shards, DLEN, picked.shape[-1])
    picked = jnp.transpose(picked, (0, 1, 3, 2))
    received = lax.all_to_all(picked, "batch", split_axis=1, concat_axis=1, tiled=True)
    picks = jnp.where(is_query, received, picked)
    (counts,) = call(
        count_kernel,
        "count",
        [picks],
        [((micro_count, shards, DLEN, DLEN), F32)],
        limit=small,
    )

    fence = lax.optimization_barrier
    first_core = core == 0
    spots_a = spots_f = None
    if direct:
        lines = [part.reshape(1, -1) for part in (norm1_gain, norm2_gain, norm3_gain, rel_table)]
        slab_a, slab_f = call(
            pack_kernel,
            "pack",
            lines,
            [((PIECE_A, D), BF), ((PIECE_F, 256), BF)],
            far=[w_query, w_key, w_value, w_out, w_gate, w_up, w_down, w_proj],
            sems=2,
            lazy=True,
        )

        def join(*parts):
            return jnp.concatenate(parts)

        def along_x(part):
            return swap(part, 0, 0, 1)

        def along_y(part):
            return swap(part, 1, 0, 0)

        def along_z(part):
            return swap(part, 0, 0, 2)

        def along_zz(part):
            return swap(part, 0, 0, 4)

        def other_core(part):
            return swap(part, 0, 1, 0)

        f0, a0 = slab_f[None], slab_a[None]
        token = jnp.zeros((8, DLEN), F32)
        f4, f2, y0, f1, a1 = along_zz(f0), along_z(f0), along_y(f0), along_x(f0), along_x(a0)
        token = tick(token)
        f4, f2, y0, f1, a1, a0, token = fence((f4, f2, y0, f1, a1, a0, token))
        f42, f142, token = fence((join(f4, f2), join(f1, f4, f2), token))
        y142, f53, f6, a4, a2 = (
            along_y(f142),
            along_x(f42),
            along_z(f4),
            along_zz(a0),
            along_z(a0),
        )
        token = tick(token)
        f53, f6, counts, mask, share, sharp, target_slots, token = fence(
            (f53, f6, counts, mask, share, sharp, target_slots, token)
        )
        f65, token = fence((join(f6, f53[0:1]), token))
        f7 = along_x(f6)

        a2, token = fence((a2, token))
        a3 = along_x(a2)
        a4, token = fence((a4, token))
        a5, a6 = along_x(a4), along_z(a4)

        y142, f65, token = fence((y142, f65, token))
        y65 = along_y(f65)

        f7, token = fence((f7, token))
        f37, f_all, token = fence((join(f53[1:2], f7), join(f0, f142, f65, f53[1:2], f7), token))
        f_all, token = fence((f_all, token))
        tf_all = other_core(f_all)

        a6, token = fence((a6, token))
        a7 = along_x(a6)
        a0142, token = fence((join(a0, a1, a4, a2), token))
        ta0142 = other_core(a0142)
        y65, f37, token = fence((y65, f37, token))
        y37, ty65 = along_y(f37), other_core(y65)
        token = tick(token)
        a3, a5, tf_all, ta0142, token = fence((a3, a5, tf_all, ta0142, token))
        a536, y_first, token = fence((join(a5, a3, a6), join(y0, y142), token))
        ta536, ty_first = other_core(a536), other_core(y_first)
        a7, token = fence((a7, token))
        ta7 = other_core(a7)
        token = tick(token)
        y37, ta536, ta7, token = fence((y37, ta536, ta7, token))
        ty37 = other_core(y37)

        order_f = (0, 1, 4, 2, 6, 5, 3, 7)
        groups_a = [
            (0, (a0142, (0, 1, 4, 2)), (a536, (5, 3, 6)), (a7, (7,))),
            (1, (ta0142, (0, 1, 4, 2)), (ta536, (5, 3, 6)), (ta7, (7,))),
        ]
        pieces_a, spots_a, pieces_f, spots_f = [], [], [], []
        for cflip, *group in groups_a:
            for part, flips in group:
                spots_a += [(cflip, m, len(pieces_a), i) for i, m in enumerate(flips)]
                pieces_a.append(part)
    else:

        def whole(part):
            return lax.all_gather(part, "batch", axis=0, tiled=True)

        wqk = jnp.stack([whole(w_query), whole(w_key)])
        wvo = jnp.stack([whole(w_value), whole(w_out)])
        gate_up = jnp.stack([whole(w_gate), whole(w_up)])
        wgu = jnp.transpose(gate_up.reshape(2, D, 2, HALF), (0, 2, 1, 3))
        wd = whole(w_down)
        wproj = whole(w_proj)
        gain_rows = [whole(gain) for gain in (norm1_gain, norm2_gain, norm3_gain)]
        gains = jnp.pad(jnp.stack(gain_rows).astype(F32), ((0, 5), (0, 0)))
        table = whole(rel_table).reshape(1, BUCKETS * H)

    onehot = bucket_onehot()
    by_entry = jnp.asarray(np.repeat(onehot.T, H, axis=0), BF)
    x = hidden_in[:, 0].reshape(ROWS, D)
    row_bf, row_f32 = ((ROWS, D), BF), ((ROWS, D), F32)
    qkv_shape, weight_shape = ((3, ROWS, D), BF), ((MICRO, H // 2, ROWS, DLEN), BF)
    pair_weights = ((2, D, D), BF)
    gain_rows = ((8, D), F32)
    proj_shape = ((D, DLEN), BF)
    kept = [qkv_shape, row_bf, weight_shape, row_f32, row_bf, row_bf]
    bias_shape, score_shape = ((H // 2, ROWS, DLEN), F32), ((H, ROWS, DLEN), F32)
    result = call(
        functools.partial(attention_forward_kernel, direct, spots_a),
        "attention_forward",
        [x, mask, by_entry] + ([] if direct else [gains, table, wqk, wvo]),
        kept + ([gain_rows, proj_shape] if direct else []),
        ([pair_weights, pair_weights, ((2, SHARDS, 16, D), BF)] if direct else [])
        + [bias_shape, score_shape],
        far=pieces_a if direct else [],
        far_outs=[pair_weights, pair_weights] if direct else [],
        sems=3 if direct else 0,
        flops=2 * ROWS * D * D * 4,
        lazy=True,
    )
    qkv, attended, weights, first, n1, n2 = result[:6]
    if direct:
        gains, wproj, wqk, wvo = result[6:]
    first, counts, share, sharp, target_slots = fence((first, counts, share, sharp, target_slots))
    if direct:
        ty_first, ty65, ty37, first, token = fence((ty_first, ty65, ty37, first, token))
        near, twin = ((f_all, order_f),), ((tf_all, order_f),)
        far = ((y_first, order_f[:4]), (y65, order_f[4:6]), (y37, order_f[6:]))
        far_twin = ((ty_first, order_f[:4]), (ty65, order_f[4:6]), (ty37, order_f[6:]))
        for yflip, cflip, group in ((0, 0, near), (0, 1, twin), (1, 0, far), (1, 1, far_twin)):
            for part, flips in group:
                spots_f += [(yflip, cflip, m, len(pieces_f), i) for i, m in enumerate(flips)]
                pieces_f.append(part)
    wide_bf = ((2, ROWS, HALF), BF)
    wgu_shape, wd_shape = ((2, 2, D, HALF), BF), ((FF, D), BF)
    lasting = [wide_bf, wide_bf, wide_bf]
    result = call(
        functools.partial(ffn_forward_kernel, direct, spots_f),
        "ffn_forward",
        [first, n2, gains, wproj] + ([] if direct else [wgu, wd]),
        [row_f32, row_bf, ((ROWS, DLEN), BF)] + ([] if direct else lasting),
        [wgu_shape, wd_shape] + lasting if direct else [],
        far=[*pieces_f, token] if direct else [],
        far_outs=lasting if direct else [],
        sems=5 if direct else 0,
        flops=2 * ROWS * D * FF * 3,
        lazy=True,
    )
    second, n3, vectors, gelu_kept, slope_kept, hidden = result

    if direct:
        longest_first = {m: swap(vectors, 1, 0, m) for m in (6, 4, 2, 0)}
        even = jnp.stack([longest_first[m] for m in (0, 2, 4, 6)])
        odd = swap(even, 0, 0, 1)
        own, odd = fence((jnp.stack([vectors, vectors]), odd))
        others = [even, odd]
    else:
        route = [(i, (i + pairs) % streams) for i in range(streams)]
        arrived = lax.ppermute(vectors, "stream", route)
        others = [lax.all_gather(arrived, "batch", axis=0)]
    block_f32 = ((micro_count, shards, DLEN, DLEN), F32)
    line_f32 = ((micro_count, shards, DLEN), F32)
    soft, score = call(
        functools.partial(similarity_kernel, direct, shards),
        "similarity",
        [own if direct else vectors[None], counts, share, *others],
        [block_f32, line_f32],
        [line_f32],
        limit=small,
        near=True,
    )
    if direct:
        blocks = jnp.broadcast_to(score[None], (shards,) + score.shape)
        scores = lax.all_to_all(blocks, "batch", split_axis=0, concat_axis=0, tiled=True)
    else:
        scores = lax.all_gather(score, "batch", axis=0)
    (dvec,) = call(
        functools.partial(vector_grad_kernel, direct, shards),
        "vector_grad",
        [soft, share, sharp, target_slots, score, scores, *others],
        [((ROWS, DLEN), BF)],
        [line_f32, ((ROWS, DLEN), F32)],
        limit=small,
        near=True,
    )

    gain_row = ((1, D), F32)
    proj_f32 = ((D, DLEN), F32)
    dgu_shape = ((2, 2, ROWS, HALF), BF)
    quarter = ((SHARDS, PIECE_F, 256), BF)
    saved = [hidden, gelu_kept, slope_kept]
    result = call(
        functools.partial(ffn_backward_kernel, direct, spots_f),
        "ffn_backward",
        [dvec, second, n2, n3, gains, wproj] + ([] if direct else [wd, *saved]),
        [row_f32, proj_f32, gain_row, dgu_shape] + ([] if direct else [row_bf]),
        [wd_shape, wide_bf, wide_bf, wide_bf, ((SHARDS, 4, 64, D), BF), ((4, *quarter[0]), BF)]
        if direct
        else [],
        far=[*saved, *pieces_f] if direct else [],
        far_outs=[quarter] * 2 + [((4, PIECE_F, 256), BF)] * 4 if direct else [],
        sems=4 if direct else 0,
        flops=2 * ROWS * D * FF * 4,
        lazy=True,
    )
    dx2, grad_proj, grad_gain, dgu = result[:4]
    if direct:
        f_own, f_twin, *f_far = result[4:]
    else:
        dy = result[4]

    if direct:
        def own_f(m, *more):
            group = 0 if m in GROUPS_F[0] else 1
            return [(base_f[group], GROUPS_F[group].index(m)), *more]

        def far_sum(i):
            return [[(f_far[i], n), (c_far[i], n)] for n in range(4)]

        c_far = [other_core(part) for part in f_far[2:]]
        c_far[0], f_twin, dgu = fence((c_far[0], f_twin, dgu))
        twin = other_core(f_twin)
        (sent_a,) = add_up(far_sum(0))
        sent_a, dgu = fence((sent_a, dgu))
        y_a = along_y(sent_a)
    middle_in = [dx2, first, dgu, gains]
    dx1, dattended, grad_gain2 = call(
        functools.partial(middle_backward_kernel, direct, spots_f),
        "middle_backward",
        middle_in + ([] if direct else [wgu, wvo]),
        [row_f32, row_bf, gain_row],
        [wgu_shape, ((D, D), BF)] if direct else [],
        far=[*pieces_f, wvo] if direct else [],
        sems=5 if direct else 0,
        flops=ROUND_FLOPS,
        lazy=True,
    )
    if direct:
        *c_far[1:], twin, dattended = fence((*c_far[1:], twin, dattended))
        (sent_b,) = add_up(far_sum(1))
        base_f = [base_up(f_own, twin, GROUPS_F[0])]
        sent_b, base_f[0], dattended = fence((sent_b, base_f[0], dattended))
    two_rows = ((2, ROWS, D), BF)
    slab_out = ((SHARDS, PIECE_A, D), BF)
    blocks_bf = ((H, ROWS, DLEN), BF)
    result = call(
        functools.partial(attention_backward_kernel, direct),
        "attention_backward",
        [dx1, dattended, x, n1, attended, weights, qkv, gains, jnp.asarray(onehot.T)]
        + [grad_proj, grad_gain2, grad_gain]
        + ([] if direct else [wqk, wvo]),
        [row_f32] if direct else [((40, D), F32), row_f32, qkv_shape, row_bf],
        ([pair_weights, pair_weights, slab_out, slab_out] if direct else [])
        + [two_rows, two_rows, two_rows]
        + ([((2, SHARDS, 16, D), F32)] if direct else [])
        + [((DLEN, 2 * DLEN), F32), ((BUCKETS, DLEN), F32)]
        + [score_shape, blocks_bf, blocks_bf, blocks_bf],
        far=[wqk, wvo] if direct else [],
        far_outs=[((count, PIECE_A, D), BF) for count in (2, 6, 2, 6)] if direct else [],
        sems=2 if direct else 0,
        flops=2 * ROWS * D * D * 7,
        lazy=True,
    )

    if direct:
        input_grad, o_first, o_rest, a_first, a_rest = result

        def own_a(m, *more):
            return [(base_a, REST_A.index(m)), *more]

        o_first, o_rest, a_first, a_rest = fence((o_first, o_rest, a_first, a_rest))
        token = jnp.ones((8, DLEN), F32)
        c_first = other_core(a_first)
        c_first, a_rest, token = fence((c_first, a_rest, token))
        (out_a37,) = add_up([[(o_first, i), (c_first, i)] for i in range(2)])
        out_a37, a_rest, token = fence((out_a37, a_rest, token))
        xa37, c_rest = along_x(out_a37), other_core(a_rest)

        y_a, sent_b, token = fence((y_a, sent_b, token))
        y_b = along_y(sent_b)
        (out_73,) = add_up([own_f(7, (y_a, 1)), own_f(3, (y_a, 3))])
        out_73, token = fence((out_73, token))
        x73 = along_x(out_73)
        token = tick(token)
        c_rest, token = fence((c_rest, token))
        base_a = base_up(o_rest, c_rest, range(len(REST_A)))
        base_f.append(base_up(f_own, twin, GROUPS_F[1]))
        x73, base_a, base_f[1], token = fence((x73, base_a, base_f[1], token))
        (out_62,) = add_up([own_f(6, (y_a, 0), (x73, 0)), own_f(2, (y_a, 2), (x73, 1))])
        out_62, token = fence((out_62, token))
        z62 = along_z(out_62)

        xa37, token = fence((xa37, token))
        out_a51, out_a62 = add_up(
            [own_a(5), own_a(1)], [own_a(6, (xa37, 1)), own_a(2, (xa37, 0))]
        )
        out_a62, token = fence((out_a62, token))
        za62 = along_z(out_a62)

        y_b, token = fence((y_b, token))
        out_5, out_1 = add_up([own_f(5, (y_b, 1))], [own_f(1, (y_b, 3))])
        out_5, token = fence((out_5, token))
        x5 = along_x(out_5)

        x5, z62, token = fence((x5, z62, token))
        (out_4,) = add_up([own_f(4, (y_b, 0), (x5, 0), (z62, 0))])
        out_4, out_a51, out_1, token = fence((out_4, out_a51, out_1, token))
        x1, xa51, z4 = along_x(out_1), along_x(out_a51), along_zz(out_4)

        za62, xa51, token = fence((za62, xa51, token))
        (out_a4,) = add_up([own_a(4, (xa51, 0), (za62, 0))])
        out_a4, token = fence((out_a4, token))
        za4 = along_zz(out_a4)

        x1, z4, token = fence((x1, z4, token))
        (mine_f,) = add_up([own_f(0, (y_b, 2), (x1, 0), (z62, 1), (z4, 0))])
        mine_f, token = fence((mine_f, token))
        far, twin_f = along_y(mine_f), other_core(mine_f)

        za4, token = fence((za4, token))
        (part_a,) = add_up([own_a(0, (xa51, 1), (za62, 1), (za4, 0))])
        part_a, token = fence((part_a, token))
        ya, twin_part = along_y(part_a), other_core(part_a)

        far, twin_f, token = fence((far, twin_f, token))
        far_twin_f = other_core(far)
        ya, far_twin_f, twin_part, token = fence((ya, far_twin_f, twin_part, token))
        twin_ya = other_core(ya)
        shard_f32, wide_f32 = ((96, D), F32), ((96, FF), F32)
        grad_g, grad_u, grad_d = call(
            finish_wide_kernel,
            "finish_wide",
            [mine_f, far, twin_f, far_twin_f],
            [wide_f32, wide_f32, ((256, D), F32)],
            far=[token],
            limit=24,
            near=True,
        )
        grad_q, grad_k, grad_v, grad_o, grad_p, *small = call(
            finish_narrow_kernel,
            "finish_narrow",
            [part_a, ya, twin_part, twin_ya],
            [shard_f32] * 4 + [((96, DLEN), F32), ((1, 96), F32), ((1, 96), F32), ((1, 96), F32)]
            + [((1, 48), F32)],
            limit=24,
            near=True,
        )
        grad_n1, grad_n2, grad_n3, grad_table = [row.reshape(-1) for row in small]
    else:
        small, input_grad, dqkv, da = result

        def summed(part):
            part = lax.psum_scatter(part, "batch", scatter_dimension=0, tiled=True)
            return lax.psum(part, "stream")

        grad_q, grad_k, grad_v = [summed(dot_tn(n1, dqkv[i])) for i in range(3)]
        grad_o = summed(dot_tn(attended, da))
        grad_g, grad_u = [
            summed(jnp.concatenate([dot_tn(n2, dgu[i, half]) for half in range(2)], axis=1))
            for i in range(2)
        ]
        grad_d = summed(jnp.concatenate([dot_tn(hidden[half], dy) for half in range(2)]))
        grad_p = summed(grad_proj)
        grad_n1, grad_n2, grad_n3 = [summed(small[i]) for i in range(3)]
        flat = lax.psum(small[8 : 8 + BUCKETS, :H].reshape(-1), EVERY)
        share_rows = flat.shape[0] // shards
        grad_table = lax.dynamic_slice_in_dim(flat, b * share_rows, share_rows, 0)

    vectors_out = vectors.reshape(micro_count, DLEN, DLEN)[:, None]
    grad_hidden = input_grad.reshape(micro_count, DLEN, D)[:, None]
    return (
        vectors_out,
        grad_hidden,
        grad_n1,
        grad_q,
        grad_k,
        grad_v,
        grad_o,
        grad_table,
        grad_n2,
        grad_g,
        grad_u,
        grad_d,
        grad_n3,
        grad_p,
    )


def solution(mesh):
    rows, lines = P("batch", None), P("batch")
    spread = P(None, "stream", "batch", None)
    return jax.shard_map(
        local,
        mesh=mesh,
        in_specs=(spread, lines, rows, rows, rows, rows, lines, lines, rows, rows, rows, lines, rows)
        + (P(), P(), P(), P(None, None, "batch", None, None)),
        out_specs=(spread, spread, lines, rows, rows, rows, rows, lines, lines)
        + (rows, rows, rows, lines, rows),
        check_vma=False,
    )
```
